32 devices in a mesh: seq: 2 (over x), fsdp: 4 (over z), rep: 4 (over y, core).
Axes of the slice: x: 2, y: 2, z: 4, core: 2. Of those that a mesh axis runs over, the one named last changes fastest.
Arguments:
- tokens: bfloat16 [16, 1024, 1088], P(('fsdp', 'rep'), 'seq'), may hold values from -6 to 6
- segments: int32 [16, 1024], P(('fsdp', 'rep'), 'seq'), may hold values from 0 to 5, as said below
- grad_out: bfloat16 [16, 1024, 1088], P(('fsdp', 'rep'), 'seq'), may hold values from -6 to 6
- attn_gain: bfloat16 [2, 1088], P(None, 'fsdp'), may hold values from 0.099609375 to 1.8984375
- attn_shift: bfloat16 [2, 1088], P(None, 'fsdp'), may hold values from -3 to 3
- w_qkv: bfloat16 [2, 1088, 3264], P(None, 'fsdp'), may hold values from -0.1875 to 0.1875
- b_query: bfloat16 [2, 1088], P(None, 'fsdp'), may hold values from -3 to 3
- b_value: bfloat16 [2, 1088], P(None, 'fsdp'), may hold values from -3 to 3
- w_out: bfloat16 [2, 1088, 1088], P(None, 'fsdp'), may hold values from -0.5 to 0.5
- b_out: bfloat16 [2, 1088], P(None, 'fsdp'), may hold values from -3 to 3
- mlp_gain: bfloat16 [2, 1088], P(None, 'fsdp'), may hold values from 0.099609375 to 1.8984375
- mlp_shift: bfloat16 [2, 1088], P(None, 'fsdp'), may hold values from -3 to 3
- w_up: bfloat16 [2, 1088, 4352], P(None, 'fsdp'), may hold values from -0.1875 to 0.1875
- b_up: bfloat16 [2, 4352], P(None, 'fsdp'), may hold values from -3 to 3
- w_down: bfloat16 [2, 4352, 1088], P(None, 'fsdp'), may hold values from -0.09375 to 0.09375
- b_down: bfloat16 [2, 1088], P(None, 'fsdp'), may hold values from -3 to 3
Outputs:
- result: bfloat16 [16, 1024, 1088], P(('fsdp', 'rep'), 'seq')
- grad_tokens: bfloat16 [16, 1024, 1088], P(('fsdp', 'rep'), 'seq')
- grad_attn_gain: float32 [2, 1088], P(None, 'fsdp')
- grad_attn_shift: float32 [2, 1088], P(None, 'fsdp')
- grad_w_qkv: float32 [2, 1088, 3264], P(None, 'fsdp')
- grad_b_query: float32 [2, 1088], P(None, 'fsdp')
- grad_b_value: float32 [2, 1088], P(None, 'fsdp')
- grad_w_out: float32 [2, 1088, 1088], P(None, 'fsdp')
- grad_b_out: float32 [2, 1088], P(None, 'fsdp')
- grad_mlp_gain: float32 [2, 1088], P(None, 'fsdp')
- grad_mlp_shift: float32 [2, 1088], P(None, 'fsdp')
- grad_w_up: float32 [2, 1088, 4352], P(None, 'fsdp')
- grad_b_up: float32 [2, 4352], P(None, 'fsdp')
- grad_w_down: float32 [2, 4352, 1088], P(None, 'fsdp')
- grad_b_down: float32 [2, 1088], P(None, 'fsdp')
The draws below stay inside these ranges and needn't reach their ends.
Inputs may be any that keep to these rules, and one draw needn't show every extreme that they name: `segments`: within a sequence segment numbers start at 0 and never fall; every document except the last of its sequence has 200 to 1000 tokens.
All inputs are finite; a program needn't handle non-finite values.
Results may differ from the reference program's by a relative error of at most 0.02.
Values may be sent and summed in bfloat16 or wider, within the bound.
A program may use at most 448 MiB of HBM per device.

```python
import math
import jax
import jax.numpy as jnp
from jax import lax

D = 1088
FF = 4352
HEAD_DIM = 64
LAYERS = 2
SEQ_LEN = 1024
SEQS = 16


def draw_segments(key, part):
    least = SEQ_LEN * 25 // 128
    lengths = jax.random.randint(key, (SEQS, 6), least, SEQ_LEN * 125 // 128 + 1)
    first_row = jnp.arange(SEQS, dtype=jnp.int32)[:, None] == 0
    lengths = jnp.where(first_row, jnp.full((SEQS, 6), least, jnp.int32), lengths).astype(jnp.int32)
    boundary = jnp.cumsum(lengths, axis=1)
    places = jnp.arange(SEQ_LEN, dtype=jnp.int32)
    return jnp.sum((places[None, :, None] >= boundary[:, None, :]).astype(jnp.int32), axis=2).astype(jnp.int32)


def steps_of(own_key, shape, split, smallest, largest):
    factor_of = 1.0
    for axis_at, parts in split:
        steps = jax.random.uniform(jax.random.fold_in(jax.random.fold_in(own_key, 6), axis_at), (parts,), jnp.float32, smallest / len(split), largest / len(split))
        factor_of = factor_of * jnp.repeat(jnp.exp(steps), shape[axis_at] // parts).reshape((-1,) + (1,) * (len(shape) - 1 - axis_at))
    return factor_of


def normal_values(stream_key, extent, scale, most, cuts=(), kind=jnp.bfloat16):
    array = jax.random.normal(stream_key, extent, jnp.float32) * scale
    if len(cuts) > 0:
        array = steps_of(stream_key, extent, cuts, -0.22, 0.18) * array
    return jnp.clip(array, min=-most, max=most).astype(kind)


def setup_inputs(seed: int = 0) -> dict:
    streams_of = jax.random.split(jax.random.key(seed), 17)
    return {
        "tokens": normal_values(streams_of[0], (SEQS, SEQ_LEN, D), 1.0, 6.0, ((0, 16), (1, 2))),
        "segments": draw_segments(jax.random.fold_in(streams_of[16], 71), 0),
        "grad_out": normal_values(streams_of[2], (SEQS, SEQ_LEN, D), 1.0, 6.0, ((0, 16), (1, 2))),
        "attn_gain": jnp.clip(1.0 + 0.18 * jax.random.normal(streams_of[3], (LAYERS, D), jnp.float32), 0.099609375, 1.8984375).astype(jnp.bfloat16),
        "attn_shift": normal_values(streams_of[4], (LAYERS, D), 0.3, 3.0, ((1, 4),)),
        "w_qkv": normal_values(streams_of[5], (LAYERS, D, 3 * D), D ** -0.5, 0.1875, ((1, 4),)),
        "b_query": normal_values(streams_of[6], (LAYERS, D), 0.5, 3.0, ((1, 4),)),
        "b_value": normal_values(streams_of[7], (LAYERS, D), 0.5, 3.0, ((1, 4),)),
        "w_out": normal_values(streams_of[8], (LAYERS, D, D), (D // 8) ** -0.5, 0.5, ((1, 4),)),
        "b_out": normal_values(streams_of[9], (LAYERS, D), 0.3, 3.0, ((1, 4),)),
        "mlp_gain": jnp.clip(1.0 + 0.18 * jax.random.normal(streams_of[10], (LAYERS, D), jnp.float32), 0.099609375, 1.8984375).astype(jnp.bfloat16),
        "mlp_shift": normal_values(streams_of[11], (LAYERS, D), 0.3, 3.0, ((1, 4),)),
        "w_up": normal_values(streams_of[12], (LAYERS, D, FF), D ** -0.5, 0.1875, ((1, 4),)),
        "b_up": normal_values(streams_of[13], (LAYERS, FF), 0.5, 3.0, ((1, 4),)),
        "w_down": normal_values(streams_of[14], (LAYERS, FF, D), FF ** -0.5, 0.09375, ((1, 4),)),
        "b_down": normal_values(streams_of[15], (LAYERS, D), 0.3, 3.0, ((1, 4),)),
    }


NORM_EPSILON = 1e-05
MASKED = -1e+30
PRECISE = lax.Precision.HIGHEST

@jax.custom_vjp
def low(v):
    return lax.optimization_barrier(v.astype(jnp.bfloat16)).astype(jnp.float32)

@jax.custom_vjp
def low_back(v):
    return v

def low_keep(v):
    return (low(v), None)

def low_pass(kept, grad):
    return (grad,)

def back_keep(v):
    return (v, None)

def back_low(kept, grad):
    return (low(grad),)
low.defvjp(low_keep, low_pass)
low_back.defvjp(back_keep, back_low)

def layer_norm(inputs, gain, bias_term):
    center = inputs - lax.optimization_barrier(jnp.mean(inputs, axis=-1, keepdims=True))
    spread = lax.optimization_barrier(jnp.mean(center * center, axis=-1, keepdims=True))
    return center * lax.rsqrt(spread + NORM_EPSILON) * gain + bias_term

def gelu_tanh(inputs):
    return jax.nn.gelu(inputs, approximate=True)

def matmul_high(left, right):
    return jnp.matmul(left, right, precision=PRECISE)

def attention(normed, w_qkv, b_query, b_value, seg_rows):
    model_width = normed.shape[-1]
    batch_size = normed.shape[0]
    length = normed.shape[1]
    head_count = model_width // HEAD_DIM
    query_scale = 1.0 / math.sqrt(HEAD_DIM)
    proj_all = matmul_high(normed, w_qkv)
    queries = low(low_back((proj_all[..., :model_width] + b_query) * query_scale))
    keys = low(low_back(proj_all[..., model_width:2 * model_width]))
    values = low(low_back(proj_all[..., 2 * model_width:] + b_value))
    head_shape = (batch_size, length, head_count, HEAD_DIM)
    scores = low_back(jnp.einsum('bthd,bshd->bhts', queries.reshape(head_shape), keys.reshape(head_shape), precision=PRECISE))
    places = jnp.arange(length)
    visible = (seg_rows[:, :, None] == seg_rows[:, None, :]) & (places[:, None] >= places[None, :])[None]
    scores = jnp.where(visible[:, None], scores, MASKED)
    row_max = lax.optimization_barrier(jnp.max(scores, axis=-1, keepdims=True))
    exponent = jnp.exp(scores - row_max)
    weights_soft = low(exponent / lax.optimization_barrier(jnp.sum(exponent, axis=-1, keepdims=True)))
    attended = jnp.einsum('bhts,bshd->bthd', weights_soft, values.reshape(head_shape), precision=PRECISE)
    return low(low_back(attended.reshape(batch_size, length, model_width)))

def block(resid, layer_params, seg_rows):
    attn_gain, attn_shift, w_qkv, b_query, b_value, w_out, b_out, mlp_gain, mlp_shift, w_up, b_up, w_down, b_down = layer_params
    normed_attn = low(layer_norm(resid, attn_gain, attn_shift))
    attended = attention(normed_attn, w_qkv, b_query, b_value, seg_rows)
    middle = resid + low_back(matmul_high(attended, w_out) + b_out)
    normed_mlp = low(layer_norm(middle, mlp_gain, mlp_shift))
    pre_act = low_back(matmul_high(normed_mlp, w_up) + b_up)
    activated = low(gelu_tanh(pre_act))
    return middle + low_back(matmul_high(activated, w_down) + b_down)

def run_layers(resid, params_float, seg_rows):
    for layer_index in range(params_float[0].shape[0]):
        resid = block(resid, tuple((item[layer_index] for item in params_float)), seg_rows)
    return resid

def reference(tokens, segments, grad_out, attn_gain, attn_shift, w_qkv, b_query, b_value, w_out, b_out, mlp_gain, mlp_shift, w_up, b_up, w_down, b_down):
    parameters = tuple((item.astype(jnp.float32) for item in (attn_gain, attn_shift, w_qkv, b_query, b_value, w_out, b_out, mlp_gain, mlp_shift, w_up, b_up, w_down, b_down)))
    groups = tokens.shape[0] // 2
    group_shape = (groups, 2, tokens.shape[1], tokens.shape[2])

    def step(carry, batch_item):
        token_rows, seg_rows, cot_rows = batch_item

        def forward(resid, params_float):
            return run_layers(resid, params_float, seg_rows)
        output, pull = jax.vjp(forward, token_rows.astype(jnp.float32), parameters)
        grad_rows, grad_params = pull(cot_rows.astype(jnp.float32))
        carry = tuple((total + extra for total, extra in zip(carry, grad_params)))
        return (carry, (output.astype(jnp.bfloat16), grad_rows.astype(jnp.bfloat16)))
    initial = tuple((jnp.zeros(item.shape, jnp.float32) for item in parameters))
    summed, (outputs, grad_rows) = lax.scan(step, initial, (tokens.reshape(group_shape), segments.reshape(groups, 2, tokens.shape[1]), grad_out.reshape(group_shape)))
    return (outputs.reshape(tokens.shape), grad_rows.reshape(tokens.shape), summed[0], summed[1], summed[2], summed[3], summed[4], summed[5], summed[6], summed[7], summed[8], summed[9], summed[10], summed[11], summed[12])
```

```python
import math

import jax
import jax.numpy as jnp
from jax import lax
from jax.experimental import pallas as pl
from jax.experimental.pallas import tpu as pltpu
from jax.sharding import PartitionSpec as P

HEAD_DIM = 64
MESH = pl.DeviceIdType.MESH


NORM_EPSILON = 1e-05
MASKED = -1e30


def layer_norm(inputs, gain, bias_term):
    center = inputs - jnp.mean(inputs, axis=-1, keepdims=True)
    spread = jnp.mean(center * center, axis=-1, keepdims=True)
    return center * lax.rsqrt(spread + NORM_EPSILON) * gain + bias_term


def gelu_tanh(inputs):
    return jax.nn.gelu(inputs, approximate=True)


def product(left, right):
    return jnp.dot(left, right, preferred_element_type=jnp.float32)


def inner_rows(left, right):
    return lax.dot_general(
        left, right, (((0,), (0,)), ((), ())), preferred_element_type=jnp.float32
    )


def outer_cols(left, right):
    return lax.dot_general(
        left, right, (((1,), (1,)), ((), ())), preferred_element_type=jnp.float32
    )


def column_sum(values_low):
    return jnp.sum(values_low.astype(jnp.float32), axis=0)


def visible_mask(seg_own, seg_all, offset):
    row_pos = offset + lax.iota(jnp.int32, seg_own.shape[0])
    col_pos = lax.iota(jnp.int32, seg_all.shape[0])
    return (seg_own[:, None] == seg_all[None, :]) & (row_pos[:, None] >= col_pos[None, :])


def head_scores(queries, keys_all, visible, head_count):
    query_heads = queries.reshape(queries.shape[0], head_count, HEAD_DIM)
    key_heads = keys_all.reshape(keys_all.shape[0], head_count, HEAD_DIM)
    scores = jnp.einsum("thd,shd->hts", query_heads, key_heads, preferred_element_type=jnp.float32)
    return jnp.where(visible[None], scores, MASKED)


def gather_layer(
    layer_index,
    attn_gain,
    attn_shift,
    w_qkv,
    b_query,
    b_value,
    w_out,
    b_out,
    mlp_gain,
    mlp_shift,
    w_up,
    b_up,
    w_down,
    b_down,
):
    return (
        lax.all_gather(attn_gain[layer_index], "fsdp", axis=0, tiled=True),
        lax.all_gather(attn_shift[layer_index], "fsdp", axis=0, tiled=True),
        lax.all_gather(w_qkv[layer_index], "fsdp", axis=0, tiled=True),
        lax.all_gather(b_query[layer_index], "fsdp", axis=0, tiled=True),
        lax.all_gather(b_value[layer_index], "fsdp", axis=0, tiled=True),
        lax.all_gather(w_out[layer_index], "fsdp", axis=0, tiled=True),
        lax.all_gather(b_out[layer_index], "fsdp", axis=0, tiled=True),
        lax.all_gather(mlp_gain[layer_index], "fsdp", axis=0, tiled=True),
        lax.all_gather(mlp_shift[layer_index], "fsdp", axis=0, tiled=True),
        lax.all_gather(w_up[layer_index], "fsdp", axis=0, tiled=True),
        lax.all_gather(b_up[layer_index], "fsdp", axis=0, tiled=True),
        lax.all_gather(w_down[layer_index], "fsdp", axis=0, tiled=True),
        lax.all_gather(b_down[layer_index], "fsdp", axis=0, tiled=True),
    )


def gather_again(
    layer_index,
    attn_gain,
    attn_shift,
    w_qkv,
    b_query,
    b_value,
    w_out,
    b_out,
    mlp_gain,
    mlp_shift,
    w_up,
    b_up,
    w_down,
    b_down,
):
    return (
        lax.all_gather(attn_gain[layer_index], "fsdp", axis=0, tiled=True),
        lax.all_gather(attn_shift[layer_index], "fsdp", axis=0, tiled=True),
        lax.all_gather(w_qkv[layer_index], "fsdp", axis=0, tiled=True),
        lax.all_gather(b_query[layer_index], "fsdp", axis=0, tiled=True),
        lax.all_gather(b_value[layer_index], "fsdp", axis=0, tiled=True),
        lax.all_gather(w_out[layer_index], "fsdp", axis=0, tiled=True),
        lax.all_gather(b_out[layer_index], "fsdp", axis=0, tiled=True),
        lax.all_gather(mlp_gain[layer_index], "fsdp", axis=0, tiled=True),
        lax.all_gather(mlp_shift[layer_index], "fsdp", axis=0, tiled=True),
        lax.all_gather(w_up[layer_index], "fsdp", axis=0, tiled=True),
        lax.all_gather(b_up[layer_index], "fsdp", axis=0, tiled=True),
        lax.all_gather(w_down[layer_index], "fsdp", axis=0, tiled=True),
        lax.all_gather(b_down[layer_index], "fsdp", axis=0, tiled=True),
    )


def forward_layer(resid, gathered, visible, pool):
    (
        attn_gain,
        attn_shift,
        w_qkv,
        b_query,
        b_value,
        w_out,
        b_out,
        mlp_gain,
        mlp_shift,
        w_up,
        b_up,
        w_down,
        b_down,
    ) = gathered
    model_width = resid.shape[1]
    head_count = model_width // HEAD_DIM
    query_scale = 1.0 / math.sqrt(HEAD_DIM)
    normed_attn = layer_norm(
        resid, attn_gain.astype(jnp.float32), attn_shift.astype(jnp.float32)
    ).astype(jnp.bfloat16)
    proj_all = product(normed_attn, w_qkv)
    queries = ((proj_all[:, :model_width] + b_query.astype(jnp.float32)) * query_scale).astype(
        jnp.bfloat16
    )
    keys_own = proj_all[:, model_width : 2 * model_width].astype(jnp.bfloat16)
    values_own = (proj_all[:, 2 * model_width :] + b_value.astype(jnp.float32)).astype(jnp.bfloat16)
    keys_all, values_all = pool.spread(keys_own), pool.spread(values_own)
    scores = head_scores(queries, keys_all, visible, head_count)
    row_max = jnp.max(scores, axis=-1, keepdims=True)
    exponent = jnp.exp(scores - row_max)
    row_sum = jnp.sum(exponent, axis=-1, keepdims=True)
    weights_soft = (exponent / row_sum).astype(jnp.bfloat16)
    log_total = row_max + jnp.log(row_sum)
    value_heads = values_all.reshape(values_all.shape[0], head_count, HEAD_DIM)
    attended = jnp.einsum(
        "hts,shd->thd", weights_soft, value_heads, preferred_element_type=jnp.float32
    )
    attended = attended.reshape(resid.shape[0], model_width).astype(jnp.bfloat16)
    middle = resid + product(attended, w_out) + b_out.astype(jnp.float32)
    normed_mlp = layer_norm(
        middle, mlp_gain.astype(jnp.float32), mlp_shift.astype(jnp.float32)
    ).astype(jnp.bfloat16)
    pre_act = product(normed_mlp, w_up) + b_up.astype(jnp.float32)
    activated = gelu_tanh(pre_act).astype(jnp.bfloat16)
    output = middle + product(activated, w_down) + b_down.astype(jnp.float32)
    stored = (
        resid,
        normed_attn,
        queries,
        keys_all,
        values_all,
        log_total,
        attended,
        middle,
        normed_mlp,
        pre_act,
        activated,
    )
    return (output, stored)


def backward_layer(grad_next, stored, gathered, visible, pool):
    (
        attn_gain,
        attn_shift,
        w_qkv,
        b_query,
        b_value,
        w_out,
        b_out,
        mlp_gain,
        mlp_shift,
        w_up,
        b_up,
        w_down,
        b_down,
    ) = gathered
    (
        resid,
        normed_attn,
        queries,
        keys_all,
        values_all,
        log_total,
        attended,
        middle,
        normed_mlp,
        pre_act,
        activated,
    ) = stored
    model_width = resid.shape[1]
    tok_rows = resid.shape[0]
    key_rows = keys_all.shape[0]
    head_count = model_width // HEAD_DIM
    query_scale = 1.0 / math.sqrt(HEAD_DIM)
    grad_mlp = grad_next.astype(jnp.bfloat16)
    grad_b_down = column_sum(grad_mlp)
    grad_w_down = inner_rows(activated, grad_mlp)
    grad_act = outer_cols(grad_mlp, w_down)
    gelu_value, gelu_pull = jax.vjp(gelu_tanh, pre_act)
    grad_pre = gelu_pull(grad_act)[0].astype(jnp.bfloat16)
    grad_b_up = column_sum(grad_pre)
    grad_w_up = inner_rows(normed_mlp, grad_pre)
    grad_nm = outer_cols(grad_pre, w_up)
    norm_value, norm_pull = jax.vjp(
        layer_norm, middle, mlp_gain.astype(jnp.float32), mlp_shift.astype(jnp.float32)
    )
    grad_middle, grad_mlp_gain, grad_mlp_shift = norm_pull(grad_nm)
    grad_middle = grad_middle + grad_next
    grad_branch = grad_middle.astype(jnp.bfloat16)
    grad_b_out = column_sum(grad_branch)
    grad_w_out = inner_rows(attended, grad_branch)
    grad_attended = outer_cols(grad_branch, w_out).astype(jnp.bfloat16)
    scores = head_scores(queries, keys_all, visible, head_count)
    weights_full = jnp.exp(scores - log_total)
    weights_soft = weights_full.astype(jnp.bfloat16)
    grad_heads = grad_attended.reshape(tok_rows, head_count, HEAD_DIM)
    query_heads = queries.reshape(tok_rows, head_count, HEAD_DIM)
    key_heads = keys_all.reshape(key_rows, head_count, HEAD_DIM)
    value_heads = values_all.reshape(key_rows, head_count, HEAD_DIM)
    grad_value_terms = jnp.einsum(
        "hts,thd->shd", weights_soft, grad_heads, preferred_element_type=jnp.float32
    )
    grad_probs = jnp.einsum(
        "thd,shd->hts", grad_heads, value_heads, preferred_element_type=jnp.float32
    )
    inner_sum = jnp.sum(weights_full * grad_probs, axis=-1, keepdims=True)
    grad_scores = (weights_full * (grad_probs - inner_sum)).astype(jnp.bfloat16)
    grad_queries = jnp.einsum(
        "hts,shd->thd", grad_scores, key_heads, preferred_element_type=jnp.float32
    )
    grad_queries = grad_queries.reshape(tok_rows, model_width).astype(jnp.bfloat16) * query_scale
    grad_key_terms = jnp.einsum(
        "hts,thd->shd", grad_scores, query_heads, preferred_element_type=jnp.float32
    )
    grad_keys = pool.collect(grad_key_terms.reshape(key_rows, model_width).astype(jnp.bfloat16))
    grad_values = pool.collect(grad_value_terms.reshape(key_rows, model_width).astype(jnp.bfloat16))
    grad_keys = grad_keys.astype(jnp.bfloat16)
    grad_values = grad_values.astype(jnp.bfloat16)
    grad_proj = jnp.concatenate([grad_queries, grad_keys, grad_values], axis=1)
    grad_b_query = column_sum(grad_queries)
    grad_b_value = column_sum(grad_values)
    grad_w_qkv = inner_rows(normed_attn, grad_proj)
    grad_na = outer_cols(grad_proj, w_qkv)
    first_value, first_pull = jax.vjp(
        layer_norm, resid, attn_gain.astype(jnp.float32), attn_shift.astype(jnp.float32)
    )
    grad_resid, grad_attn_gain, grad_attn_shift = first_pull(grad_na)
    grad_resid = grad_resid + grad_middle
    gradients = (
        grad_attn_gain,
        grad_attn_shift,
        grad_w_qkv,
        grad_b_query,
        grad_b_value,
        grad_w_out,
        grad_b_out,
        grad_mlp_gain,
        grad_mlp_shift,
        grad_w_up,
        grad_b_up,
        grad_w_down,
        grad_b_down,
    )
    return (grad_resid, gradients)


def reduce_grads(gradients):
    shares = (
        lax.psum_scatter(gradients[0], ("fsdp", "rep"), scatter_dimension=0, tiled=True),
        lax.psum_scatter(gradients[1], ("fsdp", "rep"), scatter_dimension=0, tiled=True),
        lax.psum_scatter(gradients[2], ("fsdp", "rep"), scatter_dimension=0, tiled=True),
        lax.psum_scatter(gradients[3], ("fsdp", "rep"), scatter_dimension=0, tiled=True),
        lax.psum_scatter(gradients[4], ("fsdp", "rep"), scatter_dimension=0, tiled=True),
        lax.psum_scatter(gradients[5], ("fsdp", "rep"), scatter_dimension=0, tiled=True),
        lax.psum_scatter(gradients[6], ("fsdp", "rep"), scatter_dimension=0, tiled=True),
        lax.psum_scatter(gradients[7], ("fsdp", "rep"), scatter_dimension=0, tiled=True),
        lax.psum_scatter(gradients[8], ("fsdp", "rep"), scatter_dimension=0, tiled=True),
        lax.psum_scatter(gradients[9], ("fsdp", "rep"), scatter_dimension=0, tiled=True),
        lax.psum_scatter(gradients[10], ("fsdp", "rep"), scatter_dimension=0, tiled=True),
        lax.psum_scatter(gradients[11], ("fsdp", "rep"), scatter_dimension=0, tiled=True),
        lax.psum_scatter(gradients[12], ("fsdp", "rep"), scatter_dimension=0, tiled=True),
    )
    shares = (
        lax.psum(shares[0].astype(jnp.bfloat16), "seq").astype(jnp.float32),
        lax.psum(shares[1].astype(jnp.bfloat16), "seq").astype(jnp.float32),
        lax.psum(shares[2].astype(jnp.bfloat16), "seq").astype(jnp.float32),
        lax.psum(shares[3].astype(jnp.bfloat16), "seq").astype(jnp.float32),
        lax.psum(shares[4].astype(jnp.bfloat16), "seq").astype(jnp.float32),
        lax.psum(shares[5].astype(jnp.bfloat16), "seq").astype(jnp.float32),
        lax.psum(shares[6].astype(jnp.bfloat16), "seq").astype(jnp.float32),
        lax.psum(shares[7].astype(jnp.bfloat16), "seq").astype(jnp.float32),
        lax.psum(shares[8].astype(jnp.bfloat16), "seq").astype(jnp.float32),
        lax.psum(shares[9].astype(jnp.bfloat16), "seq").astype(jnp.float32),
        lax.psum(shares[10].astype(jnp.bfloat16), "seq").astype(jnp.float32),
        lax.psum(shares[11].astype(jnp.bfloat16), "seq").astype(jnp.float32),
        lax.psum(shares[12].astype(jnp.bfloat16), "seq").astype(jnp.float32),
    )
    return (
        lax.all_gather(shares[0].astype(jnp.bfloat16), "rep", axis=0, tiled=True).astype(
            jnp.float32
        ),
        lax.all_gather(shares[1].astype(jnp.bfloat16), "rep", axis=0, tiled=True).astype(
            jnp.float32
        ),
        lax.all_gather(shares[2].astype(jnp.bfloat16), "rep", axis=0, tiled=True).astype(
            jnp.float32
        ),
        lax.all_gather(shares[3].astype(jnp.bfloat16), "rep", axis=0, tiled=True).astype(
            jnp.float32
        ),
        lax.all_gather(shares[4].astype(jnp.bfloat16), "rep", axis=0, tiled=True).astype(
            jnp.float32
        ),
        lax.all_gather(shares[5].astype(jnp.bfloat16), "rep", axis=0, tiled=True).astype(
            jnp.float32
        ),
        lax.all_gather(shares[6].astype(jnp.bfloat16), "rep", axis=0, tiled=True).astype(
            jnp.float32
        ),
        lax.all_gather(shares[7].astype(jnp.bfloat16), "rep", axis=0, tiled=True).astype(
            jnp.float32
        ),
        lax.all_gather(shares[8].astype(jnp.bfloat16), "rep", axis=0, tiled=True).astype(
            jnp.float32
        ),
        lax.all_gather(shares[9].astype(jnp.bfloat16), "rep", axis=0, tiled=True).astype(
            jnp.float32
        ),
        lax.all_gather(shares[10].astype(jnp.bfloat16), "rep", axis=0, tiled=True).astype(
            jnp.float32
        ),
        lax.all_gather(shares[11].astype(jnp.bfloat16), "rep", axis=0, tiled=True).astype(
            jnp.float32
        ),
        lax.all_gather(shares[12].astype(jnp.bfloat16), "rep", axis=0, tiled=True).astype(
            jnp.float32
        ),
    )


class Halves:
    def spread(self, rows):
        return lax.all_gather(rows, "seq", axis=0, tiled=True)

    def collect(self, rows):
        return lax.psum_scatter(rows, "seq", scatter_dimension=0, tiled=True)


class Cores:
    swap = [(0, 1), (1, 0), (2, 3), (3, 2)]

    def spread(self, rows):
        other = lax.ppermute(rows, "rep", self.swap)
        return jnp.concatenate([rows, other], axis=0)

    def collect(self, rows):
        half = rows.shape[0] // 2
        other = lax.ppermute(rows[half:], "rep", self.swap)
        return rows[:half] + other


def to_cores(rows):
    half = rows.shape[0] // 2
    spots = [(x, y, c) for x in range(2) for y in range(2) for c in range(2)]
    first = [(x * 4 + y * 2 + c, c * 4 + y * 2 + x) for x, y, c in spots]
    second = [(x * 4 + y * 2 + c, c * 4 + y * 2 + 1 - x) for x, y, c in spots]
    return jnp.concatenate(
        [
            lax.ppermute(rows[:half], ("seq", "rep"), first),
            lax.ppermute(rows[half:], ("seq", "rep"), second),
        ],
        axis=0,
    )


def from_cores(rows):
    half = rows.shape[0] // 2
    spots = [(x, y, c) for x in range(2) for y in range(2) for c in range(2)]
    first = [(c * 4 + y * 2 + x, x * 4 + y * 2 + c) for x, y, c in spots]
    second = [(c * 4 + y * 2 + 1 - x, x * 4 + y * 2 + c) for x, y, c in spots]
    return jnp.concatenate(
        [
            lax.ppermute(rows[:half], ("seq", "rep"), first),
            lax.ppermute(rows[half:], ("seq", "rep"), second),
        ],
        axis=0,
    )


ZN = 4


def neighbours():
    x, z, r = lax.axis_index("seq"), lax.axis_index("fsdp"), lax.axis_index("rep")
    y, c = r // 2, r % 2
    across = (1 - x, z, r)
    beside = (x, z, (1 - y) * 2 + c)
    twin = (x, z, y * 2 + (1 - c))
    up = (x, (z + 1) % ZN, r)
    down = (x, (z + ZN - 1) % ZN, r)
    return x, y, z, c, across, beside, twin, up, down


def greet(z, across, beside, twin, up, down):
    barrier = pltpu.get_barrier_semaphore()

    def tell(device):
        pl.semaphore_signal(barrier, inc=1, device_id=device, device_id_type=MESH)

    for device in (across, beside, twin):
        tell(device)

    @pl.when(z < ZN - 1)
    def _():
        tell(up)

    @pl.when(z > 0)
    def _():
        tell(down)

    pl.semaphore_wait(barrier, 3 + (z + ZN - 1) // ZN + (2 * ZN - 2 - z) // ZN)


ZA, ZR, GX, GY, GD1, GD2, GC = range(7)


def gather_body(units, ins, outs, holds, load_sem, store_sem, send_sem, recv_sem):
    x, y, z, c, across, beside, twin, up, down = neighbours()
    greet(z, across, beside, twin, up, down)

    def owned(u, px, py, half=None):
        k = ins[units[u][1]].shape[1] // 8
        base = (c * 4 + px * 2 + py) * k
        if half is None:
            return pl.ds(base, k)
        return pl.ds(base + half * (k // 2), k // 2)

    def rest(u):
        n = ins[units[u][1]].shape[1]
        return pl.ds(n // 8 * 8, n % 8)

    def slab(u, core):
        k = ins[units[u][1]].shape[1] // 8
        return pl.ds(core * 4 * k, 4 * k)

    def move(u, zz, rows, device, kind, source=None, send_kind=None):
        layer, m = units[u]
        target = outs[m].at[layer, zz, rows]
        return pltpu.make_async_remote_copy(
            src_ref=target if source is None else source,
            dst_ref=target,
            send_sem=send_sem.at[u, zz, kind if send_kind is None else send_kind],
            recv_sem=recv_sem.at[u, zz, kind],
            device_id=device,
            device_id_type=MESH,
        )

    def load(u):
        layer, m = units[u]
        return pltpu.make_async_copy(ins[m].at[layer], holds[m].at[layer], load_sem.at[u])

    def store(u):
        layer, m = units[u]
        return pltpu.make_async_copy(holds[m].at[layer], outs[m].at[layer, z], store_sem.at[u])

    def own_sends(u, act):
        layer, m = units[u]
        mine, left_over = owned(u, x, y), rest(u)

        @pl.when(z < ZN - 1)
        def _():
            act(move(u, z, mine, up, ZA, ins[m].at[layer, mine], 0))
            act(move(u, z, left_over, up, ZR, ins[m].at[layer, left_over], 1))

        @pl.when(z > 0)
        def _():
            act(move(u, z, mine, down, ZA, ins[m].at[layer, mine], 2))
            act(move(u, z, left_over, down, ZR, ins[m].at[layer, left_over], 3))

    def both(s, act):
        @pl.when(z >= s)
        def _():
            act(z - s, 0)

        @pl.when(z + s <= ZN - 1)
        def _():
            act(z + s, 1)

    def onward(u, zz, d, act):
        mine, left_over = owned(u, x, y), rest(u)
        if d == 0:

            @pl.when(z < ZN - 1)
            def _():
                act(move(u, zz, mine, up, ZA))
                act(move(u, zz, left_over, up, ZR))

        else:

            @pl.when(z > 0)
            def _():
                act(move(u, zz, mine, down, ZA))
                act(move(u, zz, left_over, down, ZR))

    def line_step(u, s):
        def act(zz, d):
            mine, left_over = owned(u, x, y), rest(u)
            move(u, zz, mine, across, ZA).wait_recv()
            move(u, zz, left_over, across, ZR).wait_recv()
            onward(u, zz, d, lambda copy: copy.start())
            move(u, zz, mine, across, GX).start()
            move(u, zz, mine, beside, GY).start()

        both(s, act)

    def plane_step(u, s):
        def act(zz, d):
            move(u, zz, owned(u, 1 - x, y), across, GX).wait_recv()
            move(u, zz, owned(u, 1 - x, y, 0), beside, GD1).start()
            move(u, zz, owned(u, x, 1 - y), beside, GY).wait_recv()
            move(u, zz, owned(u, x, 1 - y, 1), across, GD2).start()

        both(s, act)

    def corner_step(u, s):
        def act(zz, d):
            move(u, zz, owned(u, 1 - x, 1 - y, 0), beside, GD1).wait_recv()
            move(u, zz, owned(u, 1 - x, 1 - y, 1), across, GD2).wait_recv()
            move(u, zz, slab(u, c), twin, GC).start()

        both(s, act)

    def finish(u):
        store(u).wait()
        own_sends(u, lambda copy: copy.wait_send())
        for s in (1, 2, 3):

            def act(zz, d):
                mine = owned(u, x, y)
                move(u, zz, slab(u, 1 - c), twin, GC).wait_recv()
                onward(u, zz, d, lambda copy: copy.wait_send())
                move(u, zz, mine, across, GX).wait_send()
                move(u, zz, mine, beside, GY).wait_send()
                move(u, zz, owned(u, 1 - x, y, 0), beside, GD1).wait_send()
                move(u, zz, owned(u, x, 1 - y, 1), across, GD2).wait_send()
                move(u, zz, slab(u, c), twin, GC).wait_send()

            both(s, act)

    count = len(units)

    def at(step, u, s):
        if 0 <= u < count:
            step(u, s)

    for u in range(count):
        load(u).start()
    for u in range(2):
        own_sends(u, lambda copy: copy.start())
    for t in range(count + 5):
        if t + 2 < count:
            own_sends(t + 2, lambda copy: copy.start())
        for s in (1, 2, 3):
            at(line_step, t + 1 - s, s)
        for s in (1, 2, 3):
            at(plane_step, t - s, s)
        for s in (1, 2, 3):
            at(corner_step, t - 1 - s, s)
        if t < count:
            load(t).wait()
            store(t).start()
    for u in range(count):
        finish(u)


def gather_weights(shards):
    layers, m_count = shards[0].shape[0], len(shards)
    units = [(layer, m) for layer in range(layers) for m in range(m_count)]

    def body(*refs):
        gather_body(
            units, refs[:m_count], refs[m_count : 2 * m_count], refs[2 * m_count : 3 * m_count], *refs[3 * m_count :]
        )

    return pl.pallas_call(
        body,
        out_shape=[jax.ShapeDtypeStruct((layers, ZN) + w.shape[1:], w.dtype) for w in shards],
        in_specs=[pl.BlockSpec(memory_space=pl.ANY)] * m_count,
        out_specs=[pl.BlockSpec(memory_space=pl.ANY)] * m_count,
        scratch_shapes=[pltpu.VMEM(w.shape, w.dtype) for w in shards]
        + [
            pltpu.SemaphoreType.DMA((len(units),)),
            pltpu.SemaphoreType.DMA((len(units),)),
            pltpu.SemaphoreType.DMA((len(units), ZN, 7)),
            pltpu.SemaphoreType.DMA((len(units), ZN, 7)),
        ],
        compiler_params=pltpu.CompilerParams(
            collective_id=0, has_side_effects=True, vmem_limit_bytes=40 << 20
        ),
        name="gather_weights",
    )(*shards)


PAIRS = ((0, 1), (3, 2))
RC, R1, R2, RL, RR, RX, RY, RD1, RD2, RCC, R1B = 0, 4, 8, 12, 16, 20, 21, 22, 23, 24, 25


def reduce_body(ks, grads, outs, own, twin_in, first_in, second_in, low_in, high_in, load_sem, store_sem, send_sem, recv_sem):
    x, y, z, c, across, beside, twin, up, down = neighbours()
    greet(z, across, beside, twin, up, down)
    units = [(m, h) for h in range(2) for m in range(len(grads))]
    p = x * 2 + y

    def move(source, target, m, kind, device):
        return pltpu.make_async_remote_copy(
            src_ref=source,
            dst_ref=target,
            send_sem=send_sem.at[m, kind],
            recv_sem=recv_sem.at[m, kind],
            device_id=device,
            device_id_type=MESH,
        )

    def to_twin(m, d):
        k = ks[m]
        return move(grads[m].at[d, pl.ds((1 - c) * 4 * k, 4 * k)], twin_in[m].at[d], m, RC + d, twin)

    def load(m, d):
        k = ks[m]
        return pltpu.make_async_copy(grads[m].at[d, pl.ds(c * 4 * k, 4 * k)], own[m].at[d], load_sem.at[m, d])

    def add(m, d, at, extra, extra_at, n):
        def step(i, carry):
            own[m][d, at + i] = own[m][d, at + i] + extra[d, extra_at + i]
            return carry

        lax.fori_loop(0, n, step, 0)

    def first_moves(u):
        m, h = units[u]
        k = ks[m]
        a, b = PAIRS[h]
        return [
            move(own[m].at[a, pl.ds((1 - x) * 2 * k, 2 * k)], first_in[m].at[a], m, R1 + a, across),
            move(own[m].at[b, pl.ds((1 - y) * k, k)], first_in[m].at[b, pl.ds(0, k)], m, R1 + b, beside),
            move(own[m].at[b, pl.ds((3 - y) * k, k)], first_in[m].at[b, pl.ds(k, k)], m, R1B + h, beside),
        ]

    def second_moves(u):
        m, h = units[u]
        k = ks[m]
        a, b = PAIRS[h]
        return [
            move(own[m].at[a, pl.ds((x * 2 + 1 - y) * k, k)], second_in[m].at[a], m, R2 + a, beside),
            move(own[m].at[b, pl.ds(((1 - x) * 2 + y) * k, k)], second_in[m].at[b], m, R2 + b, across),
        ]

    def with_twin(u):
        m, h = units[u]
        for d in PAIRS[h]:
            to_twin(m, d).wait_recv()
            load(m, d).wait()
            add(m, d, 0, twin_in[m], 0, 4 * ks[m])
        for copy in first_moves(u):
            copy.start()

    def with_first(u):
        m, h = units[u]
        k = ks[m]
        a, b = PAIRS[h]
        for copy in first_moves(u):
            copy.wait_recv()
        add(m, a, x * 2 * k, first_in[m], 0, 2 * k)
        add(m, b, y * k, first_in[m], 0, k)
        add(m, b, (2 + y) * k, first_in[m], k, k)
        for copy in second_moves(u):
            copy.start()

    def with_second(u):
        m, h = units[u]
        for copy in second_moves(u):
            copy.wait_recv()
        for d in PAIRS[h]:
            add(m, d, p * ks[m], second_in[m], 0, ks[m])

    def piece(m, d):
        return own[m].at[d, pl.ds(p * ks[m], ks[m])]

    def to_down(m, d):
        return move(piece(m, d), high_in[m].at[d], m, RR + d, down)

    def to_up(m, d):
        return move(piece(m, d), low_in[m].at[d], m, RL + d, up)

    def rows_of(m, px, py, low=0, n=None):
        k = ks[m]
        return outs[m].at[pl.ds((c * 4 + px * 2 + py) * k + low, k if n is None else n)]

    def share_across(m):
        return move(piece(m, z), rows_of(m, x, y), m, RX, across)

    def share_beside(m):
        return move(piece(m, z), rows_of(m, x, y), m, RY, beside)

    def store(m):
        return pltpu.make_async_copy(piece(m, z), rows_of(m, x, y), store_sem.at[m])

    def arrived_across(m):
        return move(rows_of(m, 1 - x, y), rows_of(m, 1 - x, y), m, RX, across)

    def arrived_beside(m):
        return move(rows_of(m, x, 1 - y), rows_of(m, x, 1 - y), m, RY, beside)

    def corner(m, px, py, part):
        k = ks[m]
        low, n = (0, max(k // 2, 1)) if part == 0 else (k // 2, k - k // 2)
        rows = rows_of(m, px, py, low, n)
        return move(rows, rows, m, RD1 if part == 0 else RD2, beside if part == 0 else across)

    def to_core(m, core):
        rows = outs[m].at[pl.ds(core * 4 * ks[m], 4 * ks[m])]
        return move(rows, rows, m, RCC, twin)

    def line_step(u, s):
        m, h = units[u]
        for zz in range(ZN):
            downward = [d for d in PAIRS[h] if d < zz] if zz == ZN - 1 - s else []
            upward = [d for d in PAIRS[h] if d > zz] if zz == s else []
            last = [d for d in PAIRS[h] if d == zz] if s == ZN - 1 else []
            if not (downward or upward or last):
                continue

            @pl.when(z == zz)
            def _():
                for d in downward:
                    if zz < ZN - 1:
                        to_down(m, d).wait_recv()
                        add(m, d, p * ks[m], high_in[m], 0, ks[m])
                    to_down(m, d).start()
                for d in upward:
                    if zz > 0:
                        to_up(m, d).wait_recv()
                        add(m, d, p * ks[m], low_in[m], 0, ks[m])
                    to_up(m, d).start()
                for d in last:
                    if zz > 0:
                        to_up(m, d).wait_recv()
                        add(m, d, p * ks[m], low_in[m], 0, ks[m])
                    if zz < ZN - 1:
                        to_down(m, d).wait_recv()
                        add(m, d, p * ks[m], high_in[m], 0, ks[m])
                    share_across(m).start()
                    share_beside(m).start()
                    store(m).start()

    def where_mine(u, act):
        m, h = units[u]

        @pl.when((z >= min(PAIRS[h])) & (z <= max(PAIRS[h])))
        def _():
            act(m)

    def corner_step(u):
        def act(m):
            arrived_across(m).wait_recv()
            corner(m, 1 - x, y, 0).start()
            arrived_beside(m).wait_recv()
            if ks[m] > 1:
                corner(m, x, 1 - y, 1).start()

        where_mine(u, act)

    def core_step(u):
        def act(m):
            store(m).wait()
            corner(m, 1 - x, 1 - y, 0).wait_recv()
            if ks[m] > 1:
                corner(m, 1 - x, 1 - y, 1).wait_recv()
            to_core(m, c).start()

        where_mine(u, act)

    def finish(u):
        m, h = units[u]
        for d in PAIRS[h]:
            to_twin(m, d).wait_send()
        for copy in first_moves(u) + second_moves(u):
            copy.wait_send()
        for zz in range(ZN):

            @pl.when(z == zz)
            def _():
                for d in PAIRS[h]:
                    if d < zz:
                        to_down(m, d).wait_send()
                    if d > zz:
                        to_up(m, d).wait_send()

        def act(m):
            to_core(m, 1 - c).wait_recv()
            share_across(m).wait_send()
            share_beside(m).wait_send()
            corner(m, 1 - x, y, 0).wait_send()
            if ks[m] > 1:
                corner(m, x, 1 - y, 1).wait_send()
            to_core(m, c).wait_send()

        where_mine(u, act)

    count = len(units)

    def at(step, u, *s):
        if 0 <= u < count:
            step(u, *s)

    for u in range(count):
        m, h = units[u]
        for d in PAIRS[h]:
            to_twin(m, d).start()
            load(m, d).start()
    for t in range(count + 8):
        at(with_twin, t)
        at(with_first, t - 1)
        at(with_second, t - 2)
        for s in range(ZN):
            at(line_step, t - 2 - s, s)
        at(corner_step, t - 6)
        at(core_step, t - 7)
    for u in range(count):
        finish(u)


def reduce_pieces(grads, ks):
    m_count = len(grads)

    def body(*refs):
        groups = [refs[i * m_count : (i + 1) * m_count] for i in range(8)]
        reduce_body(ks, *groups, *refs[8 * m_count :])

    def buffers(rows):
        return [pltpu.VMEM((ZN, rows * k) + g.shape[2:], g.dtype) for g, k in zip(grads, ks)]

    return pl.pallas_call(
        body,
        out_shape=[jax.ShapeDtypeStruct((8 * k,) + g.shape[2:], g.dtype) for g, k in zip(grads, ks)],
        in_specs=[pl.BlockSpec(memory_space=pl.ANY)] * m_count,
        out_specs=[pl.BlockSpec(memory_space=pl.ANY)] * m_count,
        scratch_shapes=buffers(4)
        + buffers(4)
        + buffers(2)
        + buffers(1)
        + buffers(1)
        + buffers(1)
        + [
            pltpu.SemaphoreType.DMA((m_count, ZN)),
            pltpu.SemaphoreType.DMA((m_count,)),
            pltpu.SemaphoreType.DMA((m_count, 27)),
            pltpu.SemaphoreType.DMA((m_count, 27)),
        ],
        compiler_params=pltpu.CompilerParams(
            collective_id=1, has_side_effects=True, vmem_limit_bytes=60 << 20
        ),
        name="reduce_grads",
    )(*grads)


VECTORS = (0, 1, 3, 4, 6, 7, 8, 12, 10)
MATRICES = (2, 5, 9, 11)
WIDE = 13312


def gather_all(params):
    layers = params[0].shape[0]
    shards = [params[i].reshape(layers, -1, 16, params[i].shape[2]) for i in MATRICES]
    full = gather_weights(shards)
    vectors = jnp.concatenate([params[i].reshape(layers, -1, params[0].shape[1]) for i in VECTORS], axis=1)
    vectors = lax.all_gather(vectors, "fsdp", axis=2)
    gathered = []
    for layer in range(layers):
        entry = [None] * 13
        for at, i in enumerate(MATRICES):
            entry[i] = full[at][layer].reshape(-1, params[i].shape[2])
        row = 0
        for i in VECTORS:
            rows = params[i].shape[1] // params[0].shape[1]
            entry[i] = jnp.moveaxis(vectors[layer, row : row + rows], 0, 1).reshape(-1)
            row += rows
        gathered.append(tuple(entry))
    return gathered


def reduce_layer(gradients):
    low = [g.astype(jnp.bfloat16) for g in gradients]
    mats = [low[i].reshape(ZN, -1, 16, low[i].shape[1]) for i in MATRICES]
    rest = [jnp.swapaxes(g[:, g.shape[1] // 8 * 8 :], 1, 2).reshape(ZN, 16, -1) for g in mats]
    vectors = jnp.concatenate([low[i].reshape(ZN, -1) for i in VECTORS], axis=1)
    width = WIDE - sum(r.shape[2] for r in rest)
    vectors = jnp.pad(vectors, ((0, 0), (0, 16 * width - vectors.shape[1]))).reshape(ZN, 16, width)
    wide = jnp.concatenate(rest + [vectors], axis=2)
    wide = jnp.swapaxes(wide.reshape(ZN, 16, 8, WIDE // 8), 1, 2)
    ks = [g.shape[1] // 8 for g in mats] + [1]
    sums = reduce_pieces(mats + [wide], ks)
    tail = jnp.swapaxes(sums[-1], 0, 1).reshape(16, WIDE)
    result = [None] * 13
    col = 0
    for at, i in enumerate(MATRICES):
        columns = low[i].shape[1]
        n = mats[at].shape[1] % 8
        extra = jnp.swapaxes(tail[:, col : col + n * columns].reshape(16, n, columns), 0, 1)
        col += n * columns
        result[i] = jnp.concatenate([sums[at].reshape(-1, columns), extra.reshape(-1, columns)], axis=0)
    flat = tail[:, col:].reshape(-1)
    col = 0
    for i in VECTORS:
        n = low[i].shape[0] // ZN
        result[i] = flat[col : col + n]
        col += n
    return tuple(r.astype(jnp.float32) for r in result)


def on_cores(tokens, segments, grad_out, *params):
    rows = tokens.shape[1]
    own_x, grad_x = to_cores(tokens[0]), to_cores(grad_out[0])
    seg_own = to_cores(segments[0])
    core = lax.rem(lax.axis_index("rep"), 2)
    pool = Cores()
    places = jnp.concatenate(
        [
            core * rows + lax.iota(jnp.int32, rows // 2),
            (3 - 2 * core) * (rows // 2) + lax.iota(jnp.int32, rows // 2),
        ]
    )
    seg_all, places_all = pool.spread(seg_own), pool.spread(places)
    visible = (seg_own[:, None] == seg_all[None, :]) & (places[:, None] >= places_all[None, :])
    gathered = gather_all(params)
    layer_count = params[0].shape[0]
    resid = own_x.astype(jnp.float32)
    stored_list = []
    for layer_index in range(layer_count):
        resid, stored = forward_layer(resid, gathered[layer_index], visible, pool)
        stored_list.append(stored)
    result = from_cores(resid.astype(jnp.bfloat16))[None]
    grad_resid = grad_x.astype(jnp.float32)
    reduced = [None] * layer_count
    for layer_index in reversed(range(layer_count)):
        grad_resid, gradients = backward_layer(
            grad_resid, stored_list[layer_index], gathered[layer_index], visible, pool
        )
        reduced[layer_index] = reduce_layer(gradients)
    stacked = tuple((jnp.stack([entry[member] for entry in reduced]) for member in range(13)))
    return (result, from_cores(grad_resid.astype(jnp.bfloat16))[None]) + stacked


def on_device(
    tokens,
    segments,
    grad_out,
    attn_gain,
    attn_shift,
    w_qkv,
    b_query,
    b_value,
    w_out,
    b_out,
    mlp_gain,
    mlp_shift,
    w_up,
    b_up,
    w_down,
    b_down,
):
    seg_own = segments[0]
    seg_all = lax.all_gather(seg_own, "seq", axis=0, tiled=True)
    offset = lax.axis_index("seq") * seg_own.shape[0]
    visible = visible_mask(seg_own, seg_all, offset)
    layer_count = attn_gain.shape[0]
    resid = tokens[0].astype(jnp.float32)
    kept_weights = []
    stored_list = []
    for layer_index in range(layer_count):
        gathered = gather_layer(
            layer_index,
            attn_gain,
            attn_shift,
            w_qkv,
            b_query,
            b_value,
            w_out,
            b_out,
            mlp_gain,
            mlp_shift,
            w_up,
            b_up,
            w_down,
            b_down,
        )
        resid, stored = forward_layer(resid, gathered, visible, Halves())
        kept_weights.append(gathered)
        stored_list.append(stored)
    result = resid.astype(jnp.bfloat16)[None]
    grad_resid = grad_out[0].astype(jnp.float32)
    reduced = [None] * layer_count
    for layer_index in reversed(range(layer_count)):
        gathered = gather_again(
            layer_index,
            attn_gain,
            attn_shift,
            w_qkv,
            b_query,
            b_value,
            w_out,
            b_out,
            mlp_gain,
            mlp_shift,
            w_up,
            b_up,
            w_down,
            b_down,
        )
        grad_resid, gradients = backward_layer(
            grad_resid, stored_list[layer_index], gathered, visible, Halves()
        )
        reduced[layer_index] = reduce_grads(gradients)
    stacked = tuple((jnp.stack([entry[member] for entry in reduced]) for member in range(13)))
    return (result, grad_resid.astype(jnp.bfloat16)[None]) + stacked


def solution(mesh):
    fits = (mesh.shape["seq"], mesh.shape["fsdp"], mesh.shape["rep"]) == (2, ZN, 4)
    return jax.shard_map(
        on_cores if fits else on_device,
        mesh=mesh,
        in_specs=(
            P(("fsdp", "rep"), "seq", None),
            P(("fsdp", "rep"), "seq"),
            P(("fsdp", "rep"), "seq", None),
            P(None, "fsdp"),
            P(None, "fsdp"),
            P(None, "fsdp", None),
            P(None, "fsdp"),
            P(None, "fsdp"),
            P(None, "fsdp", None),
            P(None, "fsdp"),
            P(None, "fsdp"),
            P(None, "fsdp"),
            P(None, "fsdp", None),
            P(None, "fsdp"),
            P(None, "fsdp", None),
            P(None, "fsdp"),
        ),
        out_specs=(
            P(("fsdp", "rep"), "seq", None),
            P(("fsdp", "rep"), "seq", None),
            P(None, "fsdp"),
            P(None, "fsdp"),
            P(None, "fsdp", None),
            P(None, "fsdp"),
            P(None, "fsdp"),
            P(None, "fsdp", None),
            P(None, "fsdp"),
            P(None, "fsdp"),
            P(None, "fsdp"),
            P(None, "fsdp", None),
            P(None, "fsdp"),
            P(None, "fsdp", None),
            P(None, "fsdp"),
        ),
        check_vma=False,
    )
```

```python
import functools
import math

import jax
import jax.numpy as jnp
from jax import lax
from jax.experimental import pallas as pl
from jax.experimental.pallas import tpu as pltpu
from jax.sharding import PartitionSpec as P

HEAD_DIM = 64
MESH = pl.DeviceIdType.MESH


NORM_EPSILON = 1e-05
MASKED = -1e30


def layer_norm(inputs, gain, bias_term):
    center = inputs - jnp.mean(inputs, axis=-1, keepdims=True)
    spread = jnp.mean(center * center, axis=-1, keepdims=True)
    return center * lax.rsqrt(spread + NORM_EPSILON) * gain + bias_term


def gelu_tanh(inputs):
    return jax.nn.gelu(inputs, approximate=True)


def product(left, right):
    return jnp.dot(left, right, preferred_element_type=jnp.float32)


def inner_rows(left, right):
    return lax.dot_general(
        left, right, (((0,), (0,)), ((), ())), preferred_element_type=jnp.float32
    )


def outer_cols(left, right):
    return lax.dot_general(
        left, right, (((1,), (1,)), ((), ())), preferred_element_type=jnp.float32
    )


def column_sum(values_low):
    return jnp.sum(values_low.astype(jnp.float32), axis=0)


def visible_mask(seg_own, seg_all, offset):
    row_pos = offset + lax.iota(jnp.int32, seg_own.shape[0])
    col_pos = lax.iota(jnp.int32, seg_all.shape[0])
    return (seg_own[:, None] == seg_all[None, :]) & (row_pos[:, None] >= col_pos[None, :])


def head_scores(queries, keys_all, visible, head_count):
    query_heads = queries.reshape(queries.shape[0], head_count, HEAD_DIM)
    key_heads = keys_all.reshape(keys_all.shape[0], head_count, HEAD_DIM)
    scores = jnp.einsum("thd,shd->hts", query_heads, key_heads, preferred_element_type=jnp.float32)
    return jnp.where(visible[None], scores, MASKED)


def gather_layer(
    layer_index,
    attn_gain,
    attn_shift,
    w_qkv,
    b_query,
    b_value,
    w_out,
    b_out,
    mlp_gain,
    mlp_shift,
    w_up,
    b_up,
    w_down,
    b_down,
):
    return (
        lax.all_gather(attn_gain[layer_index], "fsdp", axis=0, tiled=True),
        lax.all_gather(attn_shift[layer_index], "fsdp", axis=0, tiled=True),
        lax.all_gather(w_qkv[layer_index], "fsdp", axis=0, tiled=True),
        lax.all_gather(b_query[layer_index], "fsdp", axis=0, tiled=True),
        lax.all_gather(b_value[layer_index], "fsdp", axis=0, tiled=True),
        lax.all_gather(w_out[layer_index], "fsdp", axis=0, tiled=True),
        lax.all_gather(b_out[layer_index], "fsdp", axis=0, tiled=True),
        lax.all_gather(mlp_gain[layer_index], "fsdp", axis=0, tiled=True),
        lax.all_gather(mlp_shift[layer_index], "fsdp", axis=0, tiled=True),
        lax.all_gather(w_up[layer_index], "fsdp", axis=0, tiled=True),
        lax.all_gather(b_up[layer_index], "fsdp", axis=0, tiled=True),
        lax.all_gather(w_down[layer_index], "fsdp", axis=0, tiled=True),
        lax.all_gather(b_down[layer_index], "fsdp", axis=0, tiled=True),
    )


def gather_again(
    layer_index,
    attn_gain,
    attn_shift,
    w_qkv,
    b_query,
    b_value,
    w_out,
    b_out,
    mlp_gain,
    mlp_shift,
    w_up,
    b_up,
    w_down,
    b_down,
):
    return (
        lax.all_gather(attn_gain[layer_index], "fsdp", axis=0, tiled=True),
        lax.all_gather(attn_shift[layer_index], "fsdp", axis=0, tiled=True),
        lax.all_gather(w_qkv[layer_index], "fsdp", axis=0, tiled=True),
        lax.all_gather(b_query[layer_index], "fsdp", axis=0, tiled=True),
        lax.all_gather(b_value[layer_index], "fsdp", axis=0, tiled=True),
        lax.all_gather(w_out[layer_index], "fsdp", axis=0, tiled=True),
        lax.all_gather(b_out[layer_index], "fsdp", axis=0, tiled=True),
        lax.all_gather(mlp_gain[layer_index], "fsdp", axis=0, tiled=True),
        lax.all_gather(mlp_shift[layer_index], "fsdp", axis=0, tiled=True),
        lax.all_gather(w_up[layer_index], "fsdp", axis=0, tiled=True),
        lax.all_gather(b_up[layer_index], "fsdp", axis=0, tiled=True),
        lax.all_gather(w_down[layer_index], "fsdp", axis=0, tiled=True),
        lax.all_gather(b_down[layer_index], "fsdp", axis=0, tiled=True),
    )


def forward_layer(resid, gathered, visible, pool):
    (
        attn_gain,
        attn_shift,
        w_qkv,
        b_query,
        b_value,
        w_out,
        b_out,
        mlp_gain,
        mlp_shift,
        w_up,
        b_up,
        w_down,
        b_down,
    ) = gathered
    model_width = resid.shape[1]
    head_count = model_width // HEAD_DIM
    query_scale = 1.0 / math.sqrt(HEAD_DIM)
    normed_attn = layer_norm(
        resid, attn_gain.astype(jnp.float32), attn_shift.astype(jnp.float32)
    ).astype(jnp.bfloat16)
    proj_all = product(normed_attn, w_qkv)
    queries = ((proj_all[:, :model_width] + b_query.astype(jnp.float32)) * query_scale).astype(
        jnp.bfloat16
    )
    keys_own = proj_all[:, model_width : 2 * model_width].astype(jnp.bfloat16)
    values_own = (proj_all[:, 2 * model_width :] + b_value.astype(jnp.float32)).astype(jnp.bfloat16)
    keys_all, values_all = pool.spread(keys_own), pool.spread(values_own)
    scores = head_scores(queries, keys_all, visible, head_count)
    row_max = jnp.max(scores, axis=-1, keepdims=True)
    exponent = jnp.exp(scores - row_max)
    row_sum = jnp.sum(exponent, axis=-1, keepdims=True)
    weights_soft = (exponent / row_sum).astype(jnp.bfloat16)
    log_total = row_max + jnp.log(row_sum)
    value_heads = values_all.reshape(values_all.shape[0], head_count, HEAD_DIM)
    attended = jnp.einsum(
        "hts,shd->thd", weights_soft, value_heads, preferred_element_type=jnp.float32
    )
    attended = attended.reshape(resid.shape[0], model_width).astype(jnp.bfloat16)
    middle = resid + product(attended, w_out) + b_out.astype(jnp.float32)
    normed_mlp = layer_norm(
        middle, mlp_gain.astype(jnp.float32), mlp_shift.astype(jnp.float32)
    ).astype(jnp.bfloat16)
    pre_act = product(normed_mlp, w_up) + b_up.astype(jnp.float32)
    activated = gelu_tanh(pre_act).astype(jnp.bfloat16)
    output = middle + product(activated, w_down) + b_down.astype(jnp.float32)
    stored = (
        resid,
        normed_attn,
        queries,
        keys_all,
        values_all,
        log_total,
        attended,
        middle,
        normed_mlp,
        pre_act,
        activated,
    )
    return (output, stored)


def backward_layer(grad_next, stored, gathered, visible, pool):
    (
        attn_gain,
        attn_shift,
        w_qkv,
        b_query,
        b_value,
        w_out,
        b_out,
        mlp_gain,
        mlp_shift,
        w_up,
        b_up,
        w_down,
        b_down,
    ) = gathered
    (
        resid,
        normed_attn,
        queries,
        keys_all,
        values_all,
        log_total,
        attended,
        middle,
        normed_mlp,
        pre_act,
        activated,
    ) = stored
    model_width = resid.shape[1]
    tok_rows = resid.shape[0]
    key_rows = keys_all.shape[0]
    head_count = model_width // HEAD_DIM
    query_scale = 1.0 / math.sqrt(HEAD_DIM)
    grad_mlp = grad_next.astype(jnp.bfloat16)
    grad_b_down = column_sum(grad_mlp)
    grad_w_down = inner_rows(activated, grad_mlp)
    grad_act = outer_cols(grad_mlp, w_down)
    gelu_value, gelu_pull = jax.vjp(gelu_tanh, pre_act)
    grad_pre = gelu_pull(grad_act)[0].astype(jnp.bfloat16)
    grad_b_up = column_sum(grad_pre)
    grad_w_up = inner_rows(normed_mlp, grad_pre)
    grad_nm = outer_cols(grad_pre, w_up)
    norm_value, norm_pull = jax.vjp(
        layer_norm, middle, mlp_gain.astype(jnp.float32), mlp_shift.astype(jnp.float32)
    )
    grad_middle, grad_mlp_gain, grad_mlp_shift = norm_pull(grad_nm)
    grad_middle = grad_middle + grad_next
    grad_branch = grad_middle.astype(jnp.bfloat16)
    grad_b_out = column_sum(grad_branch)
    grad_w_out = inner_rows(attended, grad_branch)
    grad_attended = outer_cols(grad_branch, w_out).astype(jnp.bfloat16)
    scores = head_scores(queries, keys_all, visible, head_count)
    weights_full = jnp.exp(scores - log_total)
    weights_soft = weights_full.astype(jnp.bfloat16)
    grad_heads = grad_attended.reshape(tok_rows, head_count, HEAD_DIM)
    query_heads = queries.reshape(tok_rows, head_count, HEAD_DIM)
    key_heads = keys_all.reshape(key_rows, head_count, HEAD_DIM)
    value_heads = values_all.reshape(key_rows, head_count, HEAD_DIM)
    grad_value_terms = jnp.einsum(
        "hts,thd->shd", weights_soft, grad_heads, preferred_element_type=jnp.float32
    )
    grad_probs = jnp.einsum(
        "thd,shd->hts", grad_heads, value_heads, preferred_element_type=jnp.float32
    )
    inner_sum = jnp.sum(weights_full * grad_probs, axis=-1, keepdims=True)
    grad_scores = (weights_full * (grad_probs - inner_sum)).astype(jnp.bfloat16)
    grad_queries = jnp.einsum(
        "hts,shd->thd", grad_scores, key_heads, preferred_element_type=jnp.float32
    )
    grad_queries = grad_queries.reshape(tok_rows, model_width).astype(jnp.bfloat16) * query_scale
    grad_key_terms = jnp.einsum(
        "hts,thd->shd", grad_scores, query_heads, preferred_element_type=jnp.float32
    )
    grad_keys = pool.collect(grad_key_terms.reshape(key_rows, model_width).astype(jnp.bfloat16))
    grad_values = pool.collect(grad_value_terms.reshape(key_rows, model_width).astype(jnp.bfloat16))
    grad_keys = grad_keys.astype(jnp.bfloat16)
    grad_values = grad_values.astype(jnp.bfloat16)
    grad_proj = jnp.concatenate([grad_queries, grad_keys, grad_values], axis=1)
    grad_b_query = column_sum(grad_queries)
    grad_b_value = column_sum(grad_values)
    grad_w_qkv = inner_rows(normed_attn, grad_proj)
    grad_na = outer_cols(grad_proj, w_qkv)
    first_value, first_pull = jax.vjp(
        layer_norm, resid, attn_gain.astype(jnp.float32), attn_shift.astype(jnp.float32)
    )
    grad_resid, grad_attn_gain, grad_attn_shift = first_pull(grad_na)
    grad_resid = grad_resid + grad_middle
    gradients = (
        grad_attn_gain,
        grad_attn_shift,
        grad_w_qkv,
        grad_b_query,
        grad_b_value,
        grad_w_out,
        grad_b_out,
        grad_mlp_gain,
        grad_mlp_shift,
        grad_w_up,
        grad_b_up,
        grad_w_down,
        grad_b_down,
    )
    return (grad_resid, gradients)


def reduce_grads(gradients):
    shares = (
        lax.psum_scatter(gradients[0], ("fsdp", "rep"), scatter_dimension=0, tiled=True),
        lax.psum_scatter(gradients[1], ("fsdp", "rep"), scatter_dimension=0, tiled=True),
        lax.psum_scatter(gradients[2], ("fsdp", "rep"), scatter_dimension=0, tiled=True),
        lax.psum_scatter(gradients[3], ("fsdp", "rep"), scatter_dimension=0, tiled=True),
        lax.psum_scatter(gradients[4], ("fsdp", "rep"), scatter_dimension=0, tiled=True),
        lax.psum_scatter(gradients[5], ("fsdp", "rep"), scatter_dimension=0, tiled=True),
        lax.psum_scatter(gradients[6], ("fsdp", "rep"), scatter_dimension=0, tiled=True),
        lax.psum_scatter(gradients[7], ("fsdp", "rep"), scatter_dimension=0, tiled=True),
        lax.psum_scatter(gradients[8], ("fsdp", "rep"), scatter_dimension=0, tiled=True),
        lax.psum_scatter(gradients[9], ("fsdp", "rep"), scatter_dimension=0, tiled=True),
        lax.psum_scatter(gradients[10], ("fsdp", "rep"), scatter_dimension=0, tiled=True),
        lax.psum_scatter(gradients[11], ("fsdp", "rep"), scatter_dimension=0, tiled=True),
        lax.psum_scatter(gradients[12], ("fsdp", "rep"), scatter_dimension=0, tiled=True),
    )
    shares = (
        lax.psum(shares[0].astype(jnp.bfloat16), "seq").astype(jnp.float32),
        lax.psum(shares[1].astype(jnp.bfloat16), "seq").astype(jnp.float32),
        lax.psum(shares[2].astype(jnp.bfloat16), "seq").astype(jnp.float32),
        lax.psum(shares[3].astype(jnp.bfloat16), "seq").astype(jnp.float32),
        lax.psum(shares[4].astype(jnp.bfloat16), "seq").astype(jnp.float32),
        lax.psum(shares[5].astype(jnp.bfloat16), "seq").astype(jnp.float32),
        lax.psum(shares[6].astype(jnp.bfloat16), "seq").astype(jnp.float32),
        lax.psum(shares[7].astype(jnp.bfloat16), "seq").astype(jnp.float32),
        lax.psum(shares[8].astype(jnp.bfloat16), "seq").astype(jnp.float32),
        lax.psum(shares[9].astype(jnp.bfloat16), "seq").astype(jnp.float32),
        lax.psum(shares[10].astype(jnp.bfloat16), "seq").astype(jnp.float32),
        lax.psum(shares[11].astype(jnp.bfloat16), "seq").astype(jnp.float32),
        lax.psum(shares[12].astype(jnp.bfloat16), "seq").astype(jnp.float32),
    )
    return (
        lax.all_gather(shares[0].astype(jnp.bfloat16), "rep", axis=0, tiled=True).astype(
            jnp.float32
        ),
        lax.all_gather(shares[1].astype(jnp.bfloat16), "rep", axis=0, tiled=True).astype(
            jnp.float32
        ),
        lax.all_gather(shares[2].astype(jnp.bfloat16), "rep", axis=0, tiled=True).astype(
            jnp.float32
        ),
        lax.all_gather(shares[3].astype(jnp.bfloat16), "rep", axis=0, tiled=True).astype(
            jnp.float32
        ),
        lax.all_gather(shares[4].astype(jnp.bfloat16), "rep", axis=0, tiled=True).astype(
            jnp.float32
        ),
        lax.all_gather(shares[5].astype(jnp.bfloat16), "rep", axis=0, tiled=True).astype(
            jnp.float32
        ),
        lax.all_gather(shares[6].astype(jnp.bfloat16), "rep", axis=0, tiled=True).astype(
            jnp.float32
        ),
        lax.all_gather(shares[7].astype(jnp.bfloat16), "rep", axis=0, tiled=True).astype(
            jnp.float32
        ),
        lax.all_gather(shares[8].astype(jnp.bfloat16), "rep", axis=0, tiled=True).astype(
            jnp.float32
        ),
        lax.all_gather(shares[9].astype(jnp.bfloat16), "rep", axis=0, tiled=True).astype(
            jnp.float32
        ),
        lax.all_gather(shares[10].astype(jnp.bfloat16), "rep", axis=0, tiled=True).astype(
            jnp.float32
        ),
        lax.all_gather(shares[11].astype(jnp.bfloat16), "rep", axis=0, tiled=True).astype(
            jnp.float32
        ),
        lax.all_gather(shares[12].astype(jnp.bfloat16), "rep", axis=0, tiled=True).astype(
            jnp.float32
        ),
    )


class Halves:
    def spread(self, rows):
        return lax.all_gather(rows, "seq", axis=0, tiled=True)

    def collect(self, rows):
        return lax.psum_scatter(rows, "seq", scatter_dimension=0, tiled=True)


def from_cores(rows):
    half = rows.shape[0] // 2
    spots = [(x, y, c) for x in range(2) for y in range(2) for c in range(2)]
    first = [(c * 4 + y * 2 + x, x * 4 + y * 2 + c) for x, y, c in spots]
    second = [(c * 4 + y * 2 + 1 - x, x * 4 + y * 2 + c) for x, y, c in spots]
    return jnp.concatenate(
        [
            lax.ppermute(rows[:half], ("seq", "rep"), first),
            lax.ppermute(rows[half:], ("seq", "rep"), second),
        ],
        axis=0,
    )


ZN = 4


def neighbours():
    x, z, r = lax.axis_index("seq"), lax.axis_index("fsdp"), lax.axis_index("rep")
    y, c = r // 2, r % 2
    across = (1 - x, z, r)
    beside = (x, z, (1 - y) * 2 + c)
    twin = (x, z, y * 2 + (1 - c))
    up = (x, (z + 1) % ZN, r)
    down = (x, (z + ZN - 1) % ZN, r)
    return x, y, z, c, across, beside, twin, up, down


def greet(z, c, x, across, beside, twin, diag, up, down):
    barrier = pltpu.get_barrier_semaphore()

    def tell(device):
        pl.semaphore_signal(barrier, inc=1, device_id=device, device_id_type=MESH)

    for device in (across, beside, twin):
        tell(device)
    if diag is not None:

        @pl.when(c != x)
        def _():
            tell(diag)

    @pl.when(z < ZN - 1)
    def _():
        tell(up)

    @pl.when(z > 0)
    def _():
        tell(down)

    extra = 0 if diag is None else (x + c) % 2
    pl.semaphore_wait(barrier, 3 + extra + (z + ZN - 1) // ZN + (2 * ZN - 2 - z) // ZN)


GELU_A = math.sqrt(2.0 / math.pi)
GELU_B = 0.044715
QUERY_SCALE = 1.0 / math.sqrt(HEAD_DIM)
HEAD_ROWS = 24
PACE = 2


NT = (((1,), (1,)), ((), ()))
TN = (((0,), (0,)), ((), ()))
BLOCK = 256
RANGES = (((0, 256), (256, 1024)), ((0, 768), (256, 512)))
VMEM_LIMIT = 60 << 20


def dot_nt(left, right):
    return lax.dot_general(left, right, NT, preferred_element_type=jnp.float32)


def dot_tn(left, right):
    return lax.dot_general(left, right, TN, preferred_element_type=jnp.float32)


def tiles(width, tile, act):
    whole = width // tile

    def step(i, carry):
        act(pl.multiple_of(i * tile, tile), tile)
        return carry

    lax.fori_loop(0, whole, step, 0)
    if width % tile:
        act(whole * tile, width % tile)


def tiles_between(low, high, tile, act):
    def step(i, carry):
        act(pl.multiple_of(i * tile, tile), tile)
        return carry

    if low // tile < high // tile:
        lax.fori_loop(low // tile, high // tile, step, 0)
    if high % tile:
        act(high // tile * tile, high % tile)


def norm_parts(rows):
    center = rows - jnp.mean(rows, axis=1, keepdims=True)
    scale = lax.rsqrt(jnp.mean(center * center, axis=1, keepdims=True) + NORM_EPSILON)
    return center * scale, scale


def norm_into(source, gain, shift, target):
    def act(start, size):
        rows = pl.ds(start, size)
        unit, _ = norm_parts(source[rows, :])
        target[rows, :] = (unit * gain + shift).astype(target.dtype)

    tiles(source.shape[0], 64, act)


def norm_back(source, grad, extra, gain, target, gain_grad, shift_grad, low=None):
    gain_grad[...] = jnp.zeros_like(gain_grad)
    shift_grad[...] = jnp.zeros_like(shift_grad)

    def act(start, size):
        rows = pl.ds(start, size)
        unit, scale = norm_parts(source[rows, :])
        g = grad[rows, :]
        q = g * gain
        mean_q = jnp.mean(q, axis=1, keepdims=True)
        mean_qn = jnp.mean(q * unit, axis=1, keepdims=True)
        out = extra[rows, :] + (q - mean_q - unit * mean_qn) * scale
        target[rows, :] = out
        if low is not None:
            low[rows, :] = out.astype(low.dtype)
        gain_grad[...] += jnp.sum(g * unit, axis=0, keepdims=True)
        shift_grad[...] += jnp.sum(g, axis=0, keepdims=True)

    tiles(source.shape[0], 64, act)


def whole(count):
    return [pl.BlockSpec(memory_space=pltpu.VMEM)] * count


def anywhere(count):
    return [pl.BlockSpec(memory_space=pl.ANY)] * count


def shaped(shape, dtype=jnp.float32):
    return jax.ShapeDtypeStruct(shape, dtype)


def params():
    return pltpu.CompilerParams(vmem_limit_bytes=VMEM_LIMIT)


def of_head(values, j):
    if values.shape[1] == HEAD_DIM:
        return values
    lane = lax.broadcasted_iota(jnp.int32, values.shape, 1)
    return jnp.where(lane // HEAD_DIM == j, values, jnp.zeros_like(values))


ZA, ZR, GX, GY, GD1, GD2, GC = range(7)
ROW = dict(attn_gain=0, attn_shift=1, b_query=2, b_value=3, b_out=4, mlp_gain=5, mlp_shift=6, b_down=7)
SAVED = ("x", "normed_attn", "q", "keys", "values", "attended", "lse", "middle", "normed_mlp", "slope", "activated")


def advance(steps, count):
    for _ in range(count):
        if next(steps, None) is None:
            return


def weight_moves(ins, outs, send_sem, recv_sem, place):
    x, y, z, c, across, beside, twin, up, down = place
    m_count = len(ins) - 1
    layers = ins[0].shape[0]
    units = [(layer, m) for layer in range(layers) for m in range(m_count + 1)]
    index = {unit: i for i, unit in enumerate(units)}

    def depth(u):
        return ins[u[1]].shape[1] // 8

    def owned(u, px, py, half=None):
        k = depth(u)
        base = (c * 4 + px * 2 + py) * k
        if half is None:
            return pl.ds(base, k)
        return pl.ds(base + half * (k // 2), k // 2)

    def rest(u):
        n = ins[u[1]].shape[1]
        return pl.ds(n // 8 * 8, n % 8)

    def slab(u, core):
        return pl.ds(core * 4 * depth(u), 4 * depth(u))

    def move(u, zz, rows, device, kind, source=None, send_kind=None):
        target = outs[u[1]].at[u[0], zz, rows]
        return pltpu.make_async_remote_copy(
            src_ref=target if source is None else source,
            dst_ref=target,
            send_sem=send_sem.at[index[u], zz, kind if send_kind is None else send_kind],
            recv_sem=recv_sem.at[index[u], zz, kind],
            device_id=device,
            device_id_type=MESH,
        )

    def own_sends(u, act):
        source = ins[u[1]].at[u[0]]

        def along(device, first):
            if depth(u):
                act(move(u, z, owned(u, x, y), device, ZA, source.at[owned(u, x, y)], first))
            act(move(u, z, rest(u), device, ZR, source.at[rest(u)], first + 1))

        @pl.when(z < ZN - 1)
        def _():
            along(up, 0)

        @pl.when(z > 0)
        def _():
            along(down, 2)

    def both(s, act):
        @pl.when(z >= s)
        def _():
            act(z - s, 0)

        @pl.when(z + s <= ZN - 1)
        def _():
            act(z + s, 1)

    def onward(u, zz, d, act):
        def along(device):
            if depth(u):
                act(move(u, zz, owned(u, x, y), device, ZA))
            act(move(u, zz, rest(u), device, ZR))

        if d == 0:

            @pl.when(z < ZN - 1)
            def _():
                along(up)

        else:

            @pl.when(z > 0)
            def _():
                along(down)

    def line_step(u, s):
        def act(zz, d):
            if depth(u):
                move(u, zz, owned(u, x, y), across, ZA).wait_recv()
            move(u, zz, rest(u), across, ZR).wait_recv()
            onward(u, zz, d, lambda copy: copy.start())
            if depth(u):
                move(u, zz, owned(u, x, y), across, GX).start()
                move(u, zz, owned(u, x, y), beside, GY).start()

        both(s, act)

    def plane_step(u, s):
        def act(zz, d):
            move(u, zz, owned(u, 1 - x, y), across, GX).wait_recv()
            move(u, zz, owned(u, 1 - x, y, 0), beside, GD1).start()
            move(u, zz, owned(u, x, 1 - y), beside, GY).wait_recv()
            move(u, zz, owned(u, x, 1 - y, 1), across, GD2).start()

        both(s, act)

    def corner_step(u, s):
        def act(zz, d):
            move(u, zz, owned(u, 1 - x, 1 - y, 0), beside, GD1).wait_recv()
            move(u, zz, owned(u, 1 - x, 1 - y, 1), across, GD2).wait_recv()
            move(u, zz, slab(u, c), twin, GC).start()

        both(s, act)

    def arrive(u):
        for s in range(1, ZN):
            both(s, lambda zz, d: move(u, zz, slab(u, 1 - c), twin, GC).wait_recv())

    def finish(u):
        own_sends(u, lambda copy: copy.wait_send())
        for s in range(1, ZN):

            def act(zz, d):
                onward(u, zz, d, lambda copy: copy.wait_send())
                if depth(u):
                    move(u, zz, owned(u, x, y), across, GX).wait_send()
                    move(u, zz, owned(u, x, y), beside, GY).wait_send()
                    move(u, zz, owned(u, 1 - x, y, 0), beside, GD1).wait_send()
                    move(u, zz, owned(u, x, 1 - y, 1), across, GD2).wait_send()
                    move(u, zz, slab(u, c), twin, GC).wait_send()

            both(s, act)

    matrices = [u for u in units if u[1] < m_count]
    vectors = [u for u in units if u[1] == m_count]
    count = len(matrices)

    def steps():
        for u in vectors + matrices[:2]:
            own_sends(u, lambda copy: copy.start())
        for s in range(1, ZN):
            for u in vectors:
                line_step(u, s)
        yield ("vectors",)
        for t in range(count + 4):
            if t + 2 < count:
                own_sends(matrices[t + 2], lambda copy: copy.start())
            for s in range(1, ZN):
                if 0 <= t + 1 - s < count:
                    line_step(matrices[t + 1 - s], s)
                    yield ("line",)
            for s in range(1, ZN):
                if 0 <= t - s < count:
                    plane_step(matrices[t - s], s)
                    yield ("plane",)
            for s in range(1, ZN):
                if 0 <= t - 1 - s < count:
                    corner_step(matrices[t - 1 - s], s)
                    yield ("here", matrices[t - 1 - s]) if s == ZN - 1 else ("corner",)

    return steps, arrive, lambda: [finish(u) for u in units]


def attend(core, q, keys, values, mask, attended, lse, first, last):
    def slab(start, size, head):
        cols = pl.ds(start, size)
        for variant in range(2):

            @pl.when(core == variant)
            def _():
                for row, high in RANGES[variant]:
                    rows = slice(row, row + BLOCK)
                    qs = q[rows, cols]
                    ks, vs = keys[:high, cols], values[:high, cols]
                    parts = []
                    for j in range(size // HEAD_DIM):
                        s = dot_nt(ks, of_head(qs, j)) + mask[:high, rows]
                        top = jnp.max(s, axis=0, keepdims=True)
                        e = jnp.exp(s - top)
                        total = jnp.sum(e, axis=0, keepdims=True)
                        lse[pl.ds(head + j, 1), rows] = top + jnp.log(total)
                        out = dot_tn(vs, e.astype(jnp.bfloat16)) * (1.0 / total)
                        parts.append(out[j * HEAD_DIM : (j + 1) * HEAD_DIM])
                    out = jnp.concatenate(parts, axis=0) if len(parts) > 1 else parts[0]
                    attended[rows, cols] = out.T.astype(jnp.bfloat16)

    over_slabs(q.shape[1], slab, first, last)


def over_slabs(width, slab, first, last):
    pair = 2 * HEAD_DIM
    full = width // pair

    def step(i, carry):
        slab(pl.multiple_of(i * pair, pair), pair, i * 2)
        return carry

    if first < min(last, full):
        lax.fori_loop(first, min(last, full), step, 0)
    if last > full and width % pair:
        slab(full * pair, HEAD_DIM, full * 2)


def forward_body(
    tokens, grads, segs, vectors, w_qkv, w_out, w_up, w_down,
    full_qkv, full_out, full_up, full_down, full_vectors, result, grads_here, mask_out, rows_out, *rest_refs,
):
    layers = w_qkv.shape[0]
    saved = [dict(zip(SAVED, rest_refs[i * len(SAVED) : (i + 1) * len(SAVED)])) for i in range(layers)]
    (
        wq, wo, wu, wd, xs, tok, na, nm, q, keys, values, mask, att, middle, slope, act_buf, lse,
        vecs, rows, b_up, b_proj, seg_nat, seg_row,
        send_sem, recv_sem, load_sem, save_sem, kv_send, kv_recv, in_send, in_recv, in_local, free_sem,
    ) = rest_refs[layers * len(SAVED) :]
    place = neighbours()
    x, y, z, c, across, beside, twin, up, down = place
    diag = (1 - x, z, y * 2 + (1 - c))
    here = c == x
    greet(z, c, x, across, beside, twin, diag, up, down)
    width = xs.shape[1]
    half = BLOCK
    parts = [w_qkv, w_out, w_up, w_down]
    fulls = [full_qkv, full_out, full_up, full_down]
    buffers = [wq, wo, wu, wd]
    steps, arrive, finish = weight_moves(parts + [vectors], fulls + [full_vectors], send_sem, recv_sem, place)

    def in_move(i, source, target, device):
        return pltpu.make_async_remote_copy(
            src_ref=source, dst_ref=target, send_sem=in_send.at[i], recv_sem=in_recv.at[i],
            device_id=device, device_id_type=MESH,
        )

    top, low = pl.ds(0, half), pl.ds(half, half)

    def in_copies(i, source, target):
        stay = pltpu.make_async_copy(source.at[top], target.at[top], in_local.at[i])
        return (
            stay,
            in_move(2 * i + 1, source.at[low], target.at[low], twin),
            in_move(2 * i, source.at[top], target.at[top], diag),
            in_move(2 * i + 1, source.at[low], target.at[low], across),
        )

    tok_copies = in_copies(0, tokens, tok)
    grad_copies = in_copies(1, grads, grads_here)
    seg_stay = pltpu.make_async_copy(segs, seg_nat.at[x], in_local.at[2])
    seg_twin = in_move(4, segs, seg_nat.at[x], twin)
    seg_across = in_move(4, segs, seg_nat.at[x], across)
    seg_diag = pltpu.make_async_remote_copy(
        src_ref=segs, dst_ref=seg_nat.at[x], send_sem=in_send.at[5], recv_sem=in_recv.at[5],
        device_id=diag, device_id_type=MESH,
    )

    @pl.when(here)
    def _():
        for copy in (seg_stay, seg_twin, tok_copies[0], tok_copies[1], grad_copies[0], grad_copies[1]):
            copy.start()

    @pl.when(jnp.logical_not(here))
    def _():
        for copy in (seg_across, seg_diag, tok_copies[2], tok_copies[3], grad_copies[2], grad_copies[3]):
            copy.start()

    def wait_in(copies):
        @pl.when(here)
        def _():
            copies[0].wait()
            copies[1].wait_recv()

        @pl.when(jnp.logical_not(here))
        def _():
            copies[2].wait_recv()
            copies[3].wait_recv()

    def wait_segs():
        @pl.when(here)
        def _():
            seg_stay.wait()
            seg_across.wait_recv()

        @pl.when(jnp.logical_not(here))
        def _():
            seg_twin.wait_recv()
            seg_diag.wait_recv()

    def finish_in():
        @pl.when(here)
        def _():
            grad_copies[0].wait()
            grad_copies[1].wait_recv()
            for copy in (seg_twin, tok_copies[1], grad_copies[1]):
                copy.wait_send()

        @pl.when(jnp.logical_not(here))
        def _():
            grad_copies[2].wait_recv()
            grad_copies[3].wait_recv()
            for copy in (seg_across, seg_diag, tok_copies[2], tok_copies[3], grad_copies[2], grad_copies[3]):
                copy.wait_send()

    comm = steps()
    seen = set()
    loaded = {}
    done_with = set()

    def tick(count=1):
        for _ in range(count):
            label = next(comm, None)
            if label is None:
                return False
            seen.add(label)
            if label[0] == "here":
                fetch_ready()
        return True

    def loads(u):
        layer, m = u
        n = parts[m].shape[1]
        copies = [pltpu.make_async_copy(parts[m].at[layer], buffers[m].at[pl.ds(z * n, n)], load_sem.at[m, 0])]
        for s in range(1, ZN):
            zz = (z + s) % ZN
            copies.append(
                pltpu.make_async_copy(fulls[m].at[layer, zz], buffers[m].at[pl.ds(zz * n, n)], load_sem.at[m, s])
            )
        return copies

    def fetch_ready(upto=None):
        for layer in range(layers):
            for m in range(len(parts)):
                u = (layer, m)
                if u in loaded or ("here", u) not in seen:
                    continue
                if layer and (layer - 1, m) not in done_with:
                    continue
                following = (layer, m + 1) if m + 1 < len(parts) else (layer + 1, 0)
                if u != upto and following[0] < layers and ("here", following) not in seen:
                    continue
                arrive(u)
                for copy in loads(u):
                    copy.start()
                loaded[u] = True

    def need(u):
        while ("here", u) not in seen:
            if not tick():
                break
        fetch_ready(u)
        for copy in loads(u):
            copy.wait()

    pending = []

    def save(layer, name, buffer):
        copy = pltpu.make_async_copy(buffer, saved[layer][name], save_sem.at[layer, SAVED.index(name)])
        copy.start()
        pending.append(copy)

    def settle():
        while pending:
            pending.pop().wait()

    def row(layer, name):
        return rows[layer, pl.ds(ROW[name], 1), :]

    def make_mask():
        wait_segs()
        joined = jnp.concatenate([seg_nat[0], seg_nat[1]], axis=1).astype(jnp.float32)
        seg_row[...] = jnp.broadcast_to(joined, seg_row.shape)
        column = seg_row[...].T[:, :1]
        for block in range(2):
            base = ((2 * c) if block == 0 else (3 - 2 * c)) * BLOCK
            own = seg_row[0:1, pl.ds(pl.multiple_of(base, BLOCK), BLOCK)]
            spot = lax.broadcasted_iota(jnp.int32, (mask.shape[0], BLOCK), 0)
            mine = lax.broadcasted_iota(jnp.int32, (mask.shape[0], BLOCK), 1) + base
            ok = (column == own) & (spot <= mine)
            mask[:, block * BLOCK : (block + 1) * BLOCK] = jnp.where(ok, 0.0, MASKED).astype(jnp.float32)
        copy = pltpu.make_async_copy(mask, mask_out, save_sem.at[0, len(SAVED)])
        copy.start()
        pending.append(copy)

    def make_rows(layer):
        copies = [
            pltpu.make_async_copy(vectors.at[layer, 0], vecs.at[z], load_sem.at[4, 0])
        ] + [
            pltpu.make_async_copy(full_vectors.at[layer, (z + s) % ZN, 0], vecs.at[(z + s) % ZN], load_sem.at[4, s])
            for s in range(1, ZN)
        ]
        for copy in copies:
            copy.start()
        for copy in copies:
            copy.wait()
        share = vecs.shape[2]
        b_proj[layer, 0:1, :] = jnp.zeros((1, b_proj.shape[2]), jnp.float32)
        for zz in range(ZN):
            block = vecs[zz].astype(jnp.float32)
            rows[layer, 0:8, zz * share : (zz + 1) * share] = block[0:8]
            for name, at in (("b_query", 0), ("b_value", 2 * width)):
                b_proj[layer, 0:1, at + zz * share : at + (zz + 1) * share] = block[ROW[name] : ROW[name] + 1]
            for j in range(ZN):
                at = (zz * ZN + j) * share
                b_up[layer, 0:1, at : at + share] = block[8 + j : 9 + j]

    def swap_moves(layer):
        moves = []
        for i, ref in enumerate((keys, values)):
            for block in range(2):
                at = ((2 * c) if block == 0 else (3 - 2 * c)) * BLOCK
                spot = ref.at[pl.ds(pl.multiple_of(at, BLOCK), BLOCK)]
                moves.append(
                    pltpu.make_async_remote_copy(
                        src_ref=spot, dst_ref=spot, send_sem=kv_send.at[layer, i, block],
                        recv_sem=kv_recv.at[layer, i, block], device_id=twin, device_id_type=MESH,
                    )
                )
        return moves

    def swap_waits(layer):
        moves = []
        for i, ref in enumerate((keys, values)):
            for block in range(2):
                at = ((2 - 2 * c) if block == 0 else (1 + 2 * c)) * BLOCK
                spot = ref.at[pl.ds(pl.multiple_of(at, BLOCK), BLOCK)]
                moves.append(
                    pltpu.make_async_remote_copy(
                        src_ref=spot, dst_ref=spot, send_sem=kv_send.at[layer, i, block],
                        recv_sem=kv_recv.at[layer, i, block], device_id=twin, device_id_type=MESH,
                    )
                )
        return moves

    def matrix(buffer, cols):
        return buffer[:, :, cols].reshape(-1, cols.size)

    def compute(layer):
        if layer == 0:
            make_rows(0)
            make_rows(1)
            for i in range(layers):
                copy = pltpu.make_async_copy(rows.at[i], rows_out.at[i], save_sem.at[i, len(SAVED) + 1])
                copy.start()
                pending.append(copy)
            wait_in(tok_copies)
            xs[...] = tok[...].astype(jnp.float32)
            make_mask()
        else:
            settle()
        save(layer, "x", xs)
        norm_into(xs, row(layer, "attn_gain"), row(layer, "attn_shift"), na)
        save(layer, "normed_attn", na)
        yield
        need((layer, 0))
        total = wq.shape[2]

        for low_at in range(0, total, 4 * BLOCK):
            high_at = min(low_at + 4 * BLOCK, total)
            tiles_between(low_at, high_at, BLOCK, lambda start, size: project_tile(layer, start, size))
            yield
        done_with.add((layer, 0))
        q[...] = slope[:, :width]
        if layer:
            pl.semaphore_wait(free_sem, 1)
        for block in range(2):
            at = ((2 * c) if block == 0 else (3 - 2 * c)) * BLOCK
            spot = pl.ds(pl.multiple_of(at, BLOCK), BLOCK)
            source = slice(block * BLOCK, (block + 1) * BLOCK)
            keys[spot, :] = slope[source, width : 2 * width]
            values[spot, :] = slope[source, 2 * width : 3 * width]
        for copy in swap_moves(layer):
            copy.start()
        save(layer, "q", q)
        yield
        for copy in swap_waits(layer):
            copy.wait_recv()
        save(layer, "keys", keys)
        save(layer, "values", values)
        for first in range(0, width // (2 * HEAD_DIM) + 1, 4):
            attend(c, q, keys, values, mask, att, lse, first, min(first + 4, width // (2 * HEAD_DIM) + 1))
            yield
        save(layer, "attended", att)
        save(layer, "lse", lse)
        if layer + 1 < layers:
            settle()
            for copy in swap_moves(layer):
                copy.wait_send()
            pl.semaphore_signal(free_sem, inc=1, device_id=twin, device_id_type=MESH)
        need((layer, 1))

        def out_step(start, size):
            cols = pl.ds(start, size)
            middle[:, cols] = xs[:, cols] + product(att[...], matrix(wo, cols)) + rows[layer, pl.ds(ROW["b_out"], 1), cols]

        tiles_between(0, width, BLOCK, out_step)
        done_with.add((layer, 1))
        save(layer, "middle", middle)
        yield
        norm_into(middle, row(layer, "mlp_gain"), row(layer, "mlp_shift"), nm)
        save(layer, "normed_mlp", nm)
        yield
        need((layer, 2))
        settle()

        def up_step(start, size):
            cols = pl.ds(start, size)
            u = product(nm[...], matrix(wu, cols)) + b_up[layer, 0:1, cols]
            square = u * u
            t = jnp.tanh(u * (GELU_A + (GELU_A * GELU_B) * square))
            half_up = 0.5 + 0.5 * t
            act_buf[:, cols] = (u * half_up).astype(jnp.bfloat16)
            slope[:, cols] = (
                half_up + (0.5 * u) * (1.0 - t * t) * (GELU_A + (3.0 * GELU_A * GELU_B) * square)
            ).astype(jnp.bfloat16)

        ff = wu.shape[2]
        for low_at in range(0, ff, 6 * BLOCK):
            tiles_between(low_at, min(low_at + 6 * BLOCK, ff), BLOCK, up_step)
            yield
        done_with.add((layer, 2))
        save(layer, "slope", slope)
        save(layer, "activated", act_buf)
        need((layer, 3))

        def down_step(start, size):
            cols = pl.ds(start, size)
            xs[:, cols] = middle[:, cols] + product(act_buf[...], matrix(wd, cols)) + rows[layer, pl.ds(ROW["b_down"], 1), cols]

        for low_at in range(0, width, 2 * BLOCK):
            tiles_between(low_at, min(low_at + 2 * BLOCK, width), BLOCK, down_step)
            yield
        done_with.add((layer, 3))

    def project_tile(layer, start, size):
        cols = pl.ds(start, size)
        out = product(na[...], matrix(wq, cols))
        slope[:, cols] = ((out + b_proj[layer, 0:1, cols]) * scale_of(start, size)).astype(jnp.bfloat16)

    def scale_of(start, size):
        lane = lax.broadcasted_iota(jnp.int32, (1, size), 1) + start
        return jnp.where(lane < width, QUERY_SCALE, 1.0).astype(jnp.float32)

    tick()
    for layer in range(layers):
        for _ in compute(layer):
            tick(PACE)
    while tick():
        pass
    settle()
    tok[...] = xs[...].astype(jnp.bfloat16)
    out = pltpu.make_async_copy(tok, result, save_sem.at[0, 0])
    out.start()
    for copy in swap_moves(layers - 1):
        copy.wait_send()
    finish_in()
    finish()
    out.wait()


def forward(tokens, grads, segs, vectors, weights):
    rows, width = tokens.shape
    low = jnp.bfloat16
    layers = vectors.shape[0]
    ff = weights[2].shape[3]
    units = layers * (len(weights) + 1)
    shapes = dict(
        x=((rows, width), jnp.float32),
        normed_attn=((rows, width), low),
        q=((rows, width), low),
        keys=((2 * rows, width), low),
        values=((2 * rows, width), low),
        attended=((rows, width), low),
        lse=((HEAD_ROWS, rows), jnp.float32),
        middle=((rows, width), jnp.float32),
        normed_mlp=((rows, width), low),
        slope=((rows, ff), low),
        activated=((rows, ff), low),
    )
    out_shape = (
        [shaped((layers, ZN) + w.shape[1:], low) for w in weights]
        + [
            shaped((layers, ZN) + vectors.shape[1:], low),
            shaped((rows, width), low),
            shaped((rows, width), low),
            shaped((2 * rows, rows)),
            shaped((layers, 16, width)),
        ]
        + [shaped(*shapes[name]) for _ in range(layers) for name in SAVED]
    )
    dma = pltpu.SemaphoreType.DMA
    scratch = [pltpu.VMEM((ZN * w.shape[1],) + w.shape[2:], low) for w in weights] + [
        pltpu.VMEM((rows, width), jnp.float32),
        pltpu.VMEM((rows, width), low),
        pltpu.VMEM((rows, width), low),
        pltpu.VMEM((rows, width), low),
        pltpu.VMEM((rows, width), low),
        pltpu.VMEM((2 * rows, width), low),
        pltpu.VMEM((2 * rows, width), low),
        pltpu.VMEM((2 * rows, rows), jnp.float32),
        pltpu.VMEM((rows, width), low),
        pltpu.VMEM((rows, width), jnp.float32),
        pltpu.VMEM((rows, ff), low),
        pltpu.VMEM((rows, ff), low),
        pltpu.VMEM((HEAD_ROWS, rows), jnp.float32),
        pltpu.VMEM((ZN,) + vectors.shape[2:], low),
        pltpu.VMEM((layers, 16, width), jnp.float32),
        pltpu.VMEM((layers, 8, ff), jnp.float32),
        pltpu.VMEM((layers, 8, 3 * width), jnp.float32),
        pltpu.VMEM((2, 1, rows), jnp.int32),
        pltpu.VMEM((8, 2 * rows), jnp.float32),
        dma((units, ZN, 7)),
        dma((units, ZN, 7)),
        dma((len(weights) + 1, ZN)),
        dma((layers, len(SAVED) + 2)),
        dma((layers, 2, 2)),
        dma((layers, 2, 2)),
        dma((6,)),
        dma((6,)),
        dma((3,)),
        pltpu.SemaphoreType.REGULAR,
    ]
    outs = pl.pallas_call(
        forward_body,
        out_shape=out_shape,
        in_specs=anywhere(4 + len(weights)),
        out_specs=anywhere(len(out_shape)),
        scratch_shapes=scratch,
        compiler_params=pltpu.CompilerParams(collective_id=0, has_side_effects=True, vmem_limit_bytes=VMEM_LIMIT),
        name="forward",
    )(tokens, grads, segs, vectors, *weights)
    count = len(weights)
    fulls, rest = outs[:count], outs[count + 5 :]
    _, result, grads_here, mask, vector_rows = outs[count : count + 5]
    saved = [dict(zip(SAVED, rest[i * len(SAVED) : (i + 1) * len(SAVED)])) for i in range(layers)]
    return fulls, result, grads_here, mask, vector_rows, saved


def bring(layer, own, full, buffer, sems, i):
    z = lax.axis_index("fsdp")
    n = own.shape[1]
    return [pltpu.make_async_copy(own.at[layer], buffer.at[pl.ds(z * n, n)], sems.at[i, 0])] + [
        pltpu.make_async_copy(
            full.at[layer, (z + s) % ZN], buffer.at[pl.ds((z + s) % ZN * n, n)], sems.at[i, s]
        )
        for s in range(1, ZN)
    ]


def begin(copies):
    for copy in copies:
        copy.start()


def end(copies):
    for copy in copies:
        copy.wait()


def some_rows(buffer, start, size):
    return buffer[pl.ds(start // 16, size // 16)].reshape(size, buffer.shape[2])


def mlp_back_body(
    layer, dx, middle, gain, slope, down_own, down_full, up_own, up_full, out_own, out_full,
    g_mlp, g_pre, g_middle, g_branch, g_attended, gb_down, gb_up, g_gain, g_shift, gb_out,
    w_down, w_up, w_out, g_norm, sems,
):
    copies = [
        bring(layer, down_own, down_full, w_down, sems, 0),
        bring(layer, up_own, up_full, w_up, sems, 1),
        bring(layer, out_own, out_full, w_out, sems, 2),
    ]
    for copy in copies:
        begin(copy)
    g_mlp[...] = dx[...].astype(jnp.bfloat16)
    gb_down[...] = jnp.sum(g_mlp[...].astype(jnp.float32), axis=0, keepdims=True)
    end(copies[0])

    def down_step(start, size):
        cols = pl.ds(start, size)
        g = (dot_nt(g_mlp[...], some_rows(w_down, start, size)) * slope[:, cols].astype(jnp.float32)).astype(jnp.bfloat16)
        g_pre[:, cols] = g
        gb_up[:, cols] = jnp.sum(g.astype(jnp.float32), axis=0, keepdims=True)

    tiles(g_pre.shape[1], BLOCK, down_step)
    end(copies[1])

    def up_step(start, size):
        cols = pl.ds(start, size)
        g_norm[:, cols] = dot_nt(g_pre[...], some_rows(w_up, start, size))

    tiles(dx.shape[1], BLOCK, up_step)
    norm_back(middle, g_norm, dx, gain[...], g_middle, g_gain, g_shift, g_branch)
    gb_out[...] = jnp.sum(g_branch[...].astype(jnp.float32), axis=0, keepdims=True)
    end(copies[2])

    def out_step(start, size):
        cols = pl.ds(start, size)
        g_attended[:, cols] = dot_nt(g_branch[...], some_rows(w_out, start, size)).astype(jnp.bfloat16)

    tiles(dx.shape[1], BLOCK, out_step)


def mlp_back(layer, dx, middle, slope, gain, owns, fulls):
    rows, width = dx.shape
    ff = slope.shape[1]
    low = jnp.bfloat16
    return pl.pallas_call(
        functools.partial(mlp_back_body, layer),
        out_shape=[
            shaped((rows, width), low),
            shaped((rows, ff), low),
            shaped((rows, width)),
            shaped((rows, width), low),
            shaped((rows, width), low),
            shaped((1, width)),
            shaped((1, ff)),
            shaped((1, width)),
            shaped((1, width)),
            shaped((1, width)),
        ],
        in_specs=whole(4) + anywhere(6),
        out_specs=whole(10),
        scratch_shapes=[
            pltpu.VMEM((ff // 16, 16, width), low),
            pltpu.VMEM((width // 16, 16, ff), low),
            pltpu.VMEM((width // 16, 16, width), low),
            pltpu.VMEM((rows, width), jnp.float32),
            pltpu.SemaphoreType.DMA((3, ZN)),
        ],
        compiler_params=params(),
        name="mlp_back",
    )(dx, middle, gain, slope, owns[3], fulls[3], owns[2], fulls[2], owns[1], fulls[1])


def attend_back_body(
    q, g_attended, attended, lse, mask, keys, values, g_q, g_own, g_other, inner, g_k, g_v
):
    core = lax.rem(lax.axis_index("rep"), 2)
    width = q.shape[1]
    head = lax.broadcasted_iota(jnp.int32, (HEAD_ROWS, width), 0)
    lane = lax.broadcasted_iota(jnp.int32, (HEAD_ROWS, width), 1)
    pick = (lane // HEAD_DIM == head).astype(jnp.float32).astype(jnp.bfloat16)
    both = g_attended[...].astype(jnp.float32) * attended[...].astype(jnp.float32)
    high = both.astype(jnp.bfloat16)
    rest = (both - high.astype(jnp.float32)).astype(jnp.bfloat16)
    inner[...] = dot_nt(pick, high) + dot_nt(pick, rest)
    def act(start, size, head):
        cols = pl.ds(start, size)
        g_k[...] = jnp.zeros_like(g_k)
        g_v[...] = jnp.zeros_like(g_v)
        lanes = slice(0, size)
        for variant in range(2):

            @pl.when(core == variant)
            def _():
                for row, high in RANGES[variant]:
                    rows = slice(row, row + BLOCK)
                    qs, gs = q[rows, cols], g_attended[rows, cols]
                    ks, vs = keys[:high, cols], values[:high, cols]
                    parts = []
                    for j in range(size // HEAD_DIM):
                        q_j, g_j = of_head(qs, j), of_head(gs, j)
                        s = dot_nt(ks, q_j) + mask[:high, rows]
                        p = jnp.exp(s - lse[pl.ds(head + j, 1), rows])
                        g_p = dot_nt(vs, g_j)
                        g_s = (p * (g_p - inner[pl.ds(head + j, 1), rows])).astype(jnp.bfloat16)
                        g_v[:high, lanes] += product(p.astype(jnp.bfloat16), g_j)
                        g_k[:high, lanes] += product(g_s, q_j)
                        parts.append(dot_tn(ks, g_s)[j * HEAD_DIM : (j + 1) * HEAD_DIM])
                    out = jnp.concatenate(parts, axis=0) if len(parts) > 1 else parts[0]
                    g_q[rows, cols] = out.T.astype(jnp.bfloat16) * QUERY_SCALE

        for block in range(2):
            rows = slice(block * BLOCK, (block + 1) * BLOCK)
            for target, who in ((g_own, core), (g_other, 1 - core)):
                at = ((2 * who) if block == 0 else (3 - 2 * who)) * BLOCK
                spot = pl.ds(pl.multiple_of(at, BLOCK), BLOCK)
                target[0, rows, cols] = g_k[spot, lanes].astype(jnp.bfloat16)
                target[1, rows, cols] = g_v[spot, lanes].astype(jnp.bfloat16)

    over_slabs(width, act, 0, width // (2 * HEAD_DIM) + 1)


def attend_back(q, g_attended, attended, lse, mask, keys, values):
    rows, width = q.shape
    low = jnp.bfloat16
    return pl.pallas_call(
        attend_back_body,
        out_shape=[shaped((rows, width), low), shaped((2, rows, width), low), shaped((2, rows, width), low)],
        in_specs=whole(7),
        out_specs=whole(3),
        scratch_shapes=[
            pltpu.VMEM((HEAD_ROWS, rows), jnp.float32),
            pltpu.VMEM((2 * rows, 2 * HEAD_DIM), jnp.float32),
            pltpu.VMEM((2 * rows, 2 * HEAD_DIM), jnp.float32),
        ],
        compiler_params=params(),
        name="attend_back",
    )(q, g_attended, attended, lse, mask, keys, values)


def project_back_body(
    layer, x, g_middle, gain, g_q, g_own, g_got, w_own, w_full, g_x, g_proj, gb_q, gb_v, g_gain, g_shift, w, g_norm, sem
):
    width = x.shape[1]
    load = bring(layer, w_own, w_full, w, sem, 0)
    begin(load)
    g_k = g_own[0] + g_got[0]
    g_v = g_own[1] + g_got[1]
    gb_q[...] = jnp.sum(g_q[...].astype(jnp.float32), axis=0, keepdims=True)
    gb_v[...] = jnp.sum(g_v.astype(jnp.float32), axis=0, keepdims=True)
    g_proj[:, :width] = g_q[...]
    g_proj[:, width : 2 * width] = g_k
    g_proj[:, 2 * width :] = g_v
    end(load)

    def step(start, size):
        cols = pl.ds(start, size)
        g_norm[:, cols] = dot_nt(g_proj[...], some_rows(w, start, size))

    tiles(width, BLOCK, step)
    norm_back(x, g_norm, g_middle, gain[...], g_x, g_gain, g_shift)


def project_back(layer, x, g_middle, g_q, g_own, g_got, gain, own, full):
    rows, width = x.shape
    low = jnp.bfloat16
    return pl.pallas_call(
        functools.partial(project_back_body, layer),
        out_shape=[
            shaped((rows, width)),
            shaped((rows, 3 * width), low),
            shaped((1, width)),
            shaped((1, width)),
            shaped((1, width)),
            shaped((1, width)),
        ],
        in_specs=whole(6) + anywhere(2),
        out_specs=whole(6),
        scratch_shapes=[
            pltpu.VMEM((width // 16, 16, 3 * width), low),
            pltpu.VMEM((rows, width), jnp.float32),
            pltpu.SemaphoreType.DMA((1, ZN)),
        ],
        compiler_params=params(),
        name="project_back",
    )(x, g_middle, gain, g_q, g_own, g_got, own, full)


PAIRS = ((0, 1), (3, 2))
RC, R1, R2, RL, RR, RX, RY, RD1, RD2, RCC, R1B = 0, 4, 8, 12, 16, 20, 21, 22, 23, 24, 25


def reduce_body(ks, grads, outs, own, twin_in, first_in, second_in, low_in, high_in, load_sem, store_sem, send_sem, recv_sem):
    x, y, z, c, across, beside, twin, up, down = neighbours()
    greet(z, c, x, across, beside, twin, None, up, down)
    units = [(m, h) for h in range(2) for m in range(len(grads))]
    p = x * 2 + y

    def move(source, target, m, kind, device):
        return pltpu.make_async_remote_copy(
            src_ref=source,
            dst_ref=target,
            send_sem=send_sem.at[m, kind],
            recv_sem=recv_sem.at[m, kind],
            device_id=device,
            device_id_type=MESH,
        )

    def to_twin(m, d):
        k = ks[m]
        return move(grads[m].at[d, pl.ds((1 - c) * 4 * k, 4 * k)], twin_in[m].at[d], m, RC + d, twin)

    def load(m, d):
        k = ks[m]
        return pltpu.make_async_copy(grads[m].at[d, pl.ds(c * 4 * k, 4 * k)], own[m].at[d], load_sem.at[m, d])

    def add(m, d, at, extra, extra_at, n):
        def step(i, carry):
            own[m][d, at + i] = own[m][d, at + i] + extra[d, extra_at + i]
            return carry

        lax.fori_loop(0, n, step, 0)

    def first_moves(u):
        m, h = units[u]
        k = ks[m]
        a, b = PAIRS[h]
        return [
            move(own[m].at[a, pl.ds((1 - x) * 2 * k, 2 * k)], first_in[m].at[a], m, R1 + a, across),
            move(own[m].at[b, pl.ds((1 - y) * k, k)], first_in[m].at[b, pl.ds(0, k)], m, R1 + b, beside),
            move(own[m].at[b, pl.ds((3 - y) * k, k)], first_in[m].at[b, pl.ds(k, k)], m, R1B + h, beside),
        ]

    def second_moves(u):
        m, h = units[u]
        k = ks[m]
        a, b = PAIRS[h]
        return [
            move(own[m].at[a, pl.ds((x * 2 + 1 - y) * k, k)], second_in[m].at[a], m, R2 + a, beside),
            move(own[m].at[b, pl.ds(((1 - x) * 2 + y) * k, k)], second_in[m].at[b], m, R2 + b, across),
        ]

    def with_twin(u):
        m, h = units[u]
        for d in PAIRS[h]:
            to_twin(m, d).wait_recv()
            load(m, d).wait()
            add(m, d, 0, twin_in[m], 0, 4 * ks[m])
        for copy in first_moves(u):
            copy.start()

    def with_first(u):
        m, h = units[u]
        k = ks[m]
        a, b = PAIRS[h]
        for copy in first_moves(u):
            copy.wait_recv()
        add(m, a, x * 2 * k, first_in[m], 0, 2 * k)
        add(m, b, y * k, first_in[m], 0, k)
        add(m, b, (2 + y) * k, first_in[m], k, k)
        for copy in second_moves(u):
            copy.start()

    def with_second(u):
        m, h = units[u]
        for copy in second_moves(u):
            copy.wait_recv()
        for d in PAIRS[h]:
            add(m, d, p * ks[m], second_in[m], 0, ks[m])

    def piece(m, d):
        return own[m].at[d, pl.ds(p * ks[m], ks[m])]

    def to_down(m, d):
        return move(piece(m, d), high_in[m].at[d], m, RR + d, down)

    def to_up(m, d):
        return move(piece(m, d), low_in[m].at[d], m, RL + d, up)

    def rows_of(m, px, py, low=0, n=None):
        k = ks[m]
        return outs[m].at[pl.ds((c * 4 + px * 2 + py) * k + low, k if n is None else n)]

    def share_across(m):
        return move(piece(m, z), rows_of(m, x, y), m, RX, across)

    def share_beside(m):
        return move(piece(m, z), rows_of(m, x, y), m, RY, beside)

    def store(m):
        return pltpu.make_async_copy(piece(m, z), rows_of(m, x, y), store_sem.at[m])

    def arrived_across(m):
        return move(rows_of(m, 1 - x, y), rows_of(m, 1 - x, y), m, RX, across)

    def arrived_beside(m):
        return move(rows_of(m, x, 1 - y), rows_of(m, x, 1 - y), m, RY, beside)

    def corner(m, px, py, part):
        k = ks[m]
        low, n = (0, max(k // 2, 1)) if part == 0 else (k // 2, k - k // 2)
        rows = rows_of(m, px, py, low, n)
        return move(rows, rows, m, RD1 if part == 0 else RD2, beside if part == 0 else across)

    def to_core(m, core):
        rows = outs[m].at[pl.ds(core * 4 * ks[m], 4 * ks[m])]
        return move(rows, rows, m, RCC, twin)

    def line_step(u, s):
        m, h = units[u]
        for zz in range(ZN):
            downward = [d for d in PAIRS[h] if d < zz] if zz == ZN - 1 - s else []
            upward = [d for d in PAIRS[h] if d > zz] if zz == s else []
            last = [d for d in PAIRS[h] if d == zz] if s == ZN - 1 else []
            if not (downward or upward or last):
                continue

            @pl.when(z == zz)
            def _():
                for d in downward:
                    if zz < ZN - 1:
                        to_down(m, d).wait_recv()
                        add(m, d, p * ks[m], high_in[m], 0, ks[m])
                    to_down(m, d).start()
                for d in upward:
                    if zz > 0:
                        to_up(m, d).wait_recv()
                        add(m, d, p * ks[m], low_in[m], 0, ks[m])
                    to_up(m, d).start()
                for d in last:
                    if zz > 0:
                        to_up(m, d).wait_recv()
                        add(m, d, p * ks[m], low_in[m], 0, ks[m])
                    if zz < ZN - 1:
                        to_down(m, d).wait_recv()
                        add(m, d, p * ks[m], high_in[m], 0, ks[m])
                    share_across(m).start()
                    share_beside(m).start()
                    store(m).start()

    def where_mine(u, act):
        m, h = units[u]

        @pl.when((z >= min(PAIRS[h])) & (z <= max(PAIRS[h])))
        def _():
            act(m)

    def corner_step(u):
        def act(m):
            arrived_across(m).wait_recv()
            corner(m, 1 - x, y, 0).start()
            arrived_beside(m).wait_recv()
            if ks[m] > 1:
                corner(m, x, 1 - y, 1).start()

        where_mine(u, act)

    def core_step(u):
        def act(m):
            store(m).wait()
            corner(m, 1 - x, 1 - y, 0).wait_recv()
            if ks[m] > 1:
                corner(m, 1 - x, 1 - y, 1).wait_recv()
            to_core(m, c).start()

        where_mine(u, act)

    def finish(u):
        m, h = units[u]
        for d in PAIRS[h]:
            to_twin(m, d).wait_send()
        for copy in first_moves(u) + second_moves(u):
            copy.wait_send()
        for zz in range(ZN):

            @pl.when(z == zz)
            def _():
                for d in PAIRS[h]:
                    if d < zz:
                        to_down(m, d).wait_send()
                    if d > zz:
                        to_up(m, d).wait_send()

        def act(m):
            to_core(m, 1 - c).wait_recv()
            share_across(m).wait_send()
            share_beside(m).wait_send()
            corner(m, 1 - x, y, 0).wait_send()
            if ks[m] > 1:
                corner(m, x, 1 - y, 1).wait_send()
            to_core(m, c).wait_send()

        where_mine(u, act)

    count = len(units)

    def at(step, u, *s):
        if 0 <= u < count:
            step(u, *s)

    for u in range(count):
        m, h = units[u]
        for d in PAIRS[h]:
            to_twin(m, d).start()
            load(m, d).start()
    for t in range(count + 8):
        at(with_twin, t)
        at(with_first, t - 1)
        at(with_second, t - 2)
        for s in range(ZN):
            at(line_step, t - 2 - s, s)
        at(corner_step, t - 6)
        at(core_step, t - 7)
    for u in range(count):
        finish(u)


def reduce_pieces(grads, ks):
    m_count = len(grads)

    def body(*refs):
        groups = [refs[i * m_count : (i + 1) * m_count] for i in range(8)]
        reduce_body(ks, *groups, *refs[8 * m_count :])

    def buffers(rows):
        return [pltpu.VMEM((ZN, rows * k) + g.shape[2:], g.dtype) for g, k in zip(grads, ks)]

    return pl.pallas_call(
        body,
        out_shape=[jax.ShapeDtypeStruct((8 * k,) + g.shape[2:], g.dtype) for g, k in zip(grads, ks)],
        in_specs=[pl.BlockSpec(memory_space=pl.ANY)] * m_count,
        out_specs=[pl.BlockSpec(memory_space=pl.ANY)] * m_count,
        scratch_shapes=buffers(4)
        + buffers(4)
        + buffers(2)
        + buffers(1)
        + buffers(1)
        + buffers(1)
        + [
            pltpu.SemaphoreType.DMA((m_count, ZN)),
            pltpu.SemaphoreType.DMA((m_count,)),
            pltpu.SemaphoreType.DMA((m_count, 27)),
            pltpu.SemaphoreType.DMA((m_count, 27)),
        ],
        compiler_params=pltpu.CompilerParams(
            collective_id=1, has_side_effects=True, vmem_limit_bytes=60 << 20
        ),
        name="reduce_grads",
    )(*grads)


VECTORS = (0, 1, 3, 4, 6, 7, 8, 12, 10)
MATRICES = (2, 5, 9, 11)
WIDE = 13312


def reduce_layer(gradients):
    low = [g.astype(jnp.bfloat16) for g in gradients]
    mats = [low[i].reshape(ZN, -1, 16, low[i].shape[1]) for i in MATRICES]
    rest = [jnp.swapaxes(g[:, g.shape[1] // 8 * 8 :], 1, 2).reshape(ZN, 16, -1) for g in mats]
    vectors = jnp.concatenate([low[i].reshape(ZN, -1) for i in VECTORS], axis=1)
    width = WIDE - sum(r.shape[2] for r in rest)
    vectors = jnp.pad(vectors, ((0, 0), (0, 16 * width - vectors.shape[1]))).reshape(ZN, 16, width)
    wide = jnp.concatenate(rest + [vectors], axis=2)
    wide = jnp.swapaxes(wide.reshape(ZN, 16, 8, WIDE // 8), 1, 2)
    ks = [g.shape[1] // 8 for g in mats] + [1]
    sums = reduce_pieces(mats + [wide], ks)
    tail = jnp.swapaxes(sums[-1], 0, 1).reshape(16, WIDE)
    result = [None] * 13
    col = 0
    for at, i in enumerate(MATRICES):
        columns = low[i].shape[1]
        n = mats[at].shape[1] % 8
        extra = jnp.swapaxes(tail[:, col : col + n * columns].reshape(16, n, columns), 0, 1)
        col += n * columns
        result[i] = jnp.concatenate([sums[at].reshape(-1, columns), extra.reshape(-1, columns)], axis=0)
    flat = tail[:, col:].reshape(-1)
    col = 0
    for i in VECTORS:
        n = low[i].shape[0] // ZN
        result[i] = flat[col : col + n]
        col += n
    return tuple(r.astype(jnp.float32) for r in result)


def swap_cores(rows):
    return lax.ppermute(rows, "rep", [(0, 1), (1, 0), (2, 3), (3, 2)])


def on_cores(tokens, segments, grad_out, *params):
    rows, width = tokens.shape[1:]
    layers = params[0].shape[0]
    weights = [params[i].reshape(layers, -1, 16, params[i].shape[2]) for i in MATRICES]
    vectors = jnp.concatenate([params[i].reshape(layers, -1, params[0].shape[1]) for i in VECTORS], axis=1)
    vectors = jnp.pad(vectors, ((0, 0), (0, 16 - vectors.shape[1]), (0, 0)))[:, None]
    fulls, result, grads_here, mask, vector_rows, saved = forward(
        tokens[0], grad_out[0], segments, vectors, weights
    )
    result = from_cores(result)[None]
    grad = grads_here.astype(jnp.float32)
    reduced = [None] * layers
    for layer in reversed(range(layers)):
        kept = saved[layer]
        attn_gain, mlp_gain = vector_rows[layer, 0:1], vector_rows[layer, 5:6]
        g_mlp, g_pre, g_middle, g_branch, g_attended, gb_down, gb_up, gm_gain, gm_shift, gb_out = mlp_back(
            layer, grad, kept["middle"], kept["slope"], mlp_gain, weights, fulls
        )
        g_q, g_own, g_other = attend_back(
            kept["q"], g_attended, kept["attended"], kept["lse"], mask, kept["keys"], kept["values"]
        )
        g_got = swap_cores(g_other)
        grad, g_proj, gb_q, gb_v, ga_gain, ga_shift = project_back(
            layer, kept["x"], g_middle, g_q, g_own, g_got, attn_gain, weights[0], fulls[0]
        )
        gradients = (
            ga_gain[0],
            ga_shift[0],
            inner_rows(kept["normed_attn"], g_proj),
            gb_q[0],
            gb_v[0],
            inner_rows(kept["attended"], g_branch),
            gb_out[0],
            gm_gain[0],
            gm_shift[0],
            inner_rows(kept["normed_mlp"], g_pre),
            gb_up[0],
            inner_rows(kept["activated"], g_mlp),
            gb_down[0],
        )
        reduced[layer] = reduce_layer(gradients)
    stacked = tuple((jnp.stack([entry[member] for entry in reduced]) for member in range(13)))
    return (result, from_cores(grad.astype(jnp.bfloat16))[None]) + stacked


def on_device(
    tokens,
    segments,
    grad_out,
    attn_gain,
    attn_shift,
    w_qkv,
    b_query,
    b_value,
    w_out,
    b_out,
    mlp_gain,
    mlp_shift,
    w_up,
    b_up,
    w_down,
    b_down,
):
    seg_own = segments[0]
    seg_all = lax.all_gather(seg_own, "seq", axis=0, tiled=True)
    offset = lax.axis_index("seq") * seg_own.shape[0]
    visible = visible_mask(seg_own, seg_all, offset)
    layer_count = attn_gain.shape[0]
    resid = tokens[0].astype(jnp.float32)
    kept_weights = []
    stored_list = []
    for layer_index in range(layer_count):
        gathered = gather_layer(
            layer_index,
            attn_gain,
            attn_shift,
            w_qkv,
            b_query,
            b_value,
            w_out,
            b_out,
            mlp_gain,
            mlp_shift,
            w_up,
            b_up,
            w_down,
            b_down,
        )
        resid, stored = forward_layer(resid, gathered, visible, Halves())
        kept_weights.append(gathered)
        stored_list.append(stored)
    result = resid.astype(jnp.bfloat16)[None]
    grad_resid = grad_out[0].astype(jnp.float32)
    reduced = [None] * layer_count
    for layer_index in reversed(range(layer_count)):
        gathered = gather_again(
            layer_index,
            attn_gain,
            attn_shift,
            w_qkv,
            b_query,
            b_value,
            w_out,
            b_out,
            mlp_gain,
            mlp_shift,
            w_up,
            b_up,
            w_down,
            b_down,
        )
        grad_resid, gradients = backward_layer(
            grad_resid, stored_list[layer_index], gathered, visible, Halves()
        )
        reduced[layer_index] = reduce_grads(gradients)
    stacked = tuple((jnp.stack([entry[member] for entry in reduced]) for member in range(13)))
    return (result, grad_resid.astype(jnp.bfloat16)[None]) + stacked


def solution(mesh):
    fits = (mesh.shape["seq"], mesh.shape["fsdp"], mesh.shape["rep"]) == (2, ZN, 4)
    return jax.shard_map(
        on_cores if fits else on_device,
        mesh=mesh,
        in_specs=(
            P(("fsdp", "rep"), "seq", None),
            P(("fsdp", "rep"), "seq"),
            P(("fsdp", "rep"), "seq", None),
            P(None, "fsdp"),
            P(None, "fsdp"),
            P(None, "fsdp", None),
            P(None, "fsdp"),
            P(None, "fsdp"),
            P(None, "fsdp", None),
            P(None, "fsdp"),
            P(None, "fsdp"),
            P(None, "fsdp"),
            P(None, "fsdp", None),
            P(None, "fsdp"),
            P(None, "fsdp", None),
            P(None, "fsdp"),
        ),
        out_specs=(
            P(("fsdp", "rep"), "seq", None),
            P(("fsdp", "rep"), "seq", None),
            P(None, "fsdp"),
            P(None, "fsdp"),
            P(None, "fsdp", None),
            P(None, "fsdp"),
            P(None, "fsdp"),
            P(None, "fsdp", None),
            P(None, "fsdp"),
            P(None, "fsdp"),
            P(None, "fsdp"),
            P(None, "fsdp", None),
            P(None, "fsdp"),
            P(None, "fsdp", None),
            P(None, "fsdp"),
        ),
        check_vma=False,
    )
```

```python
import functools
import math

import jax
import jax.numpy as jnp
from jax import lax
from jax.experimental import pallas as pl
from jax.experimental.pallas import tpu as pltpu
from jax.sharding import PartitionSpec as P

HEAD_DIM = 64
MESH = pl.DeviceIdType.MESH


NORM_EPSILON = 1e-05
MASKED = -1e30


def layer_norm(inputs, gain, bias_term):
    center = inputs - jnp.mean(inputs, axis=-1, keepdims=True)
    spread = jnp.mean(center * center, axis=-1, keepdims=True)
    return center * lax.rsqrt(spread + NORM_EPSILON) * gain + bias_term


def gelu_tanh(inputs):
    return jax.nn.gelu(inputs, approximate=True)


def product(left, right):
    return jnp.dot(left, right, preferred_element_type=jnp.float32)


def inner_rows(left, right):
    return lax.dot_general(
        left, right, (((0,), (0,)), ((), ())), preferred_element_type=jnp.float32
    )


def outer_cols(left, right):
    return lax.dot_general(
        left, right, (((1,), (1,)), ((), ())), preferred_element_type=jnp.float32
    )


def column_sum(values_low):
    return jnp.sum(values_low.astype(jnp.float32), axis=0)


def visible_mask(seg_own, seg_all, offset):
    row_pos = offset + lax.iota(jnp.int32, seg_own.shape[0])
    col_pos = lax.iota(jnp.int32, seg_all.shape[0])
    return (seg_own[:, None] == seg_all[None, :]) & (row_pos[:, None] >= col_pos[None, :])


def head_scores(queries, keys_all, visible, head_count):
    query_heads = queries.reshape(queries.shape[0], head_count, HEAD_DIM)
    key_heads = keys_all.reshape(keys_all.shape[0], head_count, HEAD_DIM)
    scores = jnp.einsum("thd,shd->hts", query_heads, key_heads, preferred_element_type=jnp.float32)
    return jnp.where(visible[None], scores, MASKED)


def gather_layer(
    layer_index,
    attn_gain,
    attn_shift,
    w_qkv,
    b_query,
    b_value,
    w_out,
    b_out,
    mlp_gain,
    mlp_shift,
    w_up,
    b_up,
    w_down,
    b_down,
):
    return (
        lax.all_gather(attn_gain[layer_index], "fsdp", axis=0, tiled=True),
        lax.all_gather(attn_shift[layer_index], "fsdp", axis=0, tiled=True),
        lax.all_gather(w_qkv[layer_index], "fsdp", axis=0, tiled=True),
        lax.all_gather(b_query[layer_index], "fsdp", axis=0, tiled=True),
        lax.all_gather(b_value[layer_index], "fsdp", axis=0, tiled=True),
        lax.all_gather(w_out[layer_index], "fsdp", axis=0, tiled=True),
        lax.all_gather(b_out[layer_index], "fsdp", axis=0, tiled=True),
        lax.all_gather(mlp_gain[layer_index], "fsdp", axis=0, tiled=True),
        lax.all_gather(mlp_shift[layer_index], "fsdp", axis=0, tiled=True),
        lax.all_gather(w_up[layer_index], "fsdp", axis=0, tiled=True),
        lax.all_gather(b_up[layer_index], "fsdp", axis=0, tiled=True),
        lax.all_gather(w_down[layer_index], "fsdp", axis=0, tiled=True),
        lax.all_gather(b_down[layer_index], "fsdp", axis=0, tiled=True),
    )


def gather_again(
    layer_index,
    attn_gain,
    attn_shift,
    w_qkv,
    b_query,
    b_value,
    w_out,
    b_out,
    mlp_gain,
    mlp_shift,
    w_up,
    b_up,
    w_down,
    b_down,
):
    return (
        lax.all_gather(attn_gain[layer_index], "fsdp", axis=0, tiled=True),
        lax.all_gather(attn_shift[layer_index], "fsdp", axis=0, tiled=True),
        lax.all_gather(w_qkv[layer_index], "fsdp", axis=0, tiled=True),
        lax.all_gather(b_query[layer_index], "fsdp", axis=0, tiled=True),
        lax.all_gather(b_value[layer_index], "fsdp", axis=0, tiled=True),
        lax.all_gather(w_out[layer_index], "fsdp", axis=0, tiled=True),
        lax.all_gather(b_out[layer_index], "fsdp", axis=0, tiled=True),
        lax.all_gather(mlp_gain[layer_index], "fsdp", axis=0, tiled=True),
        lax.all_gather(mlp_shift[layer_index], "fsdp", axis=0, tiled=True),
        lax.all_gather(w_up[layer_index], "fsdp", axis=0, tiled=True),
        lax.all_gather(b_up[layer_index], "fsdp", axis=0, tiled=True),
        lax.all_gather(w_down[layer_index], "fsdp", axis=0, tiled=True),
        lax.all_gather(b_down[layer_index], "fsdp", axis=0, tiled=True),
    )


def forward_layer(resid, gathered, visible, pool):
    (
        attn_gain,
        attn_shift,
        w_qkv,
        b_query,
        b_value,
        w_out,
        b_out,
        mlp_gain,
        mlp_shift,
        w_up,
        b_up,
        w_down,
        b_down,
    ) = gathered
    model_width = resid.shape[1]
    head_count = model_width // HEAD_DIM
    query_scale = 1.0 / math.sqrt(HEAD_DIM)
    normed_attn = layer_norm(
        resid, attn_gain.astype(jnp.float32), attn_shift.astype(jnp.float32)
    ).astype(jnp.bfloat16)
    proj_all = product(normed_attn, w_qkv)
    queries = ((proj_all[:, :model_width] + b_query.astype(jnp.float32)) * query_scale).astype(
        jnp.bfloat16
    )
    keys_own = proj_all[:, model_width : 2 * model_width].astype(jnp.bfloat16)
    values_own = (proj_all[:, 2 * model_width :] + b_value.astype(jnp.float32)).astype(jnp.bfloat16)
    keys_all, values_all = pool.spread(keys_own), pool.spread(values_own)
    scores = head_scores(queries, keys_all, visible, head_count)
    row_max = jnp.max(scores, axis=-1, keepdims=True)
    exponent = jnp.exp(scores - row_max)
    row_sum = jnp.sum(exponent, axis=-1, keepdims=True)
    weights_soft = (exponent / row_sum).astype(jnp.bfloat16)
    log_total = row_max + jnp.log(row_sum)
    value_heads = values_all.reshape(values_all.shape[0], head_count, HEAD_DIM)
    attended = jnp.einsum(
        "hts,shd->thd", weights_soft, value_heads, preferred_element_type=jnp.float32
    )
    attended = attended.reshape(resid.shape[0], model_width).astype(jnp.bfloat16)
    middle = resid + product(attended, w_out) + b_out.astype(jnp.float32)
    normed_mlp = layer_norm(
        middle, mlp_gain.astype(jnp.float32), mlp_shift.astype(jnp.float32)
    ).astype(jnp.bfloat16)
    pre_act = product(normed_mlp, w_up) + b_up.astype(jnp.float32)
    activated = gelu_tanh(pre_act).astype(jnp.bfloat16)
    output = middle + product(activated, w_down) + b_down.astype(jnp.float32)
    stored = (
        resid,
        normed_attn,
        queries,
        keys_all,
        values_all,
        log_total,
        attended,
        middle,
        normed_mlp,
        pre_act,
        activated,
    )
    return (output, stored)


def backward_layer(grad_next, stored, gathered, visible, pool):
    (
        attn_gain,
        attn_shift,
        w_qkv,
        b_query,
        b_value,
        w_out,
        b_out,
        mlp_gain,
        mlp_shift,
        w_up,
        b_up,
        w_down,
        b_down,
    ) = gathered
    (
        resid,
        normed_attn,
        queries,
        keys_all,
        values_all,
        log_total,
        attended,
        middle,
        normed_mlp,
        pre_act,
        activated,
    ) = stored
    model_width = resid.shape[1]
    tok_rows = resid.shape[0]
    key_rows = keys_all.shape[0]
    head_count = model_width // HEAD_DIM
    query_scale = 1.0 / math.sqrt(HEAD_DIM)
    grad_mlp = grad_next.astype(jnp.bfloat16)
    grad_b_down = column_sum(grad_mlp)
    grad_w_down = inner_rows(activated, grad_mlp)
    grad_act = outer_cols(grad_mlp, w_down)
    gelu_value, gelu_pull = jax.vjp(gelu_tanh, pre_act)
    grad_pre = gelu_pull(grad_act)[0].astype(jnp.bfloat16)
    grad_b_up = column_sum(grad_pre)
    grad_w_up = inner_rows(normed_mlp, grad_pre)
    grad_nm = outer_cols(grad_pre, w_up)
    norm_value, norm_pull = jax.vjp(
        layer_norm, middle, mlp_gain.astype(jnp.float32), mlp_shift.astype(jnp.float32)
    )
    grad_middle, grad_mlp_gain, grad_mlp_shift = norm_pull(grad_nm)
    grad_middle = grad_middle + grad_next
    grad_branch = grad_middle.astype(jnp.bfloat16)
    grad_b_out = column_sum(grad_branch)
    grad_w_out = inner_rows(attended, grad_branch)
    grad_attended = outer_cols(grad_branch, w_out).astype(jnp.bfloat16)
    scores = head_scores(queries, keys_all, visible, head_count)
    weights_full = jnp.exp(scores - log_total)
    weights_soft = weights_full.astype(jnp.bfloat16)
    grad_heads = grad_attended.reshape(tok_rows, head_count, HEAD_DIM)
    query_heads = queries.reshape(tok_rows, head_count, HEAD_DIM)
    key_heads = keys_all.reshape(key_rows, head_count, HEAD_DIM)
    value_heads = values_all.reshape(key_rows, head_count, HEAD_DIM)
    grad_value_terms = jnp.einsum(
        "hts,thd->shd", weights_soft, grad_heads, preferred_element_type=jnp.float32
    )
    grad_probs = jnp.einsum(
        "thd,shd->hts", grad_heads, value_heads, preferred_element_type=jnp.float32
    )
    inner_sum = jnp.sum(weights_full * grad_probs, axis=-1, keepdims=True)
    grad_scores = (weights_full * (grad_probs - inner_sum)).astype(jnp.bfloat16)
    grad_queries = jnp.einsum(
        "hts,shd->thd", grad_scores, key_heads, preferred_element_type=jnp.float32
    )
    grad_queries = grad_queries.reshape(tok_rows, model_width).astype(jnp.bfloat16) * query_scale
    grad_key_terms = jnp.einsum(
        "hts,thd->shd", grad_scores, query_heads, preferred_element_type=jnp.float32
    )
    grad_keys = pool.collect(grad_key_terms.reshape(key_rows, model_width).astype(jnp.bfloat16))
    grad_values = pool.collect(grad_value_terms.reshape(key_rows, model_width).astype(jnp.bfloat16))
    grad_keys = grad_keys.astype(jnp.bfloat16)
    grad_values = grad_values.astype(jnp.bfloat16)
    grad_proj = jnp.concatenate([grad_queries, grad_keys, grad_values], axis=1)
    grad_b_query = column_sum(grad_queries)
    grad_b_value = column_sum(grad_values)
    grad_w_qkv = inner_rows(normed_attn, grad_proj)
    grad_na = outer_cols(grad_proj, w_qkv)
    first_value, first_pull = jax.vjp(
        layer_norm, resid, attn_gain.astype(jnp.float32), attn_shift.astype(jnp.float32)
    )
    grad_resid, grad_attn_gain, grad_attn_shift = first_pull(grad_na)
    grad_resid = grad_resid + grad_middle
    gradients = (
        grad_attn_gain,
        grad_attn_shift,
        grad_w_qkv,
        grad_b_query,
        grad_b_value,
        grad_w_out,
        grad_b_out,
        grad_mlp_gain,
        grad_mlp_shift,
        grad_w_up,
        grad_b_up,
        grad_w_down,
        grad_b_down,
    )
    return (grad_resid, gradients)


def reduce_grads(gradients):
    shares = (
        lax.psum_scatter(gradients[0], ("fsdp", "rep"), scatter_dimension=0, tiled=True),
        lax.psum_scatter(gradients[1], ("fsdp", "rep"), scatter_dimension=0, tiled=True),
        lax.psum_scatter(gradients[2], ("fsdp", "rep"), scatter_dimension=0, tiled=True),
        lax.psum_scatter(gradients[3], ("fsdp", "rep"), scatter_dimension=0, tiled=True),
        lax.psum_scatter(gradients[4], ("fsdp", "rep"), scatter_dimension=0, tiled=True),
        lax.psum_scatter(gradients[5], ("fsdp", "rep"), scatter_dimension=0, tiled=True),
        lax.psum_scatter(gradients[6], ("fsdp", "rep"), scatter_dimension=0, tiled=True),
        lax.psum_scatter(gradients[7], ("fsdp", "rep"), scatter_dimension=0, tiled=True),
        lax.psum_scatter(gradients[8], ("fsdp", "rep"), scatter_dimension=0, tiled=True),
        lax.psum_scatter(gradients[9], ("fsdp", "rep"), scatter_dimension=0, tiled=True),
        lax.psum_scatter(gradients[10], ("fsdp", "rep"), scatter_dimension=0, tiled=True),
        lax.psum_scatter(gradients[11], ("fsdp", "rep"), scatter_dimension=0, tiled=True),
        lax.psum_scatter(gradients[12], ("fsdp", "rep"), scatter_dimension=0, tiled=True),
    )
    shares = (
        lax.psum(shares[0].astype(jnp.bfloat16), "seq").astype(jnp.float32),
        lax.psum(shares[1].astype(jnp.bfloat16), "seq").astype(jnp.float32),
        lax.psum(shares[2].astype(jnp.bfloat16), "seq").astype(jnp.float32),
        lax.psum(shares[3].astype(jnp.bfloat16), "seq").astype(jnp.float32),
        lax.psum(shares[4].astype(jnp.bfloat16), "seq").astype(jnp.float32),
        lax.psum(shares[5].astype(jnp.bfloat16), "seq").astype(jnp.float32),
        lax.psum(shares[6].astype(jnp.bfloat16), "seq").astype(jnp.float32),
        lax.psum(shares[7].astype(jnp.bfloat16), "seq").astype(jnp.float32),
        lax.psum(shares[8].astype(jnp.bfloat16), "seq").astype(jnp.float32),
        lax.psum(shares[9].astype(jnp.bfloat16), "seq").astype(jnp.float32),
        lax.psum(shares[10].astype(jnp.bfloat16), "seq").astype(jnp.float32),
        lax.psum(shares[11].astype(jnp.bfloat16), "seq").astype(jnp.float32),
        lax.psum(shares[12].astype(jnp.bfloat16), "seq").astype(jnp.float32),
    )
    return (
        lax.all_gather(shares[0].astype(jnp.bfloat16), "rep", axis=0, tiled=True).astype(
            jnp.float32
        ),
        lax.all_gather(shares[1].astype(jnp.bfloat16), "rep", axis=0, tiled=True).astype(
            jnp.float32
        ),
        lax.all_gather(shares[2].astype(jnp.bfloat16), "rep", axis=0, tiled=True).astype(
            jnp.float32
        ),
        lax.all_gather(shares[3].astype(jnp.bfloat16), "rep", axis=0, tiled=True).astype(
            jnp.float32
        ),
        lax.all_gather(shares[4].astype(jnp.bfloat16), "rep", axis=0, tiled=True).astype(
            jnp.float32
        ),
        lax.all_gather(shares[5].astype(jnp.bfloat16), "rep", axis=0, tiled=True).astype(
            jnp.float32
        ),
        lax.all_gather(shares[6].astype(jnp.bfloat16), "rep", axis=0, tiled=True).astype(
            jnp.float32
        ),
        lax.all_gather(shares[7].astype(jnp.bfloat16), "rep", axis=0, tiled=True).astype(
            jnp.float32
        ),
        lax.all_gather(shares[8].astype(jnp.bfloat16), "rep", axis=0, tiled=True).astype(
            jnp.float32
        ),
        lax.all_gather(shares[9].astype(jnp.bfloat16), "rep", axis=0, tiled=True).astype(
            jnp.float32
        ),
        lax.all_gather(shares[10].astype(jnp.bfloat16), "rep", axis=0, tiled=True).astype(
            jnp.float32
        ),
        lax.all_gather(shares[11].astype(jnp.bfloat16), "rep", axis=0, tiled=True).astype(
            jnp.float32
        ),
        lax.all_gather(shares[12].astype(jnp.bfloat16), "rep", axis=0, tiled=True).astype(
            jnp.float32
        ),
    )


class Halves:
    def spread(self, rows):
        return lax.all_gather(rows, "seq", axis=0, tiled=True)

    def collect(self, rows):
        return lax.psum_scatter(rows, "seq", scatter_dimension=0, tiled=True)


def from_cores(rows):
    half = rows.shape[0] // 2
    spots = [(x, y, c) for x in range(2) for y in range(2) for c in range(2)]
    first = [(c * 4 + y * 2 + x, x * 4 + y * 2 + c) for x, y, c in spots]
    second = [(c * 4 + y * 2 + 1 - x, x * 4 + y * 2 + c) for x, y, c in spots]
    return jnp.concatenate(
        [
            lax.ppermute(rows[:half], ("seq", "rep"), first),
            lax.ppermute(rows[half:], ("seq", "rep"), second),
        ],
        axis=0,
    )


ZN = 4


def neighbours():
    x, z, r = lax.axis_index("seq"), lax.axis_index("fsdp"), lax.axis_index("rep")
    y, c = r // 2, r % 2
    across = (1 - x, z, r)
    beside = (x, z, (1 - y) * 2 + c)
    twin = (x, z, y * 2 + (1 - c))
    up = (x, (z + 1) % ZN, r)
    down = (x, (z + ZN - 1) % ZN, r)
    return x, y, z, c, across, beside, twin, up, down


def greet(z, c, x, across, beside, twin, diag, up, down):
    barrier = pltpu.get_barrier_semaphore()

    def tell(device):
        pl.semaphore_signal(barrier, inc=1, device_id=device, device_id_type=MESH)

    for device in (across, beside, twin):
        tell(device)
    if diag is not None:

        @pl.when(c != x)
        def _():
            tell(diag)

    @pl.when(z < ZN - 1)
    def _():
        tell(up)

    @pl.when(z > 0)
    def _():
        tell(down)

    extra = 0 if diag is None else (x + c) % 2
    pl.semaphore_wait(barrier, 3 + extra + (z + ZN - 1) // ZN + (2 * ZN - 2 - z) // ZN)


GELU_A = math.sqrt(2.0 / math.pi)
GELU_B = 0.044715
QUERY_SCALE = 1.0 / math.sqrt(HEAD_DIM)
HEAD_ROWS = 24
PACE = 2
REDUCE_PACE = 6
SKEW = 2


NT = (((1,), (1,)), ((), ()))
TN = (((0,), (0,)), ((), ()))
BLOCK = 256
RANGES = (((0, 256), (256, 1024)), ((0, 768), (256, 512)))
VMEM_LIMIT = 60 << 20


def dot_nt(left, right):
    return lax.dot_general(left, right, NT, preferred_element_type=jnp.float32)


def dot_tn(left, right):
    return lax.dot_general(left, right, TN, preferred_element_type=jnp.float32)


def tiles(width, tile, act):
    whole = width // tile

    def step(i, carry):
        act(pl.multiple_of(i * tile, tile), tile)
        return carry

    lax.fori_loop(0, whole, step, 0)
    if width % tile:
        act(whole * tile, width % tile)


def tiles_between(low, high, tile, act):
    def step(i, carry):
        act(pl.multiple_of(i * tile, tile), tile)
        return carry

    if low // tile < high // tile:
        lax.fori_loop(low // tile, high // tile, step, 0)
    if high % tile:
        act(high // tile * tile, high % tile)


def norm_parts(rows):
    center = rows - jnp.mean(rows, axis=1, keepdims=True)
    scale = lax.rsqrt(jnp.mean(center * center, axis=1, keepdims=True) + NORM_EPSILON)
    return center * scale, scale


def norm_into(source, gain, shift, target):
    def act(start, size):
        rows = pl.ds(start, size)
        unit, _ = norm_parts(source[rows, :])
        target[rows, :] = (unit * gain + shift).astype(target.dtype)

    tiles(source.shape[0], 64, act)


def norm_back(source, grad, extra, gain, target, gain_grad, shift_grad, low=None):
    gain_grad[...] = jnp.zeros_like(gain_grad)
    shift_grad[...] = jnp.zeros_like(shift_grad)

    def act(start, size):
        rows = pl.ds(start, size)
        unit, scale = norm_parts(source[rows, :])
        g = grad[rows, :]
        q = g * gain
        mean_q = jnp.mean(q, axis=1, keepdims=True)
        mean_qn = jnp.mean(q * unit, axis=1, keepdims=True)
        out = extra[rows, :] + (q - mean_q - unit * mean_qn) * scale
        target[rows, :] = out
        if low is not None:
            low[rows, :] = out.astype(low.dtype)
        gain_grad[...] += jnp.sum(g * unit, axis=0, keepdims=True)
        shift_grad[...] += jnp.sum(g, axis=0, keepdims=True)

    tiles(source.shape[0], 64, act)


def whole(count):
    return [pl.BlockSpec(memory_space=pltpu.VMEM)] * count


def anywhere(count):
    return [pl.BlockSpec(memory_space=pl.ANY)] * count


def shaped(shape, dtype=jnp.float32):
    return jax.ShapeDtypeStruct(shape, dtype)


def params():
    return pltpu.CompilerParams(vmem_limit_bytes=VMEM_LIMIT)


def of_head(values, j):
    if values.shape[1] == HEAD_DIM:
        return values
    lane = lax.broadcasted_iota(jnp.int32, values.shape, 1)
    return jnp.where(lane // HEAD_DIM == j, values, jnp.zeros_like(values))


ZA, ZR, GX, GY, GD1, GD2, GC = range(7)
ROW = dict(attn_gain=0, attn_shift=1, b_query=2, b_value=3, b_out=4, mlp_gain=5, mlp_shift=6, b_down=7)
SAVED = ("x", "normed_attn", "q", "keys", "values", "attended", "lse", "middle", "normed_mlp", "slope", "activated")


def advance(steps, count):
    for _ in range(count):
        if next(steps, None) is None:
            return


def weight_moves(ins, outs, send_sem, recv_sem, place):
    x, y, z, c, across, beside, twin, up, down = place
    m_count = len(ins) - 1
    layers = ins[0].shape[0]
    units = [(layer, m) for layer in range(layers) for m in range(m_count + 1)]
    index = {unit: i for i, unit in enumerate(units)}

    def depth(u):
        return ins[u[1]].shape[1] // 8

    def owned(u, px, py, half=None):
        k = depth(u)
        base = (c * 4 + px * 2 + py) * k
        if half is None:
            return pl.ds(base, k)
        return pl.ds(base + half * (k // 2), k // 2)

    def rest(u):
        n = ins[u[1]].shape[1]
        return pl.ds(n // 8 * 8, n % 8)

    def slab(u, core):
        return pl.ds(core * 4 * depth(u), 4 * depth(u))

    def move(u, zz, rows, device, kind, source=None, send_kind=None):
        target = outs[u[1]].at[u[0], zz, rows]
        return pltpu.make_async_remote_copy(
            src_ref=target if source is None else source,
            dst_ref=target,
            send_sem=send_sem.at[index[u], zz, kind if send_kind is None else send_kind],
            recv_sem=recv_sem.at[index[u], zz, kind],
            device_id=device,
            device_id_type=MESH,
        )

    def own_sends(u, act):
        source = ins[u[1]].at[u[0]]

        def along(device, first):
            if depth(u):
                act(move(u, z, owned(u, x, y), device, ZA, source.at[owned(u, x, y)], first))
            act(move(u, z, rest(u), device, ZR, source.at[rest(u)], first + 1))

        @pl.when(z < ZN - 1)
        def _():
            along(up, 0)

        @pl.when(z > 0)
        def _():
            along(down, 2)

    def both(s, act):
        @pl.when(z >= s)
        def _():
            act(z - s, 0)

        @pl.when(z + s <= ZN - 1)
        def _():
            act(z + s, 1)

    def onward(u, zz, d, act):
        def along(device):
            if depth(u):
                act(move(u, zz, owned(u, x, y), device, ZA))
            act(move(u, zz, rest(u), device, ZR))

        if d == 0:

            @pl.when(z < ZN - 1)
            def _():
                along(up)

        else:

            @pl.when(z > 0)
            def _():
                along(down)

    def line_step(u, s):
        def act(zz, d):
            if depth(u):
                move(u, zz, owned(u, x, y), across, ZA).wait_recv()
            move(u, zz, rest(u), across, ZR).wait_recv()
            onward(u, zz, d, lambda copy: copy.start())
            if depth(u):
                move(u, zz, owned(u, x, y), across, GX).start()
                move(u, zz, owned(u, x, y), beside, GY).start()

        both(s, act)

    def plane_step(u, s):
        def act(zz, d):
            move(u, zz, owned(u, 1 - x, y), across, GX).wait_recv()
            move(u, zz, owned(u, 1 - x, y, 0), beside, GD1).start()
            move(u, zz, owned(u, x, 1 - y), beside, GY).wait_recv()
            move(u, zz, owned(u, x, 1 - y, 1), across, GD2).start()

        both(s, act)

    def corner_step(u, s):
        def act(zz, d):
            move(u, zz, owned(u, 1 - x, 1 - y, 0), beside, GD1).wait_recv()
            move(u, zz, owned(u, 1 - x, 1 - y, 1), across, GD2).wait_recv()
            move(u, zz, slab(u, c), twin, GC).start()

        both(s, act)

    def arrive(u):
        for s in range(1, ZN):
            both(s, lambda zz, d: move(u, zz, slab(u, 1 - c), twin, GC).wait_recv())

    def finish(u):
        own_sends(u, lambda copy: copy.wait_send())
        for s in range(1, ZN):

            def act(zz, d):
                onward(u, zz, d, lambda copy: copy.wait_send())
                if depth(u):
                    move(u, zz, owned(u, x, y), across, GX).wait_send()
                    move(u, zz, owned(u, x, y), beside, GY).wait_send()
                    move(u, zz, owned(u, 1 - x, y, 0), beside, GD1).wait_send()
                    move(u, zz, owned(u, x, 1 - y, 1), across, GD2).wait_send()
                    move(u, zz, slab(u, c), twin, GC).wait_send()

            both(s, act)

    matrices = [u for u in units if u[1] < m_count]
    vectors = [u for u in units if u[1] == m_count]
    count = len(matrices)

    def steps():
        for u in vectors + matrices[:2]:
            own_sends(u, lambda copy: copy.start())
        for s in range(1, ZN):
            for u in vectors:
                line_step(u, s)
        yield ("vectors",)
        for t in range(count + 4):
            if t + 2 < count:
                own_sends(matrices[t + 2], lambda copy: copy.start())
            for s in range(1, ZN):
                if 0 <= t + 1 - s < count:
                    line_step(matrices[t + 1 - s], s)
                    yield ("line",)
            for s in range(1, ZN):
                if 0 <= t - s < count:
                    plane_step(matrices[t - s], s)
                    yield ("plane",)
            for s in range(1, ZN):
                if 0 <= t - 1 - s < count:
                    corner_step(matrices[t - 1 - s], s)
                    yield ("here", matrices[t - 1 - s]) if s == ZN - 1 else ("corner",)

    return steps, arrive, lambda: [finish(u) for u in units]


def attend(core, q, keys, values, mask, attended, lse, first, last):
    def slab(start, size, head):
        cols = pl.ds(start, size)
        for variant in range(2):

            @pl.when(core == variant)
            def _():
                for row, high in RANGES[variant]:
                    rows = slice(row, row + BLOCK)
                    qs = q[rows, cols]
                    ks, vs = keys[:high, cols], values[:high, cols]
                    parts = []
                    for j in range(size // HEAD_DIM):
                        s = dot_nt(ks, of_head(qs, j)) + mask[:high, rows]
                        top = jnp.max(s, axis=0, keepdims=True)
                        e = jnp.exp(s - top)
                        total = jnp.sum(e, axis=0, keepdims=True)
                        lse[pl.ds(head + j, 1), rows] = top + jnp.log(total)
                        out = dot_tn(vs, e.astype(jnp.bfloat16)) * (1.0 / total)
                        parts.append(out[j * HEAD_DIM : (j + 1) * HEAD_DIM])
                    out = jnp.concatenate(parts, axis=0) if len(parts) > 1 else parts[0]
                    attended[rows, cols] = out.T.astype(jnp.bfloat16)

    over_slabs(q.shape[1], slab, first, last)


def over_slabs(width, slab, first, last):
    pair = 2 * HEAD_DIM
    full = width // pair

    def step(i, carry):
        slab(pl.multiple_of(i * pair, pair), pair, i * 2)
        return carry

    if first < min(last, full):
        lax.fori_loop(first, min(last, full), step, 0)
    if last > full and width % pair:
        slab(full * pair, HEAD_DIM, full * 2)


def forward_body(
    tokens, grads, segs, vectors, w_qkv, w_out, w_up, w_down,
    full_qkv, full_out, full_up, full_down, full_vectors, result, grads_here, mask_out, rows_out, *rest_refs,
):
    layers = w_qkv.shape[0]
    saved = [dict(zip(SAVED, rest_refs[i * len(SAVED) : (i + 1) * len(SAVED)])) for i in range(layers)]
    (
        wq, wo, wu, wd, xs, tok, na, nm, q, keys, values, mask, att, middle, slope, act_buf, lse,
        vecs, rows, b_up, b_proj, seg_nat, seg_row,
        send_sem, recv_sem, load_sem, own_sem, save_sem, kv_send, kv_recv, in_send, in_recv, in_local, free_sem,
    ) = rest_refs[layers * len(SAVED) :]
    place = neighbours()
    x, y, z, c, across, beside, twin, up, down = place
    diag = (1 - x, z, y * 2 + (1 - c))
    here = c == x
    greet(z, c, x, across, beside, twin, diag, up, down)
    width = xs.shape[1]
    half = BLOCK
    parts = [w_qkv, w_out, w_up, w_down]
    fulls = [full_qkv, full_out, full_up, full_down]
    buffers = [wq, wo, wu, wd]
    steps, arrive, finish = weight_moves(parts + [vectors], fulls + [full_vectors], send_sem, recv_sem, place)

    def in_move(i, source, target, device):
        return pltpu.make_async_remote_copy(
            src_ref=source, dst_ref=target, send_sem=in_send.at[i], recv_sem=in_recv.at[i],
            device_id=device, device_id_type=MESH,
        )

    top, low = pl.ds(0, half), pl.ds(half, half)

    def in_copies(i, source, target):
        stay = pltpu.make_async_copy(source.at[top], target.at[top], in_local.at[i])
        return (
            stay,
            in_move(2 * i + 1, source.at[low], target.at[low], twin),
            in_move(2 * i, source.at[top], target.at[top], diag),
            in_move(2 * i + 1, source.at[low], target.at[low], across),
        )

    tok_copies = in_copies(0, tokens, tok)
    grad_copies = in_copies(1, grads, grads_here)
    seg_stay = pltpu.make_async_copy(segs, seg_nat.at[x], in_local.at[2])
    seg_twin = in_move(4, segs, seg_nat.at[x], twin)
    seg_across = in_move(4, segs, seg_nat.at[x], across)
    seg_diag = pltpu.make_async_remote_copy(
        src_ref=segs, dst_ref=seg_nat.at[x], send_sem=in_send.at[5], recv_sem=in_recv.at[5],
        device_id=diag, device_id_type=MESH,
    )

    @pl.when(here)
    def _():
        for copy in (seg_stay, seg_twin, tok_copies[0], tok_copies[1], grad_copies[0], grad_copies[1]):
            copy.start()

    @pl.when(jnp.logical_not(here))
    def _():
        for copy in (seg_across, seg_diag, tok_copies[2], tok_copies[3], grad_copies[2], grad_copies[3]):
            copy.start()

    def wait_in(copies):
        @pl.when(here)
        def _():
            copies[0].wait()
            copies[1].wait_recv()

        @pl.when(jnp.logical_not(here))
        def _():
            copies[2].wait_recv()
            copies[3].wait_recv()

    def wait_segs():
        @pl.when(here)
        def _():
            seg_stay.wait()
            seg_across.wait_recv()

        @pl.when(jnp.logical_not(here))
        def _():
            seg_twin.wait_recv()
            seg_diag.wait_recv()

    def finish_in():
        @pl.when(here)
        def _():
            grad_copies[0].wait()
            grad_copies[1].wait_recv()
            for copy in (seg_twin, tok_copies[1], grad_copies[1]):
                copy.wait_send()

        @pl.when(jnp.logical_not(here))
        def _():
            grad_copies[2].wait_recv()
            grad_copies[3].wait_recv()
            for copy in (seg_across, seg_diag, tok_copies[2], tok_copies[3], grad_copies[2], grad_copies[3]):
                copy.wait_send()

    comm = steps()
    seen = set()
    loaded = {}
    done_with = set()

    def tick(count=1):
        for _ in range(count):
            label = next(comm, None)
            if label is None:
                return False
            seen.add(label)
            if label[0] == "here":
                fetch_ready()
        return True

    def loads(u):
        layer, m = u
        n = parts[m].shape[1]
        copies = [pltpu.make_async_copy(parts[m].at[layer], buffers[m].at[pl.ds(z * n, n)], load_sem.at[m, 0])]
        for s in range(1, ZN):
            zz = (z + s) % ZN
            copies.append(
                pltpu.make_async_copy(fulls[m].at[layer, zz], buffers[m].at[pl.ds(zz * n, n)], load_sem.at[m, s])
            )
        return copies

    def fetch_ready(upto=None):
        for layer in range(layers):
            for m in range(len(parts)):
                u = (layer, m)
                if u in loaded or ("here", u) not in seen:
                    continue
                if layer and (layer - 1, m) not in done_with:
                    continue
                following = (layer, m + 1) if m + 1 < len(parts) else (layer + 1, 0)
                if u != upto and following[0] < layers and ("here", following) not in seen:
                    continue
                arrive(u)
                if layer:
                    own_rows((layer - 1, m)).wait()
                for copy in loads(u):
                    copy.start()
                loaded[u] = True

    def own_rows(u):
        layer, m = u
        n = parts[m].shape[1]
        return pltpu.make_async_copy(buffers[m].at[pl.ds(z * n, n)], fulls[m].at[layer, z], own_sem.at[layer, m])

    def need(u):
        while ("here", u) not in seen:
            if not tick():
                break
        fetch_ready(u)
        for copy in loads(u):
            copy.wait()
        own_rows(u).start()

    pending = []

    def save(layer, name, buffer):
        copy = pltpu.make_async_copy(buffer, saved[layer][name], save_sem.at[layer, SAVED.index(name)])
        copy.start()
        pending.append(copy)

    def settle():
        while pending:
            pending.pop().wait()

    def row(layer, name):
        return rows[layer, pl.ds(ROW[name], 1), :]

    def make_mask():
        wait_segs()
        joined = jnp.concatenate([seg_nat[0], seg_nat[1]], axis=1).astype(jnp.float32)
        seg_row[...] = jnp.broadcast_to(joined, seg_row.shape)
        column = seg_row[...].T[:, :1]
        for block in range(2):
            base = ((2 * c) if block == 0 else (3 - 2 * c)) * BLOCK
            own = seg_row[0:1, pl.ds(pl.multiple_of(base, BLOCK), BLOCK)]
            spot = lax.broadcasted_iota(jnp.int32, (mask.shape[0], BLOCK), 0)
            mine = lax.broadcasted_iota(jnp.int32, (mask.shape[0], BLOCK), 1) + base
            ok = (column == own) & (spot <= mine)
            mask[:, block * BLOCK : (block + 1) * BLOCK] = jnp.where(ok, 0.0, MASKED).astype(jnp.float32)
        copy = pltpu.make_async_copy(mask, mask_out, save_sem.at[0, len(SAVED)])
        copy.start()
        pending.append(copy)

    def make_rows(layer):
        copies = [
            pltpu.make_async_copy(vectors.at[layer, 0], vecs.at[z], load_sem.at[4, 0])
        ] + [
            pltpu.make_async_copy(full_vectors.at[layer, (z + s) % ZN, 0], vecs.at[(z + s) % ZN], load_sem.at[4, s])
            for s in range(1, ZN)
        ]
        for copy in copies:
            copy.start()
        for copy in copies:
            copy.wait()
        share = vecs.shape[2]
        b_proj[layer, 0:1, :] = jnp.zeros((1, b_proj.shape[2]), jnp.float32)
        for zz in range(ZN):
            block = vecs[zz].astype(jnp.float32)
            rows[layer, 0:8, zz * share : (zz + 1) * share] = block[0:8]
            for name, at in (("b_query", 0), ("b_value", 2 * width)):
                b_proj[layer, 0:1, at + zz * share : at + (zz + 1) * share] = block[ROW[name] : ROW[name] + 1]
            for j in range(ZN):
                at = (zz * ZN + j) * share
                b_up[layer, 0:1, at : at + share] = block[8 + j : 9 + j]

    def swap_moves(layer):
        moves = []
        for i, ref in enumerate((keys, values)):
            for block in range(2):
                at = ((2 * c) if block == 0 else (3 - 2 * c)) * BLOCK
                spot = ref.at[pl.ds(pl.multiple_of(at, BLOCK), BLOCK)]
                moves.append(
                    pltpu.make_async_remote_copy(
                        src_ref=spot, dst_ref=spot, send_sem=kv_send.at[layer, i, block],
                        recv_sem=kv_recv.at[layer, i, block], device_id=twin, device_id_type=MESH,
                    )
                )
        return moves

    def swap_waits(layer):
        moves = []
        for i, ref in enumerate((keys, values)):
            for block in range(2):
                at = ((2 - 2 * c) if block == 0 else (1 + 2 * c)) * BLOCK
                spot = ref.at[pl.ds(pl.multiple_of(at, BLOCK), BLOCK)]
                moves.append(
                    pltpu.make_async_remote_copy(
                        src_ref=spot, dst_ref=spot, send_sem=kv_send.at[layer, i, block],
                        recv_sem=kv_recv.at[layer, i, block], device_id=twin, device_id_type=MESH,
                    )
                )
        return moves

    def matrix(buffer, cols):
        return buffer[:, :, cols].reshape(-1, cols.size)

    def compute(layer):
        if layer == 0:
            make_rows(0)
            make_rows(1)
            for i in range(layers):
                copy = pltpu.make_async_copy(rows.at[i], rows_out.at[i], save_sem.at[i, len(SAVED) + 1])
                copy.start()
                pending.append(copy)
            wait_in(tok_copies)
            xs[...] = tok[...].astype(jnp.float32)
            make_mask()
        else:
            settle()
        save(layer, "x", xs)
        norm_into(xs, row(layer, "attn_gain"), row(layer, "attn_shift"), na)
        save(layer, "normed_attn", na)
        yield
        need((layer, 0))
        total = wq.shape[2]

        for low_at in range(0, total, 4 * BLOCK):
            high_at = min(low_at + 4 * BLOCK, total)
            tiles_between(low_at, high_at, BLOCK, lambda start, size: project_tile(layer, start, size))
            yield
        done_with.add((layer, 0))
        q[...] = slope[:, :width]
        if layer:
            pl.semaphore_wait(free_sem, 1)
        for block in range(2):
            at = ((2 * c) if block == 0 else (3 - 2 * c)) * BLOCK
            spot = pl.ds(pl.multiple_of(at, BLOCK), BLOCK)
            source = slice(block * BLOCK, (block + 1) * BLOCK)
            keys[spot, :] = slope[source, width : 2 * width]
            values[spot, :] = slope[source, 2 * width : 3 * width]
        for copy in swap_moves(layer):
            copy.start()
        save(layer, "q", q)
        yield
        for copy in swap_waits(layer):
            copy.wait_recv()
        save(layer, "keys", keys)
        save(layer, "values", values)
        for first in range(0, width // (2 * HEAD_DIM) + 1, 4):
            attend(c, q, keys, values, mask, att, lse, first, min(first + 4, width // (2 * HEAD_DIM) + 1))
            yield
        save(layer, "attended", att)
        save(layer, "lse", lse)
        if layer + 1 < layers:
            settle()
            for copy in swap_moves(layer):
                copy.wait_send()
            pl.semaphore_signal(free_sem, inc=1, device_id=twin, device_id_type=MESH)
        need((layer, 1))

        def out_step(start, size):
            cols = pl.ds(start, size)
            middle[:, cols] = xs[:, cols] + product(att[...], matrix(wo, cols)) + rows[layer, pl.ds(ROW["b_out"], 1), cols]

        tiles_between(0, width, BLOCK, out_step)
        done_with.add((layer, 1))
        save(layer, "middle", middle)
        yield
        norm_into(middle, row(layer, "mlp_gain"), row(layer, "mlp_shift"), nm)
        save(layer, "normed_mlp", nm)
        yield
        need((layer, 2))
        settle()

        def up_step(start, size):
            cols = pl.ds(start, size)
            u = product(nm[...], matrix(wu, cols)) + b_up[layer, 0:1, cols]
            square = u * u
            t = jnp.tanh(u * (GELU_A + (GELU_A * GELU_B) * square))
            half_up = 0.5 + 0.5 * t
            act_buf[:, cols] = (u * half_up).astype(jnp.bfloat16)
            slope[:, cols] = (
                half_up + (0.5 * u) * (1.0 - t * t) * (GELU_A + (3.0 * GELU_A * GELU_B) * square)
            ).astype(jnp.bfloat16)

        ff = wu.shape[2]
        for low_at in range(0, ff, 6 * BLOCK):
            tiles_between(low_at, min(low_at + 6 * BLOCK, ff), BLOCK, up_step)
            yield
        done_with.add((layer, 2))
        save(layer, "slope", slope)
        save(layer, "activated", act_buf)
        need((layer, 3))

        def down_step(start, size):
            cols = pl.ds(start, size)
            xs[:, cols] = middle[:, cols] + product(act_buf[...], matrix(wd, cols)) + rows[layer, pl.ds(ROW["b_down"], 1), cols]

        for low_at in range(0, width, 2 * BLOCK):
            tiles_between(low_at, min(low_at + 2 * BLOCK, width), BLOCK, down_step)
            yield
        done_with.add((layer, 3))

    def project_tile(layer, start, size):
        cols = pl.ds(start, size)
        out = product(na[...], matrix(wq, cols))
        slope[:, cols] = ((out + b_proj[layer, 0:1, cols]) * scale_of(start, size)).astype(jnp.bfloat16)

    def scale_of(start, size):
        lane = lax.broadcasted_iota(jnp.int32, (1, size), 1) + start
        return jnp.where(lane < width, QUERY_SCALE, 1.0).astype(jnp.float32)

    tick()
    for layer in range(layers):
        for _ in compute(layer):
            tick(PACE)
    while tick():
        pass
    settle()
    tok[...] = xs[...].astype(jnp.bfloat16)
    out = pltpu.make_async_copy(tok, result, save_sem.at[0, 0])
    out.start()
    for copy in swap_moves(layers - 1):
        copy.wait_send()
    finish_in()
    finish()
    for m in range(len(parts)):
        own_rows((layers - 1, m)).wait()
    out.wait()


def forward(tokens, grads, segs, vectors, weights):
    rows, width = tokens.shape
    low = jnp.bfloat16
    layers = vectors.shape[0]
    ff = weights[2].shape[3]
    units = layers * (len(weights) + 1)
    shapes = dict(
        x=((rows, width), jnp.float32),
        normed_attn=((rows, width), low),
        q=((rows, width), low),
        keys=((2 * rows, width), low),
        values=((2 * rows, width), low),
        attended=((rows, width), low),
        lse=((HEAD_ROWS, rows), jnp.float32),
        middle=((rows, width), jnp.float32),
        normed_mlp=((rows, width), low),
        slope=((rows, ff), low),
        activated=((rows, ff), low),
    )
    out_shape = (
        [shaped((layers, ZN) + w.shape[1:], low) for w in weights]
        + [
            shaped((layers, ZN) + vectors.shape[1:], low),
            shaped((rows, width), low),
            shaped((rows, width), low),
            shaped((2 * rows, rows)),
            shaped((layers, 16, width)),
        ]
        + [shaped(*shapes[name]) for _ in range(layers) for name in SAVED]
    )
    dma = pltpu.SemaphoreType.DMA
    scratch = [pltpu.VMEM((ZN * w.shape[1],) + w.shape[2:], low) for w in weights] + [
        pltpu.VMEM((rows, width), jnp.float32),
        pltpu.VMEM((rows, width), low),
        pltpu.VMEM((rows, width), low),
        pltpu.VMEM((rows, width), low),
        pltpu.VMEM((rows, width), low),
        pltpu.VMEM((2 * rows, width), low),
        pltpu.VMEM((2 * rows, width), low),
        pltpu.VMEM((2 * rows, rows), jnp.float32),
        pltpu.VMEM((rows, width), low),
        pltpu.VMEM((rows, width), jnp.float32),
        pltpu.VMEM((rows, ff), low),
        pltpu.VMEM((rows, ff), low),
        pltpu.VMEM((HEAD_ROWS, rows), jnp.float32),
        pltpu.VMEM((ZN,) + vectors.shape[2:], low),
        pltpu.VMEM((layers, 16, width), jnp.float32),
        pltpu.VMEM((layers, 8, ff), jnp.float32),
        pltpu.VMEM((layers, 8, 3 * width), jnp.float32),
        pltpu.VMEM((2, 1, rows), jnp.int32),
        pltpu.VMEM((8, 2 * rows), jnp.float32),
        dma((units, ZN, 7)),
        dma((units, ZN, 7)),
        dma((len(weights) + 1, ZN)),
        dma((layers, len(weights))),
        dma((layers, len(SAVED) + 2)),
        dma((layers, 2, 2)),
        dma((layers, 2, 2)),
        dma((6,)),
        dma((6,)),
        dma((3,)),
        pltpu.SemaphoreType.REGULAR,
    ]
    outs = pl.pallas_call(
        forward_body,
        out_shape=out_shape,
        in_specs=anywhere(4 + len(weights)),
        out_specs=anywhere(len(out_shape)),
        scratch_shapes=scratch,
        compiler_params=pltpu.CompilerParams(collective_id=0, has_side_effects=True, vmem_limit_bytes=VMEM_LIMIT),
        name="forward",
    )(tokens, grads, segs, vectors, *weights)
    count = len(weights)
    fulls, rest = outs[:count], outs[count + 5 :]
    _, result, grads_here, mask, vector_rows = outs[count : count + 5]
    saved = [dict(zip(SAVED, rest[i * len(SAVED) : (i + 1) * len(SAVED)])) for i in range(layers)]
    return fulls, result, grads_here, mask, vector_rows, saved


def begin(copies):
    for copy in copies:
        copy.start()


def end(copies):
    for copy in copies:
        copy.wait()


ORDER = (0, 1, 3, 2)
RC, R1, R2, RZ, RX, RY, RD1, RD2, RCC, R1B, RZX = 0, 4, 8, 12, 16, 17, 18, 19, 20, 21, 25


class Group:
    def __init__(self, grad, out, base, k):
        self.grad, self.out, self.base, self.k = grad, out, base, k


def reduce_steps(place, groups, acc, stage, first_in, second_in, line_in, line_extra, load_sem, store_sem, send_sem, recv_sem):
    x, y, z, c, across, beside, twin, up, down = place
    p = x * 2 + y
    units = [(g, d) for g in range(len(groups)) for d in ORDER]

    def move(source, target, g, kind, device):
        return pltpu.make_async_remote_copy(
            src_ref=source, dst_ref=target, send_sem=send_sem.at[g, kind], recv_sem=recv_sem.at[g, kind],
            device_id=device, device_id_type=MESH,
        )

    def half_of(g, d, core):
        group = groups[g]
        return group.grad.at[d, pl.ds(group.base + core * 4 * group.k, 4 * group.k)]

    def to_twin(g, d):
        return move(half_of(g, d, 1 - c), acc[g].at[d], g, RC + d, twin)

    def slot(d):
        return ORDER.index(d) % 2

    def load(g, d):
        return pltpu.make_async_copy(half_of(g, d, c), stage[g].at[slot(d)], load_sem.at[g, slot(d)])

    def add(g, d, at, extra, lead, extra_at, n):
        def step(i, carry):
            acc[g][d, at + i] = acc[g][d, at + i] + extra[lead, extra_at + i]
            return carry

        lax.fori_loop(0, n, step, 0)

    def first_moves(g, d):
        k = groups[g].k
        if d in (0, 3):
            return [move(acc[g].at[d, pl.ds((1 - x) * 2 * k, 2 * k)], first_in[g].at[d], g, R1 + d, across)]
        return [
            move(acc[g].at[d, pl.ds((1 - y) * k, k)], first_in[g].at[d, pl.ds(0, k)], g, R1 + d, beside),
            move(acc[g].at[d, pl.ds((3 - y) * k, k)], first_in[g].at[d, pl.ds(k, k)], g, R1B + d, beside),
        ]

    def second_move(g, d):
        k = groups[g].k
        if d in (0, 3):
            return move(acc[g].at[d, pl.ds((x * 2 + 1 - y) * k, k)], second_in[g].at[d], g, R2 + d, beside)
        return move(acc[g].at[d, pl.ds(((1 - x) * 2 + y) * k, k)], second_in[g].at[d], g, R2 + d, across)

    def twin_step(g, d):
        to_twin(g, d).wait_recv()
        load(g, d).wait()
        add(g, d, 0, stage[g], slot(d), 0, 4 * groups[g].k)
        for copy in first_moves(g, d):
            copy.start()
        later = ORDER.index(d) + 2
        if later < len(ORDER):
            load(g, ORDER[later]).start()

    def first_step(g, d):
        k = groups[g].k
        for copy in first_moves(g, d):
            copy.wait_recv()
        if d in (0, 3):
            add(g, d, x * 2 * k, first_in[g], d, 0, 2 * k)
        else:
            add(g, d, y * k, first_in[g], d, 0, k)
            add(g, d, (2 + y) * k, first_in[g], d, k, k)
        second_move(g, d).start()

    def second_step(g, d):
        second_move(g, d).wait_recv()
        add(g, d, p * groups[g].k, second_in[g], d, 0, groups[g].k)

    def piece(g, d):
        return acc[g].at[d, pl.ds(p * groups[g].k, groups[g].k)]

    def to_down(g, d, zz):
        if d == zz - 1:
            return move(piece(g, d), line_extra[g].at[0], g, RZX, down)
        return move(piece(g, d), line_in[g].at[d], g, RZ + d, down)

    def to_up(g, d, zz):
        return move(piece(g, d), line_in[g].at[d], g, RZ + d, up)

    def rows_of(g, px, py, low=0, n=None):
        group = groups[g]
        return group.out.at[pl.ds(group.base + (c * 4 + px * 2 + py) * group.k + low, group.k if n is None else n)]

    def share_across(g):
        return move(piece(g, z), rows_of(g, x, y), g, RX, across)

    def share_beside(g):
        return move(piece(g, z), rows_of(g, x, y), g, RY, beside)

    def store(g):
        return pltpu.make_async_copy(piece(g, z), rows_of(g, x, y), store_sem.at[g])

    def arrived(g, px, py, kind):
        return move(rows_of(g, px, py), rows_of(g, px, py), g, kind, across)

    def corner(g, px, py, part):
        k = groups[g].k
        low, n = (0, max(k // 2, 1)) if part == 0 else (k // 2, k - k // 2)
        rows = rows_of(g, px, py, low, n)
        return move(rows, rows, g, RD1 if part == 0 else RD2, beside if part == 0 else across)

    def to_core(g, core):
        group = groups[g]
        rows = group.out.at[pl.ds(group.base + core * 4 * group.k, 4 * group.k)]
        return move(rows, rows, g, RCC, twin)

    def line_step(g, d, s):
        k = groups[g].k
        for zz in range(ZN):
            downward = d < zz and zz == ZN - 1 - s
            upward = d > zz and zz == s
            last = d == zz and s == ZN - 1
            if not (downward or upward or last):
                continue

            @pl.when(z == zz)
            def _():
                if downward:
                    if zz < ZN - 1:
                        to_down(g, d, zz + 1).wait_recv()
                        add(g, d, p * k, line_in[g], d, 0, k)
                    to_down(g, d, zz).start()
                if upward:
                    if zz > 0:
                        to_up(g, d, zz - 1).wait_recv()
                        add(g, d, p * k, line_in[g], d, 0, k)
                    to_up(g, d, zz).start()
                if last:
                    if zz > 0:
                        to_up(g, d, zz - 1).wait_recv()
                        add(g, d, p * k, line_in[g], d, 0, k)
                    if zz < ZN - 1:
                        to_down(g, d, zz + 1).wait_recv()
                        add(g, d, p * k, line_extra[g], 0, 0, k)
                    share_across(g).start()
                    share_beside(g).start()
                    store(g).start()

    def corner_step(g, d):
        @pl.when(z == d)
        def _():
            arrived(g, 1 - x, y, RX).wait_recv()
            corner(g, 1 - x, y, 0).start()
            arrived(g, x, 1 - y, RY).wait_recv()
            if groups[g].k > 1:
                corner(g, x, 1 - y, 1).start()

    def core_step(g, d):
        @pl.when(z == d)
        def _():
            store(g).wait()
            corner(g, 1 - x, 1 - y, 0).wait_recv()
            if groups[g].k > 1:
                corner(g, 1 - x, 1 - y, 1).wait_recv()
            to_core(g, c).start()

    def finish():
        for g, d in units:
            to_twin(g, d).wait_send()
            for copy in first_moves(g, d) + [second_move(g, d)]:
                copy.wait_send()
            for zz in range(ZN):
                if d == zz:
                    continue

                @pl.when(z == zz)
                def _():
                    (to_down(g, d, zz) if d < zz else to_up(g, d, zz)).wait_send()

            @pl.when(z == d)
            def _():
                to_core(g, 1 - c).wait_recv()
                share_across(g).wait_send()
                share_beside(g).wait_send()
                corner(g, 1 - x, y, 0).wait_send()
                if groups[g].k > 1:
                    corner(g, x, 1 - y, 1).wait_send()
                to_core(g, c).wait_send()

    count = len(units)
    stages = [(0, twin_step), (SKEW, first_step), (2 * SKEW, second_step)]
    stages += [((2 + s) * SKEW, functools.partial(line_step, s=s)) for s in range(ZN)]
    stages += [((2 + ZN) * SKEW, corner_step), ((3 + ZN) * SKEW, core_step)]

    def steps():
        for g, d in units:
            to_twin(g, d).start()
            if ORDER.index(d) < 2:
                load(g, d).start()
        yield True
        for t in range(count + stages[-1][0]):
            for delay, step in stages:
                if 0 <= t - delay < count:
                    step(*units[t - delay])
                    yield True

    return steps(), finish


def reduce_scratch(groups):
    low = jnp.bfloat16
    buffers = []
    for lead, rows in ((ZN, 4), (2, 4), (ZN, 2), (ZN, 1), (ZN, 1), (1, 1)):
        buffers += [pltpu.VMEM((lead, rows * k) + shape, low) for k, shape in groups]
    dma = pltpu.SemaphoreType.DMA
    n = len(groups)
    return buffers + [dma((n, 2)), dma((n,)), dma((n, 26)), dma((n, 26))]


def take_reduce(place, spec, grads, outs, refs):
    n = len(spec)
    groups = [Group(grads[m], outs[m], base, k) for m, base, k in spec]
    lists = [refs[i * n : (i + 1) * n] for i in range(6)]
    return reduce_steps(place, groups, *lists, *refs[6 * n : 6 * n + 4])


def spread_steps(work, comm, finish):
    for _ in work:
        if comm is not None:
            advance(comm, REDUCE_PACE)
    if comm is not None:
        for _ in comm:
            pass
        finish()


def spec_of(shapes, split):
    spec = []
    for m, shape in enumerate(shapes):
        k = shape[1] // 8
        for base in range(0, k // min(k, split)):
            spec.append((m, base * 8 * min(k, split), min(k, split)))
    return spec


def stream(source, buffer, sems, width_rows, act):
    chunks = source.shape[0]
    per = buffer.shape[1]
    whole, left = chunks // per, chunks % per

    def fetch(i, n):
        return pltpu.make_async_copy(
            source.at[pl.ds(i * per, n)], buffer.at[i % 2, pl.ds(0, n)], sems.at[i % 2]
        )

    def begin():
        fetch(0, per).start()

    def run(low, high):
        def step(i, carry):
            fetch(i, per).wait()

            @pl.when(i + 1 < whole)
            def _():
                fetch(i + 1, per).start()

            if left:

                @pl.when(i + 1 == whole)
                def _():
                    fetch(whole, left).start()

            act(pl.multiple_of(i * per * 16, per * 16), per * 16, buffer[i % 2].reshape(per * 16, -1))
            return carry

        if low < min(high, whole):
            lax.fori_loop(low, min(high, whole), step, 0)
        if high > whole and left:
            fetch(whole, left).wait()
            act(whole * per * 16, left * 16, buffer[whole % 2, :left].reshape(left * 16, -1))

    return begin, run, whole + (1 if left else 0)


def each(low, high, size):
    return [(at, min(at + size, high)) for at in range(low, high, size)]


def mlp_work(layer, ins, outs, refs):
    grad_in, middle_in, slope_in, normed_in, activated_in, gain, w_out, w_up, w_down = ins
    g_middle_out, g_branch_out, g_attended_out, dw_up, dw_down, gb_down, gb_up, g_gain, g_shift, gb_out = outs
    (
        grad, middle, g_norm, slope, g_mlp, g_branch, g_att, nm, turned,
        narrow, broad, act_tiles, down_tiles, up_tiles, load_sem, narrow_sem, broad_sem, act_sem, down_sem, up_sem,
    ) = refs
    width = grad.shape[1]
    ff = slope.shape[1]
    loads = [
        pltpu.make_async_copy(a, b, load_sem.at[i])
        for i, (a, b) in enumerate(((grad_in, grad), (middle_in, middle), (slope_in, slope), (normed_in, nm)))
    ]
    begin(loads)

    def down_act(start, size, rows):
        cols = pl.ds(start, size)
        g = (dot_nt(g_mlp[...], rows) * slope[:, cols].astype(jnp.float32)).astype(jnp.bfloat16)
        slope[:, cols] = g
        gb_up[:, cols] = jnp.sum(g.astype(jnp.float32), axis=0, keepdims=True)

    def up_act(start, size, rows):
        g_norm[:, pl.ds(start, size)] = dot_nt(slope[...], rows)

    def out_act(start, size, rows):
        g_att[:, pl.ds(start, size)] = dot_nt(g_branch[...], rows).astype(jnp.bfloat16)

    down_begin, down_run, down_n = stream(w_down.at[layer], narrow, narrow_sem, 0, down_act)
    up_begin, up_run, up_n = stream(w_up.at[layer], broad, broad_sem, 0, up_act)
    out_begin, out_run, out_n = stream(w_out.at[layer], narrow, narrow_sem, 0, out_act)
    down_begin()
    up_begin()
    loads[0].wait()
    g_mlp[...] = grad[...].astype(jnp.bfloat16)
    gb_down[...] = jnp.sum(g_mlp[...].astype(jnp.float32), axis=0, keepdims=True)
    loads[2].wait()
    yield
    for low, high in each(0, down_n, 4):
        down_run(low, high)
        yield
    out_begin()
    for low, high in each(0, up_n, 2):
        up_run(low, high)
        yield
    loads[1].wait()
    norm_back(middle, g_norm, grad, gain[...], grad, g_gain, g_shift, g_branch)
    saves = [pltpu.make_async_copy(grad, g_middle_out, load_sem.at[0]), pltpu.make_async_copy(g_branch, g_branch_out, load_sem.at[1])]
    begin(saves)
    gb_out[...] = jnp.sum(g_branch[...].astype(jnp.float32), axis=0, keepdims=True)
    yield
    out_run(0, out_n)
    saves.append(pltpu.make_async_copy(g_att, g_attended_out, load_sem.at[2]))
    begin(saves[2:])
    loads[3].wait()
    turned[...] = nm[...].T
    yield

    tile = act_tiles.shape[2]

    def bring_act(i, n):
        return pltpu.make_async_copy(
            activated_in.at[:, pl.ds(pl.multiple_of(i * tile, tile), n)], act_tiles.at[i % 2, :, pl.ds(0, n)], act_sem.at[i % 2]
        )

    def send_down(i, n):
        return pltpu.make_async_copy(
            down_tiles.at[i % 2, pl.ds(0, n // 16)], dw_down.at[pl.ds(i * (tile // 16), n // 16)], down_sem.at[i % 2]
        )

    whole, left = ff // tile, ff % tile
    bring_act(0, tile).start()

    def down_grad(i, carry):
        bring_act(i, tile).wait()

        @pl.when(i + 1 < whole)
        def _():
            bring_act(i + 1, tile).start()

        if left:

            @pl.when(i + 1 == whole)
            def _():
                bring_act(whole, left).start()

        @pl.when(i >= 2)
        def _():
            send_down(i - 2, tile).wait()

        out = dot_tn(act_tiles[i % 2], g_mlp[...]).astype(jnp.bfloat16)
        down_tiles[i % 2] = out.reshape(tile // 16, 16, width)
        send_down(i, tile).start()
        return carry

    for low, high in each(0, whole, 2):
        lax.fori_loop(low, high, down_grad, 0)
        yield
    if left:
        bring_act(whole, left).wait()
        send_down(whole - 2, tile).wait()
        out = dot_tn(act_tiles[whole % 2, :, :left], g_mlp[...]).astype(jnp.bfloat16)
        down_tiles[whole % 2, : left // 16] = out.reshape(left // 16, 16, width)
        send_down(whole, left).start()
        yield

    step = up_tiles.shape[3]

    def send_up(i):
        return pltpu.make_async_copy(
            up_tiles.at[i % 2], dw_up.at[:, :, pl.ds(pl.multiple_of(i * step, step), step)], up_sem.at[i % 2]
        )

    def up_grad(i, carry):
        @pl.when(i >= 2)
        def _():
            send_up(i - 2).wait()

        out = product(turned[...], slope[:, pl.ds(pl.multiple_of(i * step, step), step)]).astype(jnp.bfloat16)
        up_tiles[i % 2] = out.reshape(width // 16, 16, step)
        send_up(i).start()
        return carry

    for low, high in each(0, ff // step, 4):
        lax.fori_loop(low, high, up_grad, 0)
        yield
    send_up(ff // step - 2).wait()
    send_up(ff // step - 1).wait()
    send_down(whole - 1, tile).wait()
    if left:
        send_down(whole, left).wait()
    else:
        send_down(whole - 2, tile).wait()
    end(saves)


def mlp_refs(rows, width, ff):
    low = jnp.bfloat16
    dma = pltpu.SemaphoreType.DMA
    return (
        [pltpu.VMEM((rows, width), jnp.float32)] * 3
        + [pltpu.VMEM((rows, ff), low)]
        + [pltpu.VMEM((rows, width), low)] * 4
        + [
            pltpu.VMEM((width, rows), low),
            pltpu.VMEM((2, 16, 16, width), low),
            pltpu.VMEM((2, 16, 16, ff), low),
            pltpu.VMEM((2, rows, 512), low),
            pltpu.VMEM((2, 32, 16, width), low),
            pltpu.VMEM((2, width // 16, 16, BLOCK), low),
            dma((4,)), dma((2,)), dma((2,)), dma((2,)), dma((2,)), dma((2,)),
        ]
    )


def attend_work(layer, place, ins, outs, refs):
    q_in, g_att_in, lse_in, mask_in, keys_in, values_in, x_in, g_middle_in, normed_in, attended_in, g_branch_in, gain, w_qkv = ins
    g_x_out, dw_qkv, dw_out, gb_q, gb_v, g_gain, g_shift = outs
    (
        q, g_att, lse, mask, keys, values, g_q, g_k, g_v, g_nat, got, xs, grad, g_norm, g_proj, turned,
        tall, tiles_qkv, tiles_out, load_sem, tall_sem, qkv_sem, out_sem, swap_send, swap_recv,
    ) = refs
    c, twin = place[3], place[6]
    width = xs.shape[1]
    pairs = (
        (q_in, q), (g_att_in, g_att), (lse_in, lse), (mask_in, mask), (keys_in, keys), (values_in, values),
        (x_in, xs), (g_middle_in, grad),
    )
    loads = [pltpu.make_async_copy(a, b, load_sem.at[i]) for i, (a, b) in enumerate(pairs)]
    begin(loads)

    def norm_act(start, size, rows):
        g_norm[:, pl.ds(start, size)] = dot_nt(g_proj[...], rows)

    tall_begin, tall_run, tall_n = stream(w_qkv.at[layer], tall, tall_sem, 0, norm_act)
    tall_begin()
    end(loads[:6])
    yield

    def slab(start, size, head):
        cols = pl.ds(start, size)
        g_k[...] = jnp.zeros_like(g_k)
        g_v[...] = jnp.zeros_like(g_v)
        lanes = slice(0, size)
        for variant in range(2):

            @pl.when(c == variant)
            def _():
                for row, high in RANGES[variant]:
                    rows = slice(row, row + BLOCK)
                    qs, gs = q[rows, cols], g_att[rows, cols]
                    ks, vs = keys[:high, cols], values[:high, cols]
                    parts = []
                    for j in range(size // HEAD_DIM):
                        q_j, g_j = of_head(qs, j), of_head(gs, j)
                        s = dot_nt(ks, q_j) + mask[:high, rows]
                        p = jnp.exp(s - lse[pl.ds(head + j, 1), rows])
                        g_p = p * dot_nt(vs, g_j)
                        inner = jnp.sum(g_p, axis=0, keepdims=True)
                        g_s = (g_p - p * inner).astype(jnp.bfloat16)
                        g_v[:high, lanes] += product(p.astype(jnp.bfloat16), g_j)
                        g_k[:high, lanes] += product(g_s, q_j)
                        parts.append(dot_tn(ks, g_s)[j * HEAD_DIM : (j + 1) * HEAD_DIM])
                    out = jnp.concatenate(parts, axis=0) if len(parts) > 1 else parts[0]
                    g_q[rows, cols] = out.T.astype(jnp.bfloat16) * QUERY_SCALE

        g_nat[0, :, cols] = g_k[:, lanes].astype(jnp.bfloat16)
        g_nat[1, :, cols] = g_v[:, lanes].astype(jnp.bfloat16)

    slab_count = width // (2 * HEAD_DIM) + 1
    for first, last in each(0, slab_count, 2):
        over_slabs(width, slab, first, last)
        yield

    def spot(who, block):
        at = ((2 * who) if block == 0 else (3 - 2 * who)) * BLOCK
        return pl.ds(pl.multiple_of(at, BLOCK), BLOCK)

    swaps = [
        pltpu.make_async_remote_copy(
            src_ref=g_nat.at[i, spot(1 - c, block)], dst_ref=got.at[i, pl.ds(block * BLOCK, BLOCK)],
            send_sem=swap_send.at[i, block], recv_sem=swap_recv.at[i, block], device_id=twin, device_id_type=MESH,
        )
        for i in range(2)
        for block in range(2)
    ]
    begin(swaps)
    more = [
        pltpu.make_async_copy(attended_in, q, load_sem.at[0]),
        pltpu.make_async_copy(g_branch_in, g_att, load_sem.at[1]),
    ]
    begin(more)
    g_proj[:, :width] = g_q[...]
    gb_q[...] = jnp.sum(g_q[...].astype(jnp.float32), axis=0, keepdims=True)
    yield
    end(more)
    turned[...] = q[...].T
    rows = tiles_out.shape[1] * 16

    def row_grad(right, tiles_ref, sem, target, i):
        def act(start, size):
            cols = pl.ds(start, size)
            out = product(turned[pl.ds(i * rows, rows), :], right[:, cols]).astype(jnp.bfloat16)
            tiles_ref[i % 2, :, :, cols] = out.reshape(rows // 16, 16, size)

        if i >= 2:
            row_send(tiles_ref, sem, target, i - 2).wait()
        tiles_between(0, right.shape[1], BLOCK, act)
        row_send(tiles_ref, sem, target, i).start()

    def row_send(tiles_ref, sem, target, i):
        return pltpu.make_async_copy(tiles_ref.at[i % 2], target.at[pl.ds(i * (rows // 16), rows // 16)], sem.at[i % 2])

    for i in range(ZN):
        row_grad(g_att, tiles_out, out_sem, dw_out, i)
    yield
    after = pltpu.make_async_copy(normed_in, q, load_sem.at[0])
    after.start()
    for copy in swaps:
        copy.wait_recv()
    for block in range(2):
        part = slice(block * BLOCK, (block + 1) * BLOCK)
        g_proj[part, width : 2 * width] = g_nat[0, spot(c, block), :] + got[0, part, :]
        values_part = g_nat[1, spot(c, block), :] + got[1, part, :]
        g_proj[part, 2 * width :] = values_part
        total = jnp.sum(values_part.astype(jnp.float32), axis=0, keepdims=True)
        gb_v[...] = total if block == 0 else gb_v[...] + total
    yield
    for low, high in each(0, tall_n, 2):
        tall_run(low, high)
        yield
    end(loads[6:])
    norm_back(xs, g_norm, grad, gain[...], grad, g_gain, g_shift)
    save = pltpu.make_async_copy(grad, g_x_out, load_sem.at[1])
    save.start()
    after.wait()
    turned[...] = q[...].T
    yield
    for i in range(ZN):
        row_grad(g_proj, tiles_qkv, qkv_sem, dw_qkv, i)
        yield
    for i in (ZN - 2, ZN - 1):
        row_send(tiles_out, out_sem, dw_out, i).wait()
        row_send(tiles_qkv, qkv_sem, dw_qkv, i).wait()
    for copy in swaps:
        copy.wait_send()
    save.wait()


def attend_refs(rows, width):
    low = jnp.bfloat16
    dma = pltpu.SemaphoreType.DMA
    share = width // 16 // ZN
    return [
        pltpu.VMEM((rows, width), low),
        pltpu.VMEM((rows, width), low),
        pltpu.VMEM((HEAD_ROWS, rows), jnp.float32),
        pltpu.VMEM((2 * rows, rows), jnp.float32),
        pltpu.VMEM((2 * rows, width), low),
        pltpu.VMEM((2 * rows, width), low),
        pltpu.VMEM((rows, width), low),
        pltpu.VMEM((2 * rows, 2 * HEAD_DIM), jnp.float32),
        pltpu.VMEM((2 * rows, 2 * HEAD_DIM), jnp.float32),
        pltpu.VMEM((2, 2 * rows, width), low),
        pltpu.VMEM((2, rows, width), low),
        pltpu.VMEM((rows, width), jnp.float32),
        pltpu.VMEM((rows, width), jnp.float32),
        pltpu.VMEM((rows, width), jnp.float32),
        pltpu.VMEM((rows, 3 * width), low),
        pltpu.VMEM((width, rows), low),
        pltpu.VMEM((2, 16, 16, 3 * width), low),
        pltpu.VMEM((2, share, 16, 3 * width), low),
        pltpu.VMEM((2, share, 16, width), low),
        dma((8,)), dma((2,)), dma((2,)), dma((2,)), dma((2, 2)), dma((2, 2)),
    ]


def mlp_kernel(layer, grad, kept, gain, fulls, grads, spec):
    rows, width = grad.shape
    ff = kept["slope"].shape[1]
    low = jnp.bfloat16
    ins = [grad, kept["middle"], kept["slope"], kept["normed_mlp"], kept["activated"], gain, fulls[1], fulls[2], fulls[3]]
    work_out = [
        shaped((rows, width)),
        shaped((rows, width), low),
        shaped((rows, width), low),
        shaped((width // 16, 16, ff), low),
        shaped((ff // 16, 16, width), low),
    ] + [shaped((1, n)) for n in (width, ff, width, width, width)]
    work_refs = mlp_refs(rows, width, ff)
    n, extra = len(work_out), len(grads)
    in_specs = anywhere(5) + whole(1) + anywhere(3 + extra)

    def body(*refs):
        i = len(ins) + extra
        outs, more = refs[i : i + n], refs[i + n : i + n + extra]
        rest = refs[i + n + extra :]
        comm = finish = None
        if extra:
            place = neighbours()
            greet(*[place[j] for j in (2, 3, 0, 4, 5, 6)], None, *place[7:])
            comm, finish = take_reduce(place, spec, refs[len(ins) : i], more, rest[len(work_refs) :])
        work = mlp_work(layer, refs[: len(ins)], outs, rest[: len(work_refs)])
        spread_steps(work, comm, finish)

    settings = dict(collective_id=100 + layer, has_side_effects=True) if extra else {}
    outs = pl.pallas_call(
        body,
        out_shape=work_out + [shaped(g.shape[1:], low) for g in grads],
        in_specs=in_specs,
        out_specs=anywhere(5) + whole(5) + anywhere(extra),
        scratch_shapes=work_refs + (reduce_scratch([(k, grads[m].shape[2:]) for m, _, k in spec]) if extra else []),
        compiler_params=pltpu.CompilerParams(vmem_limit_bytes=VMEM_LIMIT, **settings),
        name="mlp_back",
    )(*ins, *grads)
    return outs[:n], outs[n:]


def attend_kernel(layer, kept, mask, g_att, g_middle, g_branch, gain, fulls, grads, spec):
    rows, width = g_middle.shape
    low = jnp.bfloat16
    ins = [
        kept["q"], g_att, kept["lse"], mask, kept["keys"], kept["values"], kept["x"], g_middle,
        kept["normed_attn"], kept["attended"], g_branch, gain, fulls[0],
    ]
    work_out = [
        shaped((rows, width)),
        shaped((width // 16, 16, 3 * width), low),
        shaped((width // 16, 16, width), low),
    ] + [shaped((1, width))] * 4
    work_refs = attend_refs(rows, width)
    n, extra = len(work_out), len(grads)

    def body(*refs):
        i = len(ins) + extra
        outs, more = refs[i : i + n], refs[i + n : i + n + extra]
        rest = refs[i + n + extra :]
        place = neighbours()
        greet(*[place[j] for j in (2, 3, 0, 4, 5, 6)], None, *place[7:])
        comm, finish = take_reduce(place, spec, refs[len(ins) : i], more, rest[len(work_refs) :])
        work = attend_work(layer, place, refs[: len(ins)], outs, rest[: len(work_refs)])
        spread_steps(work, comm, finish)

    outs = pl.pallas_call(
        body,
        out_shape=work_out + [shaped(g.shape[1:], low) for g in grads],
        in_specs=anywhere(11) + whole(1) + anywhere(1 + extra),
        out_specs=anywhere(3) + whole(4) + anywhere(extra),
        scratch_shapes=work_refs + reduce_scratch([(k, grads[m].shape[2:]) for m, _, k in spec]),
        compiler_params=pltpu.CompilerParams(collective_id=200 + layer, has_side_effects=True, vmem_limit_bytes=VMEM_LIMIT),
        name="attend_back",
    )(*ins, *grads)
    return outs[:n], outs[n:]


def reduce_kernel(grads, spec):
    extra = len(grads)

    def body(*refs):
        place = neighbours()
        greet(*[place[j] for j in (2, 3, 0, 4, 5, 6)], None, *place[7:])
        comm, finish = take_reduce(place, spec, refs[:extra], refs[extra : 2 * extra], refs[2 * extra :])
        spread_steps((), comm, finish)

    return pl.pallas_call(
        body,
        out_shape=[shaped(g.shape[1:], g.dtype) for g in grads],
        in_specs=anywhere(extra),
        out_specs=anywhere(extra),
        scratch_shapes=reduce_scratch([(k, grads[m].shape[2:]) for m, _, k in spec]),
        compiler_params=pltpu.CompilerParams(collective_id=2, has_side_effects=True, vmem_limit_bytes=VMEM_LIMIT),
        name="reduce_grads",
    )(*grads)


VECTORS = (0, 1, 3, 4, 6, 7, 8, 12, 10)
MATRICES = (2, 5, 9, 11)


def wide_of(weight_grads, vector_grads):
    width = weight_grads[0].shape[3]

    def pieces(g):
        left = g[:, g.shape[1] // 8 * 8 :]
        parts = left.shape[3] // width
        return jnp.swapaxes(left.reshape(ZN, left.shape[1], 16, parts, width), 2, 3).reshape(ZN, -1, 16, width)

    vectors = jnp.concatenate([g.reshape(ZN, -1) for g in vector_grads], axis=1).astype(jnp.bfloat16)
    vectors = vectors.reshape(ZN, 1, -1, width)
    vectors = jnp.pad(vectors, ((0, 0), (0, 0), (0, 16 - vectors.shape[2]), (0, 0)))
    wide = jnp.concatenate([pieces(g) for g in weight_grads] + [vectors], axis=1)
    return jnp.pad(wide, ((0, 0), (0, -wide.shape[1] % 8), (0, 0), (0, 0)))


def rows_from(sums, wide, at):
    n, _, columns = sums.shape
    left = n % 8
    parts = columns // wide.shape[2]
    tail = wide[at : at + left * parts].reshape(left, parts, 16, -1)
    tail = jnp.swapaxes(tail, 1, 2).reshape(left * 16, columns)
    rows = jnp.concatenate([sums[: n - left].reshape(-1, columns), tail], axis=0)
    return rows.astype(jnp.float32), at + left * parts


def on_cores(tokens, segments, grad_out, *params):
    rows, width = tokens.shape[1:]
    layers = params[0].shape[0]
    weights = [params[i].reshape(layers, -1, 16, params[i].shape[2]) for i in MATRICES]
    vectors = jnp.concatenate([params[i].reshape(layers, -1, params[0].shape[1]) for i in VECTORS], axis=1)
    vectors = jnp.pad(vectors, ((0, 0), (0, 16 - vectors.shape[1]), (0, 0)))[:, None]
    fulls, result, grads_here, mask, vector_rows, saved = forward(
        tokens[0], grad_out[0], segments, vectors, weights
    )
    fulls = [full.reshape(layers, -1, 16, full.shape[4]) for full in fulls]
    result = from_cores(result)[None]
    grad = grads_here.astype(jnp.float32)
    reduced = [None] * layers
    waiting, waiting_spec = [], []
    for layer in reversed(range(layers)):
        kept = saved[layer]
        attn_gain, mlp_gain = vector_rows[layer, 0:1], vector_rows[layer, 5:6]
        (g_middle, g_branch, g_att, dw_up, dw_down, gb_down, gb_up, gm_gain, gm_shift, gb_out), sums = mlp_kernel(
            layer, grad, kept, mlp_gain, fulls, waiting, waiting_spec
        )
        if waiting:
            reduced[layer + 1].extend(sums)
        dw_down = dw_down.reshape(ZN, -1, 16, width)
        down_spec = spec_of([dw_down.shape], 2)
        (grad, dw_qkv, dw_out, gb_q, gb_v, ga_gain, ga_shift), sums = attend_kernel(
            layer, kept, mask, g_att, g_middle, g_branch, attn_gain, fulls, [dw_down], down_spec
        )
        reduced[layer] = list(sums)
        waiting = [dw.reshape(ZN, -1, 16, dw.shape[2]) for dw in (dw_up, dw_out, dw_qkv)]
        vector_grads = (ga_gain, ga_shift, gb_q, gb_v, gb_out, gm_gain, gm_shift, gb_down, gb_up)
        waiting.append(wide_of([dw_down] + waiting, vector_grads))
        waiting_spec = spec_of([w.shape for w in waiting], 2)
    reduced[0].extend(reduce_kernel(waiting, waiting_spec))
    final = []
    for layer in range(layers):
        down, up, out, qkv, wide = reduced[layer]
        entry = [None] * 13
        at = 0
        for i, sums in ((11, down), (9, up), (5, out), (2, qkv)):
            entry[i], at = rows_from(sums, wide, at)
        flat = wide[at].reshape(-1).astype(jnp.float32)
        at = 0
        for i in VECTORS:
            n = params[i].shape[1]
            entry[i] = flat[at : at + n]
            at += n
        final.append(entry)
    stacked = tuple((jnp.stack([entry[member] for entry in final]) for member in range(13)))
    return (result, from_cores(grad.astype(jnp.bfloat16))[None]) + stacked


def on_device(
    tokens,
    segments,
    grad_out,
    attn_gain,
    attn_shift,
    w_qkv,
    b_query,
    b_value,
    w_out,
    b_out,
    mlp_gain,
    mlp_shift,
    w_up,
    b_up,
    w_down,
    b_down,
):
    seg_own = segments[0]
    seg_all = lax.all_gather(seg_own, "seq", axis=0, tiled=True)
    offset = lax.axis_index("seq") * seg_own.shape[0]
    visible = visible_mask(seg_own, seg_all, offset)
    layer_count = attn_gain.shape[0]
    resid = tokens[0].astype(jnp.float32)
    kept_weights = []
    stored_list = []
    for layer_index in range(layer_count):
        gathered = gather_layer(
            layer_index,
            attn_gain,
            attn_shift,
            w_qkv,
            b_query,
            b_value,
            w_out,
            b_out,
            mlp_gain,
            mlp_shift,
            w_up,
            b_up,
            w_down,
            b_down,
        )
        resid, stored = forward_layer(resid, gathered, visible, Halves())
        kept_weights.append(gathered)
        stored_list.append(stored)
    result = resid.astype(jnp.bfloat16)[None]
    grad_resid = grad_out[0].astype(jnp.float32)
    reduced = [None] * layer_count
    for layer_index in reversed(range(layer_count)):
        gathered = gather_again(
            layer_index,
            attn_gain,
            attn_shift,
            w_qkv,
            b_query,
            b_value,
            w_out,
            b_out,
            mlp_gain,
            mlp_shift,
            w_up,
            b_up,
            w_down,
            b_down,
        )
        grad_resid, gradients = backward_layer(
            grad_resid, stored_list[layer_index], gathered, visible, Halves()
        )
        reduced[layer_index] = reduce_grads(gradients)
    stacked = tuple((jnp.stack([entry[member] for entry in reduced]) for member in range(13)))
    return (result, grad_resid.astype(jnp.bfloat16)[None]) + stacked


def solution(mesh):
    fits = (mesh.shape["seq"], mesh.shape["fsdp"], mesh.shape["rep"]) == (2, ZN, 4)
    return jax.shard_map(
        on_cores if fits else on_device,
        mesh=mesh,
        in_specs=(
            P(("fsdp", "rep"), "seq", None),
            P(("fsdp", "rep"), "seq"),
            P(("fsdp", "rep"), "seq", None),
            P(None, "fsdp"),
            P(None, "fsdp"),
            P(None, "fsdp", None),
            P(None, "fsdp"),
            P(None, "fsdp"),
            P(None, "fsdp", None),
            P(None, "fsdp"),
            P(None, "fsdp"),
            P(None, "fsdp"),
            P(None, "fsdp", None),
            P(None, "fsdp"),
            P(None, "fsdp", None),
            P(None, "fsdp"),
        ),
        out_specs=(
            P(("fsdp", "rep"), "seq", None),
            P(("fsdp", "rep"), "seq", None),
            P(None, "fsdp"),
            P(None, "fsdp"),
            P(None, "fsdp", None),
            P(None, "fsdp"),
            P(None, "fsdp"),
            P(None, "fsdp", None),
            P(None, "fsdp"),
            P(None, "fsdp"),
            P(None, "fsdp"),
            P(None, "fsdp", None),
            P(None, "fsdp"),
            P(None, "fsdp", None),
            P(None, "fsdp"),
        ),
        check_vma=False,
    )
```

```python
import functools
import math

import jax
import jax.numpy as jnp
from jax import lax
from jax.experimental import pallas as pl
from jax.experimental.pallas import tpu as pltpu
from jax.sharding import PartitionSpec as P

HEAD_DIM = 64
MESH = pl.DeviceIdType.MESH


NORM_EPSILON = 1e-05
MASKED = -1e30


def layer_norm(inputs, gain, bias_term):
    center = inputs - jnp.mean(inputs, axis=-1, keepdims=True)
    spread = jnp.mean(center * center, axis=-1, keepdims=True)
    return center * lax.rsqrt(spread + NORM_EPSILON) * gain + bias_term


def gelu_tanh(inputs):
    return jax.nn.gelu(inputs, approximate=True)


def product(left, right):
    return jnp.dot(left, right, preferred_element_type=jnp.float32)


def inner_rows(left, right):
    return lax.dot_general(
        left, right, (((0,), (0,)), ((), ())), preferred_element_type=jnp.float32
    )


def outer_cols(left, right):
    return lax.dot_general(
        left, right, (((1,), (1,)), ((), ())), preferred_element_type=jnp.float32
    )


def column_sum(values_low):
    return jnp.sum(values_low.astype(jnp.float32), axis=0)


def visible_mask(seg_own, seg_all, offset):
    row_pos = offset + lax.iota(jnp.int32, seg_own.shape[0])
    col_pos = lax.iota(jnp.int32, seg_all.shape[0])
    return (seg_own[:, None] == seg_all[None, :]) & (row_pos[:, None] >= col_pos[None, :])


def head_scores(queries, keys_all, visible, head_count):
    query_heads = queries.reshape(queries.shape[0], head_count, HEAD_DIM)
    key_heads = keys_all.reshape(keys_all.shape[0], head_count, HEAD_DIM)
    scores = jnp.einsum("thd,shd->hts", query_heads, key_heads, preferred_element_type=jnp.float32)
    return jnp.where(visible[None], scores, MASKED)


def gather_layer(
    layer_index,
    attn_gain,
    attn_shift,
    w_qkv,
    b_query,
    b_value,
    w_out,
    b_out,
    mlp_gain,
    mlp_shift,
    w_up,
    b_up,
    w_down,
    b_down,
):
    return (
        lax.all_gather(attn_gain[layer_index], "fsdp", axis=0, tiled=True),
        lax.all_gather(attn_shift[layer_index], "fsdp", axis=0, tiled=True),
        lax.all_gather(w_qkv[layer_index], "fsdp", axis=0, tiled=True),
        lax.all_gather(b_query[layer_index], "fsdp", axis=0, tiled=True),
        lax.all_gather(b_value[layer_index], "fsdp", axis=0, tiled=True),
        lax.all_gather(w_out[layer_index], "fsdp", axis=0, tiled=True),
        lax.all_gather(b_out[layer_index], "fsdp", axis=0, tiled=True),
        lax.all_gather(mlp_gain[layer_index], "fsdp", axis=0, tiled=True),
        lax.all_gather(mlp_shift[layer_index], "fsdp", axis=0, tiled=True),
        lax.all_gather(w_up[layer_index], "fsdp", axis=0, tiled=True),
        lax.all_gather(b_up[layer_index], "fsdp", axis=0, tiled=True),
        lax.all_gather(w_down[layer_index], "fsdp", axis=0, tiled=True),
        lax.all_gather(b_down[layer_index], "fsdp", axis=0, tiled=True),
    )


def gather_again(
    layer_index,
    attn_gain,
    attn_shift,
    w_qkv,
    b_query,
    b_value,
    w_out,
    b_out,
    mlp_gain,
    mlp_shift,
    w_up,
    b_up,
    w_down,
    b_down,
):
    return (
        lax.all_gather(attn_gain[layer_index], "fsdp", axis=0, tiled=True),
        lax.all_gather(attn_shift[layer_index], "fsdp", axis=0, tiled=True),
        lax.all_gather(w_qkv[layer_index], "fsdp", axis=0, tiled=True),
        lax.all_gather(b_query[layer_index], "fsdp", axis=0, tiled=True),
        lax.all_gather(b_value[layer_index], "fsdp", axis=0, tiled=True),
        lax.all_gather(w_out[layer_index], "fsdp", axis=0, tiled=True),
        lax.all_gather(b_out[layer_index], "fsdp", axis=0, tiled=True),
        lax.all_gather(mlp_gain[layer_index], "fsdp", axis=0, tiled=True),
        lax.all_gather(mlp_shift[layer_index], "fsdp", axis=0, tiled=True),
        lax.all_gather(w_up[layer_index], "fsdp", axis=0, tiled=True),
        lax.all_gather(b_up[layer_index], "fsdp", axis=0, tiled=True),
        lax.all_gather(w_down[layer_index], "fsdp", axis=0, tiled=True),
        lax.all_gather(b_down[layer_index], "fsdp", axis=0, tiled=True),
    )


def forward_layer(resid, gathered, visible, pool):
    (
        attn_gain,
        attn_shift,
        w_qkv,
        b_query,
        b_value,
        w_out,
        b_out,
        mlp_gain,
        mlp_shift,
        w_up,
        b_up,
        w_down,
        b_down,
    ) = gathered
    model_width = resid.shape[1]
    head_count = model_width // HEAD_DIM
    query_scale = 1.0 / math.sqrt(HEAD_DIM)
    normed_attn = layer_norm(
        resid, attn_gain.astype(jnp.float32), attn_shift.astype(jnp.float32)
    ).astype(jnp.bfloat16)
    proj_all = product(normed_attn, w_qkv)
    queries = ((proj_all[:, :model_width] + b_query.astype(jnp.float32)) * query_scale).astype(
        jnp.bfloat16
    )
    keys_own = proj_all[:, model_width : 2 * model_width].astype(jnp.bfloat16)
    values_own = (proj_all[:, 2 * model_width :] + b_value.astype(jnp.float32)).astype(jnp.bfloat16)
    keys_all, values_all = pool.spread(keys_own), pool.spread(values_own)
    scores = head_scores(queries, keys_all, visible, head_count)
    row_max = jnp.max(scores, axis=-1, keepdims=True)
    exponent = jnp.exp(scores - row_max)
    row_sum = jnp.sum(exponent, axis=-1, keepdims=True)
    weights_soft = (exponent / row_sum).astype(jnp.bfloat16)
    log_total = row_max + jnp.log(row_sum)
    value_heads = values_all.reshape(values_all.shape[0], head_count, HEAD_DIM)
    attended = jnp.einsum(
        "hts,shd->thd", weights_soft, value_heads, preferred_element_type=jnp.float32
    )
    attended = attended.reshape(resid.shape[0], model_width).astype(jnp.bfloat16)
    middle = resid + product(attended, w_out) + b_out.astype(jnp.float32)
    normed_mlp = layer_norm(
        middle, mlp_gain.astype(jnp.float32), mlp_shift.astype(jnp.float32)
    ).astype(jnp.bfloat16)
    pre_act = product(normed_mlp, w_up) + b_up.astype(jnp.float32)
    activated = gelu_tanh(pre_act).astype(jnp.bfloat16)
    output = middle + product(activated, w_down) + b_down.astype(jnp.float32)
    stored = (
        resid,
        normed_attn,
        queries,
        keys_all,
        values_all,
        log_total,
        attended,
        middle,
        normed_mlp,
        pre_act,
        activated,
    )
    return (output, stored)


def backward_layer(grad_next, stored, gathered, visible, pool):
    (
        attn_gain,
        attn_shift,
        w_qkv,
        b_query,
        b_value,
        w_out,
        b_out,
        mlp_gain,
        mlp_shift,
        w_up,
        b_up,
        w_down,
        b_down,
    ) = gathered
    (
        resid,
        normed_attn,
        queries,
        keys_all,
        values_all,
        log_total,
        attended,
        middle,
        normed_mlp,
        pre_act,
        activated,
    ) = stored
    model_width = resid.shape[1]
    tok_rows = resid.shape[0]
    key_rows = keys_all.shape[0]
    head_count = model_width // HEAD_DIM
    query_scale = 1.0 / math.sqrt(HEAD_DIM)
    grad_mlp = grad_next.astype(jnp.bfloat16)
    grad_b_down = column_sum(grad_mlp)
    grad_w_down = inner_rows(activated, grad_mlp)
    grad_act = outer_cols(grad_mlp, w_down)
    gelu_value, gelu_pull = jax.vjp(gelu_tanh, pre_act)
    grad_pre = gelu_pull(grad_act)[0].astype(jnp.bfloat16)
    grad_b_up = column_sum(grad_pre)
    grad_w_up = inner_rows(normed_mlp, grad_pre)
    grad_nm = outer_cols(grad_pre, w_up)
    norm_value, norm_pull = jax.vjp(
        layer_norm, middle, mlp_gain.astype(jnp.float32), mlp_shift.astype(jnp.float32)
    )
    grad_middle, grad_mlp_gain, grad_mlp_shift = norm_pull(grad_nm)
    grad_middle = grad_middle + grad_next
    grad_branch = grad_middle.astype(jnp.bfloat16)
    grad_b_out = column_sum(grad_branch)
    grad_w_out = inner_rows(attended, grad_branch)
    grad_attended = outer_cols(grad_branch, w_out).astype(jnp.bfloat16)
    scores = head_scores(queries, keys_all, visible, head_count)
    weights_full = jnp.exp(scores - log_total)
    weights_soft = weights_full.astype(jnp.bfloat16)
    grad_heads = grad_attended.reshape(tok_rows, head_count, HEAD_DIM)
    query_heads = queries.reshape(tok_rows, head_count, HEAD_DIM)
    key_heads = keys_all.reshape(key_rows, head_count, HEAD_DIM)
    value_heads = values_all.reshape(key_rows, head_count, HEAD_DIM)
    grad_value_terms = jnp.einsum(
        "hts,thd->shd", weights_soft, grad_heads, preferred_element_type=jnp.float32
    )
    grad_probs = jnp.einsum(
        "thd,shd->hts", grad_heads, value_heads, preferred_element_type=jnp.float32
    )
    inner_sum = jnp.sum(weights_full * grad_probs, axis=-1, keepdims=True)
    grad_scores = (weights_full * (grad_probs - inner_sum)).astype(jnp.bfloat16)
    grad_queries = jnp.einsum(
        "hts,shd->thd", grad_scores, key_heads, preferred_element_type=jnp.float32
    )
    grad_queries = grad_queries.reshape(tok_rows, model_width).astype(jnp.bfloat16) * query_scale
    grad_key_terms = jnp.einsum(
        "hts,thd->shd", grad_scores, query_heads, preferred_element_type=jnp.float32
    )
    grad_keys = pool.collect(grad_key_terms.reshape(key_rows, model_width).astype(jnp.bfloat16))
    grad_values = pool.collect(grad_value_terms.reshape(key_rows, model_width).astype(jnp.bfloat16))
    grad_keys = grad_keys.astype(jnp.bfloat16)
    grad_values = grad_values.astype(jnp.bfloat16)
    grad_proj = jnp.concatenate([grad_queries, grad_keys, grad_values], axis=1)
    grad_b_query = column_sum(grad_queries)
    grad_b_value = column_sum(grad_values)
    grad_w_qkv = inner_rows(normed_attn, grad_proj)
    grad_na = outer_cols(grad_proj, w_qkv)
    first_value, first_pull = jax.vjp(
        layer_norm, resid, attn_gain.astype(jnp.float32), attn_shift.astype(jnp.float32)
    )
    grad_resid, grad_attn_gain, grad_attn_shift = first_pull(grad_na)
    grad_resid = grad_resid + grad_middle
    gradients = (
        grad_attn_gain,
        grad_attn_shift,
        grad_w_qkv,
        grad_b_query,
        grad_b_value,
        grad_w_out,
        grad_b_out,
        grad_mlp_gain,
        grad_mlp_shift,
        grad_w_up,
        grad_b_up,
        grad_w_down,
        grad_b_down,
    )
    return (grad_resid, gradients)


def reduce_grads(gradients):
    shares = (
        lax.psum_scatter(gradients[0], ("fsdp", "rep"), scatter_dimension=0, tiled=True),
        lax.psum_scatter(gradients[1], ("fsdp", "rep"), scatter_dimension=0, tiled=True),
        lax.psum_scatter(gradients[2], ("fsdp", "rep"), scatter_dimension=0, tiled=True),
        lax.psum_scatter(gradients[3], ("fsdp", "rep"), scatter_dimension=0, tiled=True),
        lax.psum_scatter(gradients[4], ("fsdp", "rep"), scatter_dimension=0, tiled=True),
        lax.psum_scatter(gradients[5], ("fsdp", "rep"), scatter_dimension=0, tiled=True),
        lax.psum_scatter(gradients[6], ("fsdp", "rep"), scatter_dimension=0, tiled=True),
        lax.psum_scatter(gradients[7], ("fsdp", "rep"), scatter_dimension=0, tiled=True),
        lax.psum_scatter(gradients[8], ("fsdp", "rep"), scatter_dimension=0, tiled=True),
        lax.psum_scatter(gradients[9], ("fsdp", "rep"), scatter_dimension=0, tiled=True),
        lax.psum_scatter(gradients[10], ("fsdp", "rep"), scatter_dimension=0, tiled=True),
        lax.psum_scatter(gradients[11], ("fsdp", "rep"), scatter_dimension=0, tiled=True),
        lax.psum_scatter(gradients[12], ("fsdp", "rep"), scatter_dimension=0, tiled=True),
    )
    shares = (
        lax.psum(shares[0].astype(jnp.bfloat16), "seq").astype(jnp.float32),
        lax.psum(shares[1].astype(jnp.bfloat16), "seq").astype(jnp.float32),
        lax.psum(shares[2].astype(jnp.bfloat16), "seq").astype(jnp.float32),
        lax.psum(shares[3].astype(jnp.bfloat16), "seq").astype(jnp.float32),
        lax.psum(shares[4].astype(jnp.bfloat16), "seq").astype(jnp.float32),
        lax.psum(shares[5].astype(jnp.bfloat16), "seq").astype(jnp.float32),
        lax.psum(shares[6].astype(jnp.bfloat16), "seq").astype(jnp.float32),
        lax.psum(shares[7].astype(jnp.bfloat16), "seq").astype(jnp.float32),
        lax.psum(shares[8].astype(jnp.bfloat16), "seq").astype(jnp.float32),
        lax.psum(shares[9].astype(jnp.bfloat16), "seq").astype(jnp.float32),
        lax.psum(shares[10].astype(jnp.bfloat16), "seq").astype(jnp.float32),
        lax.psum(shares[11].astype(jnp.bfloat16), "seq").astype(jnp.float32),
        lax.psum(shares[12].astype(jnp.bfloat16), "seq").astype(jnp.float32),
    )
    return (
        lax.all_gather(shares[0].astype(jnp.bfloat16), "rep", axis=0, tiled=True).astype(
            jnp.float32
        ),
        lax.all_gather(shares[1].astype(jnp.bfloat16), "rep", axis=0, tiled=True).astype(
            jnp.float32
        ),
        lax.all_gather(shares[2].astype(jnp.bfloat16), "rep", axis=0, tiled=True).astype(
            jnp.float32
        ),
        lax.all_gather(shares[3].astype(jnp.bfloat16), "rep", axis=0, tiled=True).astype(
            jnp.float32
        ),
        lax.all_gather(shares[4].astype(jnp.bfloat16), "rep", axis=0, tiled=True).astype(
            jnp.float32
        ),
        lax.all_gather(shares[5].astype(jnp.bfloat16), "rep", axis=0, tiled=True).astype(
            jnp.float32
        ),
        lax.all_gather(shares[6].astype(jnp.bfloat16), "rep", axis=0, tiled=True).astype(
            jnp.float32
        ),
        lax.all_gather(shares[7].astype(jnp.bfloat16), "rep", axis=0, tiled=True).astype(
            jnp.float32
        ),
        lax.all_gather(shares[8].astype(jnp.bfloat16), "rep", axis=0, tiled=True).astype(
            jnp.float32
        ),
        lax.all_gather(shares[9].astype(jnp.bfloat16), "rep", axis=0, tiled=True).astype(
            jnp.float32
        ),
        lax.all_gather(shares[10].astype(jnp.bfloat16), "rep", axis=0, tiled=True).astype(
            jnp.float32
        ),
        lax.all_gather(shares[11].astype(jnp.bfloat16), "rep", axis=0, tiled=True).astype(
            jnp.float32
        ),
        lax.all_gather(shares[12].astype(jnp.bfloat16), "rep", axis=0, tiled=True).astype(
            jnp.float32
        ),
    )


class Halves:
    def spread(self, rows):
        return lax.all_gather(rows, "seq", axis=0, tiled=True)

    def collect(self, rows):
        return lax.psum_scatter(rows, "seq", scatter_dimension=0, tiled=True)


ZN = 4


def neighbours():
    x, z, r = lax.axis_index("seq"), lax.axis_index("fsdp"), lax.axis_index("rep")
    y, c = r // 2, r % 2
    across = (1 - x, z, r)
    beside = (x, z, (1 - y) * 2 + c)
    twin = (x, z, y * 2 + (1 - c))
    up = (x, (z + 1) % ZN, r)
    down = (x, (z + ZN - 1) % ZN, r)
    return x, y, z, c, across, beside, twin, up, down


def greet(z, c, x, across, beside, twin, diag, up, down):
    barrier = pltpu.get_barrier_semaphore()

    def tell(device):
        pl.semaphore_signal(barrier, inc=1, device_id=device, device_id_type=MESH)

    for device in (across, beside, twin):
        tell(device)
    if diag is not None:

        @pl.when(c != x)
        def _():
            tell(diag)

    @pl.when(z < ZN - 1)
    def _():
        tell(up)

    @pl.when(z > 0)
    def _():
        tell(down)

    extra = 0 if diag is None else (x + c) % 2
    pl.semaphore_wait(barrier, 3 + extra + (z + ZN - 1) // ZN + (2 * ZN - 2 - z) // ZN)


GELU_A = math.sqrt(2.0 / math.pi)
GELU_B = 0.044715
QUERY_SCALE = 1.0 / math.sqrt(HEAD_DIM)
HEAD_ROWS = 24
PACE = 2
REDUCE_PACE = 6
SKEW = 2
AHEAD = 6


NT = (((1,), (1,)), ((), ()))
TN = (((0,), (0,)), ((), ()))
BLOCK = 256
RANGES = (((0, 256), (256, 1024)), ((0, 768), (256, 512)))
VMEM_LIMIT = 60 << 20


def dot_nt(left, right):
    return lax.dot_general(left, right, NT, preferred_element_type=jnp.float32)


def dot_tn(left, right):
    return lax.dot_general(left, right, TN, preferred_element_type=jnp.float32)


def tiles(width, tile, act):
    whole = width // tile

    def step(i, carry):
        act(pl.multiple_of(i * tile, tile), tile)
        return carry

    lax.fori_loop(0, whole, step, 0)
    if width % tile:
        act(whole * tile, width % tile)


def tiles_between(low, high, tile, act):
    def step(i, carry):
        act(pl.multiple_of(i * tile, tile), tile)
        return carry

    if low // tile < high // tile:
        lax.fori_loop(low // tile, high // tile, step, 0)
    if high % tile:
        act(high // tile * tile, high % tile)


def norm_parts(rows):
    center = rows - jnp.mean(rows, axis=1, keepdims=True)
    scale = lax.rsqrt(jnp.mean(center * center, axis=1, keepdims=True) + NORM_EPSILON)
    return center * scale, scale


def norm_into(source, gain, shift, target):
    def act(start, size):
        rows = pl.ds(start, size)
        unit, _ = norm_parts(source[rows, :])
        target[rows, :] = (unit * gain + shift).astype(target.dtype)

    tiles(source.shape[0], 64, act)


def norm_back(source, grad, extra, gain, target, gain_grad, shift_grad, low=None):
    gain_grad[...] = jnp.zeros_like(gain_grad)
    shift_grad[...] = jnp.zeros_like(shift_grad)

    def act(start, size):
        rows = pl.ds(start, size)
        unit, scale = norm_parts(source[rows, :])
        g = grad[rows, :]
        q = g * gain
        mean_q = jnp.mean(q, axis=1, keepdims=True)
        mean_qn = jnp.mean(q * unit, axis=1, keepdims=True)
        out = extra[rows, :] + (q - mean_q - unit * mean_qn) * scale
        target[rows, :] = out
        if low is not None:
            low[rows, :] = out.astype(low.dtype)
        gain_grad[...] += jnp.sum(g * unit, axis=0, keepdims=True)
        shift_grad[...] += jnp.sum(g, axis=0, keepdims=True)

    tiles(source.shape[0], 64, act)


def whole(count):
    return [pl.BlockSpec(memory_space=pltpu.VMEM)] * count


def anywhere(count):
    return [pl.BlockSpec(memory_space=pl.ANY)] * count


def shaped(shape, dtype=jnp.float32):
    return jax.ShapeDtypeStruct(shape, dtype)


def params():
    return pltpu.CompilerParams(vmem_limit_bytes=VMEM_LIMIT)


def of_head(values, j):
    if values.shape[1] == HEAD_DIM:
        return values
    lane = lax.broadcasted_iota(jnp.int32, values.shape, 1)
    return jnp.where(lane // HEAD_DIM == j, values, jnp.zeros_like(values))


ZA, ZR, GX, GY, GD1, GD2, GC = range(7)
ROW = dict(attn_gain=0, attn_shift=1, b_query=2, b_value=3, b_out=4, mlp_gain=5, mlp_shift=6, b_down=7)
SAVED = ("x", "normed_attn", "q", "keys", "values", "attended", "lse", "middle", "normed_mlp", "slope", "activated")


def advance(steps, count):
    for _ in range(count):
        if next(steps, None) is None:
            return


def weight_moves(ins, outs, send_sem, recv_sem, place):
    x, y, z, c, across, beside, twin, up, down = place
    m_count = len(ins) - 1
    layers = ins[0].shape[0]
    units = [(layer, m) for layer in range(layers) for m in range(m_count + 1)]
    index = {unit: i for i, unit in enumerate(units)}

    def depth(u):
        return ins[u[1]].shape[1] // 8

    def owned(u, px, py, half=None):
        k = depth(u)
        base = (c * 4 + px * 2 + py) * k
        if half is None:
            return pl.ds(base, k)
        return pl.ds(base + half * (k // 2), k // 2)

    def rest(u):
        n = ins[u[1]].shape[1]
        return pl.ds(n // 8 * 8, n % 8)

    def slab(u, core):
        return pl.ds(core * 4 * depth(u), 4 * depth(u))

    def move(u, zz, rows, device, kind, source=None, send_kind=None):
        target = outs[u[1]].at[u[0], zz, rows]
        return pltpu.make_async_remote_copy(
            src_ref=target if source is None else source,
            dst_ref=target,
            send_sem=send_sem.at[index[u], zz, kind if send_kind is None else send_kind],
            recv_sem=recv_sem.at[index[u], zz, kind],
            device_id=device,
            device_id_type=MESH,
        )

    def own_sends(u, act):
        source = ins[u[1]].at[u[0]]

        def along(device, first):
            if depth(u):
                act(move(u, z, owned(u, x, y), device, ZA, source.at[owned(u, x, y)], first))
            act(move(u, z, rest(u), device, ZR, source.at[rest(u)], first + 1))

        @pl.when(z < ZN - 1)
        def _():
            along(up, 0)

        @pl.when(z > 0)
        def _():
            along(down, 2)

    def both(s, act):
        @pl.when(z >= s)
        def _():
            act(z - s, 0)

        @pl.when(z + s <= ZN - 1)
        def _():
            act(z + s, 1)

    def onward(u, zz, d, act):
        def along(device):
            if depth(u):
                act(move(u, zz, owned(u, x, y), device, ZA))
            act(move(u, zz, rest(u), device, ZR))

        if d == 0:

            @pl.when(z < ZN - 1)
            def _():
                along(up)

        else:

            @pl.when(z > 0)
            def _():
                along(down)

    def line_step(u, s):
        def act(zz, d):
            if depth(u):
                move(u, zz, owned(u, x, y), across, ZA).wait_recv()
            move(u, zz, rest(u), across, ZR).wait_recv()
            onward(u, zz, d, lambda copy: copy.start())
            if depth(u):
                move(u, zz, owned(u, x, y), across, GX).start()
                move(u, zz, owned(u, x, y), beside, GY).start()

        both(s, act)

    def plane_step(u, s):
        def act(zz, d):
            move(u, zz, owned(u, 1 - x, y), across, GX).wait_recv()
            move(u, zz, owned(u, 1 - x, y, 0), beside, GD1).start()
            move(u, zz, owned(u, x, 1 - y), beside, GY).wait_recv()
            move(u, zz, owned(u, x, 1 - y, 1), across, GD2).start()

        both(s, act)

    def corner_step(u, s):
        def act(zz, d):
            move(u, zz, owned(u, 1 - x, 1 - y, 0), beside, GD1).wait_recv()
            move(u, zz, owned(u, 1 - x, 1 - y, 1), across, GD2).wait_recv()
            move(u, zz, slab(u, c), twin, GC).start()

        both(s, act)

    def arrive(u):
        for s in range(1, ZN):
            both(s, lambda zz, d: move(u, zz, slab(u, 1 - c), twin, GC).wait_recv())

    def finish(u):
        own_sends(u, lambda copy: copy.wait_send())
        for s in range(1, ZN):

            def act(zz, d):
                onward(u, zz, d, lambda copy: copy.wait_send())
                if depth(u):
                    move(u, zz, owned(u, x, y), across, GX).wait_send()
                    move(u, zz, owned(u, x, y), beside, GY).wait_send()
                    move(u, zz, owned(u, 1 - x, y, 0), beside, GD1).wait_send()
                    move(u, zz, owned(u, x, 1 - y, 1), across, GD2).wait_send()
                    move(u, zz, slab(u, c), twin, GC).wait_send()

            both(s, act)

    matrices = [u for u in units if u[1] < m_count]
    vectors = [u for u in units if u[1] == m_count]
    count = len(matrices)

    def steps():
        for u in vectors + matrices[:2]:
            own_sends(u, lambda copy: copy.start())
        for s in range(1, ZN):
            for u in vectors:
                line_step(u, s)
        yield ("vectors",)
        for t in range(count + 4):
            if t + 2 < count:
                own_sends(matrices[t + 2], lambda copy: copy.start())
            for s in range(1, ZN):
                if 0 <= t + 1 - s < count:
                    line_step(matrices[t + 1 - s], s)
                    yield ("line",)
            for s in range(1, ZN):
                if 0 <= t - s < count:
                    plane_step(matrices[t - s], s)
                    yield ("plane",)
            for s in range(1, ZN):
                if 0 <= t - 1 - s < count:
                    corner_step(matrices[t - 1 - s], s)
                    yield ("here", matrices[t - 1 - s]) if s == ZN - 1 else ("corner",)

    return steps, arrive, lambda: [finish(u) for u in units]


def attend(core, q, keys, values, mask, attended, lse, first, last):
    def slab(start, size, head):
        cols = pl.ds(start, size)
        for variant in range(2):

            @pl.when(core == variant)
            def _():
                for row, high in RANGES[variant]:
                    rows = slice(row, row + BLOCK)
                    qs = q[rows, cols]
                    ks, vs = keys[:high, cols], values[:high, cols]
                    parts = []
                    for j in range(size // HEAD_DIM):
                        s = dot_nt(ks, of_head(qs, j)) + mask[:high, rows]
                        top = jnp.max(s, axis=0, keepdims=True)
                        e = jnp.exp(s - top)
                        total = jnp.sum(e, axis=0, keepdims=True)
                        lse[pl.ds(head + j, 1), rows] = top + jnp.log(total)
                        out = dot_tn(vs, e.astype(jnp.bfloat16)) * (1.0 / total)
                        parts.append(out[j * HEAD_DIM : (j + 1) * HEAD_DIM])
                    out = jnp.concatenate(parts, axis=0) if len(parts) > 1 else parts[0]
                    attended[rows, cols] = out.T.astype(jnp.bfloat16)

    over_slabs(q.shape[1], slab, first, last)


def over_slabs(width, slab, first, last):
    pair = 2 * HEAD_DIM
    full = width // pair

    def step(i, carry):
        slab(pl.multiple_of(i * pair, pair), pair, i * 2)
        return carry

    if first < min(last, full):
        lax.fori_loop(first, min(last, full), step, 0)
    if last > full and width % pair:
        slab(full * pair, HEAD_DIM, full * 2)


def forward_body(
    tokens, grads, segs, vectors, w_qkv, w_out, w_up, w_down,
    full_qkv, full_out, full_up, full_down, full_vectors, result, grads_here, mask_out, rows_out, *rest_refs,
):
    layers = w_qkv.shape[0]
    saved = [dict(zip(SAVED, rest_refs[i * len(SAVED) : (i + 1) * len(SAVED)])) for i in range(layers)]
    (
        wq, wo, wu, wd, xs, tok, na, nm, q, keys, values, mask, att, middle, slope, act_buf, lse,
        vecs, rows, b_up, b_proj, seg_nat, seg_row,
        send_sem, recv_sem, load_sem, own_sem, save_sem, kv_send, kv_recv, in_send, in_recv, in_local, free_sem,
    ) = rest_refs[layers * len(SAVED) :]
    place = neighbours()
    x, y, z, c, across, beside, twin, up, down = place
    diag = (1 - x, z, y * 2 + (1 - c))
    here = c == x
    greet(z, c, x, across, beside, twin, diag, up, down)
    width = xs.shape[1]
    half = BLOCK
    parts = [w_qkv, w_out, w_up, w_down]
    fulls = [full_qkv, full_out, full_up, full_down]
    buffers = [wq, wo, wu, wd]
    steps, arrive, finish = weight_moves(parts + [vectors], fulls + [full_vectors], send_sem, recv_sem, place)

    def in_move(i, source, target, device):
        return pltpu.make_async_remote_copy(
            src_ref=source, dst_ref=target, send_sem=in_send.at[i], recv_sem=in_recv.at[i],
            device_id=device, device_id_type=MESH,
        )

    top, low = pl.ds(0, half), pl.ds(half, half)

    def in_copies(i, source, target):
        stay = pltpu.make_async_copy(source.at[top], target.at[top], in_local.at[i])
        return (
            stay,
            in_move(2 * i + 1, source.at[low], target.at[low], twin),
            in_move(2 * i, source.at[top], target.at[top], diag),
            in_move(2 * i + 1, source.at[low], target.at[low], across),
        )

    tok_copies = in_copies(0, tokens, tok)
    grad_copies = in_copies(1, grads, grads_here)
    seg_stay = pltpu.make_async_copy(segs, seg_nat.at[x], in_local.at[2])
    seg_twin = in_move(4, segs, seg_nat.at[x], twin)
    seg_across = in_move(4, segs, seg_nat.at[x], across)
    seg_diag = pltpu.make_async_remote_copy(
        src_ref=segs, dst_ref=seg_nat.at[x], send_sem=in_send.at[5], recv_sem=in_recv.at[5],
        device_id=diag, device_id_type=MESH,
    )

    @pl.when(here)
    def _():
        for copy in (seg_stay, seg_twin, tok_copies[0], tok_copies[1], grad_copies[0], grad_copies[1]):
            copy.start()

    @pl.when(jnp.logical_not(here))
    def _():
        for copy in (seg_across, seg_diag, tok_copies[2], tok_copies[3], grad_copies[2], grad_copies[3]):
            copy.start()

    def wait_in(copies):
        @pl.when(here)
        def _():
            copies[0].wait()
            copies[1].wait_recv()

        @pl.when(jnp.logical_not(here))
        def _():
            copies[2].wait_recv()
            copies[3].wait_recv()

    def wait_segs():
        @pl.when(here)
        def _():
            seg_stay.wait()
            seg_across.wait_recv()

        @pl.when(jnp.logical_not(here))
        def _():
            seg_twin.wait_recv()
            seg_diag.wait_recv()

    def finish_in():
        @pl.when(here)
        def _():
            grad_copies[0].wait()
            grad_copies[1].wait_recv()
            for copy in (seg_twin, tok_copies[1], grad_copies[1]):
                copy.wait_send()

        @pl.when(jnp.logical_not(here))
        def _():
            grad_copies[2].wait_recv()
            grad_copies[3].wait_recv()
            for copy in (seg_across, seg_diag, tok_copies[2], tok_copies[3], grad_copies[2], grad_copies[3]):
                copy.wait_send()

    comm = steps()
    seen = set()
    loaded = {}
    done_with = set()

    def tick(count=1):
        for _ in range(count):
            label = next(comm, None)
            if label is None:
                return False
            seen.add(label)
            if label[0] == "here":
                fetch_ready()
        return True

    def loads(u):
        layer, m = u
        n = parts[m].shape[1]
        copies = [pltpu.make_async_copy(parts[m].at[layer], buffers[m].at[pl.ds(z * n, n)], load_sem.at[m, 0])]
        for s in range(1, ZN):
            zz = (z + s) % ZN
            copies.append(
                pltpu.make_async_copy(fulls[m].at[layer, zz], buffers[m].at[pl.ds(zz * n, n)], load_sem.at[m, s])
            )
        return copies

    def fetch_ready(upto=None):
        for layer in range(layers):
            for m in range(len(parts)):
                u = (layer, m)
                if u in loaded or ("here", u) not in seen:
                    continue
                if layer and (layer - 1, m) not in done_with:
                    continue
                following = (layer, m + 1) if m + 1 < len(parts) else (layer + 1, 0)
                if u != upto and following[0] < layers and ("here", following) not in seen:
                    continue
                arrive(u)
                if layer:
                    own_rows((layer - 1, m)).wait()
                for copy in loads(u):
                    copy.start()
                loaded[u] = True

    def own_rows(u):
        layer, m = u
        n = parts[m].shape[1]
        return pltpu.make_async_copy(buffers[m].at[pl.ds(z * n, n)], fulls[m].at[layer, z], own_sem.at[layer, m])

    def need(u):
        while ("here", u) not in seen:
            if not tick():
                break
        fetch_ready(u)
        for copy in loads(u):
            copy.wait()
        own_rows(u).start()

    pending = []

    def save(layer, name, buffer):
        copy = pltpu.make_async_copy(buffer, saved[layer][name], save_sem.at[layer, SAVED.index(name)])
        copy.start()
        pending.append(copy)

    def settle():
        while pending:
            pending.pop().wait()

    def row(layer, name):
        return rows[layer, pl.ds(ROW[name], 1), :]

    def make_mask():
        wait_segs()
        joined = jnp.concatenate([seg_nat[0], seg_nat[1]], axis=1).astype(jnp.float32)
        seg_row[...] = jnp.broadcast_to(joined, seg_row.shape)
        column = seg_row[...].T[:, :1]
        for block in range(2):
            base = ((2 * c) if block == 0 else (3 - 2 * c)) * BLOCK
            own = seg_row[0:1, pl.ds(pl.multiple_of(base, BLOCK), BLOCK)]
            spot = lax.broadcasted_iota(jnp.int32, (mask.shape[0], BLOCK), 0)
            mine = lax.broadcasted_iota(jnp.int32, (mask.shape[0], BLOCK), 1) + base
            ok = (column == own) & (spot <= mine)
            mask[:, block * BLOCK : (block + 1) * BLOCK] = jnp.where(ok, 0.0, MASKED).astype(jnp.float32)
        copy = pltpu.make_async_copy(mask, mask_out, save_sem.at[0, len(SAVED)])
        copy.start()
        pending.append(copy)

    def make_rows(layer):
        copies = [
            pltpu.make_async_copy(vectors.at[layer, 0], vecs.at[z], load_sem.at[4, 0])
        ] + [
            pltpu.make_async_copy(full_vectors.at[layer, (z + s) % ZN, 0], vecs.at[(z + s) % ZN], load_sem.at[4, s])
            for s in range(1, ZN)
        ]
        for copy in copies:
            copy.start()
        for copy in copies:
            copy.wait()
        share = vecs.shape[2]
        b_proj[layer, 0:1, :] = jnp.zeros((1, b_proj.shape[2]), jnp.float32)
        for zz in range(ZN):
            block = vecs[zz].astype(jnp.float32)
            rows[layer, 0:8, zz * share : (zz + 1) * share] = block[0:8]
            for name, at in (("b_query", 0), ("b_value", 2 * width)):
                b_proj[layer, 0:1, at + zz * share : at + (zz + 1) * share] = block[ROW[name] : ROW[name] + 1]
            for j in range(ZN):
                at = (zz * ZN + j) * share
                b_up[layer, 0:1, at : at + share] = block[8 + j : 9 + j]

    def swap_moves(layer):
        moves = []
        for i, ref in enumerate((keys, values)):
            for block in range(2):
                at = ((2 * c) if block == 0 else (3 - 2 * c)) * BLOCK
                spot = ref.at[pl.ds(pl.multiple_of(at, BLOCK), BLOCK)]
                moves.append(
                    pltpu.make_async_remote_copy(
                        src_ref=spot, dst_ref=spot, send_sem=kv_send.at[layer, i, block],
                        recv_sem=kv_recv.at[layer, i, block], device_id=twin, device_id_type=MESH,
                    )
                )
        return moves

    def swap_waits(layer):
        moves = []
        for i, ref in enumerate((keys, values)):
            for block in range(2):
                at = ((2 - 2 * c) if block == 0 else (1 + 2 * c)) * BLOCK
                spot = ref.at[pl.ds(pl.multiple_of(at, BLOCK), BLOCK)]
                moves.append(
                    pltpu.make_async_remote_copy(
                        src_ref=spot, dst_ref=spot, send_sem=kv_send.at[layer, i, block],
                        recv_sem=kv_recv.at[layer, i, block], device_id=twin, device_id_type=MESH,
                    )
                )
        return moves

    def matrix(buffer, cols):
        return buffer[:, :, cols].reshape(-1, cols.size)

    def compute(layer):
        if layer == 0:
            make_rows(0)
            make_rows(1)
            for i in range(layers):
                copy = pltpu.make_async_copy(rows.at[i], rows_out.at[i], save_sem.at[i, len(SAVED) + 1])
                copy.start()
                pending.append(copy)
            wait_in(tok_copies)
            xs[...] = tok[...].astype(jnp.float32)
            make_mask()
        else:
            settle()
        save(layer, "x", xs)
        norm_into(xs, row(layer, "attn_gain"), row(layer, "attn_shift"), na)
        save(layer, "normed_attn", na)
        yield
        need((layer, 0))
        total = wq.shape[2]

        for low_at in range(0, total, 4 * BLOCK):
            high_at = min(low_at + 4 * BLOCK, total)
            tiles_between(low_at, high_at, BLOCK, lambda start, size: project_tile(layer, start, size))
            yield
        done_with.add((layer, 0))
        q[...] = slope[:, :width]
        if layer:
            pl.semaphore_wait(free_sem, 1)
        for block in range(2):
            at = ((2 * c) if block == 0 else (3 - 2 * c)) * BLOCK
            spot = pl.ds(pl.multiple_of(at, BLOCK), BLOCK)
            source = slice(block * BLOCK, (block + 1) * BLOCK)
            keys[spot, :] = slope[source, width : 2 * width]
            values[spot, :] = slope[source, 2 * width : 3 * width]
        for copy in swap_moves(layer):
            copy.start()
        save(layer, "q", q)
        yield
        for copy in swap_waits(layer):
            copy.wait_recv()
        save(layer, "keys", keys)
        save(layer, "values", values)
        for first in range(0, width // (2 * HEAD_DIM) + 1, 4):
            attend(c, q, keys, values, mask, att, lse, first, min(first + 4, width // (2 * HEAD_DIM) + 1))
            yield
        save(layer, "attended", att)
        save(layer, "lse", lse)
        if layer + 1 < layers:
            settle()
            for copy in swap_moves(layer):
                copy.wait_send()
            pl.semaphore_signal(free_sem, inc=1, device_id=twin, device_id_type=MESH)
        need((layer, 1))

        def out_step(start, size):
            cols = pl.ds(start, size)
            middle[:, cols] = xs[:, cols] + product(att[...], matrix(wo, cols)) + rows[layer, pl.ds(ROW["b_out"], 1), cols]

        tiles_between(0, width, BLOCK, out_step)
        done_with.add((layer, 1))
        save(layer, "middle", middle)
        yield
        norm_into(middle, row(layer, "mlp_gain"), row(layer, "mlp_shift"), nm)
        save(layer, "normed_mlp", nm)
        yield
        need((layer, 2))
        settle()

        def up_step(start, size):
            cols = pl.ds(start, size)
            u = product(nm[...], matrix(wu, cols)) + b_up[layer, 0:1, cols]
            square = u * u
            t = jnp.tanh(u * (GELU_A + (GELU_A * GELU_B) * square))
            half_up = 0.5 + 0.5 * t
            act_buf[:, cols] = (u * half_up).astype(jnp.bfloat16)
            slope[:, cols] = (
                half_up + (0.5 * u) * (1.0 - t * t) * (GELU_A + (3.0 * GELU_A * GELU_B) * square)
            ).astype(jnp.bfloat16)

        ff = wu.shape[2]
        for low_at in range(0, ff, 6 * BLOCK):
            tiles_between(low_at, min(low_at + 6 * BLOCK, ff), BLOCK, up_step)
            yield
        done_with.add((layer, 2))
        save(layer, "slope", slope)
        save(layer, "activated", act_buf)
        need((layer, 3))

        def down_step(start, size):
            cols = pl.ds(start, size)
            xs[:, cols] = middle[:, cols] + product(act_buf[...], matrix(wd, cols)) + rows[layer, pl.ds(ROW["b_down"], 1), cols]

        for low_at in range(0, width, 2 * BLOCK):
            tiles_between(low_at, min(low_at + 2 * BLOCK, width), BLOCK, down_step)
            yield
        done_with.add((layer, 3))

    def project_tile(layer, start, size):
        cols = pl.ds(start, size)
        out = product(na[...], matrix(wq, cols))
        slope[:, cols] = ((out + b_proj[layer, 0:1, cols]) * scale_of(start, size)).astype(jnp.bfloat16)

    def scale_of(start, size):
        lane = lax.broadcasted_iota(jnp.int32, (1, size), 1) + start
        return jnp.where(lane < width, QUERY_SCALE, 1.0).astype(jnp.float32)

    tick()
    for layer in range(layers):
        for _ in compute(layer):
            tick(PACE)
    while tick():
        pass
    settle()
    tok[...] = xs[...].astype(jnp.bfloat16)
    out = pltpu.make_async_copy(tok, result, save_sem.at[0, 0])
    out.start()
    for copy in swap_moves(layers - 1):
        copy.wait_send()
    finish_in()
    finish()
    for m in range(len(parts)):
        own_rows((layers - 1, m)).wait()
    out.wait()


def forward(tokens, grads, segs, vectors, weights):
    rows, width = tokens.shape
    low = jnp.bfloat16
    layers = vectors.shape[0]
    ff = weights[2].shape[3]
    units = layers * (len(weights) + 1)
    shapes = dict(
        x=((rows, width), jnp.float32),
        normed_attn=((rows, width), low),
        q=((rows, width), low),
        keys=((2 * rows, width), low),
        values=((2 * rows, width), low),
        attended=((rows, width), low),
        lse=((HEAD_ROWS, rows), jnp.float32),
        middle=((rows, width), jnp.float32),
        normed_mlp=((rows, width), low),
        slope=((rows, ff), low),
        activated=((rows, ff), low),
    )
    out_shape = (
        [shaped((layers, ZN) + w.shape[1:], low) for w in weights]
        + [
            shaped((layers, ZN) + vectors.shape[1:], low),
            shaped((rows, width), low),
            shaped((rows, width), low),
            shaped((2 * rows, rows)),
            shaped((layers, 16, width)),
        ]
        + [shaped(*shapes[name]) for _ in range(layers) for name in SAVED]
    )
    dma = pltpu.SemaphoreType.DMA
    scratch = [pltpu.VMEM((ZN * w.shape[1],) + w.shape[2:], low) for w in weights] + [
        pltpu.VMEM((rows, width), jnp.float32),
        pltpu.VMEM((rows, width), low),
        pltpu.VMEM((rows, width), low),
        pltpu.VMEM((rows, width), low),
        pltpu.VMEM((rows, width), low),
        pltpu.VMEM((2 * rows, width), low),
        pltpu.VMEM((2 * rows, width), low),
        pltpu.VMEM((2 * rows, rows), jnp.float32),
        pltpu.VMEM((rows, width), low),
        pltpu.VMEM((rows, width), jnp.float32),
        pltpu.VMEM((rows, ff), low),
        pltpu.VMEM((rows, ff), low),
        pltpu.VMEM((HEAD_ROWS, rows), jnp.float32),
        pltpu.VMEM((ZN,) + vectors.shape[2:], low),
        pltpu.VMEM((layers, 16, width), jnp.float32),
        pltpu.VMEM((layers, 8, ff), jnp.float32),
        pltpu.VMEM((layers, 8, 3 * width), jnp.float32),
        pltpu.VMEM((2, 1, rows), jnp.int32),
        pltpu.VMEM((8, 2 * rows), jnp.float32),
        dma((units, ZN, 7)),
        dma((units, ZN, 7)),
        dma((len(weights) + 1, ZN)),
        dma((layers, len(weights))),
        dma((layers, len(SAVED) + 2)),
        dma((layers, 2, 2)),
        dma((layers, 2, 2)),
        dma((6,)),
        dma((6,)),
        dma((3,)),
        pltpu.SemaphoreType.REGULAR,
    ]
    outs = pl.pallas_call(
        forward_body,
        out_shape=out_shape,
        in_specs=anywhere(4 + len(weights)),
        out_specs=anywhere(len(out_shape)),
        scratch_shapes=scratch,
        compiler_params=pltpu.CompilerParams(collective_id=0, has_side_effects=True, vmem_limit_bytes=VMEM_LIMIT),
        name="forward",
    )(tokens, grads, segs, vectors, *weights)
    count = len(weights)
    fulls, rest = outs[:count], outs[count + 5 :]
    _, result, grads_here, mask, vector_rows = outs[count : count + 5]
    saved = [dict(zip(SAVED, rest[i * len(SAVED) : (i + 1) * len(SAVED)])) for i in range(layers)]
    return fulls, result, grads_here, mask, vector_rows, saved


def begin(copies):
    for copy in copies:
        copy.start()


def end(copies):
    for copy in copies:
        copy.wait()


ORDER = (0, 1, 3, 2)
RC, R1, R2, RZ, RX, RY, RD1, RD2, RCC, R1B, RZX = 0, 4, 8, 12, 16, 17, 18, 19, 20, 21, 25


class Group:
    def __init__(self, grad, out, base, k, ready):
        self.grad, self.out, self.base, self.k, self.ready = grad, out, base, k, ready


def reduce_steps(place, groups, acc, stage, first_in, second_in, line_in, line_extra, load_sem, store_sem, send_sem, recv_sem):
    x, y, z, c, across, beside, twin, up, down = place
    p = x * 2 + y
    units = [(g, d) for g in range(len(groups)) for d in ORDER]

    def move(source, target, g, kind, device):
        return pltpu.make_async_remote_copy(
            src_ref=source, dst_ref=target, send_sem=send_sem.at[g, kind], recv_sem=recv_sem.at[g, kind],
            device_id=device, device_id_type=MESH,
        )

    def half_of(g, d, core):
        group = groups[g]
        return group.grad.at[d, pl.ds(group.base + core * 4 * group.k, 4 * group.k)]

    def to_twin(g, d):
        return move(half_of(g, d, 1 - c), acc[g].at[d], g, RC + d, twin)

    def slot(d):
        return ORDER.index(d) % 2

    def load(g, d):
        return pltpu.make_async_copy(half_of(g, d, c), stage[g].at[slot(d)], load_sem.at[g, slot(d)])

    def add(g, d, at, extra, lead, extra_at, n):
        def step(i, carry):
            acc[g][d, at + i] = acc[g][d, at + i] + extra[lead, extra_at + i]
            return carry

        lax.fori_loop(0, n, step, 0)

    def first_moves(g, d):
        k = groups[g].k
        if d in (0, 3):
            return [move(acc[g].at[d, pl.ds((1 - x) * 2 * k, 2 * k)], first_in[g].at[d], g, R1 + d, across)]
        return [
            move(acc[g].at[d, pl.ds((1 - y) * k, k)], first_in[g].at[d, pl.ds(0, k)], g, R1 + d, beside),
            move(acc[g].at[d, pl.ds((3 - y) * k, k)], first_in[g].at[d, pl.ds(k, k)], g, R1B + d, beside),
        ]

    def second_move(g, d):
        k = groups[g].k
        if d in (0, 3):
            return move(acc[g].at[d, pl.ds((x * 2 + 1 - y) * k, k)], second_in[g].at[d], g, R2 + d, beside)
        return move(acc[g].at[d, pl.ds(((1 - x) * 2 + y) * k, k)], second_in[g].at[d], g, R2 + d, across)

    def twin_step(g, d):
        to_twin(g, d).wait_recv()
        load(g, d).wait()
        add(g, d, 0, stage[g], slot(d), 0, 4 * groups[g].k)
        for copy in first_moves(g, d):
            copy.start()
        later = ORDER.index(d) + 2
        if later < len(ORDER):
            load(g, ORDER[later]).start()

    def first_step(g, d):
        k = groups[g].k
        for copy in first_moves(g, d):
            copy.wait_recv()
        if d in (0, 3):
            add(g, d, x * 2 * k, first_in[g], d, 0, 2 * k)
        else:
            add(g, d, y * k, first_in[g], d, 0, k)
            add(g, d, (2 + y) * k, first_in[g], d, k, k)
        second_move(g, d).start()

    def second_step(g, d):
        second_move(g, d).wait_recv()
        add(g, d, p * groups[g].k, second_in[g], d, 0, groups[g].k)

    def piece(g, d):
        return acc[g].at[d, pl.ds(p * groups[g].k, groups[g].k)]

    def to_down(g, d, zz):
        if d == zz - 1:
            return move(piece(g, d), line_extra[g].at[0], g, RZX, down)
        return move(piece(g, d), line_in[g].at[d], g, RZ + d, down)

    def to_up(g, d, zz):
        return move(piece(g, d), line_in[g].at[d], g, RZ + d, up)

    def rows_of(g, px, py, low=0, n=None):
        group = groups[g]
        return group.out.at[pl.ds(group.base + (c * 4 + px * 2 + py) * group.k + low, group.k if n is None else n)]

    def share_across(g):
        return move(piece(g, z), rows_of(g, x, y), g, RX, across)

    def share_beside(g):
        return move(piece(g, z), rows_of(g, x, y), g, RY, beside)

    def store(g):
        return pltpu.make_async_copy(piece(g, z), rows_of(g, x, y), store_sem.at[g])

    def arrived(g, px, py, kind):
        return move(rows_of(g, px, py), rows_of(g, px, py), g, kind, across)

    def corner(g, px, py, part):
        k = groups[g].k
        low, n = (0, max(k // 2, 1)) if part == 0 else (k // 2, k - k // 2)
        rows = rows_of(g, px, py, low, n)
        return move(rows, rows, g, RD1 if part == 0 else RD2, beside if part == 0 else across)

    def to_core(g, core):
        group = groups[g]
        rows = group.out.at[pl.ds(group.base + core * 4 * group.k, 4 * group.k)]
        return move(rows, rows, g, RCC, twin)

    def line_step(g, d, s):
        k = groups[g].k
        for zz in range(ZN):
            downward = d < zz and zz == ZN - 1 - s
            upward = d > zz and zz == s
            last = d == zz and s == ZN - 1
            if not (downward or upward or last):
                continue

            @pl.when(z == zz)
            def _():
                if downward:
                    if zz < ZN - 1:
                        to_down(g, d, zz + 1).wait_recv()
                        add(g, d, p * k, line_in[g], d, 0, k)
                    to_down(g, d, zz).start()
                if upward:
                    if zz > 0:
                        to_up(g, d, zz - 1).wait_recv()
                        add(g, d, p * k, line_in[g], d, 0, k)
                    to_up(g, d, zz).start()
                if last:
                    if zz > 0:
                        to_up(g, d, zz - 1).wait_recv()
                        add(g, d, p * k, line_in[g], d, 0, k)
                    if zz < ZN - 1:
                        to_down(g, d, zz + 1).wait_recv()
                        add(g, d, p * k, line_extra[g], 0, 0, k)
                    share_across(g).start()
                    share_beside(g).start()
                    store(g).start()

    def corner_step(g, d):
        @pl.when(z == d)
        def _():
            arrived(g, 1 - x, y, RX).wait_recv()
            corner(g, 1 - x, y, 0).start()
            arrived(g, x, 1 - y, RY).wait_recv()
            if groups[g].k > 1:
                corner(g, x, 1 - y, 1).start()

    def core_step(g, d):
        @pl.when(z == d)
        def _():
            store(g).wait()
            corner(g, 1 - x, 1 - y, 0).wait_recv()
            if groups[g].k > 1:
                corner(g, 1 - x, 1 - y, 1).wait_recv()
            to_core(g, c).start()

    def finish():
        for g, d in units:
            to_twin(g, d).wait_send()
            for copy in first_moves(g, d) + [second_move(g, d)]:
                copy.wait_send()
            for zz in range(ZN):
                if d == zz:
                    continue

                @pl.when(z == zz)
                def _():
                    (to_down(g, d, zz) if d < zz else to_up(g, d, zz)).wait_send()

            @pl.when(z == d)
            def _():
                to_core(g, 1 - c).wait_recv()
                share_across(g).wait_send()
                share_beside(g).wait_send()
                corner(g, 1 - x, y, 0).wait_send()
                if groups[g].k > 1:
                    corner(g, x, 1 - y, 1).wait_send()
                to_core(g, c).wait_send()

    count = len(units)
    stages = [(0, twin_step), (SKEW, first_step), (2 * SKEW, second_step)]
    stages += [((2 + s) * SKEW, functools.partial(line_step, s=s)) for s in range(ZN)]
    stages += [((2 + ZN) * SKEW, corner_step), ((3 + ZN) * SKEW, core_step)]

    def steps():
        for t in range(count + stages[-1][0]):
            for g, d in units[AHEAD + t - 1 : AHEAD + t] if t else units[:AHEAD]:
                yield groups[g].ready
                to_twin(g, d).start()
                if ORDER.index(d) < 2:
                    load(g, d).start()
            for delay, step in stages:
                if 0 <= t - delay < count:
                    step(*units[t - delay])
                    yield True

    return steps(), finish


def reduce_scratch(groups):
    low = jnp.bfloat16
    buffers = []
    for lead, rows in ((ZN, 4), (2, 4), (ZN, 2), (ZN, 1), (ZN, 1), (1, 1)):
        buffers += [pltpu.VMEM((lead, rows * k) + shape, low) for k, shape in groups]
    dma = pltpu.SemaphoreType.DMA
    n = len(groups)
    return buffers + [dma((n, 2)), dma((n,)), dma((n, 26)), dma((n, 26))]


def take_reduce(place, spec, grads, outs, refs, made_here=()):
    n = len(spec)
    groups = [Group(grads[m], outs[m], base, k, m if m in made_here else True) for m, base, k in spec]
    lists = [refs[i * n : (i + 1) * n] for i in range(6)]
    return reduce_steps(place, groups, *lists, *refs[6 * n : 6 * n + 4])


def spread_steps(work, comm, finish):
    done = {True}
    blocked = None
    for made in work:
        done.add(made)
        for _ in range(REDUCE_PACE):
            if blocked is not None and blocked not in done:
                break
            blocked = next(comm, True)
    for _ in comm:
        pass
    finish()


def ship_moves(place, source, target, local_sem, send_sem, recv_sem):
    x, y, z, c, across, beside, twin, up, down = place
    diag = (1 - x, z, y * 2 + (1 - c))
    top, low = pl.ds(0, BLOCK), pl.ds(BLOCK, BLOCK)

    def move(i, rows, device):
        return pltpu.make_async_remote_copy(
            src_ref=source.at[rows], dst_ref=target.at[rows], send_sem=send_sem.at[i], recv_sem=recv_sem.at[i],
            device_id=device, device_id_type=MESH,
        )

    stay = pltpu.make_async_copy(source.at[top], target.at[top], local_sem.at[0])

    def start():
        @pl.when(c == x)
        def _():
            stay.start()
            move(1, low, across).start()

        @pl.when(c != x)
        def _():
            move(0, top, diag).start()
            move(1, low, twin).start()

    def wait():
        @pl.when(c == x)
        def _():
            stay.wait()
            move(1, low, across).wait()

        @pl.when(c != x)
        def _():
            move(0, top, diag).wait()
            move(1, low, twin).wait()

    return start, wait


def ship_scratch():
    dma = pltpu.SemaphoreType.DMA
    return [dma((1,)), dma((2,)), dma((2,))]


def meet(ship):
    place = neighbours()
    x, y, z, c, across, beside, twin, up, down = place
    diag = (1 - x, z, y * 2 + (1 - c)) if ship else None
    greet(z, c, x, across, beside, twin, diag, up, down)
    return place


def spec_of(shapes):
    spec = []
    for m, shape in enumerate(shapes):
        k = shape[1] // 8
        split = min(k, 1 if shape[3] > 2048 else 2)
        for base in range(0, k, split):
            spec.append((m, base * 8, split))
    return spec


def stream(source, buffer, sems, width_rows, act):
    chunks = source.shape[0]
    per = buffer.shape[1]
    whole, left = chunks // per, chunks % per

    def fetch(i, n):
        return pltpu.make_async_copy(
            source.at[pl.ds(i * per, n)], buffer.at[i % 2, pl.ds(0, n)], sems.at[i % 2]
        )

    def begin():
        fetch(0, per).start()

    def run(low, high):
        def step(i, carry):
            fetch(i, per).wait()

            @pl.when(i + 1 < whole)
            def _():
                fetch(i + 1, per).start()

            if left:

                @pl.when(i + 1 == whole)
                def _():
                    fetch(whole, left).start()

            act(pl.multiple_of(i * per * 16, per * 16), per * 16, buffer[i % 2].reshape(per * 16, -1))
            return carry

        if low < min(high, whole):
            lax.fori_loop(low, min(high, whole), step, 0)
        if high > whole and left:
            fetch(whole, left).wait()
            act(whole * per * 16, left * 16, buffer[whole % 2, :left].reshape(left * 16, -1))

    return begin, run, whole + (1 if left else 0)


def each(low, high, size):
    return [(at, min(at + size, high)) for at in range(low, high, size)]


def mlp_work(layer, ins, outs, refs, made_down):
    grad_in, middle_in, slope_in, normed_in, activated_in, gain, w_out, w_up, w_down = ins
    g_middle_out, g_branch_out, g_attended_out, dw_up, dw_down, gb_down, gb_up, g_gain, g_shift, gb_out = outs
    (
        grad, middle, g_norm, slope, g_mlp, g_branch, g_att, nm, turned,
        narrow, broad, act_tiles, down_tiles, up_tiles, load_sem, narrow_sem, broad_sem, act_sem, down_sem, up_sem,
    ) = refs
    width = grad.shape[1]
    ff = slope.shape[1]
    loads = [
        pltpu.make_async_copy(a, b, load_sem.at[i])
        for i, (a, b) in enumerate(((grad_in, g_mlp if grad_in.dtype == jnp.bfloat16 else grad), (middle_in, middle), (slope_in, slope), (normed_in, nm)))
    ]
    begin(loads)

    def down_act(start, size, rows):
        cols = pl.ds(start, size)
        g = (dot_nt(g_mlp[...], rows) * slope[:, cols].astype(jnp.float32)).astype(jnp.bfloat16)
        slope[:, cols] = g
        gb_up[:, cols] = jnp.sum(g.astype(jnp.float32), axis=0, keepdims=True)

    def up_act(start, size, rows):
        g_norm[:, pl.ds(start, size)] = dot_nt(slope[...], rows)

    def out_act(start, size, rows):
        g_att[:, pl.ds(start, size)] = dot_nt(g_branch[...], rows).astype(jnp.bfloat16)

    down_begin, down_run, down_n = stream(w_down.at[layer], narrow, narrow_sem, 0, down_act)
    up_begin, up_run, up_n = stream(w_up.at[layer], broad, broad_sem, 0, up_act)
    out_begin, out_run, out_n = stream(w_out.at[layer], narrow, narrow_sem, 0, out_act)
    down_begin()
    up_begin()
    loads[0].wait()
    if grad_in.dtype == jnp.bfloat16:
        grad[...] = g_mlp[...].astype(jnp.float32)
    else:
        g_mlp[...] = grad[...].astype(jnp.bfloat16)
    gb_down[...] = jnp.sum(g_mlp[...].astype(jnp.float32), axis=0, keepdims=True)
    yield
    tile = act_tiles.shape[2]

    def bring_act(i, n):
        return pltpu.make_async_copy(
            activated_in.at[:, pl.ds(pl.multiple_of(i * tile, tile), n)], act_tiles.at[i % 2, :, pl.ds(0, n)], act_sem.at[i % 2]
        )

    def send_down(i, n):
        return pltpu.make_async_copy(
            down_tiles.at[i % 2, pl.ds(0, n // 16)], dw_down.at[pl.ds(i * (tile // 16), n // 16)], down_sem.at[i % 2]
        )

    whole, left = ff // tile, ff % tile
    bring_act(0, tile).start()

    def down_grad(i, carry):
        bring_act(i, tile).wait()

        @pl.when(i + 1 < whole)
        def _():
            bring_act(i + 1, tile).start()

        if left:

            @pl.when(i + 1 == whole)
            def _():
                bring_act(whole, left).start()

        @pl.when(i >= 2)
        def _():
            send_down(i - 2, tile).wait()

        out = dot_tn(act_tiles[i % 2], g_mlp[...]).astype(jnp.bfloat16)
        down_tiles[i % 2] = out.reshape(tile // 16, 16, width)
        send_down(i, tile).start()
        return carry

    for low, high in each(0, whole, 4):
        lax.fori_loop(low, high, down_grad, 0)
        yield
    if left:
        bring_act(whole, left).wait()
        send_down(whole - 2, tile).wait()
        out = dot_tn(act_tiles[whole % 2, :, :left], g_mlp[...]).astype(jnp.bfloat16)
        down_tiles[whole % 2, : left // 16] = out.reshape(left // 16, 16, width)
        send_down(whole, left).start()
    send_down(whole - 1, tile).wait()
    if left:
        send_down(whole, left).wait()
    else:
        send_down(whole - 2, tile).wait()
    yield made_down

    loads[2].wait()
    for low, high in each(0, down_n, 4):
        down_run(low, high)
        yield
    out_begin()
    for low, high in each(0, up_n, 2):
        up_run(low, high)
        yield
    loads[1].wait()
    norm_back(middle, g_norm, grad, gain[...], grad, g_gain, g_shift, g_branch)
    saves = [pltpu.make_async_copy(grad, g_middle_out, load_sem.at[0]), pltpu.make_async_copy(g_branch, g_branch_out, load_sem.at[1])]
    begin(saves)
    gb_out[...] = jnp.sum(g_branch[...].astype(jnp.float32), axis=0, keepdims=True)
    yield
    out_run(0, out_n)
    saves.append(pltpu.make_async_copy(g_att, g_attended_out, load_sem.at[2]))
    begin(saves[2:])
    loads[3].wait()
    turned[...] = nm[...].T
    yield

    step = up_tiles.shape[3]

    def send_up(i):
        return pltpu.make_async_copy(
            up_tiles.at[i % 2], dw_up.at[:, :, pl.ds(pl.multiple_of(i * step, step), step)], up_sem.at[i % 2]
        )

    def up_grad(i, carry):
        @pl.when(i >= 2)
        def _():
            send_up(i - 2).wait()

        out = product(turned[...], slope[:, pl.ds(pl.multiple_of(i * step, step), step)]).astype(jnp.bfloat16)
        up_tiles[i % 2] = out.reshape(width // 16, 16, step)
        send_up(i).start()
        return carry

    for low, high in each(0, ff // step, 4):
        lax.fori_loop(low, high, up_grad, 0)
        yield
    send_up(ff // step - 2).wait()
    send_up(ff // step - 1).wait()
    end(saves)


def mlp_refs(rows, width, ff):
    low = jnp.bfloat16
    dma = pltpu.SemaphoreType.DMA
    return (
        [pltpu.VMEM((rows, width), jnp.float32)] * 3
        + [pltpu.VMEM((rows, ff), low)]
        + [pltpu.VMEM((rows, width), low)] * 4
        + [
            pltpu.VMEM((width, rows), low),
            pltpu.VMEM((2, 16, 16, width), low),
            pltpu.VMEM((2, 16, 16, ff), low),
            pltpu.VMEM((2, rows, 512), low),
            pltpu.VMEM((2, 32, 16, width), low),
            pltpu.VMEM((2, width // 16, 16, BLOCK), low),
            dma((4,)), dma((2,)), dma((2,)), dma((2,)), dma((2,)), dma((2,)),
        ]
    )


def attend_work(layer, place, ins, outs, refs):
    q_in, g_att_in, lse_in, mask_in, keys_in, values_in, x_in, g_middle_in, normed_in, attended_in, g_branch_in, gain, w_qkv = ins
    g_x_out, dw_qkv, dw_out, gb_q, gb_v, g_gain, g_shift = outs
    (
        q, g_att, lse, mask, keys, values, g_q, g_k, g_v, g_nat, got, xs, grad, g_norm, g_proj, turned,
        tall, tiles_qkv, tiles_out, load_sem, tall_sem, qkv_sem, out_sem, swap_send, swap_recv,
    ) = refs
    c, twin = place[3], place[6]
    width = xs.shape[1]
    pairs = (
        (q_in, q), (g_att_in, g_att), (lse_in, lse), (mask_in, mask), (keys_in, keys), (values_in, values),
        (x_in, xs), (g_middle_in, grad),
    )
    loads = [pltpu.make_async_copy(a, b, load_sem.at[i]) for i, (a, b) in enumerate(pairs)]
    begin(loads)

    def norm_act(start, size, rows):
        g_norm[:, pl.ds(start, size)] = dot_nt(g_proj[...], rows)

    tall_begin, tall_run, tall_n = stream(w_qkv.at[layer], tall, tall_sem, 0, norm_act)
    tall_begin()
    end(loads[:6])
    yield

    def slab(start, size, head):
        cols = pl.ds(start, size)
        g_k[...] = jnp.zeros_like(g_k)
        g_v[...] = jnp.zeros_like(g_v)
        lanes = slice(0, size)
        for variant in range(2):

            @pl.when(c == variant)
            def _():
                for row, high in RANGES[variant]:
                    rows = slice(row, row + BLOCK)
                    qs, gs = q[rows, cols], g_att[rows, cols]
                    ks, vs = keys[:high, cols], values[:high, cols]
                    parts = []
                    for j in range(size // HEAD_DIM):
                        q_j, g_j = of_head(qs, j), of_head(gs, j)
                        s = dot_nt(ks, q_j) + mask[:high, rows]
                        p = jnp.exp(s - lse[pl.ds(head + j, 1), rows])
                        g_p = p * dot_nt(vs, g_j)
                        inner = jnp.sum(g_p, axis=0, keepdims=True)
                        g_s = (g_p - p * inner).astype(jnp.bfloat16)
                        g_v[:high, lanes] += product(p.astype(jnp.bfloat16), g_j)
                        g_k[:high, lanes] += product(g_s, q_j)
                        parts.append(dot_tn(ks, g_s)[j * HEAD_DIM : (j + 1) * HEAD_DIM])
                    out = jnp.concatenate(parts, axis=0) if len(parts) > 1 else parts[0]
                    g_q[rows, cols] = out.T.astype(jnp.bfloat16) * QUERY_SCALE

        g_nat[0, :, cols] = g_k[:, lanes].astype(jnp.bfloat16)
        g_nat[1, :, cols] = g_v[:, lanes].astype(jnp.bfloat16)

    slab_count = width // (2 * HEAD_DIM) + 1
    for first, last in each(0, slab_count, 2):
        over_slabs(width, slab, first, last)
        yield

    def spot(who, block):
        at = ((2 * who) if block == 0 else (3 - 2 * who)) * BLOCK
        return pl.ds(pl.multiple_of(at, BLOCK), BLOCK)

    swaps = [
        pltpu.make_async_remote_copy(
            src_ref=g_nat.at[i, spot(1 - c, block)], dst_ref=got.at[i, pl.ds(block * BLOCK, BLOCK)],
            send_sem=swap_send.at[i, block], recv_sem=swap_recv.at[i, block], device_id=twin, device_id_type=MESH,
        )
        for i in range(2)
        for block in range(2)
    ]
    begin(swaps)
    more = [
        pltpu.make_async_copy(attended_in, q, load_sem.at[0]),
        pltpu.make_async_copy(g_branch_in, g_att, load_sem.at[1]),
    ]
    begin(more)
    g_proj[:, :width] = g_q[...]
    gb_q[...] = jnp.sum(g_q[...].astype(jnp.float32), axis=0, keepdims=True)
    yield
    end(more)
    turned[...] = q[...].T
    rows = tiles_out.shape[1] * 16

    def row_grad(right, tiles_ref, sem, target, i):
        def act(start, size):
            cols = pl.ds(start, size)
            out = product(turned[pl.ds(i * rows, rows), :], right[:, cols]).astype(jnp.bfloat16)
            tiles_ref[i % 2, :, :, cols] = out.reshape(rows // 16, 16, size)

        if i >= 2:
            row_send(tiles_ref, sem, target, i - 2).wait()
        tiles_between(0, right.shape[1], BLOCK, act)
        row_send(tiles_ref, sem, target, i).start()

    def row_send(tiles_ref, sem, target, i):
        return pltpu.make_async_copy(tiles_ref.at[i % 2], target.at[pl.ds(i * (rows // 16), rows // 16)], sem.at[i % 2])

    for i in range(ZN):
        row_grad(g_att, tiles_out, out_sem, dw_out, i)
    yield
    after = pltpu.make_async_copy(normed_in, q, load_sem.at[0])
    after.start()
    for copy in swaps:
        copy.wait_recv()
    for block in range(2):
        part = slice(block * BLOCK, (block + 1) * BLOCK)
        g_proj[part, width : 2 * width] = g_nat[0, spot(c, block), :] + got[0, part, :]
        values_part = g_nat[1, spot(c, block), :] + got[1, part, :]
        g_proj[part, 2 * width :] = values_part
        total = jnp.sum(values_part.astype(jnp.float32), axis=0, keepdims=True)
        gb_v[...] = total if block == 0 else gb_v[...] + total
    yield
    for low, high in each(0, tall_n, 2):
        tall_run(low, high)
        yield
    end(loads[6:])
    norm_back(xs, g_norm, grad, gain[...], grad, g_gain, g_shift)
    if g_x_out.dtype == jnp.bfloat16:
        g_att[...] = grad[...].astype(jnp.bfloat16)
        save = pltpu.make_async_copy(g_att, g_x_out, load_sem.at[1])
    else:
        save = pltpu.make_async_copy(grad, g_x_out, load_sem.at[1])
    save.start()
    after.wait()
    turned[...] = q[...].T
    yield
    for i in range(ZN):
        row_grad(g_proj, tiles_qkv, qkv_sem, dw_qkv, i)
        yield
    for i in (ZN - 2, ZN - 1):
        row_send(tiles_out, out_sem, dw_out, i).wait()
        row_send(tiles_qkv, qkv_sem, dw_qkv, i).wait()
    for copy in swaps:
        copy.wait_send()
    save.wait()


def attend_refs(rows, width):
    low = jnp.bfloat16
    dma = pltpu.SemaphoreType.DMA
    share = width // 16 // ZN
    return [
        pltpu.VMEM((rows, width), low),
        pltpu.VMEM((rows, width), low),
        pltpu.VMEM((HEAD_ROWS, rows), jnp.float32),
        pltpu.VMEM((2 * rows, rows), jnp.float32),
        pltpu.VMEM((2 * rows, width), low),
        pltpu.VMEM((2 * rows, width), low),
        pltpu.VMEM((rows, width), low),
        pltpu.VMEM((2 * rows, 2 * HEAD_DIM), jnp.float32),
        pltpu.VMEM((2 * rows, 2 * HEAD_DIM), jnp.float32),
        pltpu.VMEM((2, 2 * rows, width), low),
        pltpu.VMEM((2, rows, width), low),
        pltpu.VMEM((rows, width), jnp.float32),
        pltpu.VMEM((rows, width), jnp.float32),
        pltpu.VMEM((rows, width), jnp.float32),
        pltpu.VMEM((rows, 3 * width), low),
        pltpu.VMEM((width, rows), low),
        pltpu.VMEM((2, 16, 16, 3 * width), low),
        pltpu.VMEM((2, share, 16, 3 * width), low),
        pltpu.VMEM((2, share, 16, width), low),
        dma((8,)), dma((2,)), dma((2,)), dma((2,)), dma((2, 2)), dma((2, 2)),
    ]


def mlp_kernel(layer, grad, kept, gain, fulls, grads):
    rows, width = grad.shape
    ff = kept["slope"].shape[1]
    low = jnp.bfloat16
    ins = [grad, kept["middle"], kept["slope"], kept["normed_mlp"], kept["activated"], gain, fulls[1], fulls[2], fulls[3]]
    down_shape = (ZN, ff // 16 // ZN, 16, width)
    work_out = [
        shaped((rows, width)),
        shaped((rows, width), low),
        shaped((rows, width), low),
        shaped((width // 16, 16, ff), low),
        shaped((ff // 16, 16, width), low),
    ] + [shaped((1, n)) for n in (width, ff, width, width, width)]
    work_refs = mlp_refs(rows, width, ff)
    n, extra = len(work_out), len(grads)
    shapes = [g.shape for g in grads] + [down_shape]
    spec = spec_of(shapes)

    def body(*refs):
        i = len(ins) + extra
        outs, more = refs[i : i + n], refs[i + n : i + n + extra + 1]
        rest = refs[i + n + extra + 1 :]
        place = meet(False)
        down_rows = Rows(outs[4], down_shape[1])
        comm, finish = take_reduce(
            place, spec, list(refs[len(ins) : i]) + [down_rows], more, rest[len(work_refs) :], (extra,)
        )
        work = mlp_work(layer, refs[: len(ins)], outs, rest[: len(work_refs)], extra)
        spread_steps(work, comm, finish)

    outs = pl.pallas_call(
        body,
        out_shape=work_out + [shaped(shape[1:], low) for shape in shapes],
        in_specs=anywhere(5) + whole(1) + anywhere(3 + extra),
        out_specs=anywhere(5) + whole(5) + anywhere(extra + 1),
        scratch_shapes=work_refs + reduce_scratch([(k, shapes[m][2:]) for m, _, k in spec]),
        compiler_params=pltpu.CompilerParams(
            collective_id=100 + layer, has_side_effects=True, vmem_limit_bytes=VMEM_LIMIT
        ),
        name="mlp_back",
    )(*ins, *grads)
    return outs[:n], outs[n:]


class Rows:
    def __init__(self, ref, n):
        self.ref, self.n, self.at = ref, n, self

    def __getitem__(self, where):
        d, chunks = where
        return self.ref.at[pl.ds(d * self.n + chunks.start, chunks.size)]


def attend_kernel(layer, kept, mask, g_att, g_middle, g_branch, gain, fulls, grads, ship):
    rows, width = g_middle.shape
    low = jnp.bfloat16
    ins = [
        kept["q"], g_att, kept["lse"], mask, kept["keys"], kept["values"], kept["x"], g_middle,
        kept["normed_attn"], kept["attended"], g_branch, gain, fulls[0],
    ]
    work_out = [
        shaped((rows, width), jnp.float32 if layer else low),
        shaped((width // 16, 16, 3 * width), low),
        shaped((width // 16, 16, width), low),
    ] + [shaped((1, width))] * 4
    work_refs = attend_refs(rows, width)
    ships = [ship] if ship is not None else []
    n, extra, k = len(work_out), len(grads), len(ships)
    spec = spec_of([g.shape for g in grads])
    buffers = reduce_scratch([(depth, grads[m].shape[2:]) for m, _, depth in spec])

    def body(*refs):
        i = len(ins) + extra + k
        outs, more = refs[i : i + n], refs[i + n : i + n + extra]
        rest = refs[i + n + extra + k :]
        place = meet(bool(k))
        if k:
            start, wait = ship_moves(place, refs[i - 1], refs[i + n + extra], *rest[-3:])
            start()
        comm, finish = take_reduce(place, spec, refs[len(ins) : i - k], more, rest[len(work_refs) :])
        work = attend_work(layer, place, refs[: len(ins)], outs, rest[: len(work_refs)])
        spread_steps(work, comm, finish)
        if k:
            wait()

    outs = pl.pallas_call(
        body,
        out_shape=work_out + [shaped(g.shape[1:], low) for g in grads] + [shaped(v.shape, v.dtype) for v in ships],
        in_specs=anywhere(11) + whole(1) + anywhere(1 + extra + k),
        out_specs=anywhere(3) + whole(4) + anywhere(extra + k),
        scratch_shapes=work_refs + buffers + (ship_scratch() if k else []),
        compiler_params=pltpu.CompilerParams(
            collective_id=200 + layer, has_side_effects=True, vmem_limit_bytes=VMEM_LIMIT
        ),
        name="attend_back",
    )(*ins, *grads, *ships)
    return outs[:n], outs[n : n + extra], outs[n + extra :]


def reduce_kernel(grads, ship):
    extra = len(grads)
    spec = spec_of([g.shape for g in grads])

    def body(*refs):
        place = meet(True)
        rest = refs[2 * extra + 2 :]
        start, wait = ship_moves(place, refs[extra], refs[2 * extra + 1], *rest[-3:])
        start()
        comm, finish = take_reduce(place, spec, refs[:extra], refs[extra + 1 : 2 * extra + 1], rest)
        spread_steps((), comm, finish)
        wait()

    outs = pl.pallas_call(
        body,
        out_shape=[shaped(g.shape[1:], g.dtype) for g in grads] + [shaped(ship.shape, ship.dtype)],
        in_specs=anywhere(extra + 1),
        out_specs=anywhere(extra + 1),
        scratch_shapes=reduce_scratch([(k, grads[m].shape[2:]) for m, _, k in spec]) + ship_scratch(),
        compiler_params=pltpu.CompilerParams(collective_id=2, has_side_effects=True, vmem_limit_bytes=VMEM_LIMIT),
        name="reduce_grads",
    )(*grads, ship)
    return outs[:extra], outs[extra]


def assemble_body(layers, *refs):
    ins = [refs[layer * 5 : (layer + 1) * 5] for layer in range(layers)]
    outs = refs[layers * 5 : layers * 5 + 4]
    vectors = refs[layers * 5 + 4 : layers * 5 + 13]
    rest = refs[layers * 5 + 13 :]
    held, made = rest[:5], rest[5:9]
    in_sem, out_sem = rest[9:]
    width = held[4].shape[3]
    loads, stores = [], []
    for layer in range(layers):
        loads.append(
            [pltpu.make_async_copy(ins[layer][m], held[m].at[layer], in_sem.at[layer, m]) for m in range(5)]
        )
        begin(loads[-1])
    for layer in range(layers):
        loads[layer][4].wait()
        piece = 0
        for m in range(4):
            loads[layer][m].wait()
            n = held[m].shape[1]
            whole_n = n // 8 * 8
            if layer:
                stores[m].wait()

            def widen(i, carry, m=m):
                made[m][i] = held[m][layer, i].astype(jnp.float32)
                return carry

            lax.fori_loop(0, whole_n, widen, 0)
            for i in range(whole_n, n):
                for at in range(0, held[m].shape[3], width):
                    made[m][i, :, at : at + width] = held[4][layer, piece].astype(jnp.float32)
                    piece += 1
            copy = pltpu.make_async_copy(made[m], outs[m].at[layer], out_sem.at[layer, m])
            copy.start()
            if layer:
                stores[m] = copy
            else:
                stores.append(copy)
        flat = held[4][layer, piece].astype(jnp.float32)
        at = 0
        for ref in vectors:
            n = ref.shape[1]
            ref[layer : layer + 1, :] = flat[at // width : at // width + 1, at % width : at % width + n]
            at += n
    for copy in stores:
        copy.wait()


def assemble(reduced, vector_sizes):
    layers = len(reduced)
    low = jnp.bfloat16
    shapes = [r.shape for r in reduced[0]]
    dma = pltpu.SemaphoreType.DMA
    outs = pl.pallas_call(
        functools.partial(assemble_body, layers),
        out_shape=[shaped((layers,) + shape) for shape in shapes[:4]] + [shaped((layers, n)) for n in vector_sizes],
        in_specs=anywhere(5 * layers),
        out_specs=anywhere(4) + whole(len(vector_sizes)),
        scratch_shapes=[pltpu.VMEM((layers,) + shape, low) for shape in shapes]
        + [pltpu.VMEM(shape, jnp.float32) for shape in shapes[:4]]
        + [dma((layers, 5)), dma((layers, 4))],
        compiler_params=params(),
        name="assemble",
    )(*[r for entry in reduced for r in entry])
    return outs[:4], outs[4:]


VECTORS = (0, 1, 3, 4, 6, 7, 8, 12, 10)
MATRICES = (2, 5, 9, 11)


def wide_of(weight_grads, vector_grads):
    width = weight_grads[0].shape[3]

    def pieces(g):
        left = g[:, g.shape[1] // 8 * 8 :]
        parts = left.shape[3] // width
        return jnp.swapaxes(left.reshape(ZN, left.shape[1], 16, parts, width), 2, 3).reshape(ZN, -1, 16, width)

    vectors = jnp.concatenate([g.reshape(ZN, -1) for g in vector_grads], axis=1).astype(jnp.bfloat16)
    vectors = vectors.reshape(ZN, 1, -1, width)
    vectors = jnp.pad(vectors, ((0, 0), (0, 0), (0, 16 - vectors.shape[2]), (0, 0)))
    wide = jnp.concatenate([pieces(g) for g in weight_grads] + [vectors], axis=1)
    return jnp.pad(wide, ((0, 0), (0, -wide.shape[1] % 8), (0, 0), (0, 0)))


def on_cores(tokens, segments, grad_out, *params):
    rows, width = tokens.shape[1:]
    layers = params[0].shape[0]
    weights = [params[i].reshape(layers, -1, 16, params[i].shape[2]) for i in MATRICES]
    vectors = jnp.concatenate([params[i].reshape(layers, -1, params[0].shape[1]) for i in VECTORS], axis=1)
    vectors = jnp.pad(vectors, ((0, 0), (0, 16 - vectors.shape[1]), (0, 0)))[:, None]
    fulls, result, grad, mask, vector_rows, saved = forward(tokens[0], grad_out[0], segments, vectors, weights)
    fulls = [full.reshape(layers, -1, 16, full.shape[4]) for full in fulls]
    reduced = [None] * layers
    waiting = []
    ship = result
    for layer in reversed(range(layers)):
        kept = saved[layer]
        attn_gain, mlp_gain = vector_rows[layer, 0:1], vector_rows[layer, 5:6]
        (g_middle, g_branch, g_att, dw_up, dw_down, gb_down, gb_up, gm_gain, gm_shift, gb_out), sums = mlp_kernel(
            layer, grad, kept, mlp_gain, fulls, waiting
        )
        if waiting:
            reduced[layer + 1].extend(sums[:-1])
        reduced[layer] = [sums[-1]]
        dw_up, dw_down = dw_up.reshape(ZN, -1, 16, dw_up.shape[2]), dw_down.reshape(ZN, -1, 16, width)
        (grad, dw_qkv, dw_out, gb_q, gb_v, ga_gain, ga_shift), sums, shipped = attend_kernel(
            layer, kept, mask, g_att, g_middle, g_branch, attn_gain, fulls, [dw_up], ship
        )
        if ship is not None:
            result, ship = shipped[0], None
        reduced[layer].extend(sums)
        waiting = [dw.reshape(ZN, -1, 16, dw.shape[2]) for dw in (dw_out, dw_qkv)]
        vector_grads = (ga_gain, ga_shift, gb_q, gb_v, gb_out, gm_gain, gm_shift, gb_down, gb_up)
        waiting.append(wide_of([dw_down, dw_up] + waiting, vector_grads))
    sums, grad = reduce_kernel(waiting, grad)
    reduced[0].extend(sums)
    (down, up, out, qkv), vector_outs = assemble(reduced, [params[i].shape[1] for i in VECTORS])
    final = [None] * 13
    for i, value in ((11, down), (9, up), (5, out), (2, qkv)):
        final[i] = value.reshape(layers, -1, value.shape[3])
    for i, value in zip(VECTORS, vector_outs):
        final[i] = value
    return (result[None], grad[None], *final)


def on_device(
    tokens,
    segments,
    grad_out,
    attn_gain,
    attn_shift,
    w_qkv,
    b_query,
    b_value,
    w_out,
    b_out,
    mlp_gain,
    mlp_shift,
    w_up,
    b_up,
    w_down,
    b_down,
):
    seg_own = segments[0]
    seg_all = lax.all_gather(seg_own, "seq", axis=0, tiled=True)
    offset = lax.axis_index("seq") * seg_own.shape[0]
    visible = visible_mask(seg_own, seg_all, offset)
    layer_count = attn_gain.shape[0]
    resid = tokens[0].astype(jnp.float32)
    kept_weights = []
    stored_list = []
    for layer_index in range(layer_count):
        gathered = gather_layer(
            layer_index,
            attn_gain,
            attn_shift,
            w_qkv,
            b_query,
            b_value,
            w_out,
            b_out,
            mlp_gain,
            mlp_shift,
            w_up,
            b_up,
            w_down,
            b_down,
        )
        resid, stored = forward_layer(resid, gathered, visible, Halves())
        kept_weights.append(gathered)
        stored_list.append(stored)
    result = resid.astype(jnp.bfloat16)[None]
    grad_resid = grad_out[0].astype(jnp.float32)
    reduced = [None] * layer_count
    for layer_index in reversed(range(layer_count)):
        gathered = gather_again(
            layer_index,
            attn_gain,
            attn_shift,
            w_qkv,
            b_query,
            b_value,
            w_out,
            b_out,
            mlp_gain,
            mlp_shift,
            w_up,
            b_up,
            w_down,
            b_down,
        )
        grad_resid, gradients = backward_layer(
            grad_resid, stored_list[layer_index], gathered, visible, Halves()
        )
        reduced[layer_index] = reduce_grads(gradients)
    stacked = tuple((jnp.stack([entry[member] for entry in reduced]) for member in range(13)))
    return (result, grad_resid.astype(jnp.bfloat16)[None]) + stacked


def solution(mesh):
    fits = (mesh.shape["seq"], mesh.shape["fsdp"], mesh.shape["rep"]) == (2, ZN, 4)
    return jax.shard_map(
        on_cores if fits else on_device,
        mesh=mesh,
        in_specs=(
            P(("fsdp", "rep"), "seq", None),
            P(("fsdp", "rep"), "seq"),
            P(("fsdp", "rep"), "seq", None),
            P(None, "fsdp"),
            P(None, "fsdp"),
            P(None, "fsdp", None),
            P(None, "fsdp"),
            P(None, "fsdp"),
            P(None, "fsdp", None),
            P(None, "fsdp"),
            P(None, "fsdp"),
            P(None, "fsdp"),
            P(None, "fsdp", None),
            P(None, "fsdp"),
            P(None, "fsdp", None),
            P(None, "fsdp"),
        ),
        out_specs=(
            P(("fsdp", "rep"), "seq", None),
            P(("fsdp", "rep"), "seq", None),
            P(None, "fsdp"),
            P(None, "fsdp"),
            P(None, "fsdp", None),
            P(None, "fsdp"),
            P(None, "fsdp"),
            P(None, "fsdp", None),
            P(None, "fsdp"),
            P(None, "fsdp"),
            P(None, "fsdp"),
            P(None, "fsdp", None),
            P(None, "fsdp"),
            P(None, "fsdp", None),
            P(None, "fsdp"),
        ),
        check_vma=False,
    )
```

```python
import functools
import math

import jax
import jax.numpy as jnp
from jax import lax
from jax.experimental import pallas as pl
from jax.experimental.pallas import tpu as pltpu
from jax.sharding import PartitionSpec as P

HEAD_DIM = 64
MESH = pl.DeviceIdType.MESH


NORM_EPSILON = 1e-05
MASKED = -1e30


def layer_norm(inputs, gain, bias_term):
    center = inputs - jnp.mean(inputs, axis=-1, keepdims=True)
    spread = jnp.mean(center * center, axis=-1, keepdims=True)
    return center * lax.rsqrt(spread + NORM_EPSILON) * gain + bias_term


def gelu_tanh(inputs):
    return jax.nn.gelu(inputs, approximate=True)


def product(left, right):
    return jnp.dot(left, right, preferred_element_type=jnp.float32)


def inner_rows(left, right):
    return lax.dot_general(
        left, right, (((0,), (0,)), ((), ())), preferred_element_type=jnp.float32
    )


def outer_cols(left, right):
    return lax.dot_general(
        left, right, (((1,), (1,)), ((), ())), preferred_element_type=jnp.float32
    )


def column_sum(values_low):
    return jnp.sum(values_low.astype(jnp.float32), axis=0)


def visible_mask(seg_own, seg_all, offset):
    row_pos = offset + lax.iota(jnp.int32, seg_own.shape[0])
    col_pos = lax.iota(jnp.int32, seg_all.shape[0])
    return (seg_own[:, None] == seg_all[None, :]) & (row_pos[:, None] >= col_pos[None, :])


def head_scores(queries, keys_all, visible, head_count):
    query_heads = queries.reshape(queries.shape[0], head_count, HEAD_DIM)
    key_heads = keys_all.reshape(keys_all.shape[0], head_count, HEAD_DIM)
    scores = jnp.einsum("thd,shd->hts", query_heads, key_heads, preferred_element_type=jnp.float32)
    return jnp.where(visible[None], scores, MASKED)


def gather_layer(
    layer_index,
    attn_gain,
    attn_shift,
    w_qkv,
    b_query,
    b_value,
    w_out,
    b_out,
    mlp_gain,
    mlp_shift,
    w_up,
    b_up,
    w_down,
    b_down,
):
    return (
        lax.all_gather(attn_gain[layer_index], "fsdp", axis=0, tiled=True),
        lax.all_gather(attn_shift[layer_index], "fsdp", axis=0, tiled=True),
        lax.all_gather(w_qkv[layer_index], "fsdp", axis=0, tiled=True),
        lax.all_gather(b_query[layer_index], "fsdp", axis=0, tiled=True),
        lax.all_gather(b_value[layer_index], "fsdp", axis=0, tiled=True),
        lax.all_gather(w_out[layer_index], "fsdp", axis=0, tiled=True),
        lax.all_gather(b_out[layer_index], "fsdp", axis=0, tiled=True),
        lax.all_gather(mlp_gain[layer_index], "fsdp", axis=0, tiled=True),
        lax.all_gather(mlp_shift[layer_index], "fsdp", axis=0, tiled=True),
        lax.all_gather(w_up[layer_index], "fsdp", axis=0, tiled=True),
        lax.all_gather(b_up[layer_index], "fsdp", axis=0, tiled=True),
        lax.all_gather(w_down[layer_index], "fsdp", axis=0, tiled=True),
        lax.all_gather(b_down[layer_index], "fsdp", axis=0, tiled=True),
    )


def gather_again(
    layer_index,
    attn_gain,
    attn_shift,
    w_qkv,
    b_query,
    b_value,
    w_out,
    b_out,
    mlp_gain,
    mlp_shift,
    w_up,
    b_up,
    w_down,
    b_down,
):
    return (
        lax.all_gather(attn_gain[layer_index], "fsdp", axis=0, tiled=True),
        lax.all_gather(attn_shift[layer_index], "fsdp", axis=0, tiled=True),
        lax.all_gather(w_qkv[layer_index], "fsdp", axis=0, tiled=True),
        lax.all_gather(b_query[layer_index], "fsdp", axis=0, tiled=True),
        lax.all_gather(b_value[layer_index], "fsdp", axis=0, tiled=True),
        lax.all_gather(w_out[layer_index], "fsdp", axis=0, tiled=True),
        lax.all_gather(b_out[layer_index], "fsdp", axis=0, tiled=True),
        lax.all_gather(mlp_gain[layer_index], "fsdp", axis=0, tiled=True),
        lax.all_gather(mlp_shift[layer_index], "fsdp", axis=0, tiled=True),
        lax.all_gather(w_up[layer_index], "fsdp", axis=0, tiled=True),
        lax.all_gather(b_up[layer_index], "fsdp", axis=0, tiled=True),
        lax.all_gather(w_down[layer_index], "fsdp", axis=0, tiled=True),
        lax.all_gather(b_down[layer_index], "fsdp", axis=0, tiled=True),
    )


def forward_layer(resid, gathered, visible, pool):
    (
        attn_gain,
        attn_shift,
        w_qkv,
        b_query,
        b_value,
        w_out,
        b_out,
        mlp_gain,
        mlp_shift,
        w_up,
        b_up,
        w_down,
        b_down,
    ) = gathered
    model_width = resid.shape[1]
    head_count = model_width // HEAD_DIM
    query_scale = 1.0 / math.sqrt(HEAD_DIM)
    normed_attn = layer_norm(
        resid, attn_gain.astype(jnp.float32), attn_shift.astype(jnp.float32)
    ).astype(jnp.bfloat16)
    proj_all = product(normed_attn, w_qkv)
    queries = ((proj_all[:, :model_width] + b_query.astype(jnp.float32)) * query_scale).astype(
        jnp.bfloat16
    )
    keys_own = proj_all[:, model_width : 2 * model_width].astype(jnp.bfloat16)
    values_own = (proj_all[:, 2 * model_width :] + b_value.astype(jnp.float32)).astype(jnp.bfloat16)
    keys_all, values_all = pool.spread(keys_own), pool.spread(values_own)
    scores = head_scores(queries, keys_all, visible, head_count)
    row_max = jnp.max(scores, axis=-1, keepdims=True)
    exponent = jnp.exp(scores - row_max)
    row_sum = jnp.sum(exponent, axis=-1, keepdims=True)
    weights_soft = (exponent / row_sum).astype(jnp.bfloat16)
    log_total = row_max + jnp.log(row_sum)
    value_heads = values_all.reshape(values_all.shape[0], head_count, HEAD_DIM)
    attended = jnp.einsum(
        "hts,shd->thd", weights_soft, value_heads, preferred_element_type=jnp.float32
    )
    attended = attended.reshape(resid.shape[0], model_width).astype(jnp.bfloat16)
    middle = resid + product(attended, w_out) + b_out.astype(jnp.float32)
    normed_mlp = layer_norm(
        middle, mlp_gain.astype(jnp.float32), mlp_shift.astype(jnp.float32)
    ).astype(jnp.bfloat16)
    pre_act = product(normed_mlp, w_up) + b_up.astype(jnp.float32)
    activated = gelu_tanh(pre_act).astype(jnp.bfloat16)
    output = middle + product(activated, w_down) + b_down.astype(jnp.float32)
    stored = (
        resid,
        normed_attn,
        queries,
        keys_all,
        values_all,
        log_total,
        attended,
        middle,
        normed_mlp,
        pre_act,
        activated,
    )
    return (output, stored)


def backward_layer(grad_next, stored, gathered, visible, pool):
    (
        attn_gain,
        attn_shift,
        w_qkv,
        b_query,
        b_value,
        w_out,
        b_out,
        mlp_gain,
        mlp_shift,
        w_up,
        b_up,
        w_down,
        b_down,
    ) = gathered
    (
        resid,
        normed_attn,
        queries,
        keys_all,
        values_all,
        log_total,
        attended,
        middle,
        normed_mlp,
        pre_act,
        activated,
    ) = stored
    model_width = resid.shape[1]
    tok_rows = resid.shape[0]
    key_rows = keys_all.shape[0]
    head_count = model_width // HEAD_DIM
    query_scale = 1.0 / math.sqrt(HEAD_DIM)
    grad_mlp = grad_next.astype(jnp.bfloat16)
    grad_b_down = column_sum(grad_mlp)
    grad_w_down = inner_rows(activated, grad_mlp)
    grad_act = outer_cols(grad_mlp, w_down)
    gelu_value, gelu_pull = jax.vjp(gelu_tanh, pre_act)
    grad_pre = gelu_pull(grad_act)[0].astype(jnp.bfloat16)
    grad_b_up = column_sum(grad_pre)
    grad_w_up = inner_rows(normed_mlp, grad_pre)
    grad_nm = outer_cols(grad_pre, w_up)
    norm_value, norm_pull = jax.vjp(
        layer_norm, middle, mlp_gain.astype(jnp.float32), mlp_shift.astype(jnp.float32)
    )
    grad_middle, grad_mlp_gain, grad_mlp_shift = norm_pull(grad_nm)
    grad_middle = grad_middle + grad_next
    grad_branch = grad_middle.astype(jnp.bfloat16)
    grad_b_out = column_sum(grad_branch)
    grad_w_out = inner_rows(attended, grad_branch)
    grad_attended = outer_cols(grad_branch, w_out).astype(jnp.bfloat16)
    scores = head_scores(queries, keys_all, visible, head_count)
    weights_full = jnp.exp(scores - log_total)
    weights_soft = weights_full.astype(jnp.bfloat16)
    grad_heads = grad_attended.reshape(tok_rows, head_count, HEAD_DIM)
    query_heads = queries.reshape(tok_rows, head_count, HEAD_DIM)
    key_heads = keys_all.reshape(key_rows, head_count, HEAD_DIM)
    value_heads = values_all.reshape(key_rows, head_count, HEAD_DIM)
    grad_value_terms = jnp.einsum(
        "hts,thd->shd", weights_soft, grad_heads, preferred_element_type=jnp.float32
    )
    grad_probs = jnp.einsum(
        "thd,shd->hts", grad_heads, value_heads, preferred_element_type=jnp.float32
    )
    inner_sum = jnp.sum(weights_full * grad_probs, axis=-1, keepdims=True)
    grad_scores = (weights_full * (grad_probs - inner_sum)).astype(jnp.bfloat16)
    grad_queries = jnp.einsum(
        "hts,shd->thd", grad_scores, key_heads, preferred_element_type=jnp.float32
    )
    grad_queries = grad_queries.reshape(tok_rows, model_width).astype(jnp.bfloat16) * query_scale
    grad_key_terms = jnp.einsum(
        "hts,thd->shd", grad_scores, query_heads, preferred_element_type=jnp.float32
    )
    grad_keys = pool.collect(grad_key_terms.reshape(key_rows, model_width).astype(jnp.bfloat16))
    grad_values = pool.collect(grad_value_terms.reshape(key_rows, model_width).astype(jnp.bfloat16))
    grad_keys = grad_keys.astype(jnp.bfloat16)
    grad_values = grad_values.astype(jnp.bfloat16)
    grad_proj = jnp.concatenate([grad_queries, grad_keys, grad_values], axis=1)
    grad_b_query = column_sum(grad_queries)
    grad_b_value = column_sum(grad_values)
    grad_w_qkv = inner_rows(normed_attn, grad_proj)
    grad_na = outer_cols(grad_proj, w_qkv)
    first_value, first_pull = jax.vjp(
        layer_norm, resid, attn_gain.astype(jnp.float32), attn_shift.astype(jnp.float32)
    )
    grad_resid, grad_attn_gain, grad_attn_shift = first_pull(grad_na)
    grad_resid = grad_resid + grad_middle
    gradients = (
        grad_attn_gain,
        grad_attn_shift,
        grad_w_qkv,
        grad_b_query,
        grad_b_value,
        grad_w_out,
        grad_b_out,
        grad_mlp_gain,
        grad_mlp_shift,
        grad_w_up,
        grad_b_up,
        grad_w_down,
        grad_b_down,
    )
    return (grad_resid, gradients)


def reduce_grads(gradients):
    shares = (
        lax.psum_scatter(gradients[0], ("fsdp", "rep"), scatter_dimension=0, tiled=True),
        lax.psum_scatter(gradients[1], ("fsdp", "rep"), scatter_dimension=0, tiled=True),
        lax.psum_scatter(gradients[2], ("fsdp", "rep"), scatter_dimension=0, tiled=True),
        lax.psum_scatter(gradients[3], ("fsdp", "rep"), scatter_dimension=0, tiled=True),
        lax.psum_scatter(gradients[4], ("fsdp", "rep"), scatter_dimension=0, tiled=True),
        lax.psum_scatter(gradients[5], ("fsdp", "rep"), scatter_dimension=0, tiled=True),
        lax.psum_scatter(gradients[6], ("fsdp", "rep"), scatter_dimension=0, tiled=True),
        lax.psum_scatter(gradients[7], ("fsdp", "rep"), scatter_dimension=0, tiled=True),
        lax.psum_scatter(gradients[8], ("fsdp", "rep"), scatter_dimension=0, tiled=True),
        lax.psum_scatter(gradients[9], ("fsdp", "rep"), scatter_dimension=0, tiled=True),
        lax.psum_scatter(gradients[10], ("fsdp", "rep"), scatter_dimension=0, tiled=True),
        lax.psum_scatter(gradients[11], ("fsdp", "rep"), scatter_dimension=0, tiled=True),
        lax.psum_scatter(gradients[12], ("fsdp", "rep"), scatter_dimension=0, tiled=True),
    )
    shares = (
        lax.psum(shares[0].astype(jnp.bfloat16), "seq").astype(jnp.float32),
        lax.psum(shares[1].astype(jnp.bfloat16), "seq").astype(jnp.float32),
        lax.psum(shares[2].astype(jnp.bfloat16), "seq").astype(jnp.float32),
        lax.psum(shares[3].astype(jnp.bfloat16), "seq").astype(jnp.float32),
        lax.psum(shares[4].astype(jnp.bfloat16), "seq").astype(jnp.float32),
        lax.psum(shares[5].astype(jnp.bfloat16), "seq").astype(jnp.float32),
        lax.psum(shares[6].astype(jnp.bfloat16), "seq").astype(jnp.float32),
        lax.psum(shares[7].astype(jnp.bfloat16), "seq").astype(jnp.float32),
        lax.psum(shares[8].astype(jnp.bfloat16), "seq").astype(jnp.float32),
        lax.psum(shares[9].astype(jnp.bfloat16), "seq").astype(jnp.float32),
        lax.psum(shares[10].astype(jnp.bfloat16), "seq").astype(jnp.float32),
        lax.psum(shares[11].astype(jnp.bfloat16), "seq").astype(jnp.float32),
        lax.psum(shares[12].astype(jnp.bfloat16), "seq").astype(jnp.float32),
    )
    return (
        lax.all_gather(shares[0].astype(jnp.bfloat16), "rep", axis=0, tiled=True).astype(
            jnp.float32
        ),
        lax.all_gather(shares[1].astype(jnp.bfloat16), "rep", axis=0, tiled=True).astype(
            jnp.float32
        ),
        lax.all_gather(shares[2].astype(jnp.bfloat16), "rep", axis=0, tiled=True).astype(
            jnp.float32
        ),
        lax.all_gather(shares[3].astype(jnp.bfloat16), "rep", axis=0, tiled=True).astype(
            jnp.float32
        ),
        lax.all_gather(shares[4].astype(jnp.bfloat16), "rep", axis=0, tiled=True).astype(
            jnp.float32
        ),
        lax.all_gather(shares[5].astype(jnp.bfloat16), "rep", axis=0, tiled=True).astype(
            jnp.float32
        ),
        lax.all_gather(shares[6].astype(jnp.bfloat16), "rep", axis=0, tiled=True).astype(
            jnp.float32
        ),
        lax.all_gather(shares[7].astype(jnp.bfloat16), "rep", axis=0, tiled=True).astype(
            jnp.float32
        ),
        lax.all_gather(shares[8].astype(jnp.bfloat16), "rep", axis=0, tiled=True).astype(
            jnp.float32
        ),
        lax.all_gather(shares[9].astype(jnp.bfloat16), "rep", axis=0, tiled=True).astype(
            jnp.float32
        ),
        lax.all_gather(shares[10].astype(jnp.bfloat16), "rep", axis=0, tiled=True).astype(
            jnp.float32
        ),
        lax.all_gather(shares[11].astype(jnp.bfloat16), "rep", axis=0, tiled=True).astype(
            jnp.float32
        ),
        lax.all_gather(shares[12].astype(jnp.bfloat16), "rep", axis=0, tiled=True).astype(
            jnp.float32
        ),
    )


class Halves:
    def spread(self, rows):
        return lax.all_gather(rows, "seq", axis=0, tiled=True)

    def collect(self, rows):
        return lax.psum_scatter(rows, "seq", scatter_dimension=0, tiled=True)


ZN = 4


def neighbours():
    x, z, r = lax.axis_index("seq"), lax.axis_index("fsdp"), lax.axis_index("rep")
    y, c = r // 2, r % 2
    across = (1 - x, z, r)
    beside = (x, z, (1 - y) * 2 + c)
    twin = (x, z, y * 2 + (1 - c))
    up = (x, (z + 1) % ZN, r)
    down = (x, (z + ZN - 1) % ZN, r)
    return x, y, z, c, across, beside, twin, up, down


def greet(z, c, x, across, beside, twin, diag, up, down):
    barrier = pltpu.get_barrier_semaphore()

    def tell(device):
        pl.semaphore_signal(barrier, inc=1, device_id=device, device_id_type=MESH)

    for device in (across, beside, twin):
        tell(device)
    if diag is not None:

        @pl.when(c != x)
        def _():
            tell(diag)

    @pl.when(z < ZN - 1)
    def _():
        tell(up)

    @pl.when(z > 0)
    def _():
        tell(down)

    extra = 0 if diag is None else (x + c) % 2
    pl.semaphore_wait(barrier, 3 + extra + (z + ZN - 1) // ZN + (2 * ZN - 2 - z) // ZN)


GELU_A = math.sqrt(2.0 / math.pi)
GELU_B = 0.044715
QUERY_SCALE = 1.0 / math.sqrt(HEAD_DIM)
HEAD_ROWS = 24
PACE = 4
LEAD = 3
GAP = 2
TILE = 512
REDUCE_PACE = 6
SKEW = 2
AHEAD = 6


NT = (((1,), (1,)), ((), ()))
TN = (((0,), (0,)), ((), ()))
BLOCK = 256
RANGES = (((0, 256), (256, 1024)), ((0, 768), (256, 512)))
VMEM_LIMIT = 60 << 20


def dot_nt(left, right):
    return lax.dot_general(left, right, NT, preferred_element_type=jnp.float32)


def dot_tn(left, right):
    return lax.dot_general(left, right, TN, preferred_element_type=jnp.float32)


def tiles(width, tile, act):
    whole = width // tile

    def step(i, carry):
        act(pl.multiple_of(i * tile, tile), tile)
        return carry

    lax.fori_loop(0, whole, step, 0)
    if width % tile:
        act(whole * tile, width % tile)


def tiles_between(low, high, tile, act):
    def step(i, carry):
        act(pl.multiple_of(i * tile, tile), tile)
        return carry

    if low // tile < high // tile:
        lax.fori_loop(low // tile, high // tile, step, 0)
    if high % tile:
        act(high // tile * tile, high % tile)


def norm_parts(rows):
    center = rows - jnp.mean(rows, axis=1, keepdims=True)
    scale = lax.rsqrt(jnp.mean(center * center, axis=1, keepdims=True) + NORM_EPSILON)
    return center * scale, scale


def norm_into(source, gain, shift, target):
    def act(start, size):
        rows = pl.ds(start, size)
        unit, _ = norm_parts(source[rows, :])
        target[rows, :] = (unit * gain + shift).astype(target.dtype)

    tiles(source.shape[0], 64, act)


def norm_back(source, grad, extra, gain, target, gain_grad, shift_grad, low=None):
    gain_grad[...] = jnp.zeros_like(gain_grad)
    shift_grad[...] = jnp.zeros_like(shift_grad)

    def act(start, size):
        rows = pl.ds(start, size)
        unit, scale = norm_parts(source[rows, :])
        g = grad[rows, :]
        q = g * gain
        mean_q = jnp.mean(q, axis=1, keepdims=True)
        mean_qn = jnp.mean(q * unit, axis=1, keepdims=True)
        out = extra[rows, :] + (q - mean_q - unit * mean_qn) * scale
        target[rows, :] = out
        if low is not None:
            low[rows, :] = out.astype(low.dtype)
        gain_grad[...] += jnp.sum(g * unit, axis=0, keepdims=True)
        shift_grad[...] += jnp.sum(g, axis=0, keepdims=True)

    tiles(source.shape[0], 64, act)


def whole(count):
    return [pl.BlockSpec(memory_space=pltpu.VMEM)] * count


def anywhere(count):
    return [pl.BlockSpec(memory_space=pl.ANY)] * count


def shaped(shape, dtype=jnp.float32):
    return jax.ShapeDtypeStruct(shape, dtype)


def params():
    return pltpu.CompilerParams(vmem_limit_bytes=VMEM_LIMIT)


def of_head(values, j):
    if values.shape[1] == HEAD_DIM:
        return values
    lane = lax.broadcasted_iota(jnp.int32, values.shape, 1)
    return jnp.where(lane // HEAD_DIM == j, values, jnp.zeros_like(values))


ZA, ZR, GX, GY, GD1, GD2, GC = range(7)
ROW = dict(attn_gain=0, attn_shift=1, b_query=2, b_value=3, b_out=4, mlp_gain=5, mlp_shift=6, b_down=7)
SAVED = ("x", "normed_attn", "q", "keys", "values", "attended", "lse", "middle", "normed_mlp", "slope", "activated")


def advance(steps, count):
    for _ in range(count):
        if next(steps, None) is None:
            return


def gather_units(layers, shapes):
    units = []
    for layer in range(layers):
        for m, shape in enumerate(shapes):
            n = shape[1] // 8
            k = min(n, 1 if shape[3] > 2048 else 2)
            bases = range(0, max(n, 1), max(k, 1))
            units += [(layer, m, base * 8, k, base + k >= n) for base in bases]
    return units


def weight_moves(ins, outs, send_sem, recv_sem, place):
    x, y, z, c, across, beside, twin, up, down = place
    m_count = len(ins) - 1
    layers = ins[0].shape[0]
    units = gather_units(layers, [w.shape for w in ins])
    index = {unit: i for i, unit in enumerate(units)}

    def depth(u):
        return u[3]

    def corners(u, px, py, act):
        k = depth(u)
        for half, device, kind in ((0, beside, GD1), (1, across, GD2)):
            if k > 1 or half == index[u] % 2:
                act(half if k > 1 else None, device, kind)

    def owned(u, px, py, half=None):
        k = depth(u)
        base = u[2] + (c * 4 + px * 2 + py) * k
        if half is None:
            return pl.ds(base, k)
        return pl.ds(base + half * (k // 2), k // 2)

    def rest(u):
        n = ins[u[1]].shape[1]
        return pl.ds(n // 8 * 8, n % 8)

    def slab(u, core):
        return pl.ds(u[2] + core * 4 * depth(u), 4 * depth(u))

    def move(u, zz, rows, device, kind, source=None, send_kind=None):
        target = outs[u[1]].at[u[0], zz, rows]
        return pltpu.make_async_remote_copy(
            src_ref=target if source is None else source,
            dst_ref=target,
            send_sem=send_sem.at[index[u], zz, kind if send_kind is None else send_kind],
            recv_sem=recv_sem.at[index[u], zz, kind],
            device_id=device,
            device_id_type=MESH,
        )

    def own_sends(u, act):
        source = ins[u[1]].at[u[0]]

        def along(device, first):
            if depth(u):
                act(move(u, z, owned(u, x, y), device, ZA, source.at[owned(u, x, y)], first))
            if u[4]:
                act(move(u, z, rest(u), device, ZR, source.at[rest(u)], first + 1))

        @pl.when(z < ZN - 1)
        def _():
            along(up, 0)

        @pl.when(z > 0)
        def _():
            along(down, 2)

    def both(s, act):
        @pl.when(z >= s)
        def _():
            act(z - s, 0)

        @pl.when(z + s <= ZN - 1)
        def _():
            act(z + s, 1)

    def onward(u, zz, d, act):
        def along(device):
            if depth(u):
                act(move(u, zz, owned(u, x, y), device, ZA))
            if u[4]:
                act(move(u, zz, rest(u), device, ZR))

        if d == 0:

            @pl.when(z < ZN - 1)
            def _():
                along(up)

        else:

            @pl.when(z > 0)
            def _():
                along(down)

    def line_step(u, s):
        def act(zz, d):
            if depth(u):
                move(u, zz, owned(u, x, y), across, ZA).wait_recv()
            if u[4]:
                move(u, zz, rest(u), across, ZR).wait_recv()
            onward(u, zz, d, lambda copy: copy.start())
            if depth(u):
                move(u, zz, owned(u, x, y), across, GX).start()
                move(u, zz, owned(u, x, y), beside, GY).start()

        both(s, act)

    def plane_step(u, s):
        def act(zz, d):
            def pass_on(half, device, kind):
                if kind == GD1:
                    move(u, zz, owned(u, 1 - x, y, half), device, kind).start()
                else:
                    move(u, zz, owned(u, x, 1 - y, half), device, kind).start()

            move(u, zz, owned(u, 1 - x, y), across, GX).wait_recv()
            move(u, zz, owned(u, x, 1 - y), beside, GY).wait_recv()
            corners(u, x, y, pass_on)

        both(s, act)

    def corner_step(u, s):
        def act(zz, d):
            corners(
                u, x, y, lambda half, device, kind: move(u, zz, owned(u, 1 - x, 1 - y, half), device, kind).wait_recv()
            )
            move(u, zz, slab(u, c), twin, GC).start()

        both(s, act)

    def arrive(whole):
        for u in units:
            if u[:2] == whole:
                for s in range(1, ZN):
                    both(s, lambda zz, d: move(u, zz, slab(u, 1 - c), twin, GC).wait_recv())

    def finish(u):
        own_sends(u, lambda copy: copy.wait_send())
        for s in range(1, ZN):

            def act(zz, d):
                onward(u, zz, d, lambda copy: copy.wait_send())
                if depth(u):
                    move(u, zz, owned(u, x, y), across, GX).wait_send()
                    move(u, zz, owned(u, x, y), beside, GY).wait_send()
                    corners(
                        u, x, y, lambda half, device, kind: move(u, zz, owned(u, x, y, half), device, kind).wait_send()
                    )
                    move(u, zz, slab(u, c), twin, GC).wait_send()

            both(s, act)

    matrices = [u for u in units if u[1] < m_count]
    vectors = [u for u in units if u[1] == m_count]
    def steps():
        first = [u for u in matrices if u[:2] == matrices[0][:2]]
        rest_units = [u for u in matrices if u not in first]
        count = len(rest_units)
        for u in vectors + first:
            own_sends(u, lambda copy: copy.start())
        for s in range(1, ZN):
            for u in vectors:
                line_step(u, s)
        yield ("vectors",)
        for s in range(1, ZN):
            for u in first:
                line_step(u, s)
                yield ("line",)
            if s == 1:
                for u in rest_units[:LEAD]:
                    own_sends(u, lambda copy: copy.start())
        early = [[(plane_step, u, s) for u in first] for s in range(1, ZN)]
        early += [[(corner_step, u, s) for u in first] for s in range(1, ZN)]
        for t in range(count + 4 * GAP):
            if t + LEAD < count:
                own_sends(rest_units[t + LEAD], lambda copy: copy.start())
            for step, u, s in sum(early[t * 2 : t * 2 + 2], []):
                step(u, s)
                here = step is corner_step and s == ZN - 1 and u[4]
                yield ("here", u[:2]) if here else ("early",)
            for delay, step in ((0, line_step), (1, plane_step), (2, corner_step)):
                for s in range(1, ZN):
                    i = t - (s - 1 + delay) * GAP
                    if not 0 <= i < count:
                        continue
                    u = rest_units[i]
                    step(u, s)
                    here = step is corner_step and s == ZN - 1 and u[4]
                    yield ("here", u[:2]) if here else ("step",)

    return steps, arrive, lambda: [finish(u) for u in units]


def attend(core, q, keys, values, mask, attended, lse, first, last):
    def slab(start, size, head):
        cols = pl.ds(start, size)
        for variant in range(2):

            @pl.when(core == variant)
            def _():
                for row, high in RANGES[variant]:
                    rows = slice(row, row + BLOCK)
                    qs = q[rows, cols]
                    ks, vs = keys[:high, cols], values[:high, cols]
                    parts = []
                    for j in range(size // HEAD_DIM):
                        s = dot_nt(ks, of_head(qs, j)) + mask[:high, rows]
                        top = jnp.max(s, axis=0, keepdims=True)
                        e = jnp.exp(s - top)
                        total = jnp.sum(e, axis=0, keepdims=True)
                        lse[pl.ds(head + j, 1), rows] = top + jnp.log(total)
                        out = dot_tn(vs, e.astype(jnp.bfloat16)) * (1.0 / total)
                        parts.append(out[j * HEAD_DIM : (j + 1) * HEAD_DIM])
                    out = jnp.concatenate(parts, axis=0) if len(parts) > 1 else parts[0]
                    attended[rows, cols] = out.T.astype(jnp.bfloat16)

    over_slabs(q.shape[1], slab, first, last)


def over_slabs(width, slab, first, last):
    pair = 2 * HEAD_DIM
    full = width // pair

    def step(i, carry):
        slab(pl.multiple_of(i * pair, pair), pair, i * 2)
        return carry

    if first < min(last, full):
        lax.fori_loop(first, min(last, full), step, 0)
    if last > full and width % pair:
        slab(full * pair, HEAD_DIM, full * 2)


def forward_body(
    tokens, grads, segs, vectors, w_qkv, w_out, w_up, w_down,
    full_qkv, full_out, full_up, full_down, full_vectors, result, grads_here, mask_out, rows_out, *rest_refs,
):
    layers = w_qkv.shape[0]
    saved = [dict(zip(SAVED, rest_refs[i * len(SAVED) : (i + 1) * len(SAVED)])) for i in range(layers)]
    (
        wq, wo, wu, wd, xs, tok, na, nm, q, keys, values, mask, att, middle, slope, act_buf, lse,
        vecs, rows, b_up, b_proj, seg_nat, seg_row,
        send_sem, recv_sem, load_sem, own_sem, save_sem, kv_send, kv_recv, in_send, in_recv, in_local, free_sem,
    ) = rest_refs[layers * len(SAVED) :]
    place = neighbours()
    x, y, z, c, across, beside, twin, up, down = place
    diag = (1 - x, z, y * 2 + (1 - c))
    here = c == x
    greet(z, c, x, across, beside, twin, diag, up, down)
    width = xs.shape[1]
    half = BLOCK
    parts = [w_qkv, w_out, w_up, w_down]
    fulls = [full_qkv, full_out, full_up, full_down]
    buffers = [wq, wo, wu, wd]
    steps, arrive, finish = weight_moves(parts + [vectors], fulls + [full_vectors], send_sem, recv_sem, place)

    def in_move(i, source, target, device):
        return pltpu.make_async_remote_copy(
            src_ref=source, dst_ref=target, send_sem=in_send.at[i], recv_sem=in_recv.at[i],
            device_id=device, device_id_type=MESH,
        )

    top, low = pl.ds(0, half), pl.ds(half, half)

    def in_copies(i, source, target):
        stay = pltpu.make_async_copy(source.at[top], target.at[top], in_local.at[i])
        return (
            stay,
            in_move(2 * i + 1, source.at[low], target.at[low], twin),
            in_move(2 * i, source.at[top], target.at[top], diag),
            in_move(2 * i + 1, source.at[low], target.at[low], across),
        )

    tok_copies = in_copies(0, tokens, tok)
    grad_copies = in_copies(1, grads, grads_here)
    seg_stay = pltpu.make_async_copy(segs, seg_nat.at[x], in_local.at[2])
    seg_twin = in_move(4, segs, seg_nat.at[x], twin)
    seg_across = in_move(4, segs, seg_nat.at[x], across)
    seg_diag = pltpu.make_async_remote_copy(
        src_ref=segs, dst_ref=seg_nat.at[x], send_sem=in_send.at[5], recv_sem=in_recv.at[5],
        device_id=diag, device_id_type=MESH,
    )

    @pl.when(here)
    def _():
        for copy in (seg_stay, seg_twin, tok_copies[0], tok_copies[1], grad_copies[0], grad_copies[1]):
            copy.start()

    @pl.when(jnp.logical_not(here))
    def _():
        for copy in (seg_across, seg_diag, tok_copies[2], tok_copies[3], grad_copies[2], grad_copies[3]):
            copy.start()

    def wait_in(copies):
        @pl.when(here)
        def _():
            copies[0].wait()
            copies[1].wait_recv()

        @pl.when(jnp.logical_not(here))
        def _():
            copies[2].wait_recv()
            copies[3].wait_recv()

    def wait_segs():
        @pl.when(here)
        def _():
            seg_stay.wait()
            seg_across.wait_recv()

        @pl.when(jnp.logical_not(here))
        def _():
            seg_twin.wait_recv()
            seg_diag.wait_recv()

    def finish_in():
        @pl.when(here)
        def _():
            grad_copies[0].wait()
            grad_copies[1].wait_recv()
            for copy in (seg_twin, tok_copies[1], grad_copies[1]):
                copy.wait_send()

        @pl.when(jnp.logical_not(here))
        def _():
            grad_copies[2].wait_recv()
            grad_copies[3].wait_recv()
            for copy in (seg_across, seg_diag, tok_copies[2], tok_copies[3], grad_copies[2], grad_copies[3]):
                copy.wait_send()

    comm = steps()
    seen = set()
    loaded = {}
    done_with = set()

    def tick(count=1):
        for _ in range(count):
            label = next(comm, None)
            if label is None:
                return False
            seen.add(label)
            if label[0] == "here":
                fetch_ready()
        return True

    def loads(u):
        layer, m = u
        n = parts[m].shape[1]
        copies = [pltpu.make_async_copy(parts[m].at[layer], buffers[m].at[pl.ds(z * n, n)], load_sem.at[m, 0])]
        for s in range(1, ZN):
            zz = (z + s) % ZN
            copies.append(
                pltpu.make_async_copy(fulls[m].at[layer, zz], buffers[m].at[pl.ds(zz * n, n)], load_sem.at[m, s])
            )
        return copies

    def fetch_ready(upto=None):
        for layer in range(layers):
            for m in range(len(parts)):
                u = (layer, m)
                if u in loaded or ("here", u) not in seen:
                    continue
                if layer and (layer - 1, m) not in done_with:
                    continue
                following = (layer, m + 1) if m + 1 < len(parts) else (layer + 1, 0)
                if u != upto and following[0] < layers and ("here", following) not in seen:
                    continue
                arrive(u)
                if layer:
                    own_rows((layer - 1, m)).wait()
                for copy in loads(u):
                    copy.start()
                loaded[u] = True

    def own_rows(u):
        layer, m = u
        n = parts[m].shape[1]
        return pltpu.make_async_copy(buffers[m].at[pl.ds(z * n, n)], fulls[m].at[layer, z], own_sem.at[layer, m])

    def need(u):
        while ("here", u) not in seen:
            if not tick():
                break
        fetch_ready(u)
        for copy in loads(u):
            copy.wait()
        own_rows(u).start()

    pending = []

    def save(layer, name, buffer):
        copy = pltpu.make_async_copy(buffer, saved[layer][name], save_sem.at[layer, SAVED.index(name)])
        copy.start()
        pending.append(copy)

    def settle():
        while pending:
            pending.pop().wait()

    def row(layer, name):
        return rows[layer, pl.ds(ROW[name], 1), :]

    def make_mask():
        wait_segs()
        joined = jnp.concatenate([seg_nat[0], seg_nat[1]], axis=1).astype(jnp.float32)
        seg_row[...] = jnp.broadcast_to(joined, seg_row.shape)
        column = seg_row[...].T[:, :1]
        for block in range(2):
            base = ((2 * c) if block == 0 else (3 - 2 * c)) * BLOCK
            own = seg_row[0:1, pl.ds(pl.multiple_of(base, BLOCK), BLOCK)]
            spot = lax.broadcasted_iota(jnp.int32, (mask.shape[0], BLOCK), 0)
            mine = lax.broadcasted_iota(jnp.int32, (mask.shape[0], BLOCK), 1) + base
            ok = (column == own) & (spot <= mine)
            mask[:, block * BLOCK : (block + 1) * BLOCK] = jnp.where(ok, 0.0, MASKED).astype(jnp.float32)
        copy = pltpu.make_async_copy(mask, mask_out, save_sem.at[0, len(SAVED)])
        copy.start()
        pending.append(copy)

    def make_rows(layer):
        copies = [
            pltpu.make_async_copy(vectors.at[layer, 0], vecs.at[z], load_sem.at[4, 0])
        ] + [
            pltpu.make_async_copy(full_vectors.at[layer, (z + s) % ZN, 0], vecs.at[(z + s) % ZN], load_sem.at[4, s])
            for s in range(1, ZN)
        ]
        for copy in copies:
            copy.start()
        for copy in copies:
            copy.wait()
        share = vecs.shape[2]
        b_proj[layer, 0:1, :] = jnp.zeros((1, b_proj.shape[2]), jnp.float32)
        for zz in range(ZN):
            block = vecs[zz].astype(jnp.float32)
            rows[layer, 0:8, zz * share : (zz + 1) * share] = block[0:8]
            for name, at in (("b_query", 0), ("b_value", 2 * width)):
                b_proj[layer, 0:1, at + zz * share : at + (zz + 1) * share] = block[ROW[name] : ROW[name] + 1]
            for j in range(ZN):
                at = (zz * ZN + j) * share
                b_up[layer, 0:1, at : at + share] = block[8 + j : 9 + j]

    def swap_moves(layer):
        moves = []
        for i, ref in enumerate((keys, values)):
            for block in range(2):
                at = ((2 * c) if block == 0 else (3 - 2 * c)) * BLOCK
                spot = ref.at[pl.ds(pl.multiple_of(at, BLOCK), BLOCK)]
                moves.append(
                    pltpu.make_async_remote_copy(
                        src_ref=spot, dst_ref=spot, send_sem=kv_send.at[layer, i, block],
                        recv_sem=kv_recv.at[layer, i, block], device_id=twin, device_id_type=MESH,
                    )
                )
        return moves

    def swap_waits(layer):
        moves = []
        for i, ref in enumerate((keys, values)):
            for block in range(2):
                at = ((2 - 2 * c) if block == 0 else (1 + 2 * c)) * BLOCK
                spot = ref.at[pl.ds(pl.multiple_of(at, BLOCK), BLOCK)]
                moves.append(
                    pltpu.make_async_remote_copy(
                        src_ref=spot, dst_ref=spot, send_sem=kv_send.at[layer, i, block],
                        recv_sem=kv_recv.at[layer, i, block], device_id=twin, device_id_type=MESH,
                    )
                )
        return moves

    def matrix(buffer, cols):
        return buffer[:, :, cols].reshape(-1, cols.size)

    def compute(layer):
        if layer == 0:
            for i in range(layers):
                make_rows(i)
                yield
            for i in range(layers):
                copy = pltpu.make_async_copy(rows.at[i], rows_out.at[i], save_sem.at[i, len(SAVED) + 1])
                copy.start()
                pending.append(copy)
            make_mask()
            yield
            wait_in(tok_copies)
            xs[...] = tok[...].astype(jnp.float32)
        else:
            settle()
        save(layer, "x", xs)
        norm_into(xs, row(layer, "attn_gain"), row(layer, "attn_shift"), na)
        save(layer, "normed_attn", na)
        yield
        need((layer, 0))
        total = wq.shape[2]

        for low_at in range(0, total, 4 * BLOCK):
            high_at = min(low_at + 4 * BLOCK, total)
            tiles_between(low_at, high_at, TILE, lambda start, size: project_tile(layer, start, size))
            yield
        done_with.add((layer, 0))
        q[...] = slope[:, :width]
        if layer:
            pl.semaphore_wait(free_sem, 1)
        for block in range(2):
            at = ((2 * c) if block == 0 else (3 - 2 * c)) * BLOCK
            spot = pl.ds(pl.multiple_of(at, BLOCK), BLOCK)
            source = slice(block * BLOCK, (block + 1) * BLOCK)
            keys[spot, :] = slope[source, width : 2 * width]
            values[spot, :] = slope[source, 2 * width : 3 * width]
        for copy in swap_moves(layer):
            copy.start()
        save(layer, "q", q)
        yield
        for copy in swap_waits(layer):
            copy.wait_recv()
        save(layer, "keys", keys)
        save(layer, "values", values)
        for first in range(0, width // (2 * HEAD_DIM) + 1, 4):
            attend(c, q, keys, values, mask, att, lse, first, min(first + 4, width // (2 * HEAD_DIM) + 1))
            yield
        save(layer, "attended", att)
        save(layer, "lse", lse)
        if layer + 1 < layers:
            settle()
            for copy in swap_moves(layer):
                copy.wait_send()
            pl.semaphore_signal(free_sem, inc=1, device_id=twin, device_id_type=MESH)
        need((layer, 1))

        def out_step(start, size):
            cols = pl.ds(start, size)
            middle[:, cols] = xs[:, cols] + product(att[...], matrix(wo, cols)) + rows[layer, pl.ds(ROW["b_out"], 1), cols]

        tiles_between(0, width, BLOCK, out_step)
        done_with.add((layer, 1))
        save(layer, "middle", middle)
        yield
        norm_into(middle, row(layer, "mlp_gain"), row(layer, "mlp_shift"), nm)
        save(layer, "normed_mlp", nm)
        yield
        need((layer, 2))
        settle()

        def up_step(start, size):
            cols = pl.ds(start, size)
            u = product(nm[...], matrix(wu, cols)) + b_up[layer, 0:1, cols]
            square = u * u
            t = jnp.tanh(u * (GELU_A + (GELU_A * GELU_B) * square))
            half_up = 0.5 + 0.5 * t
            act_buf[:, cols] = (u * half_up).astype(jnp.bfloat16)
            slope[:, cols] = (
                half_up + (0.5 * u) * (1.0 - t * t) * (GELU_A + (3.0 * GELU_A * GELU_B) * square)
            ).astype(jnp.bfloat16)

        ff = wu.shape[2]
        for low_at in range(0, ff, 6 * BLOCK):
            tiles_between(low_at, min(low_at + 6 * BLOCK, ff), TILE, up_step)
            yield
        done_with.add((layer, 2))
        save(layer, "slope", slope)
        save(layer, "activated", act_buf)
        need((layer, 3))

        def down_step(start, size):
            cols = pl.ds(start, size)
            xs[:, cols] = middle[:, cols] + product(act_buf[...], matrix(wd, cols)) + rows[layer, pl.ds(ROW["b_down"], 1), cols]

        for low_at in range(0, width, 2 * BLOCK):
            tiles_between(low_at, min(low_at + 2 * BLOCK, width), BLOCK, down_step)
            yield
        done_with.add((layer, 3))

    def project_tile(layer, start, size):
        cols = pl.ds(start, size)
        out = product(na[...], matrix(wq, cols))
        slope[:, cols] = ((out + b_proj[layer, 0:1, cols]) * scale_of(start, size)).astype(jnp.bfloat16)

    def scale_of(start, size):
        lane = lax.broadcasted_iota(jnp.int32, (1, size), 1) + start
        return jnp.where(lane < width, QUERY_SCALE, 1.0).astype(jnp.float32)

    tick()
    for layer in range(layers):
        for _ in compute(layer):
            tick(PACE)
    while tick():
        pass
    settle()
    tok[...] = xs[...].astype(jnp.bfloat16)
    out = pltpu.make_async_copy(tok, result, save_sem.at[0, 0])
    out.start()
    for copy in swap_moves(layers - 1):
        copy.wait_send()
    finish_in()
    finish()
    for m in range(len(parts)):
        own_rows((layers - 1, m)).wait()
    out.wait()


def forward(tokens, grads, segs, vectors, weights):
    rows, width = tokens.shape
    low = jnp.bfloat16
    layers = vectors.shape[0]
    ff = weights[2].shape[3]
    units = len(gather_units(layers, [w.shape for w in weights] + [vectors.shape]))
    shapes = dict(
        x=((rows, width), jnp.float32),
        normed_attn=((rows, width), low),
        q=((rows, width), low),
        keys=((2 * rows, width), low),
        values=((2 * rows, width), low),
        attended=((rows, width), low),
        lse=((HEAD_ROWS, rows), jnp.float32),
        middle=((rows, width), jnp.float32),
        normed_mlp=((rows, width), low),
        slope=((rows, ff), low),
        activated=((rows, ff), low),
    )
    out_shape = (
        [shaped((layers, ZN) + w.shape[1:], low) for w in weights]
        + [
            shaped((layers, ZN) + vectors.shape[1:], low),
            shaped((rows, width), low),
            shaped((rows, width), low),
            shaped((2 * rows, rows)),
            shaped((layers, 16, width)),
        ]
        + [shaped(*shapes[name]) for _ in range(layers) for name in SAVED]
    )
    dma = pltpu.SemaphoreType.DMA
    scratch = [pltpu.VMEM((ZN * w.shape[1],) + w.shape[2:], low) for w in weights] + [
        pltpu.VMEM((rows, width), jnp.float32),
        pltpu.VMEM((rows, width), low),
        pltpu.VMEM((rows, width), low),
        pltpu.VMEM((rows, width), low),
        pltpu.VMEM((rows, width), low),
        pltpu.VMEM((2 * rows, width), low),
        pltpu.VMEM((2 * rows, width), low),
        pltpu.VMEM((2 * rows, rows), jnp.float32),
        pltpu.VMEM((rows, width), low),
        pltpu.VMEM((rows, width), jnp.float32),
        pltpu.VMEM((rows, ff), low),
        pltpu.VMEM((rows, ff), low),
        pltpu.VMEM((HEAD_ROWS, rows), jnp.float32),
        pltpu.VMEM((ZN,) + vectors.shape[2:], low),
        pltpu.VMEM((layers, 16, width), jnp.float32),
        pltpu.VMEM((layers, 8, ff), jnp.float32),
        pltpu.VMEM((layers, 8, 3 * width), jnp.float32),
        pltpu.VMEM((2, 1, rows), jnp.int32),
        pltpu.VMEM((8, 2 * rows), jnp.float32),
        dma((units, ZN, 7)),
        dma((units, ZN, 7)),
        dma((len(weights) + 1, ZN)),
        dma((layers, len(weights))),
        dma((layers, len(SAVED) + 2)),
        dma((layers, 2, 2)),
        dma((layers, 2, 2)),
        dma((6,)),
        dma((6,)),
        dma((3,)),
        pltpu.SemaphoreType.REGULAR,
    ]
    outs = pl.pallas_call(
        forward_body,
        out_shape=out_shape,
        in_specs=anywhere(4 + len(weights)),
        out_specs=anywhere(len(out_shape)),
        scratch_shapes=scratch,
        compiler_params=pltpu.CompilerParams(collective_id=0, has_side_effects=True, vmem_limit_bytes=VMEM_LIMIT),
        name="forward",
    )(tokens, grads, segs, vectors, *weights)
    count = len(weights)
    fulls, rest = outs[:count], outs[count + 5 :]
    _, result, grads_here, mask, vector_rows = outs[count : count + 5]
    saved = [dict(zip(SAVED, rest[i * len(SAVED) : (i + 1) * len(SAVED)])) for i in range(layers)]
    return fulls, result, grads_here, mask, vector_rows, saved


def begin(copies):
    for copy in copies:
        copy.start()


def end(copies):
    for copy in copies:
        copy.wait()


ORDER = (0, 1, 3, 2)
RC, R1, R2, RZ, RX, RY, RD1, RD2, RCC, R1B, RZX = 0, 4, 8, 12, 16, 17, 18, 19, 20, 21, 25


class Group:
    def __init__(self, grad, out, base, k, ready):
        self.grad, self.out, self.base, self.k, self.ready = grad, out, base, k, ready


def reduce_steps(place, groups, acc, stage, first_in, second_in, line_in, line_extra, load_sem, store_sem, send_sem, recv_sem):
    x, y, z, c, across, beside, twin, up, down = place
    p = x * 2 + y
    units = [(g, d) for g in range(len(groups)) for d in ORDER]

    def move(source, target, g, kind, device):
        return pltpu.make_async_remote_copy(
            src_ref=source, dst_ref=target, send_sem=send_sem.at[g, kind], recv_sem=recv_sem.at[g, kind],
            device_id=device, device_id_type=MESH,
        )

    def half_of(g, d, core):
        group = groups[g]
        return group.grad.at[d, pl.ds(group.base + core * 4 * group.k, 4 * group.k)]

    def to_twin(g, d):
        return move(half_of(g, d, 1 - c), acc[g].at[d], g, RC + d, twin)

    def slot(d):
        return ORDER.index(d) % 2

    def load(g, d):
        return pltpu.make_async_copy(half_of(g, d, c), stage[g].at[slot(d)], load_sem.at[g, slot(d)])

    def add(g, d, at, extra, lead, extra_at, n):
        def step(i, carry):
            acc[g][d, at + i] = acc[g][d, at + i] + extra[lead, extra_at + i]
            return carry

        lax.fori_loop(0, n, step, 0)

    def first_moves(g, d):
        k = groups[g].k
        if d in (0, 3):
            return [move(acc[g].at[d, pl.ds((1 - x) * 2 * k, 2 * k)], first_in[g].at[d], g, R1 + d, across)]
        return [
            move(acc[g].at[d, pl.ds((1 - y) * k, k)], first_in[g].at[d, pl.ds(0, k)], g, R1 + d, beside),
            move(acc[g].at[d, pl.ds((3 - y) * k, k)], first_in[g].at[d, pl.ds(k, k)], g, R1B + d, beside),
        ]

    def second_move(g, d):
        k = groups[g].k
        if d in (0, 3):
            return move(acc[g].at[d, pl.ds((x * 2 + 1 - y) * k, k)], second_in[g].at[d], g, R2 + d, beside)
        return move(acc[g].at[d, pl.ds(((1 - x) * 2 + y) * k, k)], second_in[g].at[d], g, R2 + d, across)

    def twin_step(g, d):
        to_twin(g, d).wait_recv()
        load(g, d).wait()
        add(g, d, 0, stage[g], slot(d), 0, 4 * groups[g].k)
        for copy in first_moves(g, d):
            copy.start()
        later = ORDER.index(d) + 2
        if later < len(ORDER):
            load(g, ORDER[later]).start()

    def first_step(g, d):
        k = groups[g].k
        for copy in first_moves(g, d):
            copy.wait_recv()
        if d in (0, 3):
            add(g, d, x * 2 * k, first_in[g], d, 0, 2 * k)
        else:
            add(g, d, y * k, first_in[g], d, 0, k)
            add(g, d, (2 + y) * k, first_in[g], d, k, k)
        second_move(g, d).start()

    def second_step(g, d):
        second_move(g, d).wait_recv()
        add(g, d, p * groups[g].k, second_in[g], d, 0, groups[g].k)

    def piece(g, d):
        return acc[g].at[d, pl.ds(p * groups[g].k, groups[g].k)]

    def to_down(g, d, zz):
        if d == zz - 1:
            return move(piece(g, d), line_extra[g].at[0], g, RZX, down)
        return move(piece(g, d), line_in[g].at[d], g, RZ + d, down)

    def to_up(g, d, zz):
        return move(piece(g, d), line_in[g].at[d], g, RZ + d, up)

    def rows_of(g, px, py, low=0, n=None):
        group = groups[g]
        return group.out.at[pl.ds(group.base + (c * 4 + px * 2 + py) * group.k + low, group.k if n is None else n)]

    def share_across(g):
        return move(piece(g, z), rows_of(g, x, y), g, RX, across)

    def share_beside(g):
        return move(piece(g, z), rows_of(g, x, y), g, RY, beside)

    def store(g):
        return pltpu.make_async_copy(piece(g, z), rows_of(g, x, y), store_sem.at[g])

    def arrived(g, px, py, kind):
        return move(rows_of(g, px, py), rows_of(g, px, py), g, kind, across)

    def corner(g, px, py, part):
        k = groups[g].k
        low, n = (0, max(k // 2, 1)) if part == 0 else (k // 2, k - k // 2)
        rows = rows_of(g, px, py, low, n)
        return move(rows, rows, g, RD1 if part == 0 else RD2, beside if part == 0 else across)

    def to_core(g, core):
        group = groups[g]
        rows = group.out.at[pl.ds(group.base + core * 4 * group.k, 4 * group.k)]
        return move(rows, rows, g, RCC, twin)

    def line_step(g, d, s):
        k = groups[g].k
        for zz in range(ZN):
            downward = d < zz and zz == ZN - 1 - s
            upward = d > zz and zz == s
            last = d == zz and s == ZN - 1
            if not (downward or upward or last):
                continue

            @pl.when(z == zz)
            def _():
                if downward:
                    if zz < ZN - 1:
                        to_down(g, d, zz + 1).wait_recv()
                        add(g, d, p * k, line_in[g], d, 0, k)
                    to_down(g, d, zz).start()
                if upward:
                    if zz > 0:
                        to_up(g, d, zz - 1).wait_recv()
                        add(g, d, p * k, line_in[g], d, 0, k)
                    to_up(g, d, zz).start()
                if last:
                    if zz > 0:
                        to_up(g, d, zz - 1).wait_recv()
                        add(g, d, p * k, line_in[g], d, 0, k)
                    if zz < ZN - 1:
                        to_down(g, d, zz + 1).wait_recv()
                        add(g, d, p * k, line_extra[g], 0, 0, k)
                    share_across(g).start()
                    share_beside(g).start()
                    store(g).start()

    def corner_step(g, d):
        @pl.when(z == d)
        def _():
            arrived(g, 1 - x, y, RX).wait_recv()
            corner(g, 1 - x, y, 0).start()
            arrived(g, x, 1 - y, RY).wait_recv()
            if groups[g].k > 1:
                corner(g, x, 1 - y, 1).start()

    def core_step(g, d):
        @pl.when(z == d)
        def _():
            store(g).wait()
            corner(g, 1 - x, 1 - y, 0).wait_recv()
            if groups[g].k > 1:
                corner(g, 1 - x, 1 - y, 1).wait_recv()
            to_core(g, c).start()

    def finish():
        for g, d in units:
            to_twin(g, d).wait_send()
            for copy in first_moves(g, d) + [second_move(g, d)]:
                copy.wait_send()
            for zz in range(ZN):
                if d == zz:
                    continue

                @pl.when(z == zz)
                def _():
                    (to_down(g, d, zz) if d < zz else to_up(g, d, zz)).wait_send()

            @pl.when(z == d)
            def _():
                to_core(g, 1 - c).wait_recv()
                share_across(g).wait_send()
                share_beside(g).wait_send()
                corner(g, 1 - x, y, 0).wait_send()
                if groups[g].k > 1:
                    corner(g, x, 1 - y, 1).wait_send()
                to_core(g, c).wait_send()

    count = len(units)
    stages = [(0, twin_step), (SKEW, first_step), (2 * SKEW, second_step)]
    stages += [((2 + s) * SKEW, functools.partial(line_step, s=s)) for s in range(ZN)]
    stages += [((2 + ZN) * SKEW, corner_step), ((3 + ZN) * SKEW, core_step)]

    def steps():
        for t in range(count + stages[-1][0]):
            for g, d in units[AHEAD + t - 1 : AHEAD + t] if t else units[:AHEAD]:
                yield groups[g].ready
                to_twin(g, d).start()
                if ORDER.index(d) < 2:
                    load(g, d).start()
            for delay, step in stages:
                if 0 <= t - delay < count:
                    step(*units[t - delay])
                    yield True

    return steps(), finish


def reduce_scratch(groups):
    low = jnp.bfloat16
    buffers = []
    for lead, rows in ((ZN, 4), (2, 4), (ZN, 2), (ZN, 1), (ZN, 1), (1, 1)):
        buffers += [pltpu.VMEM((lead, rows * k) + shape, low) for k, shape in groups]
    dma = pltpu.SemaphoreType.DMA
    n = len(groups)
    return buffers + [dma((n, 2)), dma((n,)), dma((n, 26)), dma((n, 26))]


def take_reduce(place, spec, grads, outs, refs, made_here=()):
    n = len(spec)
    groups = [Group(grads[m], outs[m], base, k, m if m in made_here else True) for m, base, k in spec]
    lists = [refs[i * n : (i + 1) * n] for i in range(6)]
    return reduce_steps(place, groups, *lists, *refs[6 * n : 6 * n + 4])


def spread_steps(work, comm, finish):
    done = {True}
    blocked = None
    for made in work:
        done.add(made)
        for _ in range(REDUCE_PACE):
            if blocked is not None and blocked not in done:
                break
            blocked = next(comm, True)
    for _ in comm:
        pass
    finish()


def ship_moves(place, source, target, local_sem, send_sem, recv_sem):
    x, y, z, c, across, beside, twin, up, down = place
    diag = (1 - x, z, y * 2 + (1 - c))
    top, low = pl.ds(0, BLOCK), pl.ds(BLOCK, BLOCK)

    def move(i, rows, device):
        return pltpu.make_async_remote_copy(
            src_ref=source.at[rows], dst_ref=target.at[rows], send_sem=send_sem.at[i], recv_sem=recv_sem.at[i],
            device_id=device, device_id_type=MESH,
        )

    stay = pltpu.make_async_copy(source.at[top], target.at[top], local_sem.at[0])

    def start():
        @pl.when(c == x)
        def _():
            stay.start()
            move(1, low, across).start()

        @pl.when(c != x)
        def _():
            move(0, top, diag).start()
            move(1, low, twin).start()

    def wait():
        @pl.when(c == x)
        def _():
            stay.wait()
            move(1, low, across).wait()

        @pl.when(c != x)
        def _():
            move(0, top, diag).wait()
            move(1, low, twin).wait()

    return start, wait


def ship_scratch():
    dma = pltpu.SemaphoreType.DMA
    return [dma((1,)), dma((2,)), dma((2,))]


def meet(ship):
    place = neighbours()
    x, y, z, c, across, beside, twin, up, down = place
    diag = (1 - x, z, y * 2 + (1 - c)) if ship else None
    greet(z, c, x, across, beside, twin, diag, up, down)
    return place


def spec_of(shapes):
    spec = []
    for m, shape in enumerate(shapes):
        k = shape[1] // 8
        split = min(k, 1 if shape[3] > 2048 else 2)
        for base in range(0, k, split):
            spec.append((m, base * 8, split))
    return spec


def stream(source, buffer, sems, width_rows, act):
    chunks = source.shape[0]
    per = buffer.shape[1]
    whole, left = chunks // per, chunks % per

    def fetch(i, n):
        return pltpu.make_async_copy(
            source.at[pl.ds(i * per, n)], buffer.at[i % 2, pl.ds(0, n)], sems.at[i % 2]
        )

    def begin():
        fetch(0, per).start()

    def run(low, high):
        def step(i, carry):
            fetch(i, per).wait()

            @pl.when(i + 1 < whole)
            def _():
                fetch(i + 1, per).start()

            if left:

                @pl.when(i + 1 == whole)
                def _():
                    fetch(whole, left).start()

            act(pl.multiple_of(i * per * 16, per * 16), per * 16, buffer[i % 2].reshape(per * 16, -1))
            return carry

        if low < min(high, whole):
            lax.fori_loop(low, min(high, whole), step, 0)
        if high > whole and left:
            fetch(whole, left).wait()
            act(whole * per * 16, left * 16, buffer[whole % 2, :left].reshape(left * 16, -1))

    return begin, run, whole + (1 if left else 0)


def each(low, high, size):
    return [(at, min(at + size, high)) for at in range(low, high, size)]


def mlp_work(layer, ins, outs, refs, made_down):
    grad_in, middle_in, slope_in, normed_in, activated_in, gain, w_out, w_up, w_down = ins
    g_middle_out, g_branch_out, g_attended_out, dw_up, dw_down, gb_down, gb_up, g_gain, g_shift, gb_out = outs
    (
        grad, middle, g_norm, slope, g_mlp, g_branch, g_att, nm, turned,
        narrow, broad, act_tiles, down_tiles, up_tiles, load_sem, narrow_sem, broad_sem, act_sem, down_sem, up_sem,
    ) = refs
    width = grad.shape[1]
    ff = slope.shape[1]
    loads = [
        pltpu.make_async_copy(a, b, load_sem.at[i])
        for i, (a, b) in enumerate(((grad_in, g_mlp if grad_in.dtype == jnp.bfloat16 else grad), (middle_in, middle), (slope_in, slope), (normed_in, nm)))
    ]
    begin(loads)

    def down_act(start, size, rows):
        cols = pl.ds(start, size)
        g = (dot_nt(g_mlp[...], rows) * slope[:, cols].astype(jnp.float32)).astype(jnp.bfloat16)
        slope[:, cols] = g
        gb_up[:, cols] = jnp.sum(g.astype(jnp.float32), axis=0, keepdims=True)

    def up_act(start, size, rows):
        g_norm[:, pl.ds(start, size)] = dot_nt(slope[...], rows)

    def out_act(start, size, rows):
        g_att[:, pl.ds(start, size)] = dot_nt(g_branch[...], rows).astype(jnp.bfloat16)

    down_begin, down_run, down_n = stream(w_down.at[layer], narrow, narrow_sem, 0, down_act)
    up_begin, up_run, up_n = stream(w_up.at[layer], broad, broad_sem, 0, up_act)
    out_begin, out_run, out_n = stream(w_out.at[layer], narrow, narrow_sem, 0, out_act)
    down_begin()
    up_begin()
    loads[0].wait()
    if grad_in.dtype == jnp.bfloat16:
        grad[...] = g_mlp[...].astype(jnp.float32)
    else:
        g_mlp[...] = grad[...].astype(jnp.bfloat16)
    gb_down[...] = jnp.sum(g_mlp[...].astype(jnp.float32), axis=0, keepdims=True)
    yield
    tile = act_tiles.shape[2]

    def bring_act(i, n):
        return pltpu.make_async_copy(
            activated_in.at[:, pl.ds(pl.multiple_of(i * tile, tile), n)], act_tiles.at[i % 2, :, pl.ds(0, n)], act_sem.at[i % 2]
        )

    def send_down(i, n):
        return pltpu.make_async_copy(
            down_tiles.at[i % 2, pl.ds(0, n // 16)], dw_down.at[pl.ds(i * (tile // 16), n // 16)], down_sem.at[i % 2]
        )

    whole, left = ff // tile, ff % tile
    bring_act(0, tile).start()

    def down_grad(i, carry):
        bring_act(i, tile).wait()

        @pl.when(i + 1 < whole)
        def _():
            bring_act(i + 1, tile).start()

        if left:

            @pl.when(i + 1 == whole)
            def _():
                bring_act(whole, left).start()

        @pl.when(i >= 2)
        def _():
            send_down(i - 2, tile).wait()

        out = dot_tn(act_tiles[i % 2], g_mlp[...]).astype(jnp.bfloat16)
        down_tiles[i % 2] = out.reshape(tile // 16, 16, width)
        send_down(i, tile).start()
        return carry

    for low, high in each(0, whole, 4):
        lax.fori_loop(low, high, down_grad, 0)
        yield
    if left:
        bring_act(whole, left).wait()
        send_down(whole - 2, tile).wait()
        out = dot_tn(act_tiles[whole % 2, :, :left], g_mlp[...]).astype(jnp.bfloat16)
        down_tiles[whole % 2, : left // 16] = out.reshape(left // 16, 16, width)
        send_down(whole, left).start()
    send_down(whole - 1, tile).wait()
    if left:
        send_down(whole, left).wait()
    else:
        send_down(whole - 2, tile).wait()
    yield made_down

    loads[2].wait()
    for low, high in each(0, down_n, 4):
        down_run(low, high)
        yield
    out_begin()
    for low, high in each(0, up_n, 2):
        up_run(low, high)
        yield
    loads[1].wait()
    norm_back(middle, g_norm, grad, gain[...], grad, g_gain, g_shift, g_branch)
    saves = [pltpu.make_async_copy(grad, g_middle_out, load_sem.at[0]), pltpu.make_async_copy(g_branch, g_branch_out, load_sem.at[1])]
    begin(saves)
    gb_out[...] = jnp.sum(g_branch[...].astype(jnp.float32), axis=0, keepdims=True)
    yield
    out_run(0, out_n)
    saves.append(pltpu.make_async_copy(g_att, g_attended_out, load_sem.at[2]))
    begin(saves[2:])
    loads[3].wait()
    turned[...] = nm[...].T
    yield

    step = up_tiles.shape[3]

    def send_up(i):
        return pltpu.make_async_copy(
            up_tiles.at[i % 2], dw_up.at[:, :, pl.ds(pl.multiple_of(i * step, step), step)], up_sem.at[i % 2]
        )

    def up_grad(i, carry):
        @pl.when(i >= 2)
        def _():
            send_up(i - 2).wait()

        out = product(turned[...], slope[:, pl.ds(pl.multiple_of(i * step, step), step)]).astype(jnp.bfloat16)
        up_tiles[i % 2] = out.reshape(width // 16, 16, step)
        send_up(i).start()
        return carry

    for low, high in each(0, ff // step, 4):
        lax.fori_loop(low, high, up_grad, 0)
        yield
    send_up(ff // step - 2).wait()
    send_up(ff // step - 1).wait()
    end(saves)


def mlp_refs(rows, width, ff):
    low = jnp.bfloat16
    dma = pltpu.SemaphoreType.DMA
    return (
        [pltpu.VMEM((rows, width), jnp.float32)] * 3
        + [pltpu.VMEM((rows, ff), low)]
        + [pltpu.VMEM((rows, width), low)] * 4
        + [
            pltpu.VMEM((width, rows), low),
            pltpu.VMEM((2, 16, 16, width), low),
            pltpu.VMEM((2, 16, 16, ff), low),
            pltpu.VMEM((2, rows, 512), low),
            pltpu.VMEM((2, 32, 16, width), low),
            pltpu.VMEM((2, width // 16, 16, BLOCK), low),
            dma((4,)), dma((2,)), dma((2,)), dma((2,)), dma((2,)), dma((2,)),
        ]
    )


def attend_work(layer, place, ins, outs, refs):
    q_in, g_att_in, lse_in, mask_in, keys_in, values_in, x_in, g_middle_in, normed_in, attended_in, g_branch_in, gain, w_qkv = ins
    g_x_out, dw_qkv, dw_out, gb_q, gb_v, g_gain, g_shift = outs
    (
        q, g_att, lse, mask, keys, values, g_q, g_k, g_v, g_nat, got, xs, grad, g_norm, g_proj, turned,
        tall, tiles_qkv, tiles_out, load_sem, tall_sem, qkv_sem, out_sem, swap_send, swap_recv,
    ) = refs
    c, twin = place[3], place[6]
    width = xs.shape[1]
    pairs = (
        (q_in, q), (g_att_in, g_att), (lse_in, lse), (mask_in, mask), (keys_in, keys), (values_in, values),
        (x_in, xs), (g_middle_in, grad),
    )
    loads = [pltpu.make_async_copy(a, b, load_sem.at[i]) for i, (a, b) in enumerate(pairs)]
    begin(loads)

    def norm_act(start, size, rows):
        g_norm[:, pl.ds(start, size)] = dot_nt(g_proj[...], rows)

    tall_begin, tall_run, tall_n = stream(w_qkv.at[layer], tall, tall_sem, 0, norm_act)
    tall_begin()
    end(loads[:6])
    yield

    def slab(start, size, head):
        cols = pl.ds(start, size)
        g_k[...] = jnp.zeros_like(g_k)
        g_v[...] = jnp.zeros_like(g_v)
        lanes = slice(0, size)
        for variant in range(2):

            @pl.when(c == variant)
            def _():
                for row, high in RANGES[variant]:
                    rows = slice(row, row + BLOCK)
                    qs, gs = q[rows, cols], g_att[rows, cols]
                    ks, vs = keys[:high, cols], values[:high, cols]
                    parts = []
                    for j in range(size // HEAD_DIM):
                        q_j, g_j = of_head(qs, j), of_head(gs, j)
                        s = dot_nt(ks, q_j) + mask[:high, rows]
                        p = jnp.exp(s - lse[pl.ds(head + j, 1), rows])
                        g_p = p * dot_nt(vs, g_j)
                        inner = jnp.sum(g_p, axis=0, keepdims=True)
                        g_s = (g_p - p * inner).astype(jnp.bfloat16)
                        g_v[:high, lanes] += product(p.astype(jnp.bfloat16), g_j)
                        g_k[:high, lanes] += product(g_s, q_j)
                        parts.append(dot_tn(ks, g_s)[j * HEAD_DIM : (j + 1) * HEAD_DIM])
                    out = jnp.concatenate(parts, axis=0) if len(parts) > 1 else parts[0]
                    g_q[rows, cols] = out.T.astype(jnp.bfloat16) * QUERY_SCALE

        g_nat[0, :, cols] = g_k[:, lanes].astype(jnp.bfloat16)
        g_nat[1, :, cols] = g_v[:, lanes].astype(jnp.bfloat16)

    slab_count = width // (2 * HEAD_DIM) + 1
    for first, last in each(0, slab_count, 2):
        over_slabs(width, slab, first, last)
        yield

    def spot(who, block):
        at = ((2 * who) if block == 0 else (3 - 2 * who)) * BLOCK
        return pl.ds(pl.multiple_of(at, BLOCK), BLOCK)

    swaps = [
        pltpu.make_async_remote_copy(
            src_ref=g_nat.at[i, spot(1 - c, block)], dst_ref=got.at[i, pl.ds(block * BLOCK, BLOCK)],
            send_sem=swap_send.at[i, block], recv_sem=swap_recv.at[i, block], device_id=twin, device_id_type=MESH,
        )
        for i in range(2)
        for block in range(2)
    ]
    begin(swaps)
    more = [
        pltpu.make_async_copy(attended_in, q, load_sem.at[0]),
        pltpu.make_async_copy(g_branch_in, g_att, load_sem.at[1]),
    ]
    begin(more)
    g_proj[:, :width] = g_q[...]
    gb_q[...] = jnp.sum(g_q[...].astype(jnp.float32), axis=0, keepdims=True)
    yield
    end(more)
    turned[...] = q[...].T
    rows = tiles_out.shape[1] * 16

    def row_grad(right, tiles_ref, sem, target, i):
        def act(start, size):
            cols = pl.ds(start, size)
            out = product(turned[pl.ds(i * rows, rows), :], right[:, cols]).astype(jnp.bfloat16)
            tiles_ref[i % 2, :, :, cols] = out.reshape(rows // 16, 16, size)

        if i >= 2:
            row_send(tiles_ref, sem, target, i - 2).wait()
        tiles_between(0, right.shape[1], BLOCK, act)
        row_send(tiles_ref, sem, target, i).start()

    def row_send(tiles_ref, sem, target, i):
        return pltpu.make_async_copy(tiles_ref.at[i % 2], target.at[pl.ds(i * (rows // 16), rows // 16)], sem.at[i % 2])

    for i in range(ZN):
        row_grad(g_att, tiles_out, out_sem, dw_out, i)
    yield
    after = pltpu.make_async_copy(normed_in, q, load_sem.at[0])
    after.start()
    for copy in swaps:
        copy.wait_recv()
    for block in range(2):
        part = slice(block * BLOCK, (block + 1) * BLOCK)
        g_proj[part, width : 2 * width] = g_nat[0, spot(c, block), :] + got[0, part, :]
        values_part = g_nat[1, spot(c, block), :] + got[1, part, :]
        g_proj[part, 2 * width :] = values_part
        total = jnp.sum(values_part.astype(jnp.float32), axis=0, keepdims=True)
        gb_v[...] = total if block == 0 else gb_v[...] + total
    yield
    for low, high in each(0, tall_n, 2):
        tall_run(low, high)
        yield
    end(loads[6:])
    norm_back(xs, g_norm, grad, gain[...], grad, g_gain, g_shift)
    if g_x_out.dtype == jnp.bfloat16:
        g_att[...] = grad[...].astype(jnp.bfloat16)
        save = pltpu.make_async_copy(g_att, g_x_out, load_sem.at[1])
    else:
        save = pltpu.make_async_copy(grad, g_x_out, load_sem.at[1])
    save.start()
    after.wait()
    turned[...] = q[...].T
    yield
    for i in range(ZN):
        row_grad(g_proj, tiles_qkv, qkv_sem, dw_qkv, i)
        yield
    for i in (ZN - 2, ZN - 1):
        row_send(tiles_out, out_sem, dw_out, i).wait()
        row_send(tiles_qkv, qkv_sem, dw_qkv, i).wait()
    for copy in swaps:
        copy.wait_send()
    save.wait()


def attend_refs(rows, width):
    low = jnp.bfloat16
    dma = pltpu.SemaphoreType.DMA
    share = width // 16 // ZN
    return [
        pltpu.VMEM((rows, width), low),
        pltpu.VMEM((rows, width), low),
        pltpu.VMEM((HEAD_ROWS, rows), jnp.float32),
        pltpu.VMEM((2 * rows, rows), jnp.float32),
        pltpu.VMEM((2 * rows, width), low),
        pltpu.VMEM((2 * rows, width), low),
        pltpu.VMEM((rows, width), low),
        pltpu.VMEM((2 * rows, 2 * HEAD_DIM), jnp.float32),
        pltpu.VMEM((2 * rows, 2 * HEAD_DIM), jnp.float32),
        pltpu.VMEM((2, 2 * rows, width), low),
        pltpu.VMEM((2, rows, width), low),
        pltpu.VMEM((rows, width), jnp.float32),
        pltpu.VMEM((rows, width), jnp.float32),
        pltpu.VMEM((rows, width), jnp.float32),
        pltpu.VMEM((rows, 3 * width), low),
        pltpu.VMEM((width, rows), low),
        pltpu.VMEM((2, 16, 16, 3 * width), low),
        pltpu.VMEM((2, share, 16, 3 * width), low),
        pltpu.VMEM((2, share, 16, width), low),
        dma((8,)), dma((2,)), dma((2,)), dma((2,)), dma((2, 2)), dma((2, 2)),
    ]


def mlp_kernel(layer, grad, kept, gain, fulls, grads):
    rows, width = grad.shape
    ff = kept["slope"].shape[1]
    low = jnp.bfloat16
    ins = [grad, kept["middle"], kept["slope"], kept["normed_mlp"], kept["activated"], gain, fulls[1], fulls[2], fulls[3]]
    down_shape = (ZN, ff // 16 // ZN, 16, width)
    work_out = [
        shaped((rows, width)),
        shaped((rows, width), low),
        shaped((rows, width), low),
        shaped((width // 16, 16, ff), low),
        shaped((ff // 16, 16, width), low),
    ] + [shaped((1, n)) for n in (width, ff, width, width, width)]
    work_refs = mlp_refs(rows, width, ff)
    n, extra = len(work_out), len(grads)
    shapes = [g.shape for g in grads] + [down_shape]
    spec = spec_of(shapes)

    def body(*refs):
        i = len(ins) + extra
        outs, more = refs[i : i + n], refs[i + n : i + n + extra + 1]
        rest = refs[i + n + extra + 1 :]
        place = meet(False)
        down_rows = Rows(outs[4], down_shape[1])
        comm, finish = take_reduce(
            place, spec, list(refs[len(ins) : i]) + [down_rows], more, rest[len(work_refs) :], (extra,)
        )
        work = mlp_work(layer, refs[: len(ins)], outs, rest[: len(work_refs)], extra)
        spread_steps(work, comm, finish)

    outs = pl.pallas_call(
        body,
        out_shape=work_out + [shaped(shape[1:], low) for shape in shapes],
        in_specs=anywhere(5) + whole(1) + anywhere(3 + extra),
        out_specs=anywhere(5) + whole(5) + anywhere(extra + 1),
        scratch_shapes=work_refs + reduce_scratch([(k, shapes[m][2:]) for m, _, k in spec]),
        compiler_params=pltpu.CompilerParams(
            collective_id=100 + layer, has_side_effects=True, vmem_limit_bytes=VMEM_LIMIT
        ),
        name="mlp_back",
    )(*ins, *grads)
    return outs[:n], outs[n:]


class Rows:
    def __init__(self, ref, n):
        self.ref, self.n, self.at = ref, n, self

    def __getitem__(self, where):
        d, chunks = where
        return self.ref.at[pl.ds(d * self.n + chunks.start, chunks.size)]


def attend_kernel(layer, kept, mask, g_att, g_middle, g_branch, gain, fulls, grads, ship):
    rows, width = g_middle.shape
    low = jnp.bfloat16
    ins = [
        kept["q"], g_att, kept["lse"], mask, kept["keys"], kept["values"], kept["x"], g_middle,
        kept["normed_attn"], kept["attended"], g_branch, gain, fulls[0],
    ]
    work_out = [
        shaped((rows, width), jnp.float32 if layer else low),
        shaped((width // 16, 16, 3 * width), low),
        shaped((width // 16, 16, width), low),
    ] + [shaped((1, width))] * 4
    work_refs = attend_refs(rows, width)
    ships = [ship] if ship is not None else []
    n, extra, k = len(work_out), len(grads), len(ships)
    spec = spec_of([g.shape for g in grads])
    buffers = reduce_scratch([(depth, grads[m].shape[2:]) for m, _, depth in spec])

    def body(*refs):
        i = len(ins) + extra + k
        outs, more = refs[i : i + n], refs[i + n : i + n + extra]
        rest = refs[i + n + extra + k :]
        place = meet(bool(k))
        if k:
            start, wait = ship_moves(place, refs[i - 1], refs[i + n + extra], *rest[-3:])
            start()
        comm, finish = take_reduce(place, spec, refs[len(ins) : i - k], more, rest[len(work_refs) :])
        work = attend_work(layer, place, refs[: len(ins)], outs, rest[: len(work_refs)])
        spread_steps(work, comm, finish)
        if k:
            wait()

    outs = pl.pallas_call(
        body,
        out_shape=work_out + [shaped(g.shape[1:], low) for g in grads] + [shaped(v.shape, v.dtype) for v in ships],
        in_specs=anywhere(11) + whole(1) + anywhere(1 + extra + k),
        out_specs=anywhere(3) + whole(4) + anywhere(extra + k),
        scratch_shapes=work_refs + buffers + (ship_scratch() if k else []),
        compiler_params=pltpu.CompilerParams(
            collective_id=200 + layer, has_side_effects=True, vmem_limit_bytes=VMEM_LIMIT
        ),
        name="attend_back",
    )(*ins, *grads, *ships)
    return outs[:n], outs[n : n + extra], outs[n + extra :]


def reduce_kernel(grads, ship):
    extra = len(grads)
    spec = spec_of([g.shape for g in grads])

    def body(*refs):
        place = meet(True)
        rest = refs[2 * extra + 2 :]
        start, wait = ship_moves(place, refs[extra], refs[2 * extra + 1], *rest[-3:])
        start()
        comm, finish = take_reduce(place, spec, refs[:extra], refs[extra + 1 : 2 * extra + 1], rest)
        spread_steps((), comm, finish)
        wait()

    outs = pl.pallas_call(
        body,
        out_shape=[shaped(g.shape[1:], g.dtype) for g in grads] + [shaped(ship.shape, ship.dtype)],
        in_specs=anywhere(extra + 1),
        out_specs=anywhere(extra + 1),
        scratch_shapes=reduce_scratch([(k, grads[m].shape[2:]) for m, _, k in spec]) + ship_scratch(),
        compiler_params=pltpu.CompilerParams(collective_id=2, has_side_effects=True, vmem_limit_bytes=VMEM_LIMIT),
        name="reduce_grads",
    )(*grads, ship)
    return outs[:extra], outs[extra]


def assemble_body(layers, *refs):
    ins = [refs[layer * 5 : (layer + 1) * 5] for layer in range(layers)]
    outs = refs[layers * 5 : layers * 5 + 4]
    vectors = refs[layers * 5 + 4 : layers * 5 + 13]
    rest = refs[layers * 5 + 13 :]
    held, made = rest[:5], rest[5:9]
    in_sem, out_sem = rest[9:]
    width = held[4].shape[3]
    loads, stores = [], []
    for layer in range(layers):
        loads.append(
            [pltpu.make_async_copy(ins[layer][m], held[m].at[layer], in_sem.at[layer, m]) for m in range(5)]
        )
        begin(loads[-1])
    for layer in range(layers):
        loads[layer][4].wait()
        piece = 0
        for m in range(4):
            loads[layer][m].wait()
            n = held[m].shape[1]
            whole_n = n // 8 * 8
            if layer:
                stores[m].wait()

            def widen(i, carry, m=m):
                made[m][i] = held[m][layer, i].astype(jnp.float32)
                return carry

            lax.fori_loop(0, whole_n, widen, 0)
            for i in range(whole_n, n):
                for at in range(0, held[m].shape[3], width):
                    made[m][i, :, at : at + width] = held[4][layer, piece].astype(jnp.float32)
                    piece += 1
            copy = pltpu.make_async_copy(made[m], outs[m].at[layer], out_sem.at[layer, m])
            copy.start()
            if layer:
                stores[m] = copy
            else:
                stores.append(copy)
        flat = held[4][layer, piece].astype(jnp.float32)
        at = 0
        for ref in vectors:
            n = ref.shape[1]
            ref[layer : layer + 1, :] = flat[at // width : at // width + 1, at % width : at % width + n]
            at += n
    for copy in stores:
        copy.wait()


def assemble(reduced, vector_sizes):
    layers = len(reduced)
    low = jnp.bfloat16
    shapes = [r.shape for r in reduced[0]]
    dma = pltpu.SemaphoreType.DMA
    outs = pl.pallas_call(
        functools.partial(assemble_body, layers),
        out_shape=[shaped((layers,) + shape) for shape in shapes[:4]] + [shaped((layers, n)) for n in vector_sizes],
        in_specs=anywhere(5 * layers),
        out_specs=anywhere(4) + whole(len(vector_sizes)),
        scratch_shapes=[pltpu.VMEM((layers,) + shape, low) for shape in shapes]
        + [pltpu.VMEM(shape, jnp.float32) for shape in shapes[:4]]
        + [dma((layers, 5)), dma((layers, 4))],
        compiler_params=params(),
        name="assemble",
    )(*[r for entry in reduced for r in entry])
    return outs[:4], outs[4:]


VECTORS = (0, 1, 3, 4, 6, 7, 8, 12, 10)
MATRICES = (2, 5, 9, 11)


def wide_of(weight_grads, vector_grads):
    width = weight_grads[0].shape[3]

    def pieces(g):
        left = g[:, g.shape[1] // 8 * 8 :]
        parts = left.shape[3] // width
        return jnp.swapaxes(left.reshape(ZN, left.shape[1], 16, parts, width), 2, 3).reshape(ZN, -1, 16, width)

    vectors = jnp.concatenate([g.reshape(ZN, -1) for g in vector_grads], axis=1).astype(jnp.bfloat16)
    vectors = vectors.reshape(ZN, 1, -1, width)
    vectors = jnp.pad(vectors, ((0, 0), (0, 0), (0, 16 - vectors.shape[2]), (0, 0)))
    wide = jnp.concatenate([pieces(g) for g in weight_grads] + [vectors], axis=1)
    return jnp.pad(wide, ((0, 0), (0, -wide.shape[1] % 8), (0, 0), (0, 0)))


def on_cores(tokens, segments, grad_out, *params):
    rows, width = tokens.shape[1:]
    layers = params[0].shape[0]
    weights = [params[i].reshape(layers, -1, 16, params[i].shape[2]) for i in MATRICES]
    vectors = jnp.concatenate([params[i].reshape(layers, -1, params[0].shape[1]) for i in VECTORS], axis=1)
    vectors = jnp.pad(vectors, ((0, 0), (0, 16 - vectors.shape[1]), (0, 0)))[:, None]
    fulls, result, grad, mask, vector_rows, saved = forward(tokens[0], grad_out[0], segments, vectors, weights)
    fulls = [full.reshape(layers, -1, 16, full.shape[4]) for full in fulls]
    reduced = [None] * layers
    waiting = []
    ship = result
    for layer in reversed(range(layers)):
        kept = saved[layer]
        attn_gain, mlp_gain = vector_rows[layer, 0:1], vector_rows[layer, 5:6]
        (g_middle, g_branch, g_att, dw_up, dw_down, gb_down, gb_up, gm_gain, gm_shift, gb_out), sums = mlp_kernel(
            layer, grad, kept, mlp_gain, fulls, waiting
        )
        if waiting:
            reduced[layer + 1].extend(sums[:-1])
        reduced[layer] = [sums[-1]]
        dw_up, dw_down = dw_up.reshape(ZN, -1, 16, dw_up.shape[2]), dw_down.reshape(ZN, -1, 16, width)
        (grad, dw_qkv, dw_out, gb_q, gb_v, ga_gain, ga_shift), sums, shipped = attend_kernel(
            layer, kept, mask, g_att, g_middle, g_branch, attn_gain, fulls, [dw_up], ship
        )
        if ship is not None:
            result, ship = shipped[0], None
        reduced[layer].extend(sums)
        waiting = [dw.reshape(ZN, -1, 16, dw.shape[2]) for dw in (dw_out, dw_qkv)]
        vector_grads = (ga_gain, ga_shift, gb_q, gb_v, gb_out, gm_gain, gm_shift, gb_down, gb_up)
        waiting.append(wide_of([dw_down, dw_up] + waiting, vector_grads))
    sums, grad = reduce_kernel(waiting, grad)
    reduced[0].extend(sums)
    (down, up, out, qkv), vector_outs = assemble(reduced, [params[i].shape[1] for i in VECTORS])
    final = [None] * 13
    for i, value in ((11, down), (9, up), (5, out), (2, qkv)):
        final[i] = value.reshape(layers, -1, value.shape[3])
    for i, value in zip(VECTORS, vector_outs):
        final[i] = value
    return (result[None], grad[None], *final)


def on_device(
    tokens,
    segments,
    grad_out,
    attn_gain,
    attn_shift,
    w_qkv,
    b_query,
    b_value,
    w_out,
    b_out,
    mlp_gain,
    mlp_shift,
    w_up,
    b_up,
    w_down,
    b_down,
):
    seg_own = segments[0]
    seg_all = lax.all_gather(seg_own, "seq", axis=0, tiled=True)
    offset = lax.axis_index("seq") * seg_own.shape[0]
    visible = visible_mask(seg_own, seg_all, offset)
    layer_count = attn_gain.shape[0]
    resid = tokens[0].astype(jnp.float32)
    kept_weights = []
    stored_list = []
    for layer_index in range(layer_count):
        gathered = gather_layer(
            layer_index,
            attn_gain,
            attn_shift,
            w_qkv,
            b_query,
            b_value,
            w_out,
            b_out,
            mlp_gain,
            mlp_shift,
            w_up,
            b_up,
            w_down,
            b_down,
        )
        resid, stored = forward_layer(resid, gathered, visible, Halves())
        kept_weights.append(gathered)
        stored_list.append(stored)
    result = resid.astype(jnp.bfloat16)[None]
    grad_resid = grad_out[0].astype(jnp.float32)
    reduced = [None] * layer_count
    for layer_index in reversed(range(layer_count)):
        gathered = gather_again(
            layer_index,
            attn_gain,
            attn_shift,
            w_qkv,
            b_query,
            b_value,
            w_out,
            b_out,
            mlp_gain,
            mlp_shift,
            w_up,
            b_up,
            w_down,
            b_down,
        )
        grad_resid, gradients = backward_layer(
            grad_resid, stored_list[layer_index], gathered, visible, Halves()
        )
        reduced[layer_index] = reduce_grads(gradients)
    stacked = tuple((jnp.stack([entry[member] for entry in reduced]) for member in range(13)))
    return (result, grad_resid.astype(jnp.bfloat16)[None]) + stacked


def solution(mesh):
    fits = (mesh.shape["seq"], mesh.shape["fsdp"], mesh.shape["rep"]) == (2, ZN, 4)
    return jax.shard_map(
        on_cores if fits else on_device,
        mesh=mesh,
        in_specs=(
            P(("fsdp", "rep"), "seq", None),
            P(("fsdp", "rep"), "seq"),
            P(("fsdp", "rep"), "seq", None),
            P(None, "fsdp"),
            P(None, "fsdp"),
            P(None, "fsdp", None),
            P(None, "fsdp"),
            P(None, "fsdp"),
            P(None, "fsdp", None),
            P(None, "fsdp"),
            P(None, "fsdp"),
            P(None, "fsdp"),
            P(None, "fsdp", None),
            P(None, "fsdp"),
            P(None, "fsdp", None),
            P(None, "fsdp"),
        ),
        out_specs=(
            P(("fsdp", "rep"), "seq", None),
            P(("fsdp", "rep"), "seq", None),
            P(None, "fsdp"),
            P(None, "fsdp"),
            P(None, "fsdp", None),
            P(None, "fsdp"),
            P(None, "fsdp"),
            P(None, "fsdp", None),
            P(None, "fsdp"),
            P(None, "fsdp"),
            P(None, "fsdp"),
            P(None, "fsdp", None),
            P(None, "fsdp"),
            P(None, "fsdp", None),
            P(None, "fsdp"),
        ),
        check_vma=False,
    )
```

```python
import functools
import math

import jax
import jax.numpy as jnp
from jax import lax
from jax.experimental import pallas as pl
from jax.experimental.pallas import tpu as pltpu
from jax.sharding import PartitionSpec as P

HEAD_DIM = 64
MESH = pl.DeviceIdType.MESH


NORM_EPSILON = 1e-05
MASKED = -1e30


def layer_norm(inputs, gain, bias_term):
    center = inputs - jnp.mean(inputs, axis=-1, keepdims=True)
    spread = jnp.mean(center * center, axis=-1, keepdims=True)
    return center * lax.rsqrt(spread + NORM_EPSILON) * gain + bias_term


def gelu_tanh(inputs):
    return jax.nn.gelu(inputs, approximate=True)


def product(left, right):
    return jnp.dot(left, right, preferred_element_type=jnp.float32)


def inner_rows(left, right):
    return lax.dot_general(
        left, right, (((0,), (0,)), ((), ())), preferred_element_type=jnp.float32
    )


def outer_cols(left, right):
    return lax.dot_general(
        left, right, (((1,), (1,)), ((), ())), preferred_element_type=jnp.float32
    )


def column_sum(values_low):
    return jnp.sum(values_low.astype(jnp.float32), axis=0)


def visible_mask(seg_own, seg_all, offset):
    row_pos = offset + lax.iota(jnp.int32, seg_own.shape[0])
    col_pos = lax.iota(jnp.int32, seg_all.shape[0])
    return (seg_own[:, None] == seg_all[None, :]) & (row_pos[:, None] >= col_pos[None, :])


def head_scores(queries, keys_all, visible, head_count):
    query_heads = queries.reshape(queries.shape[0], head_count, HEAD_DIM)
    key_heads = keys_all.reshape(keys_all.shape[0], head_count, HEAD_DIM)
    scores = jnp.einsum("thd,shd->hts", query_heads, key_heads, preferred_element_type=jnp.float32)
    return jnp.where(visible[None], scores, MASKED)


def gather_layer(
    layer_index,
    attn_gain,
    attn_shift,
    w_qkv,
    b_query,
    b_value,
    w_out,
    b_out,
    mlp_gain,
    mlp_shift,
    w_up,
    b_up,
    w_down,
    b_down,
):
    return (
        lax.all_gather(attn_gain[layer_index], "fsdp", axis=0, tiled=True),
        lax.all_gather(attn_shift[layer_index], "fsdp", axis=0, tiled=True),
        lax.all_gather(w_qkv[layer_index], "fsdp", axis=0, tiled=True),
        lax.all_gather(b_query[layer_index], "fsdp", axis=0, tiled=True),
        lax.all_gather(b_value[layer_index], "fsdp", axis=0, tiled=True),
        lax.all_gather(w_out[layer_index], "fsdp", axis=0, tiled=True),
        lax.all_gather(b_out[layer_index], "fsdp", axis=0, tiled=True),
        lax.all_gather(mlp_gain[layer_index], "fsdp", axis=0, tiled=True),
        lax.all_gather(mlp_shift[layer_index], "fsdp", axis=0, tiled=True),
        lax.all_gather(w_up[layer_index], "fsdp", axis=0, tiled=True),
        lax.all_gather(b_up[layer_index], "fsdp", axis=0, tiled=True),
        lax.all_gather(w_down[layer_index], "fsdp", axis=0, tiled=True),
        lax.all_gather(b_down[layer_index], "fsdp", axis=0, tiled=True),
    )


def gather_again(
    layer_index,
    attn_gain,
    attn_shift,
    w_qkv,
    b_query,
    b_value,
    w_out,
    b_out,
    mlp_gain,
    mlp_shift,
    w_up,
    b_up,
    w_down,
    b_down,
):
    return (
        lax.all_gather(attn_gain[layer_index], "fsdp", axis=0, tiled=True),
        lax.all_gather(attn_shift[layer_index], "fsdp", axis=0, tiled=True),
        lax.all_gather(w_qkv[layer_index], "fsdp", axis=0, tiled=True),
        lax.all_gather(b_query[layer_index], "fsdp", axis=0, tiled=True),
        lax.all_gather(b_value[layer_index], "fsdp", axis=0, tiled=True),
        lax.all_gather(w_out[layer_index], "fsdp", axis=0, tiled=True),
        lax.all_gather(b_out[layer_index], "fsdp", axis=0, tiled=True),
        lax.all_gather(mlp_gain[layer_index], "fsdp", axis=0, tiled=True),
        lax.all_gather(mlp_shift[layer_index], "fsdp", axis=0, tiled=True),
        lax.all_gather(w_up[layer_index], "fsdp", axis=0, tiled=True),
        lax.all_gather(b_up[layer_index], "fsdp", axis=0, tiled=True),
        lax.all_gather(w_down[layer_index], "fsdp", axis=0, tiled=True),
        lax.all_gather(b_down[layer_index], "fsdp", axis=0, tiled=True),
    )


def forward_layer(resid, gathered, visible, pool):
    (
        attn_gain,
        attn_shift,
        w_qkv,
        b_query,
        b_value,
        w_out,
        b_out,
        mlp_gain,
        mlp_shift,
        w_up,
        b_up,
        w_down,
        b_down,
    ) = gathered
    model_width = resid.shape[1]
    head_count = model_width // HEAD_DIM
    query_scale = 1.0 / math.sqrt(HEAD_DIM)
    normed_attn = layer_norm(
        resid, attn_gain.astype(jnp.float32), attn_shift.astype(jnp.float32)
    ).astype(jnp.bfloat16)
    proj_all = product(normed_attn, w_qkv)
    queries = ((proj_all[:, :model_width] + b_query.astype(jnp.float32)) * query_scale).astype(
        jnp.bfloat16
    )
    keys_own = proj_all[:, model_width : 2 * model_width].astype(jnp.bfloat16)
    values_own = (proj_all[:, 2 * model_width :] + b_value.astype(jnp.float32)).astype(jnp.bfloat16)
    keys_all, values_all = pool.spread(keys_own), pool.spread(values_own)
    scores = head_scores(queries, keys_all, visible, head_count)
    row_max = jnp.max(scores, axis=-1, keepdims=True)
    exponent = jnp.exp(scores - row_max)
    row_sum = jnp.sum(exponent, axis=-1, keepdims=True)
    weights_soft = (exponent / row_sum).astype(jnp.bfloat16)
    log_total = row_max + jnp.log(row_sum)
    value_heads = values_all.reshape(values_all.shape[0], head_count, HEAD_DIM)
    attended = jnp.einsum(
        "hts,shd->thd", weights_soft, value_heads, preferred_element_type=jnp.float32
    )
    attended = attended.reshape(resid.shape[0], model_width).astype(jnp.bfloat16)
    middle = resid + product(attended, w_out) + b_out.astype(jnp.float32)
    normed_mlp = layer_norm(
        middle, mlp_gain.astype(jnp.float32), mlp_shift.astype(jnp.float32)
    ).astype(jnp.bfloat16)
    pre_act = product(normed_mlp, w_up) + b_up.astype(jnp.float32)
    activated = gelu_tanh(pre_act).astype(jnp.bfloat16)
    output = middle + product(activated, w_down) + b_down.astype(jnp.float32)
    stored = (
        resid,
        normed_attn,
        queries,
        keys_all,
        values_all,
        log_total,
        attended,
        middle,
        normed_mlp,
        pre_act,
        activated,
    )
    return (output, stored)


def backward_layer(grad_next, stored, gathered, visible, pool):
    (
        attn_gain,
        attn_shift,
        w_qkv,
        b_query,
        b_value,
        w_out,
        b_out,
        mlp_gain,
        mlp_shift,
        w_up,
        b_up,
        w_down,
        b_down,
    ) = gathered
    (
        resid,
        normed_attn,
        queries,
        keys_all,
        values_all,
        log_total,
        attended,
        middle,
        normed_mlp,
        pre_act,
        activated,
    ) = stored
    model_width = resid.shape[1]
    tok_rows = resid.shape[0]
    key_rows = keys_all.shape[0]
    head_count = model_width // HEAD_DIM
    query_scale = 1.0 / math.sqrt(HEAD_DIM)
    grad_mlp = grad_next.astype(jnp.bfloat16)
    grad_b_down = column_sum(grad_mlp)
    grad_w_down = inner_rows(activated, grad_mlp)
    grad_act = outer_cols(grad_mlp, w_down)
    gelu_value, gelu_pull = jax.vjp(gelu_tanh, pre_act)
    grad_pre = gelu_pull(grad_act)[0].astype(jnp.bfloat16)
    grad_b_up = column_sum(grad_pre)
    grad_w_up = inner_rows(normed_mlp, grad_pre)
    grad_nm = outer_cols(grad_pre, w_up)
    norm_value, norm_pull = jax.vjp(
        layer_norm, middle, mlp_gain.astype(jnp.float32), mlp_shift.astype(jnp.float32)
    )
    grad_middle, grad_mlp_gain, grad_mlp_shift = norm_pull(grad_nm)
    grad_middle = grad_middle + grad_next
    grad_branch = grad_middle.astype(jnp.bfloat16)
    grad_b_out = column_sum(grad_branch)
    grad_w_out = inner_rows(attended, grad_branch)
    grad_attended = outer_cols(grad_branch, w_out).astype(jnp.bfloat16)
    scores = head_scores(queries, keys_all, visible, head_count)
    weights_full = jnp.exp(scores - log_total)
    weights_soft = weights_full.astype(jnp.bfloat16)
    grad_heads = grad_attended.reshape(tok_rows, head_count, HEAD_DIM)
    query_heads = queries.reshape(tok_rows, head_count, HEAD_DIM)
    key_heads = keys_all.reshape(key_rows, head_count, HEAD_DIM)
    value_heads = values_all.reshape(key_rows, head_count, HEAD_DIM)
    grad_value_terms = jnp.einsum(
        "hts,thd->shd", weights_soft, grad_heads, preferred_element_type=jnp.float32
    )
    grad_probs = jnp.einsum(
        "thd,shd->hts", grad_heads, value_heads, preferred_element_type=jnp.float32
    )
    inner_sum = jnp.sum(weights_full * grad_probs, axis=-1, keepdims=True)
    grad_scores = (weights_full * (grad_probs - inner_sum)).astype(jnp.bfloat16)
    grad_queries = jnp.einsum(
        "hts,shd->thd", grad_scores, key_heads, preferred_element_type=jnp.float32
    )
    grad_queries = grad_queries.reshape(tok_rows, model_width).astype(jnp.bfloat16) * query_scale
    grad_key_terms = jnp.einsum(
        "hts,thd->shd", grad_scores, query_heads, preferred_element_type=jnp.float32
    )
    grad_keys = pool.collect(grad_key_terms.reshape(key_rows, model_width).astype(jnp.bfloat16))
    grad_values = pool.collect(grad_value_terms.reshape(key_rows, model_width).astype(jnp.bfloat16))
    grad_keys = grad_keys.astype(jnp.bfloat16)
    grad_values = grad_values.astype(jnp.bfloat16)
    grad_proj = jnp.concatenate([grad_queries, grad_keys, grad_values], axis=1)
    grad_b_query = column_sum(grad_queries)
    grad_b_value = column_sum(grad_values)
    grad_w_qkv = inner_rows(normed_attn, grad_proj)
    grad_na = outer_cols(grad_proj, w_qkv)
    first_value, first_pull = jax.vjp(
        layer_norm, resid, attn_gain.astype(jnp.float32), attn_shift.astype(jnp.float32)
    )
    grad_resid, grad_attn_gain, grad_attn_shift = first_pull(grad_na)
    grad_resid = grad_resid + grad_middle
    gradients = (
        grad_attn_gain,
        grad_attn_shift,
        grad_w_qkv,
        grad_b_query,
        grad_b_value,
        grad_w_out,
        grad_b_out,
        grad_mlp_gain,
        grad_mlp_shift,
        grad_w_up,
        grad_b_up,
        grad_w_down,
        grad_b_down,
    )
    return (grad_resid, gradients)


def reduce_grads(gradients):
    shares = (
        lax.psum_scatter(gradients[0], ("fsdp", "rep"), scatter_dimension=0, tiled=True),
        lax.psum_scatter(gradients[1], ("fsdp", "rep"), scatter_dimension=0, tiled=True),
        lax.psum_scatter(gradients[2], ("fsdp", "rep"), scatter_dimension=0, tiled=True),
        lax.psum_scatter(gradients[3], ("fsdp", "rep"), scatter_dimension=0, tiled=True),
        lax.psum_scatter(gradients[4], ("fsdp", "rep"), scatter_dimension=0, tiled=True),
        lax.psum_scatter(gradients[5], ("fsdp", "rep"), scatter_dimension=0, tiled=True),
        lax.psum_scatter(gradients[6], ("fsdp", "rep"), scatter_dimension=0, tiled=True),
        lax.psum_scatter(gradients[7], ("fsdp", "rep"), scatter_dimension=0, tiled=True),
        lax.psum_scatter(gradients[8], ("fsdp", "rep"), scatter_dimension=0, tiled=True),
        lax.psum_scatter(gradients[9], ("fsdp", "rep"), scatter_dimension=0, tiled=True),
        lax.psum_scatter(gradients[10], ("fsdp", "rep"), scatter_dimension=0, tiled=True),
        lax.psum_scatter(gradients[11], ("fsdp", "rep"), scatter_dimension=0, tiled=True),
        lax.psum_scatter(gradients[12], ("fsdp", "rep"), scatter_dimension=0, tiled=True),
    )
    shares = (
        lax.psum(shares[0].astype(jnp.bfloat16), "seq").astype(jnp.float32),
        lax.psum(shares[1].astype(jnp.bfloat16), "seq").astype(jnp.float32),
        lax.psum(shares[2].astype(jnp.bfloat16), "seq").astype(jnp.float32),
        lax.psum(shares[3].astype(jnp.bfloat16), "seq").astype(jnp.float32),
        lax.psum(shares[4].astype(jnp.bfloat16), "seq").astype(jnp.float32),
        lax.psum(shares[5].astype(jnp.bfloat16), "seq").astype(jnp.float32),
        lax.psum(shares[6].astype(jnp.bfloat16), "seq").astype(jnp.float32),
        lax.psum(shares[7].astype(jnp.bfloat16), "seq").astype(jnp.float32),
        lax.psum(shares[8].astype(jnp.bfloat16), "seq").astype(jnp.float32),
        lax.psum(shares[9].astype(jnp.bfloat16), "seq").astype(jnp.float32),
        lax.psum(shares[10].astype(jnp.bfloat16), "seq").astype(jnp.float32),
        lax.psum(shares[11].astype(jnp.bfloat16), "seq").astype(jnp.float32),
        lax.psum(shares[12].astype(jnp.bfloat16), "seq").astype(jnp.float32),
    )
    return (
        lax.all_gather(shares[0].astype(jnp.bfloat16), "rep", axis=0, tiled=True).astype(
            jnp.float32
        ),
        lax.all_gather(shares[1].astype(jnp.bfloat16), "rep", axis=0, tiled=True).astype(
            jnp.float32
        ),
        lax.all_gather(shares[2].astype(jnp.bfloat16), "rep", axis=0, tiled=True).astype(
            jnp.float32
        ),
        lax.all_gather(shares[3].astype(jnp.bfloat16), "rep", axis=0, tiled=True).astype(
            jnp.float32
        ),
        lax.all_gather(shares[4].astype(jnp.bfloat16), "rep", axis=0, tiled=True).astype(
            jnp.float32
        ),
        lax.all_gather(shares[5].astype(jnp.bfloat16), "rep", axis=0, tiled=True).astype(
            jnp.float32
        ),
        lax.all_gather(shares[6].astype(jnp.bfloat16), "rep", axis=0, tiled=True).astype(
            jnp.float32
        ),
        lax.all_gather(shares[7].astype(jnp.bfloat16), "rep", axis=0, tiled=True).astype(
            jnp.float32
        ),
        lax.all_gather(shares[8].astype(jnp.bfloat16), "rep", axis=0, tiled=True).astype(
            jnp.float32
        ),
        lax.all_gather(shares[9].astype(jnp.bfloat16), "rep", axis=0, tiled=True).astype(
            jnp.float32
        ),
        lax.all_gather(shares[10].astype(jnp.bfloat16), "rep", axis=0, tiled=True).astype(
            jnp.float32
        ),
        lax.all_gather(shares[11].astype(jnp.bfloat16), "rep", axis=0, tiled=True).astype(
            jnp.float32
        ),
        lax.all_gather(shares[12].astype(jnp.bfloat16), "rep", axis=0, tiled=True).astype(
            jnp.float32
        ),
    )


class Halves:
    def spread(self, rows):
        return lax.all_gather(rows, "seq", axis=0, tiled=True)

    def collect(self, rows):
        return lax.psum_scatter(rows, "seq", scatter_dimension=0, tiled=True)


ZN = 4


def neighbours():
    x, z, r = lax.axis_index("seq"), lax.axis_index("fsdp"), lax.axis_index("rep")
    y, c = r // 2, r % 2
    across = (1 - x, z, r)
    beside = (x, z, (1 - y) * 2 + c)
    twin = (x, z, y * 2 + (1 - c))
    up = (x, (z + 1) % ZN, r)
    down = (x, (z + ZN - 1) % ZN, r)
    return x, y, z, c, across, beside, twin, up, down


def greet(z, c, x, across, beside, twin, diag, up, down):
    barrier = pltpu.get_barrier_semaphore()

    def tell(device):
        pl.semaphore_signal(barrier, inc=1, device_id=device, device_id_type=MESH)

    for device in (across, beside, twin):
        tell(device)
    if diag is not None:

        @pl.when(c != x)
        def _():
            tell(diag)

    @pl.when(z < ZN - 1)
    def _():
        tell(up)

    @pl.when(z > 0)
    def _():
        tell(down)

    extra = 0 if diag is None else (x + c) % 2
    pl.semaphore_wait(barrier, 3 + extra + (z + ZN - 1) // ZN + (2 * ZN - 2 - z) // ZN)


GELU_A = math.sqrt(2.0 / math.pi)
GELU_B = 0.044715
QUERY_SCALE = 1.0 / math.sqrt(HEAD_DIM)
HEAD_ROWS = 24
PACE = 4
LEAD = 3
GAP = 2
TILE = 512
SKEW = 2
AHEAD = 6


NT = (((1,), (1,)), ((), ()))
TN = (((0,), (0,)), ((), ()))
BLOCK = 256
RANGES = (((0, 256), (256, 1024)), ((0, 768), (256, 512)))
VMEM_LIMIT = 60 << 20


def dot_nt(left, right):
    return lax.dot_general(left, right, NT, preferred_element_type=jnp.float32)


def dot_tn(left, right):
    return lax.dot_general(left, right, TN, preferred_element_type=jnp.float32)


def tiles(width, tile, act):
    whole = width // tile

    def step(i, carry):
        act(pl.multiple_of(i * tile, tile), tile)
        return carry

    lax.fori_loop(0, whole, step, 0)
    if width % tile:
        act(whole * tile, width % tile)


def tiles_between(low, high, tile, act):
    def step(i, carry):
        act(pl.multiple_of(i * tile, tile), tile)
        return carry

    if low // tile < high // tile:
        lax.fori_loop(low // tile, high // tile, step, 0)
    if high % tile:
        act(high // tile * tile, high % tile)


def norm_parts(rows):
    center = rows - jnp.mean(rows, axis=1, keepdims=True)
    scale = lax.rsqrt(jnp.mean(center * center, axis=1, keepdims=True) + NORM_EPSILON)
    return center * scale, scale


def norm_into(source, gain, shift, target):
    def act(start, size):
        rows = pl.ds(start, size)
        unit, _ = norm_parts(source[rows, :])
        target[rows, :] = (unit * gain + shift).astype(target.dtype)

    tiles(source.shape[0], 64, act)


def norm_back(source, grad, extra, gain, target, gain_grad, shift_grad, low=None):
    gain_grad[...] = jnp.zeros_like(gain_grad)
    shift_grad[...] = jnp.zeros_like(shift_grad)

    def act(start, size):
        rows = pl.ds(start, size)
        unit, scale = norm_parts(source[rows, :])
        g = grad[rows, :]
        q = g * gain
        mean_q = jnp.mean(q, axis=1, keepdims=True)
        mean_qn = jnp.mean(q * unit, axis=1, keepdims=True)
        out = extra[rows, :] + (q - mean_q - unit * mean_qn) * scale
        target[rows, :] = out
        if low is not None:
            low[rows, :] = out.astype(low.dtype)
        gain_grad[...] += jnp.sum(g * unit, axis=0, keepdims=True)
        shift_grad[...] += jnp.sum(g, axis=0, keepdims=True)

    tiles(source.shape[0], 64, act)


def whole(count):
    return [pl.BlockSpec(memory_space=pltpu.VMEM)] * count


def anywhere(count):
    return [pl.BlockSpec(memory_space=pl.ANY)] * count


def shaped(shape, dtype=jnp.float32):
    return jax.ShapeDtypeStruct(shape, dtype)


def params():
    return pltpu.CompilerParams(vmem_limit_bytes=VMEM_LIMIT)


def of_head(values, j):
    if values.shape[1] == HEAD_DIM:
        return values
    lane = lax.broadcasted_iota(jnp.int32, values.shape, 1)
    return jnp.where(lane // HEAD_DIM == j, values, jnp.zeros_like(values))


ZA, ZR, GX, GY, GD1, GD2, GC = range(7)
ROW = dict(attn_gain=0, attn_shift=1, b_query=2, b_value=3, b_out=4, mlp_gain=5, mlp_shift=6, b_down=7)
SAVED = ("x", "normed_attn", "q", "keys", "values", "attended", "lse", "middle", "normed_mlp", "slope", "activated")


def advance(steps, count):
    for _ in range(count):
        if next(steps, None) is None:
            return


def gather_units(layers, shapes):
    units = []
    for layer in range(layers):
        for m, shape in enumerate(shapes):
            n = shape[1] // 8
            k = min(n, 1 if shape[3] > 2048 else 2)
            bases = range(0, max(n, 1), max(k, 1))
            units += [(layer, m, base * 8, k, base + k >= n) for base in bases]
    return units


def weight_moves(ins, outs, send_sem, recv_sem, place):
    x, y, z, c, across, beside, twin, up, down = place
    m_count = len(ins) - 1
    layers = ins[0].shape[0]
    units = gather_units(layers, [w.shape for w in ins])
    index = {unit: i for i, unit in enumerate(units)}

    def depth(u):
        return u[3]

    def corners(u, px, py, act):
        k = depth(u)
        for half, device, kind in ((0, beside, GD1), (1, across, GD2)):
            if k > 1 or half == index[u] % 2:
                act(half if k > 1 else None, device, kind)

    def owned(u, px, py, half=None):
        k = depth(u)
        base = u[2] + (c * 4 + px * 2 + py) * k
        if half is None:
            return pl.ds(base, k)
        return pl.ds(base + half * (k // 2), k // 2)

    def rest(u):
        n = ins[u[1]].shape[1]
        return pl.ds(n // 8 * 8, n % 8)

    def slab(u, core):
        return pl.ds(u[2] + core * 4 * depth(u), 4 * depth(u))

    def move(u, zz, rows, device, kind, source=None, send_kind=None):
        target = outs[u[1]].at[u[0], zz, rows]
        return pltpu.make_async_remote_copy(
            src_ref=target if source is None else source,
            dst_ref=target,
            send_sem=send_sem.at[index[u], zz, kind if send_kind is None else send_kind],
            recv_sem=recv_sem.at[index[u], zz, kind],
            device_id=device,
            device_id_type=MESH,
        )

    def own_sends(u, act):
        source = ins[u[1]].at[u[0]]

        def along(device, first):
            if depth(u):
                act(move(u, z, owned(u, x, y), device, ZA, source.at[owned(u, x, y)], first))
            if u[4]:
                act(move(u, z, rest(u), device, ZR, source.at[rest(u)], first + 1))

        @pl.when(z < ZN - 1)
        def _():
            along(up, 0)

        @pl.when(z > 0)
        def _():
            along(down, 2)

    def both(s, act):
        @pl.when(z >= s)
        def _():
            act(z - s, 0)

        @pl.when(z + s <= ZN - 1)
        def _():
            act(z + s, 1)

    def onward(u, zz, d, act):
        def along(device):
            if depth(u):
                act(move(u, zz, owned(u, x, y), device, ZA))
            if u[4]:
                act(move(u, zz, rest(u), device, ZR))

        if d == 0:

            @pl.when(z < ZN - 1)
            def _():
                along(up)

        else:

            @pl.when(z > 0)
            def _():
                along(down)

    def line_step(u, s):
        def act(zz, d):
            if depth(u):
                move(u, zz, owned(u, x, y), across, ZA).wait_recv()
            if u[4]:
                move(u, zz, rest(u), across, ZR).wait_recv()
            onward(u, zz, d, lambda copy: copy.start())
            if depth(u):
                move(u, zz, owned(u, x, y), across, GX).start()
                move(u, zz, owned(u, x, y), beside, GY).start()

        both(s, act)

    def plane_step(u, s):
        def act(zz, d):
            def pass_on(half, device, kind):
                if kind == GD1:
                    move(u, zz, owned(u, 1 - x, y, half), device, kind).start()
                else:
                    move(u, zz, owned(u, x, 1 - y, half), device, kind).start()

            move(u, zz, owned(u, 1 - x, y), across, GX).wait_recv()
            move(u, zz, owned(u, x, 1 - y), beside, GY).wait_recv()
            corners(u, x, y, pass_on)

        both(s, act)

    def corner_step(u, s):
        def act(zz, d):
            corners(
                u, x, y, lambda half, device, kind: move(u, zz, owned(u, 1 - x, 1 - y, half), device, kind).wait_recv()
            )
            move(u, zz, slab(u, c), twin, GC).start()

        both(s, act)

    def arrive(whole):
        for u in units:
            if u[:2] == whole:
                for s in range(1, ZN):
                    both(s, lambda zz, d: move(u, zz, slab(u, 1 - c), twin, GC).wait_recv())

    def finish(u):
        own_sends(u, lambda copy: copy.wait_send())
        for s in range(1, ZN):

            def act(zz, d):
                onward(u, zz, d, lambda copy: copy.wait_send())
                if depth(u):
                    move(u, zz, owned(u, x, y), across, GX).wait_send()
                    move(u, zz, owned(u, x, y), beside, GY).wait_send()
                    corners(
                        u, x, y, lambda half, device, kind: move(u, zz, owned(u, x, y, half), device, kind).wait_send()
                    )
                    move(u, zz, slab(u, c), twin, GC).wait_send()

            both(s, act)

    matrices = [u for u in units if u[1] < m_count]
    vectors = [u for u in units if u[1] == m_count]
    def steps():
        first = [u for u in matrices if u[:2] == matrices[0][:2]]
        rest_units = [u for u in matrices if u not in first]
        count = len(rest_units)
        for u in vectors + first:
            own_sends(u, lambda copy: copy.start())
        for s in range(1, ZN):
            for u in vectors:
                line_step(u, s)
        yield ("vectors",)
        for s in range(1, ZN):
            for u in first:
                line_step(u, s)
                yield ("line",)
            if s == 1:
                for u in rest_units[:LEAD]:
                    own_sends(u, lambda copy: copy.start())
        early = [[(plane_step, u, s) for u in first] for s in range(1, ZN)]
        early += [[(corner_step, u, s) for u in first] for s in range(1, ZN)]
        for t in range(count + 4 * GAP):
            if t + LEAD < count:
                own_sends(rest_units[t + LEAD], lambda copy: copy.start())
            for step, u, s in sum(early[t * 2 : t * 2 + 2], []):
                step(u, s)
                here = step is corner_step and s == ZN - 1 and u[4]
                yield ("here", u[:2]) if here else ("early",)
            for delay, step in ((0, line_step), (1, plane_step), (2, corner_step)):
                for s in range(1, ZN):
                    i = t - (s - 1 + delay) * GAP
                    if not 0 <= i < count:
                        continue
                    u = rest_units[i]
                    step(u, s)
                    here = step is corner_step and s == ZN - 1 and u[4]
                    yield ("here", u[:2]) if here else ("step",)

    return steps, arrive, lambda: [finish(u) for u in units]


def attend(core, q, keys, values, mask, attended, lse, first, last):
    def slab(start, size, head):
        cols = pl.ds(start, size)
        for variant in range(2):

            @pl.when(core == variant)
            def _():
                for row, high in RANGES[variant]:
                    rows = slice(row, row + BLOCK)
                    qs = q[rows, cols]
                    ks, vs = keys[:high, cols], values[:high, cols]
                    parts = []
                    for j in range(size // HEAD_DIM):
                        s = dot_nt(ks, of_head(qs, j)) + mask[:high, rows]
                        top = jnp.max(s, axis=0, keepdims=True)
                        e = jnp.exp(s - top)
                        total = jnp.sum(e, axis=0, keepdims=True)
                        lse[pl.ds(head + j, 1), rows] = top + jnp.log(total)
                        out = dot_tn(vs, e.astype(jnp.bfloat16)) * (1.0 / total)
                        parts.append(out[j * HEAD_DIM : (j + 1) * HEAD_DIM])
                    out = jnp.concatenate(parts, axis=0) if len(parts) > 1 else parts[0]
                    attended[rows, cols] = out.T.astype(jnp.bfloat16)

    over_slabs(q.shape[1], slab, first, last)


def over_slabs(width, slab, first, last):
    pair = 2 * HEAD_DIM
    full = width // pair

    def step(i, carry):
        slab(pl.multiple_of(i * pair, pair), pair, i * 2)
        return carry

    if first < min(last, full):
        lax.fori_loop(first, min(last, full), step, 0)
    if last > full and width % pair:
        slab(full * pair, HEAD_DIM, full * 2)


def forward_body(
    tokens, grads, segs, vectors, w_qkv, w_out, w_up, w_down,
    full_qkv, full_out, full_up, full_down, full_vectors, result, grads_here, mask_out, rows_out, *rest_refs,
):
    layers = w_qkv.shape[0]
    saved = [dict(zip(SAVED, rest_refs[i * len(SAVED) : (i + 1) * len(SAVED)])) for i in range(layers)]
    (
        wq, wo, wu, wd, xs, tok, na, nm, q, keys, values, mask, att, middle, slope, act_buf, lse,
        vecs, rows, b_up, b_proj, seg_nat, seg_row,
        send_sem, recv_sem, load_sem, own_sem, save_sem, kv_send, kv_recv, in_send, in_recv, in_local, free_sem,
    ) = rest_refs[layers * len(SAVED) :]
    place = neighbours()
    x, y, z, c, across, beside, twin, up, down = place
    diag = (1 - x, z, y * 2 + (1 - c))
    here = c == x
    greet(z, c, x, across, beside, twin, diag, up, down)
    width = xs.shape[1]
    half = BLOCK
    parts = [w_qkv, w_out, w_up, w_down]
    fulls = [full_qkv, full_out, full_up, full_down]
    buffers = [wq, wo, wu, wd]
    steps, arrive, finish = weight_moves(parts + [vectors], fulls + [full_vectors], send_sem, recv_sem, place)

    def in_move(i, source, target, device):
        return pltpu.make_async_remote_copy(
            src_ref=source, dst_ref=target, send_sem=in_send.at[i], recv_sem=in_recv.at[i],
            device_id=device, device_id_type=MESH,
        )

    top, low = pl.ds(0, half), pl.ds(half, half)

    def in_copies(i, source, target):
        stay = pltpu.make_async_copy(source.at[top], target.at[top], in_local.at[i])
        return (
            stay,
            in_move(2 * i + 1, source.at[low], target.at[low], twin),
            in_move(2 * i, source.at[top], target.at[top], diag),
            in_move(2 * i + 1, source.at[low], target.at[low], across),
        )

    tok_copies = in_copies(0, tokens, tok)
    grad_copies = in_copies(1, grads, grads_here)
    seg_stay = pltpu.make_async_copy(segs, seg_nat.at[x], in_local.at[2])
    seg_twin = in_move(4, segs, seg_nat.at[x], twin)
    seg_across = in_move(4, segs, seg_nat.at[x], across)
    seg_diag = pltpu.make_async_remote_copy(
        src_ref=segs, dst_ref=seg_nat.at[x], send_sem=in_send.at[5], recv_sem=in_recv.at[5],
        device_id=diag, device_id_type=MESH,
    )

    @pl.when(here)
    def _():
        for copy in (seg_stay, seg_twin, tok_copies[0], tok_copies[1], grad_copies[0], grad_copies[1]):
            copy.start()

    @pl.when(jnp.logical_not(here))
    def _():
        for copy in (seg_across, seg_diag, tok_copies[2], tok_copies[3], grad_copies[2], grad_copies[3]):
            copy.start()

    def wait_in(copies):
        @pl.when(here)
        def _():
            copies[0].wait()
            copies[1].wait_recv()

        @pl.when(jnp.logical_not(here))
        def _():
            copies[2].wait_recv()
            copies[3].wait_recv()

    def wait_segs():
        @pl.when(here)
        def _():
            seg_stay.wait()
            seg_across.wait_recv()

        @pl.when(jnp.logical_not(here))
        def _():
            seg_twin.wait_recv()
            seg_diag.wait_recv()

    def finish_in():
        @pl.when(here)
        def _():
            grad_copies[0].wait()
            grad_copies[1].wait_recv()
            for copy in (seg_twin, tok_copies[1], grad_copies[1]):
                copy.wait_send()

        @pl.when(jnp.logical_not(here))
        def _():
            grad_copies[2].wait_recv()
            grad_copies[3].wait_recv()
            for copy in (seg_across, seg_diag, tok_copies[2], tok_copies[3], grad_copies[2], grad_copies[3]):
                copy.wait_send()

    comm = steps()
    seen = set()
    loaded = {}
    done_with = set()

    def tick(count=1):
        for _ in range(count):
            label = next(comm, None)
            if label is None:
                return False
            seen.add(label)
            if label[0] == "here":
                fetch_ready()
        return True

    def loads(u):
        layer, m = u
        n = parts[m].shape[1]
        copies = [pltpu.make_async_copy(parts[m].at[layer], buffers[m].at[pl.ds(z * n, n)], load_sem.at[m, 0])]
        for s in range(1, ZN):
            zz = (z + s) % ZN
            copies.append(
                pltpu.make_async_copy(fulls[m].at[layer, zz], buffers[m].at[pl.ds(zz * n, n)], load_sem.at[m, s])
            )
        return copies

    def fetch_ready(upto=None):
        for layer in range(layers):
            for m in range(len(parts)):
                u = (layer, m)
                if u in loaded or ("here", u) not in seen:
                    continue
                if layer and (layer - 1, m) not in done_with:
                    continue
                following = (layer, m + 1) if m + 1 < len(parts) else (layer + 1, 0)
                if u != upto and following[0] < layers and ("here", following) not in seen:
                    continue
                arrive(u)
                if layer:
                    own_rows((layer - 1, m)).wait()
                for copy in loads(u):
                    copy.start()
                loaded[u] = True

    def own_rows(u):
        layer, m = u
        n = parts[m].shape[1]
        return pltpu.make_async_copy(buffers[m].at[pl.ds(z * n, n)], fulls[m].at[layer, z], own_sem.at[layer, m])

    def need(u):
        while ("here", u) not in seen:
            if not tick():
                break
        fetch_ready(u)
        for copy in loads(u):
            copy.wait()
        own_rows(u).start()

    pending = []

    def save(layer, name, buffer):
        copy = pltpu.make_async_copy(buffer, saved[layer][name], save_sem.at[layer, SAVED.index(name)])
        copy.start()
        pending.append(copy)

    def settle():
        while pending:
            pending.pop().wait()

    def row(layer, name):
        return rows[layer, pl.ds(ROW[name], 1), :]

    def make_mask():
        wait_segs()
        joined = jnp.concatenate([seg_nat[0], seg_nat[1]], axis=1).astype(jnp.float32)
        seg_row[...] = jnp.broadcast_to(joined, seg_row.shape)
        column = seg_row[...].T[:, :1]
        for block in range(2):
            base = ((2 * c) if block == 0 else (3 - 2 * c)) * BLOCK
            own = seg_row[0:1, pl.ds(pl.multiple_of(base, BLOCK), BLOCK)]
            spot = lax.broadcasted_iota(jnp.int32, (mask.shape[0], BLOCK), 0)
            mine = lax.broadcasted_iota(jnp.int32, (mask.shape[0], BLOCK), 1) + base
            ok = (column == own) & (spot <= mine)
            mask[:, block * BLOCK : (block + 1) * BLOCK] = jnp.where(ok, 0.0, MASKED).astype(jnp.float32)
        copy = pltpu.make_async_copy(mask, mask_out, save_sem.at[0, len(SAVED)])
        copy.start()
        pending.append(copy)

    def make_rows(layer):
        copies = [
            pltpu.make_async_copy(vectors.at[layer, 0], vecs.at[z], load_sem.at[4, 0])
        ] + [
            pltpu.make_async_copy(full_vectors.at[layer, (z + s) % ZN, 0], vecs.at[(z + s) % ZN], load_sem.at[4, s])
            for s in range(1, ZN)
        ]
        for copy in copies:
            copy.start()
        for copy in copies:
            copy.wait()
        share = vecs.shape[2]
        b_proj[layer, 0:1, :] = jnp.zeros((1, b_proj.shape[2]), jnp.float32)
        for zz in range(ZN):
            block = vecs[zz].astype(jnp.float32)
            rows[layer, 0:8, zz * share : (zz + 1) * share] = block[0:8]
            for name, at in (("b_query", 0), ("b_value", 2 * width)):
                b_proj[layer, 0:1, at + zz * share : at + (zz + 1) * share] = block[ROW[name] : ROW[name] + 1]
            for j in range(ZN):
                at = (zz * ZN + j) * share
                b_up[layer, 0:1, at : at + share] = block[8 + j : 9 + j]

    def swap_moves(layer):
        moves = []
        for i, ref in enumerate((keys, values)):
            for block in range(2):
                at = ((2 * c) if block == 0 else (3 - 2 * c)) * BLOCK
                spot = ref.at[pl.ds(pl.multiple_of(at, BLOCK), BLOCK)]
                moves.append(
                    pltpu.make_async_remote_copy(
                        src_ref=spot, dst_ref=spot, send_sem=kv_send.at[layer, i, block],
                        recv_sem=kv_recv.at[layer, i, block], device_id=twin, device_id_type=MESH,
                    )
                )
        return moves

    def swap_waits(layer):
        moves = []
        for i, ref in enumerate((keys, values)):
            for block in range(2):
                at = ((2 - 2 * c) if block == 0 else (1 + 2 * c)) * BLOCK
                spot = ref.at[pl.ds(pl.multiple_of(at, BLOCK), BLOCK)]
                moves.append(
                    pltpu.make_async_remote_copy(
                        src_ref=spot, dst_ref=spot, send_sem=kv_send.at[layer, i, block],
                        recv_sem=kv_recv.at[layer, i, block], device_id=twin, device_id_type=MESH,
                    )
                )
        return moves

    def matrix(buffer, cols):
        return buffer[:, :, cols].reshape(-1, cols.size)

    def compute(layer):
        if layer == 0:
            for i in range(layers):
                make_rows(i)
                yield
            for i in range(layers):
                copy = pltpu.make_async_copy(rows.at[i], rows_out.at[i], save_sem.at[i, len(SAVED) + 1])
                copy.start()
                pending.append(copy)
            make_mask()
            yield
            wait_in(tok_copies)
            xs[...] = tok[...].astype(jnp.float32)
        else:
            settle()
        save(layer, "x", xs)
        norm_into(xs, row(layer, "attn_gain"), row(layer, "attn_shift"), na)
        save(layer, "normed_attn", na)
        yield
        need((layer, 0))
        total = wq.shape[2]

        for low_at in range(0, total, 4 * BLOCK):
            high_at = min(low_at + 4 * BLOCK, total)
            tiles_between(low_at, high_at, TILE, lambda start, size: project_tile(layer, start, size))
            yield
        done_with.add((layer, 0))
        q[...] = slope[:, :width]
        if layer:
            pl.semaphore_wait(free_sem, 1)
        for block in range(2):
            at = ((2 * c) if block == 0 else (3 - 2 * c)) * BLOCK
            spot = pl.ds(pl.multiple_of(at, BLOCK), BLOCK)
            source = slice(block * BLOCK, (block + 1) * BLOCK)
            keys[spot, :] = slope[source, width : 2 * width]
            values[spot, :] = slope[source, 2 * width : 3 * width]
        for copy in swap_moves(layer):
            copy.start()
        save(layer, "q", q)
        yield
        for copy in swap_waits(layer):
            copy.wait_recv()
        save(layer, "keys", keys)
        save(layer, "values", values)
        for first in range(0, width // (2 * HEAD_DIM) + 1, 4):
            attend(c, q, keys, values, mask, att, lse, first, min(first + 4, width // (2 * HEAD_DIM) + 1))
            yield
        save(layer, "attended", att)
        save(layer, "lse", lse)
        if layer + 1 < layers:
            settle()
            for copy in swap_moves(layer):
                copy.wait_send()
            pl.semaphore_signal(free_sem, inc=1, device_id=twin, device_id_type=MESH)
        need((layer, 1))

        def out_step(start, size):
            cols = pl.ds(start, size)
            middle[:, cols] = xs[:, cols] + product(att[...], matrix(wo, cols)) + rows[layer, pl.ds(ROW["b_out"], 1), cols]

        tiles_between(0, width, BLOCK, out_step)
        done_with.add((layer, 1))
        save(layer, "middle", middle)
        yield
        norm_into(middle, row(layer, "mlp_gain"), row(layer, "mlp_shift"), nm)
        save(layer, "normed_mlp", nm)
        yield
        need((layer, 2))
        settle()

        def up_step(start, size):
            cols = pl.ds(start, size)
            u = product(nm[...], matrix(wu, cols)) + b_up[layer, 0:1, cols]
            square = u * u
            t = jnp.tanh(u * (GELU_A + (GELU_A * GELU_B) * square))
            half_up = 0.5 + 0.5 * t
            act_buf[:, cols] = (u * half_up).astype(jnp.bfloat16)
            slope[:, cols] = (
                half_up + (0.5 * u) * (1.0 - t * t) * (GELU_A + (3.0 * GELU_A * GELU_B) * square)
            ).astype(jnp.bfloat16)

        ff = wu.shape[2]
        for low_at in range(0, ff, 6 * BLOCK):
            tiles_between(low_at, min(low_at + 6 * BLOCK, ff), TILE, up_step)
            yield
        done_with.add((layer, 2))
        save(layer, "slope", slope)
        save(layer, "activated", act_buf)
        need((layer, 3))

        def down_step(start, size):
            cols = pl.ds(start, size)
            xs[:, cols] = middle[:, cols] + product(act_buf[...], matrix(wd, cols)) + rows[layer, pl.ds(ROW["b_down"], 1), cols]

        for low_at in range(0, width, 2 * BLOCK):
            tiles_between(low_at, min(low_at + 2 * BLOCK, width), BLOCK, down_step)
            yield
        done_with.add((layer, 3))

    def project_tile(layer, start, size):
        cols = pl.ds(start, size)
        out = product(na[...], matrix(wq, cols))
        slope[:, cols] = ((out + b_proj[layer, 0:1, cols]) * scale_of(start, size)).astype(jnp.bfloat16)

    def scale_of(start, size):
        lane = lax.broadcasted_iota(jnp.int32, (1, size), 1) + start
        return jnp.where(lane < width, QUERY_SCALE, 1.0).astype(jnp.float32)

    tick()
    for layer in range(layers):
        for _ in compute(layer):
            tick(PACE)
    while tick():
        pass
    settle()
    tok[...] = xs[...].astype(jnp.bfloat16)
    out = pltpu.make_async_copy(tok, result, save_sem.at[0, 0])
    out.start()
    for copy in swap_moves(layers - 1):
        copy.wait_send()
    finish_in()
    finish()
    for m in range(len(parts)):
        own_rows((layers - 1, m)).wait()
    out.wait()


def forward(tokens, grads, segs, vectors, weights):
    rows, width = tokens.shape
    low = jnp.bfloat16
    layers = vectors.shape[0]
    ff = weights[2].shape[3]
    units = len(gather_units(layers, [w.shape for w in weights] + [vectors.shape]))
    shapes = dict(
        x=((rows, width), jnp.float32),
        normed_attn=((rows, width), low),
        q=((rows, width), low),
        keys=((2 * rows, width), low),
        values=((2 * rows, width), low),
        attended=((rows, width), low),
        lse=((HEAD_ROWS, rows), jnp.float32),
        middle=((rows, width), jnp.float32),
        normed_mlp=((rows, width), low),
        slope=((rows, ff), low),
        activated=((rows, ff), low),
    )
    out_shape = (
        [shaped((layers, ZN) + w.shape[1:], low) for w in weights]
        + [
            shaped((layers, ZN) + vectors.shape[1:], low),
            shaped((rows, width), low),
            shaped((rows, width), low),
            shaped((2 * rows, rows)),
            shaped((layers, 16, width)),
        ]
        + [shaped(*shapes[name]) for _ in range(layers) for name in SAVED]
    )
    dma = pltpu.SemaphoreType.DMA
    scratch = [pltpu.VMEM((ZN * w.shape[1],) + w.shape[2:], low) for w in weights] + [
        pltpu.VMEM((rows, width), jnp.float32),
        pltpu.VMEM((rows, width), low),
        pltpu.VMEM((rows, width), low),
        pltpu.VMEM((rows, width), low),
        pltpu.VMEM((rows, width), low),
        pltpu.VMEM((2 * rows, width), low),
        pltpu.VMEM((2 * rows, width), low),
        pltpu.VMEM((2 * rows, rows), jnp.float32),
        pltpu.VMEM((rows, width), low),
        pltpu.VMEM((rows, width), jnp.float32),
        pltpu.VMEM((rows, ff), low),
        pltpu.VMEM((rows, ff), low),
        pltpu.VMEM((HEAD_ROWS, rows), jnp.float32),
        pltpu.VMEM((ZN,) + vectors.shape[2:], low),
        pltpu.VMEM((layers, 16, width), jnp.float32),
        pltpu.VMEM((layers, 8, ff), jnp.float32),
        pltpu.VMEM((layers, 8, 3 * width), jnp.float32),
        pltpu.VMEM((2, 1, rows), jnp.int32),
        pltpu.VMEM((8, 2 * rows), jnp.float32),
        dma((units, ZN, 7)),
        dma((units, ZN, 7)),
        dma((len(weights) + 1, ZN)),
        dma((layers, len(weights))),
        dma((layers, len(SAVED) + 2)),
        dma((layers, 2, 2)),
        dma((layers, 2, 2)),
        dma((6,)),
        dma((6,)),
        dma((3,)),
        pltpu.SemaphoreType.REGULAR,
    ]
    outs = pl.pallas_call(
        forward_body,
        out_shape=out_shape,
        in_specs=anywhere(4 + len(weights)),
        out_specs=anywhere(len(out_shape)),
        scratch_shapes=scratch,
        compiler_params=pltpu.CompilerParams(collective_id=0, has_side_effects=True, vmem_limit_bytes=VMEM_LIMIT),
        name="forward",
    )(tokens, grads, segs, vectors, *weights)
    count = len(weights)
    fulls, rest = outs[:count], outs[count + 5 :]
    _, result, grads_here, mask, vector_rows = outs[count : count + 5]
    saved = [dict(zip(SAVED, rest[i * len(SAVED) : (i + 1) * len(SAVED)])) for i in range(layers)]
    return fulls, result, grads_here, mask, vector_rows, saved


def begin(copies):
    for copy in copies:
        copy.start()


def end(copies):
    for copy in copies:
        copy.wait()


ORDER = (0, 1, 3, 2)
RC, R1, R2, RZ, RX, RY, RD1, RD2, RCC, R1B, RZX = 0, 4, 8, 12, 16, 17, 18, 19, 20, 21, 25


class Group:
    def __init__(self, grad, out, base, k, ready):
        self.grad, self.out, self.base, self.k, self.ready = grad, out, base, k, ready


def reduce_steps(place, groups, acc, stage, first_in, second_in, line_in, line_extra, load_sem, store_sem, send_sem, recv_sem):
    x, y, z, c, across, beside, twin, up, down = place
    p = x * 2 + y
    units = [(g, d) for g in range(len(groups)) for d in ORDER]

    def move(source, target, g, kind, device):
        return pltpu.make_async_remote_copy(
            src_ref=source, dst_ref=target, send_sem=send_sem.at[g, kind], recv_sem=recv_sem.at[g, kind],
            device_id=device, device_id_type=MESH,
        )

    def half_of(g, d, core):
        group = groups[g]
        return group.grad.at[d, pl.ds(group.base + core * 4 * group.k, 4 * group.k)]

    def to_twin(g, d):
        return move(half_of(g, d, 1 - c), acc[g].at[d], g, RC + d, twin)

    def slot(d):
        return ORDER.index(d) % 2

    def load(g, d):
        return pltpu.make_async_copy(half_of(g, d, c), stage[g].at[slot(d)], load_sem.at[g, slot(d)])

    def add(g, d, at, extra, lead, extra_at, n):
        def step(i, carry):
            acc[g][d, at + i] = acc[g][d, at + i] + extra[lead, extra_at + i]
            return carry

        lax.fori_loop(0, n, step, 0)

    def first_moves(g, d):
        k = groups[g].k
        if d in (0, 3):
            return [move(acc[g].at[d, pl.ds((1 - x) * 2 * k, 2 * k)], first_in[g].at[d], g, R1 + d, across)]
        return [
            move(acc[g].at[d, pl.ds((1 - y) * k, k)], first_in[g].at[d, pl.ds(0, k)], g, R1 + d, beside),
            move(acc[g].at[d, pl.ds((3 - y) * k, k)], first_in[g].at[d, pl.ds(k, k)], g, R1B + d, beside),
        ]

    def second_move(g, d):
        k = groups[g].k
        if d in (0, 3):
            return move(acc[g].at[d, pl.ds((x * 2 + 1 - y) * k, k)], second_in[g].at[d], g, R2 + d, beside)
        return move(acc[g].at[d, pl.ds(((1 - x) * 2 + y) * k, k)], second_in[g].at[d], g, R2 + d, across)

    def twin_step(g, d):
        to_twin(g, d).wait_recv()
        load(g, d).wait()
        add(g, d, 0, stage[g], slot(d), 0, 4 * groups[g].k)
        for copy in first_moves(g, d):
            copy.start()
        later = ORDER.index(d) + 2
        if later < len(ORDER):
            load(g, ORDER[later]).start()

    def first_step(g, d):
        k = groups[g].k
        for copy in first_moves(g, d):
            copy.wait_recv()
        if d in (0, 3):
            add(g, d, x * 2 * k, first_in[g], d, 0, 2 * k)
        else:
            add(g, d, y * k, first_in[g], d, 0, k)
            add(g, d, (2 + y) * k, first_in[g], d, k, k)
        second_move(g, d).start()

    def second_step(g, d):
        second_move(g, d).wait_recv()
        add(g, d, p * groups[g].k, second_in[g], d, 0, groups[g].k)

    def piece(g, d):
        return acc[g].at[d, pl.ds(p * groups[g].k, groups[g].k)]

    def to_down(g, d, zz):
        if d == zz - 1:
            return move(piece(g, d), line_extra[g].at[0], g, RZX, down)
        return move(piece(g, d), line_in[g].at[d], g, RZ + d, down)

    def to_up(g, d, zz):
        return move(piece(g, d), line_in[g].at[d], g, RZ + d, up)

    def rows_of(g, px, py, low=0, n=None):
        group = groups[g]
        return group.out.at[pl.ds(group.base + (c * 4 + px * 2 + py) * group.k + low, group.k if n is None else n)]

    def share_across(g):
        return move(piece(g, z), rows_of(g, x, y), g, RX, across)

    def share_beside(g):
        return move(piece(g, z), rows_of(g, x, y), g, RY, beside)

    def store(g):
        return pltpu.make_async_copy(piece(g, z), rows_of(g, x, y), store_sem.at[g])

    def arrived(g, px, py, kind):
        return move(rows_of(g, px, py), rows_of(g, px, py), g, kind, across)

    def corner(g, px, py, part):
        k = groups[g].k
        low, n = (0, max(k // 2, 1)) if part == 0 else (k // 2, k - k // 2)
        rows = rows_of(g, px, py, low, n)
        return move(rows, rows, g, RD1 if part == 0 else RD2, beside if part == 0 else across)

    def to_core(g, core):
        group = groups[g]
        rows = group.out.at[pl.ds(group.base + core * 4 * group.k, 4 * group.k)]
        return move(rows, rows, g, RCC, twin)

    def line_step(g, d, s):
        k = groups[g].k
        for zz in range(ZN):
            downward = d < zz and zz == ZN - 1 - s
            upward = d > zz and zz == s
            last = d == zz and s == ZN - 1
            if not (downward or upward or last):
                continue

            @pl.when(z == zz)
            def _():
                if downward:
                    if zz < ZN - 1:
                        to_down(g, d, zz + 1).wait_recv()
                        add(g, d, p * k, line_in[g], d, 0, k)
                    to_down(g, d, zz).start()
                if upward:
                    if zz > 0:
                        to_up(g, d, zz - 1).wait_recv()
                        add(g, d, p * k, line_in[g], d, 0, k)
                    to_up(g, d, zz).start()
                if last:
                    if zz > 0:
                        to_up(g, d, zz - 1).wait_recv()
                        add(g, d, p * k, line_in[g], d, 0, k)
                    if zz < ZN - 1:
                        to_down(g, d, zz + 1).wait_recv()
                        add(g, d, p * k, line_extra[g], 0, 0, k)
                    share_across(g).start()
                    share_beside(g).start()
                    store(g).start()

    def corner_step(g, d):
        @pl.when(z == d)
        def _():
            arrived(g, 1 - x, y, RX).wait_recv()
            corner(g, 1 - x, y, 0).start()
            arrived(g, x, 1 - y, RY).wait_recv()
            if groups[g].k > 1:
                corner(g, x, 1 - y, 1).start()

    def core_step(g, d):
        @pl.when(z == d)
        def _():
            store(g).wait()
            corner(g, 1 - x, 1 - y, 0).wait_recv()
            if groups[g].k > 1:
                corner(g, 1 - x, 1 - y, 1).wait_recv()
            to_core(g, c).start()

    def finish():
        for g, d in units:
            to_twin(g, d).wait_send()
            for copy in first_moves(g, d) + [second_move(g, d)]:
                copy.wait_send()
            for zz in range(ZN):
                if d == zz:
                    continue

                @pl.when(z == zz)
                def _():
                    (to_down(g, d, zz) if d < zz else to_up(g, d, zz)).wait_send()

            @pl.when(z == d)
            def _():
                to_core(g, 1 - c).wait_recv()
                share_across(g).wait_send()
                share_beside(g).wait_send()
                corner(g, 1 - x, y, 0).wait_send()
                if groups[g].k > 1:
                    corner(g, x, 1 - y, 1).wait_send()
                to_core(g, c).wait_send()

    count = len(units)
    stages = [(0, twin_step), (SKEW, first_step), (2 * SKEW, second_step)]
    stages += [((2 + s) * SKEW, functools.partial(line_step, s=s)) for s in range(ZN)]
    stages += [((2 + ZN) * SKEW, corner_step), ((3 + ZN) * SKEW, core_step)]

    def steps():
        for t in range(count + stages[-1][0]):
            for g, d in units[AHEAD + t - 1 : AHEAD + t] if t else units[:AHEAD]:
                yield groups[g].ready
                to_twin(g, d).start()
                if ORDER.index(d) < 2:
                    load(g, d).start()
            for delay, step in stages:
                if 0 <= t - delay < count:
                    step(*units[t - delay])
                    yield True

    return steps(), finish


def reduce_scratch(groups):
    low = jnp.bfloat16
    buffers = []
    for lead, rows in ((ZN, 4), (2, 4), (ZN, 2), (ZN, 1), (ZN, 1), (1, 1)):
        buffers += [pltpu.VMEM((lead, rows * k) + shape, low) for k, shape in groups]
    dma = pltpu.SemaphoreType.DMA
    n = len(groups)
    return buffers + [dma((n, 2)), dma((n,)), dma((n, 26)), dma((n, 26))]


def take_reduce(place, spec, grads, outs, refs, made_here=()):
    n = len(spec)
    groups = [Group(grads[m], outs[m], base, k, m if m in made_here else True) for m, base, k in spec]
    lists = [refs[i * n : (i + 1) * n] for i in range(6)]
    return reduce_steps(place, groups, *lists, *refs[6 * n : 6 * n + 4])


def spread_steps(work, comm, finish, pace):
    done = {True}
    blocked = None
    for made in work:
        done.add(made)
        for _ in range(pace):
            if blocked is not None and blocked not in done:
                break
            blocked = next(comm, True)
    for _ in comm:
        pass
    finish()


def ship_moves(place, source, target, local_sem, send_sem, recv_sem):
    x, y, z, c, across, beside, twin, up, down = place
    diag = (1 - x, z, y * 2 + (1 - c))
    top, low = pl.ds(0, BLOCK), pl.ds(BLOCK, BLOCK)

    def move(i, rows, device):
        return pltpu.make_async_remote_copy(
            src_ref=source.at[rows], dst_ref=target.at[rows], send_sem=send_sem.at[i], recv_sem=recv_sem.at[i],
            device_id=device, device_id_type=MESH,
        )

    stay = pltpu.make_async_copy(source.at[top], target.at[top], local_sem.at[0])

    def start():
        @pl.when(c == x)
        def _():
            stay.start()
            move(1, low, across).start()

        @pl.when(c != x)
        def _():
            move(0, top, diag).start()
            move(1, low, twin).start()

    def wait():
        @pl.when(c == x)
        def _():
            stay.wait()
            move(1, low, across).wait()

        @pl.when(c != x)
        def _():
            move(0, top, diag).wait()
            move(1, low, twin).wait()

    return start, wait


def ship_scratch():
    dma = pltpu.SemaphoreType.DMA
    return [dma((1,)), dma((2,)), dma((2,))]


def meet(ship):
    place = neighbours()
    x, y, z, c, across, beside, twin, up, down = place
    diag = (1 - x, z, y * 2 + (1 - c)) if ship else None
    greet(z, c, x, across, beside, twin, diag, up, down)
    return place


def spec_of(shapes, narrow, wide):
    spec = []
    for m, shape in enumerate(shapes):
        k = shape[1] // 8
        split = min(k, wide if shape[3] > 2048 else narrow)
        for base in range(0, k, split):
            spec.append((m, base * 8, split))
    return spec


def stream(source, buffer, sems, width_rows, act):
    chunks = source.shape[0]
    per = buffer.shape[1]
    whole, left = chunks // per, chunks % per

    def fetch(i, n):
        return pltpu.make_async_copy(
            source.at[pl.ds(i * per, n)], buffer.at[i % 2, pl.ds(0, n)], sems.at[i % 2]
        )

    def begin():
        fetch(0, per).start()

    def run(low, high):
        def step(i, carry):
            fetch(i, per).wait()

            @pl.when(i + 1 < whole)
            def _():
                fetch(i + 1, per).start()

            if left:

                @pl.when(i + 1 == whole)
                def _():
                    fetch(whole, left).start()

            act(pl.multiple_of(i * per * 16, per * 16), per * 16, buffer[i % 2].reshape(per * 16, -1))
            return carry

        if low < min(high, whole):
            lax.fori_loop(low, min(high, whole), step, 0)
        if high > whole and left:
            fetch(whole, left).wait()
            act(whole * per * 16, left * 16, buffer[whole % 2, :left].reshape(left * 16, -1))

    return begin, run, whole + (1 if left else 0)


def each(low, high, size):
    return [(at, min(at + size, high)) for at in range(low, high, size)]


def mlp_work(layer, ins, outs, refs, made_down):
    grad_in, middle_in, slope_in, normed_in, activated_in, gain, w_out, w_up, w_down = ins
    g_middle_out, g_branch_out, g_attended_out, dw_up, dw_down, gb_down, gb_up, g_gain, g_shift, gb_out = outs
    (
        grad, middle, g_norm, slope, g_mlp, g_branch, g_att, nm, turned,
        narrow, broad, act_tiles, down_tiles, up_tiles, load_sem, narrow_sem, broad_sem, act_sem, down_sem, up_sem,
    ) = refs
    width = grad.shape[1]
    ff = slope.shape[1]
    loads = [
        pltpu.make_async_copy(a, b, load_sem.at[i])
        for i, (a, b) in enumerate(((grad_in, g_mlp if grad_in.dtype == jnp.bfloat16 else grad), (middle_in, middle), (slope_in, slope), (normed_in, nm)))
    ]
    begin(loads)

    def down_act(start, size, rows):
        cols = pl.ds(start, size)
        g = (dot_nt(g_mlp[...], rows) * slope[:, cols].astype(jnp.float32)).astype(jnp.bfloat16)
        slope[:, cols] = g
        gb_up[:, cols] = jnp.sum(g.astype(jnp.float32), axis=0, keepdims=True)

    def up_act(start, size, rows):
        g_norm[:, pl.ds(start, size)] = dot_nt(slope[...], rows)

    def out_act(start, size, rows):
        g_att[:, pl.ds(start, size)] = dot_nt(g_branch[...], rows).astype(jnp.bfloat16)

    down_begin, down_run, down_n = stream(w_down.at[layer], narrow, narrow_sem, 0, down_act)
    up_begin, up_run, up_n = stream(w_up.at[layer], broad, broad_sem, 0, up_act)
    out_begin, out_run, out_n = stream(w_out.at[layer], narrow, narrow_sem, 0, out_act)
    down_begin()
    up_begin()
    loads[0].wait()
    if grad_in.dtype == jnp.bfloat16:
        grad[...] = g_mlp[...].astype(jnp.float32)
    else:
        g_mlp[...] = grad[...].astype(jnp.bfloat16)
    gb_down[...] = jnp.sum(g_mlp[...].astype(jnp.float32), axis=0, keepdims=True)
    yield
    tile = act_tiles.shape[2]

    def bring_act(i, n):
        return pltpu.make_async_copy(
            activated_in.at[:, pl.ds(pl.multiple_of(i * tile, tile), n)], act_tiles.at[i % 2, :, pl.ds(0, n)], act_sem.at[i % 2]
        )

    def send_down(i, n):
        return pltpu.make_async_copy(
            down_tiles.at[i % 2, pl.ds(0, n // 16)], dw_down.at[pl.ds(i * (tile // 16), n // 16)], down_sem.at[i % 2]
        )

    whole, left = ff // tile, ff % tile
    bring_act(0, tile).start()

    def down_grad(i, carry):
        bring_act(i, tile).wait()

        @pl.when(i + 1 < whole)
        def _():
            bring_act(i + 1, tile).start()

        if left:

            @pl.when(i + 1 == whole)
            def _():
                bring_act(whole, left).start()

        @pl.when(i >= 2)
        def _():
            send_down(i - 2, tile).wait()

        out = dot_tn(act_tiles[i % 2], g_mlp[...]).astype(jnp.bfloat16)
        down_tiles[i % 2] = out.reshape(tile // 16, 16, width)
        send_down(i, tile).start()
        return carry

    for low, high in each(0, whole, 4):
        lax.fori_loop(low, high, down_grad, 0)
        yield
    if left:
        bring_act(whole, left).wait()
        send_down(whole - 2, tile).wait()
        out = dot_tn(act_tiles[whole % 2, :, :left], g_mlp[...]).astype(jnp.bfloat16)
        down_tiles[whole % 2, : left // 16] = out.reshape(left // 16, 16, width)
        send_down(whole, left).start()
    send_down(whole - 1, tile).wait()
    if left:
        send_down(whole, left).wait()
    else:
        send_down(whole - 2, tile).wait()
    yield made_down

    loads[2].wait()
    for low, high in each(0, down_n, 2):
        down_run(low, high)
        yield
    out_begin()
    for low, high in each(0, up_n, 2):
        up_run(low, high)
        yield
    loads[1].wait()
    norm_back(middle, g_norm, grad, gain[...], grad, g_gain, g_shift, g_branch)
    saves = [pltpu.make_async_copy(grad, g_middle_out, load_sem.at[0]), pltpu.make_async_copy(g_branch, g_branch_out, load_sem.at[1])]
    begin(saves)
    gb_out[...] = jnp.sum(g_branch[...].astype(jnp.float32), axis=0, keepdims=True)
    yield
    out_run(0, out_n)
    saves.append(pltpu.make_async_copy(g_att, g_attended_out, load_sem.at[2]))
    begin(saves[2:])
    loads[3].wait()
    turned[...] = nm[...].T
    yield

    step = up_tiles.shape[3]

    def send_up(i):
        return pltpu.make_async_copy(
            up_tiles.at[i % 2], dw_up.at[:, :, pl.ds(pl.multiple_of(i * step, step), step)], up_sem.at[i % 2]
        )

    def up_grad(i, carry):
        @pl.when(i >= 2)
        def _():
            send_up(i - 2).wait()

        out = product(turned[...], slope[:, pl.ds(pl.multiple_of(i * step, step), step)]).astype(jnp.bfloat16)
        up_tiles[i % 2] = out.reshape(width // 16, 16, step)
        send_up(i).start()
        return carry

    for low, high in each(0, ff // step, 4):
        lax.fori_loop(low, high, up_grad, 0)
        yield
    send_up(ff // step - 2).wait()
    send_up(ff // step - 1).wait()
    end(saves)


def mlp_refs(rows, width, ff):
    low = jnp.bfloat16
    dma = pltpu.SemaphoreType.DMA
    return (
        [pltpu.VMEM((rows, width), jnp.float32)] * 3
        + [pltpu.VMEM((rows, ff), low)]
        + [pltpu.VMEM((rows, width), low)] * 4
        + [
            pltpu.VMEM((width, rows), low),
            pltpu.VMEM((2, 32, 16, width), low),
            pltpu.VMEM((2, 16, 16, ff), low),
            pltpu.VMEM((2, rows, 512), low),
            pltpu.VMEM((2, 32, 16, width), low),
            pltpu.VMEM((2, width // 16, 16, BLOCK), low),
            dma((4,)), dma((2,)), dma((2,)), dma((2,)), dma((2,)), dma((2,)),
        ]
    )


def attend_work(layer, place, ins, outs, refs):
    q_in, g_att_in, lse_in, mask_in, keys_in, values_in, x_in, g_middle_in, normed_in, attended_in, g_branch_in, gain, w_qkv = ins
    g_x_out, dw_qkv, dw_out, gb_q, gb_v, g_gain, g_shift = outs
    (
        q, g_att, lse, mask, keys, values, g_q, g_k, g_v, g_nat, got, xs, grad, g_norm, g_proj, turned,
        tall, tiles_qkv, tiles_out, load_sem, tall_sem, qkv_sem, out_sem, swap_send, swap_recv,
    ) = refs
    c, twin = place[3], place[6]
    width = xs.shape[1]
    pairs = (
        (q_in, q), (g_att_in, g_att), (lse_in, lse), (mask_in, mask), (keys_in, keys), (values_in, values),
        (x_in, xs), (g_middle_in, grad),
    )
    loads = [pltpu.make_async_copy(a, b, load_sem.at[i]) for i, (a, b) in enumerate(pairs)]
    begin(loads)

    def norm_act(start, size, rows):
        g_norm[:, pl.ds(start, size)] = dot_nt(g_proj[...], rows)

    tall_begin, tall_run, tall_n = stream(w_qkv.at[layer], tall, tall_sem, 0, norm_act)
    tall_begin()
    end(loads[:6])
    yield

    def slab(start, size, head):
        cols = pl.ds(start, size)
        g_k[...] = jnp.zeros_like(g_k)
        g_v[...] = jnp.zeros_like(g_v)
        lanes = slice(0, size)
        for variant in range(2):

            @pl.when(c == variant)
            def _():
                for row, high in RANGES[variant]:
                    rows = slice(row, row + BLOCK)
                    qs, gs = q[rows, cols], g_att[rows, cols]
                    ks, vs = keys[:high, cols], values[:high, cols]
                    parts = []
                    for j in range(size // HEAD_DIM):
                        q_j, g_j = of_head(qs, j), of_head(gs, j)
                        s = dot_nt(ks, q_j) + mask[:high, rows]
                        p = jnp.exp(s - lse[pl.ds(head + j, 1), rows])
                        g_p = p * dot_nt(vs, g_j)
                        inner = jnp.sum(g_p, axis=0, keepdims=True)
                        g_s = (g_p - p * inner).astype(jnp.bfloat16)
                        g_v[:high, lanes] += product(p.astype(jnp.bfloat16), g_j)
                        g_k[:high, lanes] += product(g_s, q_j)
                        parts.append(dot_tn(ks, g_s)[j * HEAD_DIM : (j + 1) * HEAD_DIM])
                    out = jnp.concatenate(parts, axis=0) if len(parts) > 1 else parts[0]
                    g_q[rows, cols] = out.T.astype(jnp.bfloat16) * QUERY_SCALE

        g_nat[0, :, cols] = g_k[:, lanes].astype(jnp.bfloat16)
        g_nat[1, :, cols] = g_v[:, lanes].astype(jnp.bfloat16)

    slab_count = width // (2 * HEAD_DIM) + 1
    for first, last in each(0, slab_count, 2):
        over_slabs(width, slab, first, last)
        yield

    def spot(who, block):
        at = ((2 * who) if block == 0 else (3 - 2 * who)) * BLOCK
        return pl.ds(pl.multiple_of(at, BLOCK), BLOCK)

    swaps = [
        pltpu.make_async_remote_copy(
            src_ref=g_nat.at[i, spot(1 - c, block)], dst_ref=got.at[i, pl.ds(block * BLOCK, BLOCK)],
            send_sem=swap_send.at[i, block], recv_sem=swap_recv.at[i, block], device_id=twin, device_id_type=MESH,
        )
        for i in range(2)
        for block in range(2)
    ]
    begin(swaps)
    more = [
        pltpu.make_async_copy(attended_in, q, load_sem.at[0]),
        pltpu.make_async_copy(g_branch_in, g_att, load_sem.at[1]),
    ]
    begin(more)
    g_proj[:, :width] = g_q[...]
    gb_q[...] = jnp.sum(g_q[...].astype(jnp.float32), axis=0, keepdims=True)
    yield
    end(more)
    turned[...] = q[...].T
    rows = tiles_out.shape[1] * 16

    def row_grad(right, tiles_ref, sem, target, i):
        def act(start, size):
            cols = pl.ds(start, size)
            out = product(turned[pl.ds(i * rows, rows), :], right[:, cols]).astype(jnp.bfloat16)
            tiles_ref[i % 2, :, :, cols] = out.reshape(rows // 16, 16, size)

        if i >= 2:
            row_send(tiles_ref, sem, target, i - 2).wait()
        tiles_between(0, right.shape[1], TILE, act)
        row_send(tiles_ref, sem, target, i).start()

    def row_send(tiles_ref, sem, target, i):
        return pltpu.make_async_copy(tiles_ref.at[i % 2], target.at[pl.ds(i * (rows // 16), rows // 16)], sem.at[i % 2])

    for i in range(ZN):
        row_grad(g_att, tiles_out, out_sem, dw_out, i)
    yield
    after = pltpu.make_async_copy(normed_in, q, load_sem.at[0])
    after.start()
    for copy in swaps:
        copy.wait_recv()
    for block in range(2):
        part = slice(block * BLOCK, (block + 1) * BLOCK)
        g_proj[part, width : 2 * width] = g_nat[0, spot(c, block), :] + got[0, part, :]
        values_part = g_nat[1, spot(c, block), :] + got[1, part, :]
        g_proj[part, 2 * width :] = values_part
        total = jnp.sum(values_part.astype(jnp.float32), axis=0, keepdims=True)
        gb_v[...] = total if block == 0 else gb_v[...] + total
    yield
    for low, high in each(0, tall_n, 2):
        tall_run(low, high)
        yield
    end(loads[6:])
    norm_back(xs, g_norm, grad, gain[...], grad, g_gain, g_shift)
    if g_x_out.dtype == jnp.bfloat16:
        g_att[...] = grad[...].astype(jnp.bfloat16)
        save = pltpu.make_async_copy(g_att, g_x_out, load_sem.at[1])
    else:
        save = pltpu.make_async_copy(grad, g_x_out, load_sem.at[1])
    save.start()
    after.wait()
    turned[...] = q[...].T
    yield
    for i in range(ZN):
        row_grad(g_proj, tiles_qkv, qkv_sem, dw_qkv, i)
        yield
    for i in (ZN - 2, ZN - 1):
        row_send(tiles_out, out_sem, dw_out, i).wait()
        row_send(tiles_qkv, qkv_sem, dw_qkv, i).wait()
    for copy in swaps:
        copy.wait_send()
    save.wait()


def attend_refs(rows, width):
    low = jnp.bfloat16
    dma = pltpu.SemaphoreType.DMA
    share = width // 16 // ZN
    return [
        pltpu.VMEM((rows, width), low),
        pltpu.VMEM((rows, width), low),
        pltpu.VMEM((HEAD_ROWS, rows), jnp.float32),
        pltpu.VMEM((2 * rows, rows), jnp.float32),
        pltpu.VMEM((2 * rows, width), low),
        pltpu.VMEM((2 * rows, width), low),
        pltpu.VMEM((rows, width), low),
        pltpu.VMEM((2 * rows, 2 * HEAD_DIM), jnp.float32),
        pltpu.VMEM((2 * rows, 2 * HEAD_DIM), jnp.float32),
        pltpu.VMEM((2, 2 * rows, width), low),
        pltpu.VMEM((2, rows, width), low),
        pltpu.VMEM((rows, width), jnp.float32),
        pltpu.VMEM((rows, width), jnp.float32),
        pltpu.VMEM((rows, width), jnp.float32),
        pltpu.VMEM((rows, 3 * width), low),
        pltpu.VMEM((width, rows), low),
        pltpu.VMEM((2, 16, 16, 3 * width), low),
        pltpu.VMEM((2, share, 16, 3 * width), low),
        pltpu.VMEM((2, share, 16, width), low),
        dma((8,)), dma((2,)), dma((2,)), dma((2,)), dma((2, 2)), dma((2, 2)),
    ]


def mlp_kernel(layer, grad, kept, gain, fulls, grads):
    rows, width = grad.shape
    ff = kept["slope"].shape[1]
    low = jnp.bfloat16
    ins = [grad, kept["middle"], kept["slope"], kept["normed_mlp"], kept["activated"], gain, fulls[1], fulls[2], fulls[3]]
    down_shape = (ZN, ff // 16 // ZN, 16, width)
    work_out = [
        shaped((rows, width)),
        shaped((rows, width), low),
        shaped((rows, width), low),
        shaped((width // 16, 16, ff), low),
        shaped((ff // 16, 16, width), low),
    ] + [shaped((1, n)) for n in (width, ff, width, width, width)]
    work_refs = mlp_refs(rows, width, ff)
    n, extra = len(work_out), len(grads)
    shapes = [g.shape for g in grads] + [down_shape]
    spec = spec_of(shapes, 4, 2)

    def body(*refs):
        i = len(ins) + extra
        outs, more = refs[i : i + n], refs[i + n : i + n + extra + 1]
        rest = refs[i + n + extra + 1 :]
        place = meet(False)
        down_rows = Rows(outs[4], down_shape[1])
        comm, finish = take_reduce(
            place, spec, list(refs[len(ins) : i]) + [down_rows], more, rest[len(work_refs) :], (extra,)
        )
        work = mlp_work(layer, refs[: len(ins)], outs, rest[: len(work_refs)], extra)
        spread_steps(work, comm, finish, 6 if extra else 3)

    outs = pl.pallas_call(
        body,
        out_shape=work_out + [shaped(shape[1:], low) for shape in shapes],
        in_specs=anywhere(5) + whole(1) + anywhere(3 + extra),
        out_specs=anywhere(5) + whole(5) + anywhere(extra + 1),
        scratch_shapes=work_refs + reduce_scratch([(k, shapes[m][2:]) for m, _, k in spec]),
        compiler_params=pltpu.CompilerParams(
            collective_id=100 + layer, has_side_effects=True, vmem_limit_bytes=VMEM_LIMIT
        ),
        name="mlp_back",
    )(*ins, *grads)
    return outs[:n], outs[n:]


class Rows:
    def __init__(self, ref, n):
        self.ref, self.n, self.at = ref, n, self

    def __getitem__(self, where):
        d, chunks = where
        return self.ref.at[pl.ds(d * self.n + chunks.start, chunks.size)]


def attend_kernel(layer, kept, mask, g_att, g_middle, g_branch, gain, fulls, grads, ship):
    rows, width = g_middle.shape
    low = jnp.bfloat16
    ins = [
        kept["q"], g_att, kept["lse"], mask, kept["keys"], kept["values"], kept["x"], g_middle,
        kept["normed_attn"], kept["attended"], g_branch, gain, fulls[0],
    ]
    work_out = [
        shaped((rows, width), jnp.float32 if layer else low),
        shaped((width // 16, 16, 3 * width), low),
        shaped((width // 16, 16, width), low),
    ] + [shaped((1, width))] * 4
    work_refs = attend_refs(rows, width)
    ships = [ship] if ship is not None else []
    n, extra, k = len(work_out), len(grads), len(ships)
    spec = spec_of([g.shape for g in grads], 2, 1)
    buffers = reduce_scratch([(depth, grads[m].shape[2:]) for m, _, depth in spec])

    def body(*refs):
        i = len(ins) + extra + k
        outs, more = refs[i : i + n], refs[i + n : i + n + extra]
        rest = refs[i + n + extra + k :]
        place = meet(bool(k))
        if k:
            start, wait = ship_moves(place, refs[i - 1], refs[i + n + extra], *rest[-3:])
            start()
        comm, finish = take_reduce(place, spec, refs[len(ins) : i - k], more, rest[len(work_refs) :])
        work = attend_work(layer, place, refs[: len(ins)], outs, rest[: len(work_refs)])
        spread_steps(work, comm, finish, 6)
        if k:
            wait()

    outs = pl.pallas_call(
        body,
        out_shape=work_out + [shaped(g.shape[1:], low) for g in grads] + [shaped(v.shape, v.dtype) for v in ships],
        in_specs=anywhere(11) + whole(1) + anywhere(1 + extra + k),
        out_specs=anywhere(3) + whole(4) + anywhere(extra + k),
        scratch_shapes=work_refs + buffers + (ship_scratch() if k else []),
        compiler_params=pltpu.CompilerParams(
            collective_id=200 + layer, has_side_effects=True, vmem_limit_bytes=VMEM_LIMIT
        ),
        name="attend_back",
    )(*ins, *grads, *ships)
    return outs[:n], outs[n : n + extra], outs[n + extra :]


def reduce_kernel(grads, ship):
    extra = len(grads)
    spec = spec_of([g.shape for g in grads], 2, 1)

    def body(*refs):
        place = meet(True)
        rest = refs[2 * extra + 2 :]
        start, wait = ship_moves(place, refs[extra], refs[2 * extra + 1], *rest[-3:])
        start()
        comm, finish = take_reduce(place, spec, refs[:extra], refs[extra + 1 : 2 * extra + 1], rest)
        spread_steps((), comm, finish, 1)
        wait()

    outs = pl.pallas_call(
        body,
        out_shape=[shaped(g.shape[1:], g.dtype) for g in grads] + [shaped(ship.shape, ship.dtype)],
        in_specs=anywhere(extra + 1),
        out_specs=anywhere(extra + 1),
        scratch_shapes=reduce_scratch([(k, grads[m].shape[2:]) for m, _, k in spec]) + ship_scratch(),
        compiler_params=pltpu.CompilerParams(collective_id=2, has_side_effects=True, vmem_limit_bytes=VMEM_LIMIT),
        name="reduce_grads",
    )(*grads, ship)
    return outs[:extra], outs[extra]


def assemble_body(layers, *refs):
    ins = [refs[layer * 5 : (layer + 1) * 5] for layer in range(layers)]
    outs = refs[layers * 5 : layers * 5 + 4]
    vectors = refs[layers * 5 + 4 : layers * 5 + 13]
    rest = refs[layers * 5 + 13 :]
    held, made = rest[:5], rest[5:9]
    in_sem, out_sem = rest[9:]
    width = held[4].shape[3]
    loads, stores = [], []
    for layer in range(layers):
        loads.append(
            [pltpu.make_async_copy(ins[layer][m], held[m].at[layer], in_sem.at[layer, m]) for m in range(5)]
        )
        begin(loads[-1])
    for layer in range(layers):
        loads[layer][4].wait()
        piece = 0
        for m in range(4):
            loads[layer][m].wait()
            n = held[m].shape[1]
            whole_n = n // 8 * 8
            if layer:
                stores[m].wait()

            def widen(i, carry, m=m):
                made[m][i] = held[m][layer, i].astype(jnp.float32)
                return carry

            lax.fori_loop(0, whole_n, widen, 0)
            for i in range(whole_n, n):
                for at in range(0, held[m].shape[3], width):
                    made[m][i, :, at : at + width] = held[4][layer, piece].astype(jnp.float32)
                    piece += 1
            copy = pltpu.make_async_copy(made[m], outs[m].at[layer], out_sem.at[layer, m])
            copy.start()
            if layer:
                stores[m] = copy
            else:
                stores.append(copy)
        flat = held[4][layer, piece].astype(jnp.float32)
        at = 0
        for ref in vectors:
            n = ref.shape[1]
            ref[layer : layer + 1, :] = flat[at // width : at // width + 1, at % width : at % width + n]
            at += n
    for copy in stores:
        copy.wait()


def assemble(reduced, vector_sizes):
    layers = len(reduced)
    low = jnp.bfloat16
    shapes = [r.shape for r in reduced[0]]
    dma = pltpu.SemaphoreType.DMA
    outs = pl.pallas_call(
        functools.partial(assemble_body, layers),
        out_shape=[shaped((layers,) + shape) for shape in shapes[:4]] + [shaped((layers, n)) for n in vector_sizes],
        in_specs=anywhere(5 * layers),
        out_specs=anywhere(4) + whole(len(vector_sizes)),
        scratch_shapes=[pltpu.VMEM((layers,) + shape, low) for shape in shapes]
        + [pltpu.VMEM(shape, jnp.float32) for shape in shapes[:4]]
        + [dma((layers, 5)), dma((layers, 4))],
        compiler_params=params(),
        name="assemble",
    )(*[r for entry in reduced for r in entry])
    return outs[:4], outs[4:]


VECTORS = (0, 1, 3, 4, 6, 7, 8, 12, 10)
MATRICES = (2, 5, 9, 11)


def wide_of(weight_grads, vector_grads):
    width = weight_grads[0].shape[3]

    def pieces(g):
        left = g[:, g.shape[1] // 8 * 8 :]
        parts = left.shape[3] // width
        return jnp.swapaxes(left.reshape(ZN, left.shape[1], 16, parts, width), 2, 3).reshape(ZN, -1, 16, width)

    vectors = jnp.concatenate([g.reshape(ZN, -1) for g in vector_grads], axis=1).astype(jnp.bfloat16)
    vectors = vectors.reshape(ZN, 1, -1, width)
    vectors = jnp.pad(vectors, ((0, 0), (0, 0), (0, 16 - vectors.shape[2]), (0, 0)))
    wide = jnp.concatenate([pieces(g) for g in weight_grads] + [vectors], axis=1)
    return jnp.pad(wide, ((0, 0), (0, -wide.shape[1] % 8), (0, 0), (0, 0)))


def on_cores(tokens, segments, grad_out, *params):
    rows, width = tokens.shape[1:]
    layers = params[0].shape[0]
    weights = [params[i].reshape(layers, -1, 16, params[i].shape[2]) for i in MATRICES]
    vectors = jnp.concatenate([params[i].reshape(layers, -1, params[0].shape[1]) for i in VECTORS], axis=1)
    vectors = jnp.pad(vectors, ((0, 0), (0, 16 - vectors.shape[1]), (0, 0)))[:, None]
    fulls, result, grad, mask, vector_rows, saved = forward(tokens[0], grad_out[0], segments, vectors, weights)
    fulls = [full.reshape(layers, -1, 16, full.shape[4]) for full in fulls]
    reduced = [None] * layers
    waiting = []
    ship = result
    for layer in reversed(range(layers)):
        kept = saved[layer]
        attn_gain, mlp_gain = vector_rows[layer, 0:1], vector_rows[layer, 5:6]
        (g_middle, g_branch, g_att, dw_up, dw_down, gb_down, gb_up, gm_gain, gm_shift, gb_out), sums = mlp_kernel(
            layer, grad, kept, mlp_gain, fulls, waiting
        )
        if waiting:
            reduced[layer + 1].extend(sums[:-1])
        reduced[layer] = [sums[-1]]
        dw_up, dw_down = dw_up.reshape(ZN, -1, 16, dw_up.shape[2]), dw_down.reshape(ZN, -1, 16, width)
        (grad, dw_qkv, dw_out, gb_q, gb_v, ga_gain, ga_shift), sums, shipped = attend_kernel(
            layer, kept, mask, g_att, g_middle, g_branch, attn_gain, fulls, [dw_up], ship
        )
        if ship is not None:
            result, ship = shipped[0], None
        reduced[layer].extend(sums)
        waiting = [dw.reshape(ZN, -1, 16, dw.shape[2]) for dw in (dw_out, dw_qkv)]
        vector_grads = (ga_gain, ga_shift, gb_q, gb_v, gb_out, gm_gain, gm_shift, gb_down, gb_up)
        waiting.append(wide_of([dw_down, dw_up] + waiting, vector_grads))
    sums, grad = reduce_kernel(waiting, grad)
    reduced[0].extend(sums)
    (down, up, out, qkv), vector_outs = assemble(reduced, [params[i].shape[1] for i in VECTORS])
    final = [None] * 13
    for i, value in ((11, down), (9, up), (5, out), (2, qkv)):
        final[i] = value.reshape(layers, -1, value.shape[3])
    for i, value in zip(VECTORS, vector_outs):
        final[i] = value
    return (result[None], grad[None], *final)


def on_device(
    tokens,
    segments,
    grad_out,
    attn_gain,
    attn_shift,
    w_qkv,
    b_query,
    b_value,
    w_out,
    b_out,
    mlp_gain,
    mlp_shift,
    w_up,
    b_up,
    w_down,
    b_down,
):
    seg_own = segments[0]
    seg_all = lax.all_gather(seg_own, "seq", axis=0, tiled=True)
    offset = lax.axis_index("seq") * seg_own.shape[0]
    visible = visible_mask(seg_own, seg_all, offset)
    layer_count = attn_gain.shape[0]
    resid = tokens[0].astype(jnp.float32)
    kept_weights = []
    stored_list = []
    for layer_index in range(layer_count):
        gathered = gather_layer(
            layer_index,
            attn_gain,
            attn_shift,
            w_qkv,
            b_query,
            b_value,
            w_out,
            b_out,
            mlp_gain,
            mlp_shift,
            w_up,
            b_up,
            w_down,
            b_down,
        )
        resid, stored = forward_layer(resid, gathered, visible, Halves())
        kept_weights.append(gathered)
        stored_list.append(stored)
    result = resid.astype(jnp.bfloat16)[None]
    grad_resid = grad_out[0].astype(jnp.float32)
    reduced = [None] * layer_count
    for layer_index in reversed(range(layer_count)):
        gathered = gather_again(
            layer_index,
            attn_gain,
            attn_shift,
            w_qkv,
            b_query,
            b_value,
            w_out,
            b_out,
            mlp_gain,
            mlp_shift,
            w_up,
            b_up,
            w_down,
            b_down,
        )
        grad_resid, gradients = backward_layer(
            grad_resid, stored_list[layer_index], gathered, visible, Halves()
        )
        reduced[layer_index] = reduce_grads(gradients)
    stacked = tuple((jnp.stack([entry[member] for entry in reduced]) for member in range(13)))
    return (result, grad_resid.astype(jnp.bfloat16)[None]) + stacked


def solution(mesh):
    fits = (mesh.shape["seq"], mesh.shape["fsdp"], mesh.shape["rep"]) == (2, ZN, 4)
    return jax.shard_map(
        on_cores if fits else on_device,
        mesh=mesh,
        in_specs=(
            P(("fsdp", "rep"), "seq", None),
            P(("fsdp", "rep"), "seq"),
            P(("fsdp", "rep"), "seq", None),
            P(None, "fsdp"),
            P(None, "fsdp"),
            P(None, "fsdp", None),
            P(None, "fsdp"),
            P(None, "fsdp"),
            P(None, "fsdp", None),
            P(None, "fsdp"),
            P(None, "fsdp"),
            P(None, "fsdp"),
            P(None, "fsdp", None),
            P(None, "fsdp"),
            P(None, "fsdp", None),
            P(None, "fsdp"),
        ),
        out_specs=(
            P(("fsdp", "rep"), "seq", None),
            P(("fsdp", "rep"), "seq", None),
            P(None, "fsdp"),
            P(None, "fsdp"),
            P(None, "fsdp", None),
            P(None, "fsdp"),
            P(None, "fsdp"),
            P(None, "fsdp", None),
            P(None, "fsdp"),
            P(None, "fsdp"),
            P(None, "fsdp"),
            P(None, "fsdp", None),
            P(None, "fsdp"),
            P(None, "fsdp", None),
            P(None, "fsdp"),
        ),
        check_vma=False,
    )
```
